128 devices in a mesh: section: 4 (over x_hi, core), dp: 16 (over y, z), tensor: 2 (over x_lo).
Axes of the slice: x: 4 (x_hi: 2, x_lo: 2; x = x_hi * 2 + x_lo), y: 4, z: 4, core: 2. Of those that a mesh axis runs over, the one named last changes fastest.
Arguments:
- inputs: bfloat16 [32, 866, 768], P('dp'), may hold values from -6 to 6
- cotangent: bfloat16 [32, 866, 768], P('dp'), may hold values from -6 to 6
- norm_gain: float32 [4, 768], P('section'), may hold values from 0.1 to 1.9
- norm_bias: float32 [4, 768], P('section'), may hold values from -1.5 to 1.5
- qkv_weight: bfloat16 [4, 3, 768, 768], P('section', None, None, 'tensor'), may hold values from -0.21875 to 0.21875
- qv_bias: float32 [4, 2, 768], P('section', None, 'tensor'), may hold values from -1.5 to 1.5
- out_weight: bfloat16 [4, 768, 768], P('section', 'tensor'), may hold values from -0.4375 to 0.4375
- end_bias: float32 [4, 768], P('section'), may hold values from -1.5 to 1.5
- up_weight: bfloat16 [4, 768, 3072], P('section', None, 'tensor'), may hold values from -0.21875 to 0.21875
- up_bias: float32 [4, 3072], P('section', 'tensor'), may hold values from -1.5 to 1.5
- down_weight: bfloat16 [4, 3072, 768], P('section', 'tensor'), may hold values from -0.109375 to 0.109375
Outputs:
- hidden_states: float32 [4, 32, 866, 768], P('section', 'dp')
- input_grads: float32 [4, 32, 866, 768], P('section', 'dp')
- norm_gain_grad: float32 [4, 768], P('section', 'dp')
- norm_bias_grad: float32 [4, 768], P('section', 'dp')
- qkv_weight_grad: float32 [4, 3, 768, 768], P('section', None, 'dp', 'tensor')
- qv_bias_grad: float32 [4, 2, 768], P('section', None, 'tensor')
- out_weight_grad: float32 [4, 768, 768], P('section', 'tensor', 'dp')
- end_bias_grad: float32 [4, 768], P('section', 'dp')
- up_weight_grad: float32 [4, 768, 3072], P('section', 'dp', 'tensor')
- up_bias_grad: float32 [4, 3072], P('section', 'tensor')
- down_weight_grad: float32 [4, 3072, 768], P('section', 'tensor', 'dp')
The draws below stay inside these ranges and needn't reach their ends.
All inputs are finite; a program needn't handle non-finite values.
Results may differ from the reference program's by a relative error of at most 0.013.
Values sent between devices are 32-bit elements; how exact they have to be, the bound alone decides.
A program may use at most 384 MiB of HBM per device.

```python
import math
import jax
import jax.numpy as jnp
from jax import lax

HEADS = 12
HEAD_DIM = 64
FF = 3072
D = 768
LENGTH = 866
SECTIONS = 4
CLIPS = 32
N_TENSOR = 2


def steps_of(own_key, extent, split, low, largest):
    def one(dim, shards_of):
        draws = jax.random.uniform(jax.random.fold_in(jax.random.fold_in(own_key, 6), dim), (shards_of,), jnp.float32, low / len(split), largest / len(split))
        return jnp.repeat(jnp.exp(draws), extent[dim] // shards_of).reshape((-1,) + (1,) * (len(extent) - dim - 1))

    factor_of = one(*split[0])
    for cut in split[1:]:
        factor_of = factor_of * one(*cut)
    return factor_of


def scatter_about(own_key, extent, scale, most, cuts=(), held_as=jnp.bfloat16):
    entries = scale * jax.random.normal(own_key, extent, jnp.float32)
    if cuts:
        entries = entries * steps_of(own_key, extent, cuts, -0.22, 0.18)
    return jnp.clip(entries, -most, most).astype(held_as)


def setup_inputs(seed: int = 0) -> dict:
    key_list = jax.random.split(jax.random.key(seed), 12)
    return {
        "inputs": scatter_about(key_list[0], (CLIPS, LENGTH, D), 1.0, 6.0, ((0, 16),)),
        "cotangent": scatter_about(key_list[1], (CLIPS, LENGTH, D), 1.0, 6.0, ((0, 16),)),
        "norm_gain": jnp.clip(1.0 + 0.18 * jax.random.normal(key_list[2], (SECTIONS, D), jnp.float32), 0.1, 1.9),
        "norm_bias": scatter_about(key_list[3], (SECTIONS, D), 0.25, 1.5, ((0, 4),), jnp.float32),
        "qkv_weight": scatter_about(key_list[4], (SECTIONS, 3, D, D), D ** -0.5, 0.21875, ((0, 4), (3, 2))),
        "qv_bias": scatter_about(key_list[5], (SECTIONS, 2, D), 0.25, 1.5, ((0, 4), (2, 2)), jnp.float32),
        "out_weight": scatter_about(key_list[6], (SECTIONS, D, D), (D // 4) ** -0.5, 0.4375, ((0, 4), (1, 2))),
        "end_bias": scatter_about(key_list[7], (SECTIONS, D), 0.25, 1.5, ((0, 4),), jnp.float32),
        "up_weight": scatter_about(key_list[8], (SECTIONS, D, FF), D ** -0.5, 0.21875, ((0, 4), (2, 2))),
        "up_bias": scatter_about(key_list[9], (SECTIONS, FF), 0.25, 1.5, ((0, 4), (1, 2)), jnp.float32),
        "down_weight": scatter_about(key_list[10], (SECTIONS, FF, D), FF ** -0.5, 0.109375, ((0, 4), (1, 2))),
    }


@jax.custom_vjp
def low(v):
    return lax.optimization_barrier(v.astype(jnp.bfloat16)).astype(jnp.float32)

@jax.custom_vjp
def low_back(v):
    return v

def low_keep(v):
    return (low(v), None)

def low_pass(kept, grad):
    return (grad,)

def back_keep(v):
    return (v, None)

def back_low(kept, grad):
    return (low(grad),)
low.defvjp(low_keep, low_pass)
low_back.defvjp(back_keep, back_low)
layer_eps = 1e-06

def matmul(left, right):
    return jnp.dot(left, right, precision=lax.Precision.HIGHEST)

def layer_norm(inputs, scale_gain, shift_bias):
    average = lax.optimization_barrier(jnp.mean(inputs, axis=-1, keepdims=True))
    centred = inputs - average
    spread = lax.optimization_barrier(jnp.mean(centred * centred, axis=-1, keepdims=True))
    return centred * lax.rsqrt(spread + layer_eps) * scale_gain + shift_bias

def device_sum(left, right):
    length = left.shape[0]
    inner_width = left.shape[1] // N_TENSOR
    pieces = left.reshape(length, N_TENSOR, inner_width).transpose(1, 0, 2)
    blocks = right.reshape(N_TENSOR, inner_width, right.shape[1])
    partial_sums = jnp.einsum('pli,pid->pld', pieces, blocks, precision=lax.Precision.HIGHEST)
    return lax.optimization_barrier(jnp.sum(partial_sums, axis=0))

def attention(queries, key_rows, value_rows):
    length = queries.shape[0]
    factor = 1.0 / math.sqrt(HEAD_DIM)
    query_heads = queries.reshape(length, HEADS, HEAD_DIM)
    key_heads = key_rows.reshape(length, HEADS, HEAD_DIM)
    value_heads = value_rows.reshape(length, HEADS, HEAD_DIM)
    scores = low_back(jnp.einsum('qhd,khd->hqk', query_heads, key_heads, precision=lax.Precision.HIGHEST) * factor)
    row_max = lax.optimization_barrier(jnp.max(scores, axis=-1, keepdims=True))
    exponent = jnp.exp(scores - row_max)
    attn_weights = low(exponent / lax.optimization_barrier(jnp.sum(exponent, axis=-1, keepdims=True)))
    mixed_rows = jnp.einsum('hqk,khd->qhd', attn_weights, value_heads, precision=lax.Precision.HIGHEST)
    return mixed_rows.reshape(length, HEADS * HEAD_DIM)

def attention_layer(hidden, gain, shift, qkv_weight, qv_bias, out_weight, end_bias):
    normed = low(layer_norm(hidden, gain, shift))
    queries = low_back(low(matmul(normed, qkv_weight[0]) + qv_bias[0]))
    key_rows = low_back(low(matmul(normed, qkv_weight[1])))
    value_rows = low_back(low(matmul(normed, qkv_weight[2]) + qv_bias[1]))
    mixed_rows = low_back(low(attention(queries, key_rows, value_rows)))
    return low_back(device_sum(mixed_rows, out_weight) + end_bias)

def feed_layer(hidden, gain, shift, up_weight, up_bias, down_weight, end_bias):
    normed = low(layer_norm(hidden, gain, shift))
    raised = low_back(matmul(normed, up_weight) + up_bias)
    activated = low(jax.nn.gelu(raised, approximate=False))
    return low_back(device_sum(activated, down_weight) + end_bias)

def forward(clip_rows, perturb, params):
    norm_gain, norm_bias, qkv_weight, qv_bias, out_weight, end_bias, up_weight, up_bias, down_weight = params
    states = []
    hidden = clip_rows
    for section in range(SECTIONS):
        hidden = hidden + perturb[section]
        if section % 2 == 0:
            branch = attention_layer(hidden, norm_gain[section], norm_bias[section], qkv_weight[section], qv_bias[section], out_weight[section], end_bias[section])
        else:
            branch = feed_layer(hidden, norm_gain[section], norm_bias[section], up_weight[section], up_bias[section], down_weight[section], end_bias[section])
        hidden = hidden + branch
        states.append(hidden)
    return jnp.stack(states)

def reference(inputs, cotangent, norm_gain, norm_bias, qkv_weight, qv_bias, out_weight, end_bias, up_weight, up_bias, down_weight):
    params = tuple((argument.astype(jnp.float32) for argument in (norm_gain, norm_bias, qkv_weight, qv_bias, out_weight, end_bias, up_weight, up_bias, down_weight)))

    def per_clip(totals, clip_data):
        clip_in, clip_grad = clip_data
        no_shift = jnp.zeros((SECTIONS,) + clip_in.shape, jnp.float32)
        states, pullback = jax.vjp(forward, clip_in.astype(jnp.float32), no_shift, params)
        cotangents = jnp.zeros_like(states).at[SECTIONS - 1].set(clip_grad.astype(jnp.float32))
        grad_clip, grad_perturb, grad_params = pullback(cotangents)
        totals = jax.tree.map(jnp.add, totals, grad_params)
        return (totals, (states, grad_perturb))
    initial = tuple((jnp.zeros_like(argument) for argument in params))
    totals, (states, perturb_grads) = lax.scan(per_clip, initial, (inputs, cotangent))
    hidden_states = jnp.transpose(states, (1, 0, 2, 3))
    input_grads = jnp.transpose(perturb_grads, (1, 0, 2, 3))
    return (hidden_states, input_grads, totals[0], totals[1], totals[2], totals[3], totals[4], totals[5], totals[6], totals[7], totals[8])
```

```python
import functools

import jax
import jax.numpy as jnp
from jax import lax
from jax.experimental import pallas as pl
from jax.experimental.pallas import tpu as pltpu
from jax.sharding import PartitionSpec as P

MESH = pl.DeviceIdType.MESH
ANY = pl.ANY
F32 = jnp.float32
BF16 = jnp.bfloat16

HEAD_DIM = 64
EPS = 1e-06
LENGTH = 866
ROWS = 896
BLOCK = 224
D = 768
PAIRS = 6
Q_BLOCKS = ((0, 256), (256, 256), (512, 384))
VMEM_BYTES = 60 * 1024 * 1024

CHUNK = 768


def call(body, out_shape, in_specs, out_specs, grid=(), scratch=(), flops=0, moved=0, **more):
    return pl.pallas_call(
        body,
        out_shape=out_shape,
        grid=grid,
        in_specs=in_specs,
        out_specs=out_specs,
        scratch_shapes=scratch,
        cost_estimate=pl.CostEstimate(flops=flops, bytes_accessed=moved, transcendentals=0),
        compiler_params=pltpu.CompilerParams(vmem_limit_bytes=VMEM_BYTES, **more),
    )


def shape(dims, dtype):
    return jax.ShapeDtypeStruct(dims, dtype)


def whole(*dims):
    return pl.BlockSpec(dims, lambda *_: (0,) * len(dims), pipeline_mode=pl.Buffered(1))


def rows_of(width):
    return pl.BlockSpec((BLOCK, width), lambda i: (i, 0))


def dot(a, b, ca=1, cb=0):
    return lax.dot_general(a, b, (((ca,), (cb,)), ((), ())), preferred_element_type=F32)


def normalized(h):
    average = jnp.mean(h, axis=-1, keepdims=True)
    centred = h - average
    spread = jnp.mean(centred * centred, axis=-1, keepdims=True)
    r = lax.rsqrt(spread + EPS)
    return centred * r, r


def norm_back(g, h, gain, grad_normed):
    xhat, r = normalized(h)
    t = grad_normed * gain
    t_mean = jnp.mean(t, axis=-1, keepdims=True)
    tx_mean = jnp.mean(t * xhat, axis=-1, keepdims=True)
    return g + r * (t - t_mean - xhat * tx_mean), xhat


def add_rows(vec_ref, rows, first):
    @pl.when(first)
    def _():
        vec_ref[...] = jnp.zeros_like(vec_ref)

    for at, values in rows:
        vec_ref[at : at + 1, :] += jnp.sum(values, axis=0, keepdims=True)


def ff_forward_body(h_ref, gain_ref, shift_ref, up_ref, upb_ref, down_ref, end_ref,
                    out_ref, act_ref, slope_ref, normed_ref):
    h = h_ref[...]
    xhat, _ = normalized(h)
    normed = (xhat * gain_ref[...] + shift_ref[...]).astype(BF16)
    normed_ref[...] = normed
    total = h + end_ref[...]
    for c in range(0, 3072, 512):
        cols = slice(c, c + 512)
        x = dot(normed, up_ref[:, cols]) + upb_ref[:, cols]
        phi = 0.5 * (1.0 + lax.erf(x * 0.7071067811865476))
        density = jnp.exp(-0.5 * x * x) * 0.3989422804014327
        act = (x * phi).astype(BF16)
        act_ref[:, cols] = act
        slope_ref[:, cols] = phi + x * density
        total = total + dot(act, down_ref[cols, :])
    out_ref[...] = total


def ff_forward(h, gain, shift, up, up_bias, down, end):
    return call(
        ff_forward_body,
        (shape((ROWS, D), F32), shape((ROWS, 3072), BF16), shape((ROWS, 3072), F32),
         shape((ROWS, D), BF16)),
        [rows_of(D), whole(1, D), whole(1, D), whole(D, 3072), whole(1, 3072), whole(3072, D),
         whole(1, D)],
        (rows_of(D), rows_of(3072), rows_of(3072), rows_of(D)),
        grid=(ROWS // BLOCK,),
    )(h, gain, shift, up, up_bias, down, end)


def ff_backward_body(g_ref, h_ref, gain_ref, slope_ref, up_ref, down_ref,
                     out_ref, gr_ref, gb_ref, vec_ref, ups_ref):
    first = pl.program_id(0) == 0
    g = g_ref[...]
    gb = g.astype(BF16)
    gb_ref[...] = gb
    grad_normed = jnp.zeros((BLOCK, D), F32)

    @pl.when(first)
    def _():
        ups_ref[...] = jnp.zeros_like(ups_ref)

    for c in range(0, 3072, 512):
        cols = slice(c, c + 512)
        ga = dot(gb, down_ref[cols, :], 1, 1)
        gr = (ga * slope_ref[:, cols]).astype(BF16)
        gr_ref[:, cols] = gr
        ups_ref[:, cols] += jnp.sum(gr.astype(F32), axis=0, keepdims=True)
        grad_normed = grad_normed + dot(gr, up_ref[:, cols], 1, 1)
    out, xhat = norm_back(g, h_ref[...], gain_ref[...], grad_normed)
    out_ref[...] = out
    add_rows(vec_ref, ((0, grad_normed * xhat), (1, grad_normed), (2, gb.astype(F32))), first)


def ff_backward(g, h, gain, slope, up, down):
    return call(
        ff_backward_body,
        (shape((ROWS, D), F32), shape((ROWS, 3072), BF16), shape((ROWS, D), BF16),
         shape((8, D), F32), shape((1, 3072), F32)),
        [rows_of(D), rows_of(D), whole(1, D), rows_of(3072), whole(D, 3072), whole(3072, D)],
        (rows_of(D), rows_of(3072), rows_of(D), whole(8, D), whole(1, 3072)),
        grid=(ROWS // BLOCK,),
    )(g, h, gain, slope, up, down)


def pair_rows():
    return pl.BlockSpec((PAIRS, BLOCK, 128), lambda i: (0, i, 0))


def qkv_body(h_ref, gain_ref, shift_ref, w_ref, qb_ref, vb_ref, q_ref, k_ref, v_ref, normed_ref):
    xhat, _ = normalized(h_ref[...])
    normed = (xhat * gain_ref[...] + shift_ref[...]).astype(BF16)
    normed_ref[...] = normed
    for half in range(2):
        base = half * 1152
        cols = slice(half * 384, half * 384 + 384)
        q = (dot(normed, w_ref[:, base : base + 384]) + qb_ref[:, cols]).astype(BF16)
        q = (q.astype(F32) * 0.125).astype(BF16)
        k = dot(normed, w_ref[:, base + 384 : base + 768]).astype(BF16)
        v = (dot(normed, w_ref[:, base + 768 : base + 1152]) + vb_ref[:, cols]).astype(BF16)
        for j in range(3):
            lanes = slice(j * 128, j * 128 + 128)
            q_ref[half * 3 + j] = q[:, lanes]
            k_ref[half * 3 + j] = k[:, lanes]
            v_ref[half * 3 + j] = v[:, lanes]


def head_mask(dims, axis, head):
    at = lax.broadcasted_iota(jnp.int32, dims, axis)
    return at < HEAD_DIM if head == 0 else at >= HEAD_DIM


def key_masked(s):
    cut = 864
    tail = s[cut:, :]
    at = lax.broadcasted_iota(jnp.int32, tail.shape, 0)
    tail = jnp.where(at < LENGTH - cut, tail, -1e30)
    return jnp.concatenate([s[:cut, :], tail], axis=0)


def attend_body(q_ref, k_ref, v_ref, o_ref, lse_ref):
    k = k_ref[0]
    v_t = v_ref[0].T
    lse_ref[...] = jnp.zeros_like(lse_ref)
    v_heads = [jnp.where(head_mask(v_t.shape, 0, head), v_t, 0) for head in range(2)]
    for start, size in Q_BLOCKS:
        rows = slice(start, start + size)
        q = q_ref[0, rows, :]
        out = jnp.zeros((128, size), F32)
        for head in range(2):
            q_head = jnp.where(head_mask(q.shape, 1, head), q, 0)
            s = key_masked(dot(k, q_head, 1, 1))
            top = jnp.max(s, axis=0, keepdims=True)
            e = jnp.exp(s - top)
            total = jnp.sum(e, axis=0, keepdims=True)
            p = (e * (1.0 / total)).astype(BF16)
            out = out + dot(v_heads[head], p)
            lse_ref[0, head : head + 1, rows] = top + jnp.log(total)
        o_ref[0, rows, :] = out.T.astype(BF16)


def attend(q, k, v):
    pair = pl.BlockSpec((1, ROWS, 128), lambda j: (j, 0, 0))
    row = pl.BlockSpec((1, 8, ROWS), lambda j: (j, 0, 0))
    return call(
        attend_body,
        (shape((PAIRS, ROWS, 128), BF16), shape((PAIRS, 8, ROWS), F32)),
        [pair] * 3,
        (pair, row),
        grid=(PAIRS,),
    )(q, k, v)


def out_proj_body(o_ref, h_ref, w_ref, end_ref, out_ref, mixed_ref):
    mixed = jnp.concatenate([o_ref[j] for j in range(PAIRS)], axis=1)
    mixed_ref[...] = mixed
    out_ref[...] = h_ref[...] + (dot(mixed, w_ref[...]) + end_ref[...])


def attention_forward(h, gain, shift, w, q_bias, v_bias, w_out, end):
    q, k, v, normed = call(
        qkv_body,
        (shape((PAIRS, ROWS, 128), BF16),) * 3 + (shape((ROWS, D), BF16),),
        [rows_of(D), whole(1, D), whole(1, D), whole(D, 2304), whole(1, D), whole(1, D)],
        (pair_rows(), pair_rows(), pair_rows(), rows_of(D)),
        grid=(ROWS // BLOCK,),
    )(h, gain, shift, w, q_bias, v_bias)
    o, lse = attend(q, k, v)
    out, mixed = call(
        out_proj_body,
        (shape((ROWS, D), F32), shape((ROWS, D), BF16)),
        [pair_rows(), rows_of(D), whole(D, D), whole(1, D)],
        (rows_of(D), rows_of(D)),
        grid=(ROWS // BLOCK,),
    )(o, h, w_out, end)
    return out, (q, k, v, o, lse, mixed, normed)


def mixed_back_body(g_ref, w_ref, gb_ref, gm_ref):
    gb = g_ref[...].astype(BF16)
    gb_ref[...] = gb
    gm = dot(gb, w_ref[...], 1, 1).astype(BF16)
    for j in range(PAIRS):
        gm_ref[j] = gm[:, j * 128 : j * 128 + 128]


def attend_back_body(q_ref, k_ref, v_ref, o_ref, gm_ref, lse_ref, gq_ref, gk_ref, gv_ref):
    k, v = k_ref[0], v_ref[0]
    k_t = k.T
    k_heads = [jnp.where(head_mask(k_t.shape, 0, head), k_t, 0) for head in range(2)]
    grad_k = jnp.zeros((ROWS, 128), F32)
    grad_v = jnp.zeros((ROWS, 128), F32)
    for start, size in Q_BLOCKS:
        rows = slice(start, start + size)
        q, gm = q_ref[0, rows, :], gm_ref[0, rows, :]
        product = gm.astype(F32) * o_ref[0, rows, :].astype(F32)
        grad_q = jnp.zeros((128, size), F32)
        for head in range(2):
            q_head = jnp.where(head_mask(q.shape, 1, head), q, 0)
            gm_head = jnp.where(head_mask(gm.shape, 1, head), gm, 0)
            ones = jnp.where(head_mask((8, 128), 1, head), 1.0, 0.0)
            inner = lax.dot_general(
                ones, product, (((1,), (1,)), ((), ())),
                precision=lax.Precision.HIGHEST, preferred_element_type=F32,
            )[0:1, :]
            s = key_masked(dot(k, q_head, 1, 1))
            p = jnp.exp(s - lse_ref[0, head : head + 1, rows])
            gp = dot(v, gm_head, 1, 1)
            gs = (p * (gp - inner)).astype(BF16)
            grad_v = grad_v + dot(p.astype(BF16), gm_head)
            grad_k = grad_k + dot(gs, q_head)
            grad_q = grad_q + dot(k_heads[head], gs)
        gq_ref[0, rows, :] = (grad_q.T * 0.125).astype(BF16)
    gk_ref[0] = grad_k.astype(BF16)
    gv_ref[0] = grad_v.astype(BF16)


def qkv_back_body(g_ref, h_ref, gain_ref, gb_ref, gq_ref, gk_ref, gv_ref, w_ref,
                  out_ref, gqkv_ref, vec_ref):
    first = pl.program_id(0) == 0
    parts = []
    for half in range(2):
        for ref in (gq_ref, gk_ref, gv_ref):
            parts.extend(ref[half * 3 + j] for j in range(3))
    gqkv = jnp.concatenate(parts, axis=1)
    gqkv_ref[...] = gqkv
    grad_normed = dot(gqkv, w_ref[...], 1, 1)
    out, xhat = norm_back(g_ref[...], h_ref[...], gain_ref[...], grad_normed)
    out_ref[...] = out
    grad_q = jnp.concatenate([gq_ref[j] for j in range(PAIRS)], axis=1).astype(F32)
    grad_v = jnp.concatenate([gv_ref[j] for j in range(PAIRS)], axis=1).astype(F32)
    add_rows(
        vec_ref,
        ((0, grad_normed * xhat), (1, grad_normed), (2, gb_ref[...].astype(F32)),
         (3, grad_q), (4, grad_v)),
        first,
    )


def attention_backward(g, h, gain, w, w_out, q, k, v, o, lse):
    gb, gm = call(
        mixed_back_body,
        (shape((ROWS, D), BF16), shape((PAIRS, ROWS, 128), BF16)),
        [rows_of(D), whole(D, D)],
        (rows_of(D), pair_rows()),
        grid=(ROWS // BLOCK,),
    )(g, w_out)
    pair = pl.BlockSpec((1, ROWS, 128), lambda j: (j, 0, 0))
    row = pl.BlockSpec((1, 8, ROWS), lambda j: (j, 0, 0))
    gq, gk, gv = call(
        attend_back_body,
        (shape((PAIRS, ROWS, 128), BF16),) * 3,
        [pair] * 5 + [row],
        (pair,) * 3,
        grid=(PAIRS,),
    )(q, k, v, o, gm, lse)
    out, gqkv, vec = call(
        qkv_back_body,
        (shape((ROWS, D), F32), shape((ROWS, 2304), BF16), shape((8, D), F32)),
        [rows_of(D), rows_of(D), whole(1, D), rows_of(D), pair_rows(), pair_rows(), pair_rows(),
         whole(D, 2304)],
        (rows_of(D), rows_of(2304), whole(8, D)),
        grid=(ROWS // BLOCK,),
    )(g, h, gain, gb, gq, gk, gv, w)
    return out, gqkv, gb, vec


def weight_grad_body(first_blocks, normed_ref, gb_ref, x1_ref, x2_ref, out_ref, normed_t, gb_t):
    half, n = pl.program_id(0), pl.program_id(1)

    @pl.when((half == 0) & (n == 0))
    def _():
        normed_t[...] = normed_ref[...].T
        gb_t[...] = gb_ref[...].T

    @pl.when(n < first_blocks)
    def _():
        out_ref[0] = dot(normed_t[...], x1_ref[...])

    @pl.when(n >= first_blocks)
    def _():
        out_ref[0] = dot(gb_t[...], x2_ref[...])


def weight_grads(normed, gb, x1, x2, width):
    b1 = x1.shape[1] // 2 // width
    b2 = x2.shape[1] // 2 // width
    return call(
        functools.partial(weight_grad_body, b1),
        shape((2, D, (b1 + b2) * width), F32),
        [whole(ROWS, D), whole(ROWS, D),
         pl.BlockSpec((ROWS, width), lambda h, n: (0, h * b1 + jnp.minimum(n, b1 - 1))),
         pl.BlockSpec((ROWS, width), lambda h, n: (0, h * b2 + jnp.maximum(n - b1, 0)))],
        pl.BlockSpec((1, D, width), lambda h, n: (h, 0, n)),
        grid=(2, b1 + b2),
        scratch=[pltpu.VMEM((D, ROWS), BF16), pltpu.VMEM((D, ROWS), BF16)],
    )(normed, gb, x1, x2)


def place():
    s, r, p = lax.axis_index("section"), lax.axis_index("dp"), lax.axis_index("tensor")
    return s, r, p, r // 4, r % 4


def on_dp(y, z):
    return {"dp": y * 4 + z}


def greet(peers):
    barrier = pltpu.get_barrier_semaphore()
    for peer in peers:
        pl.semaphore_signal(barrier, inc=1, device_id=peer, device_id_type=MESH)
    pl.semaphore_wait(barrier, len(peers))


def remote(src, dst, send, recv, device):
    return pltpu.make_async_remote_copy(
        src_ref=src, dst_ref=dst, send_sem=send, recv_sem=recv, device_id=device,
        device_id_type=MESH,
    )


def gather_body(qkv_in, out_in, up_in, down_in, qvb_in, upb_in,
                qkv, out, up, down, qvb, upb, send0, recv0, send1, recv1, send2, recv2):
    s, r, p, y, z = place()
    partner = {"tensor": 1 - p}
    z_peers = [on_dp(y, (z + d) % 4) for d in range(1, 4)]
    y_peers = [on_dp((y + d) % 4, z) for d in range(1, 4)]
    greet([partner] + z_peers + y_peers)

    def run(whole_pair, z_first, y_first):
        pieces = [(src, view, True) for src, view in z_first]
        pieces += [(src, view, False) for src, view in y_first]
        copies0 = [
            remote(src, view(y, z), send0.at[i], recv0.at[i], partner)
            for i, (src, view, _) in enumerate(pieces)
        ]
        bias = remote(whole_pair[0], whole_pair[1], send0.at[3], recv0.at[3], partner)
        for copy in copies0:
            copy.start()
        bias.start()
        copies1 = []
        for i, (src, view, along_z) in enumerate(pieces):
            copies0[i].wait_recv()
            part = view(y, z)
            copies1.append([
                remote(part, part, send1.at[i, d], recv1.at[i, d],
                       z_peers[d] if along_z else y_peers[d])
                for d in range(3)
            ])
            for copy in copies1[-1]:
                copy.start()
        copies2 = []
        for i, (src, view, along_z) in enumerate(pieces):
            for copy in copies1[i]:
                copy.wait_recv()
            part = view(y, slice(None)) if along_z else view(slice(None), z)
            copies2.append([
                remote(part, part, send2.at[i, d], recv2.at[i, d],
                       y_peers[d] if along_z else z_peers[d])
                for d in range(3)
            ])
            for copy in copies2[-1]:
                copy.start()
        for group in copies2:
            for copy in group:
                copy.wait_recv()
        bias.wait_recv()
        for copy in copies0 + [bias]:
            copy.wait_send()
        for group in copies1 + copies2:
            for copy in group:
                copy.wait_send()

    @pl.when(s % 2 == 0)
    def _():
        run(
            (qvb_in, qvb),
            [(qkv_in.at[0:2], lambda a, b: qkv.at[0:2, a, b])],
            [(qkv_in.at[2], lambda a, b: qkv.at[2, a, b]), (out_in, lambda a, b: out.at[a, b])],
        )

    @pl.when(s % 2 == 1)
    def _():
        run(
            (upb_in, upb),
            [(up_in, lambda a, b: up.at[a, b])],
            [(down_in, lambda a, b: down.at[a, b])],
        )


def gather_halves(qkv, out, up, down, qv_bias, up_bias):
    dma = pltpu.SemaphoreType.DMA
    any_spec = pl.BlockSpec(memory_space=ANY)
    return call(
        gather_body,
        (shape((3, 4, 4, 48, 384), F32), shape((4, 4, 24, D), F32), shape((4, 4, 48, 1536), F32),
         shape((4, 4, 96, D), F32), shape((2, 384), F32), shape((1, 1536), F32)),
        [any_spec] * 6,
        (any_spec,) * 6,
        scratch=[dma((4,)), dma((4,)), dma((3, 3)), dma((3, 3)), dma((3, 3)), dma((3, 3))],
        collective_id=1,
        has_side_effects=True,
    )(qkv, out, up, down, qv_bias, up_bias)


def handoff_body(source, target, rows_ref, out_ref, send, recv):
    s, r, p, _, _ = place()
    across = {source, target} == {1, 2}
    other = 1 - p if across else p
    barrier = pltpu.get_barrier_semaphore()
    half = ROWS // 2

    def copies(device):
        return [
            remote(rows_ref.at[pl.ds(i * half, half)], out_ref.at[pl.ds(i * half, half)],
                   send.at[i], recv.at[i], device)
            for i in range(2)
        ]

    @pl.when(s == target)
    def _():
        sender = {"section": source, "tensor": other}
        pl.semaphore_signal(barrier, inc=1, device_id=sender, device_id_type=MESH)
        for copy in copies(sender):
            copy.wait_recv()

    @pl.when(s == source)
    def _():
        pl.semaphore_wait(barrier, 1)
        group = copies({"section": target, "tensor": other})
        for copy in group:
            copy.start()
        for copy in group:
            copy.wait_send()


def handoff(rows, source, target):
    dma = pltpu.SemaphoreType.DMA
    any_spec = pl.BlockSpec(memory_space=ANY)
    return call(
        functools.partial(handoff_body, source, target),
        shape((ROWS, D), F32),
        [any_spec],
        any_spec,
        scratch=[dma((2,)), dma((2,))],
        collective_id=2 + source * 4 + target,
        has_side_effects=True,
    )(rows)


def finish_body(h0, h1, h2, h3, g0, g1, g2, g3, w0, w1, w2, w3, v0, v1, v2, v3,
                hid, gin, out, vec,
                acc, r1, r2, fin, r3, va, v1r, v2r,
                own, s1, q1, s2, q2, s3, q3, xs, xr, xo, vs, vr, vo):
    s, r, p, y, z = place()
    partner = {"tensor": 1 - p}
    z_peers = [on_dp(y, (z + d) % 4) for d in range(1, 4)]
    y_peers = [on_dp((y + d) % 4, z) for d in range(1, 4)]
    greet([partner] + z_peers + y_peers)
    clip = jnp.where(s < 2, p, 1 - p)

    def run(h, g, w, v, chunks):
        jobs = [(c * CHUNK, c < chunks // 2) for c in range(chunks)]
        first, second, third = [], [], []
        vload = pltpu.make_async_copy(v, va, vo.at[0])
        vload.start()
        for j, (c, z_first) in enumerate(jobs):
            cols = pl.ds(c, CHUNK)
            if z_first:
                here = w.at[:, :, z, :, cols]
                there = [w.at[:, :, (z + d) % 4, :, cols] for d in range(1, 4)]
                peers = z_peers
            else:
                here = w.at[:, y, :, :, cols]
                there = [w.at[:, (y + d) % 4, :, :, cols] for d in range(1, 4)]
                peers = y_peers
            load = pltpu.make_async_copy(here, acc.at[j], own.at[j])
            load.start()
            group = [
                remote(there[d], r1.at[j, d], s1.at[j, d], q1.at[j, d], peers[d]) for d in range(3)
            ]
            for copy in group:
                copy.start()
            first.append((load, group))
        vload.wait()
        vgroup = [remote(va, v1r.at[d], vs.at[d], vr.at[d], z_peers[d]) for d in range(3)]
        for copy in vgroup:
            copy.start()
        exchange = [
            remote(h, hid.at[clip], xs.at[0], xr.at[0], partner),
            remote(g, gin.at[clip], xs.at[1], xr.at[1], partner),
        ]
        arriving = [
            remote(h, hid.at[1 - clip], xs.at[0], xr.at[0], partner),
            remote(g, gin.at[1 - clip], xs.at[1], xr.at[1], partner),
        ]
        local = [
            pltpu.make_async_copy(h, hid.at[clip], xo.at[0]),
            pltpu.make_async_copy(g, gin.at[clip], xo.at[1]),
        ]
        for copy in exchange + local:
            copy.start()

        for j, (c, z_first) in enumerate(jobs):
            load, group = first[j]
            load.wait()
            for copy in group:
                copy.wait_recv()

            def total(i, carry, j=j):
                a, b = i // 4, i % 4
                acc[j, a, b] += r1[j, 0, a, b] + r1[j, 1, a, b] + r1[j, 2, a, b]
                return carry

            lax.fori_loop(0, 8, total, 0)
            peers = y_peers if z_first else z_peers
            mine = y if z_first else z
            group = [
                remote(acc.at[j, :, (mine + d + 1) % 4], r2.at[j, d], s2.at[j, d], q2.at[j, d],
                       peers[d])
                for d in range(3)
            ]
            for copy in group:
                copy.start()
            second.append(group)
        for copy in vgroup:
            copy.wait()
        va[...] = va[...] + v1r[0] + v1r[1] + v1r[2]
        vgroup = [remote(va, v2r.at[d], vs.at[3 + d], vr.at[3 + d], y_peers[d]) for d in range(3)]
        for copy in vgroup:
            copy.start()
        for j, (c, z_first) in enumerate(jobs):
            for copy in second[j]:
                copy.wait_recv()
            mine = y if z_first else z
            for a in range(2):
                fin[j, a] = acc[j, a, mine] + r2[j, 0, a] + r2[j, 1, a] + r2[j, 2, a]
            copy = remote(fin.at[j, 1], r3.at[j], s3.at[j], q3.at[j], partner)
            copy.start()
            third.append(copy)
        for copy in vgroup:
            copy.wait()
        vec[0] = va[...] + v2r[0] + v2r[1] + v2r[2]
        vlast = remote(vec.at[0], vec.at[1], vs.at[6], vr.at[6], partner)
        vlast.start()
        for j, (c, _) in enumerate(jobs):
            third[j].wait_recv()
            out[:, c : c + CHUNK] = fin[j, 0] + r3[j]
        vlast.wait()
        for copy in local:
            copy.wait()
        for copy in arriving:
            copy.wait_recv()
        for copy in exchange + third:
            copy.wait_send()
        for _, group in first:
            for copy in group:
                copy.wait_send()
        for group in second:
            for copy in group:
                copy.wait_send()

    for t, refs in enumerate(zip((h0, h1, h2, h3), (g0, g1, g2, g3), (w0, w1, w2, w3),
                                 (v0, v1, v2, v3))):
        pl.when(s == t)(functools.partial(run, *refs, 2 if t % 2 == 0 else 4))


def finish(hs, gs, ws, vs):
    dma = pltpu.SemaphoreType.DMA
    any_spec = pl.BlockSpec(memory_space=ANY)
    vmem = pl.BlockSpec(memory_space=pltpu.VMEM)
    return call(
        finish_body,
        (shape((2, ROWS, D), F32), shape((2, ROWS, D), F32), shape((48, 3072), F32),
         shape((2, 8, D), F32)),
        [any_spec] * 16,
        (any_spec, any_spec, vmem, vmem),
        scratch=[
            pltpu.VMEM((4, 2, 4, 48, CHUNK), F32),
            pltpu.VMEM((4, 3, 2, 4, 48, CHUNK), F32),
            pltpu.VMEM((4, 3, 2, 48, CHUNK), F32),
            pltpu.VMEM((4, 2, 48, CHUNK), F32),
            pltpu.VMEM((4, 48, CHUNK), F32),
            pltpu.VMEM((8, D), F32),
            pltpu.VMEM((3, 8, D), F32),
            pltpu.VMEM((3, 8, D), F32),
            dma((4,)), dma((4, 3)), dma((4, 3)), dma((4, 3)), dma((4, 3)), dma((4,)), dma((4,)),
            dma((2,)), dma((2,)), dma((2,)), dma((7,)), dma((7,)), dma((1,)),
        ],
        collective_id=20,
        has_side_effects=True,
    )(*hs, *gs, *ws, *vs)


def unwritten(shapes):
    any_spec = pl.BlockSpec(memory_space=ANY)
    return pl.pallas_call(
        lambda *refs: None,
        out_shape=tuple(shapes),
        out_specs=(any_spec,) * len(shapes),
    )()


def only_at(active, run, operands):
    like = jax.eval_shape(run, *operands)
    leaves, tree = jax.tree.flatten(like)

    def skip(*_):
        return jax.tree.unflatten(tree, unwritten([shape(x.shape, x.dtype) for x in leaves]))

    return lax.cond(active, run, skip, *operands)


def pad_rows(x):
    return jnp.pad(x.astype(F32), ((0, ROWS - LENGTH), (0, 0)))


def per_device(inputs, cotangent, norm_gain, norm_bias, qkv_weight, qv_bias, out_weight, end_bias,
               up_weight, up_bias, down_weight):
    s, r, p = lax.axis_index("section"), lax.axis_index("dp"), lax.axis_index("tensor")
    clip = jnp.where(s < 2, p, 1 - p)
    qkv, out_w, up, down = qkv_weight[0], out_weight[0], up_weight[0], down_weight[0]

    def slice_of(x, axis, size):
        return lax.dynamic_slice_in_dim(x, r * size, size, axis).astype(F32)

    qkv_o, out_o, up_o, down_o, qvb_o, upb_o = gather_halves(
        slice_of(qkv, 1, 48), slice_of(out_w, 0, 24), slice_of(up, 0, 48), slice_of(down, 0, 96),
        qv_bias[0], up_bias,
    )

    def attn_forward(h):
        mine = jnp.transpose(qkv, (1, 0, 2)).reshape(D, 1152)
        theirs = jnp.transpose(qkv_o.reshape(3, D, 384), (1, 0, 2)).reshape(D, 1152)
        w = jnp.concatenate([mine, theirs.astype(BF16)], axis=1)
        w_out = jnp.concatenate([out_w, out_o.reshape(384, D).astype(BF16)], axis=0)
        q_bias = jnp.concatenate([qv_bias[0, 0], qvb_o[0]])[None]
        v_bias = jnp.concatenate([qv_bias[0, 1], qvb_o[1]])[None]
        out, kept = attention_forward(
            h, norm_gain, norm_bias, w, q_bias, v_bias, w_out, end_bias)
        return out, kept + (w, w_out)

    def ff_forward_step(h):
        w_up = jnp.concatenate([up, up_o.reshape(D, 1536).astype(BF16)], axis=1)
        w_down = jnp.concatenate([down, down_o.reshape(1536, D).astype(BF16)], axis=0)
        bias = jnp.concatenate([up_bias, upb_o], axis=1)
        out, act, slope, normed = ff_forward(
            h, norm_gain, norm_bias, w_up, bias, w_down, end_bias)
        return out, (act, slope, normed, w_up, w_down)

    def attn_backward(g, h, kept):
        q, k, v, o, lse, mixed, normed, w, w_out = kept
        return attention_backward(g, h, norm_gain, w, w_out, q, k, v, o, lse)

    def ff_backward_step(g, h, kept):
        act, slope, normed, w_up, w_down = kept
        out, gr, gb, vec, ups = ff_backward(g, h, norm_gain, slope, w_up, w_down)
        vec = jnp.concatenate([vec[:3], ups.reshape(4, D), vec[7:]], axis=0)
        return out, gr, gb, vec

    def attn_grads(x1, gb, kept):
        return weight_grads(kept[6], gb, x1, kept[5], 384)

    def ff_grads(x1, gb, kept):
        return weight_grads(kept[2], gb, x1, kept[0], 768)

    received = [pad_rows(lax.dynamic_index_in_dim(inputs, clip, 0, keepdims=False))]
    produced, kept = [], []
    for t in range(4):
        out, saved = only_at(s == t, ff_forward_step if t % 2 else attn_forward, (received[t],))
        produced.append(out)
        kept.append(saved)
        if t < 3:
            received.append(handoff(out, t, t + 1))

    grads, weight_parts, vecs = [None] * 4, [None] * 4, [None] * 4
    g = pad_rows(lax.dynamic_index_in_dim(cotangent, clip, 0, keepdims=False))
    for t in (3, 2, 1, 0):
        grads[t], x1, gb, vecs[t] = only_at(
            s == t, ff_backward_step if t % 2 else attn_backward, (g, received[t], kept[t]))
        if t > 0:
            g = handoff(grads[t], t, t - 1)
        weight_parts[t] = only_at(
            s == t, ff_grads if t % 2 else attn_grads, (x1, gb, kept[t]))

    split = [w.reshape(2, 4, 4, 48, w.shape[2]) for w in weight_parts]
    hid, gin, sums, vec = finish(produced, grads, split, vecs)

    attn = s % 2 == 0
    both = vec[0] + vec[1]

    def mine(row):
        return lax.dynamic_slice_in_dim(both[row], r * 48, 48)[None]

    def when(flag, x):
        return jnp.where(flag, x, 0.0)[None]

    qkv_grad = jnp.transpose(sums[:, :1152].reshape(48, 3, 384), (1, 0, 2))
    qv_grad = vec[0, 3:5, :384] + vec[1, 3:5, 384:]
    up_bias_grad = (vec[0, 3:5] + vec[1, 5:7]).reshape(1536)
    return (
        hid[None, :, :LENGTH],
        gin[None, :, :LENGTH],
        mine(0),
        mine(1),
        when(attn, qkv_grad),
        when(attn, qv_grad),
        when(attn, sums[:, 1152:1536].T),
        mine(2),
        when(~attn, sums[:, :1536]),
        when(~attn, up_bias_grad),
        when(~attn, sums[:, 1536:].T),
    )


def solution(mesh):
    return jax.shard_map(
        per_device,
        mesh=mesh,
        in_specs=(
            P("dp", None, None),
            P("dp", None, None),
            P("section", None),
            P("section", None),
            P("section", None, None, "tensor"),
            P("section", None, "tensor"),
            P("section", "tensor", None),
            P("section", None),
            P("section", None, "tensor"),
            P("section", "tensor"),
            P("section", "tensor", None),
        ),
        out_specs=(
            P("section", "dp", None, None),
            P("section", "dp", None, None),
            P("section", "dp"),
            P("section", "dp"),
            P("section", None, "dp", "tensor"),
            P("section", None, "tensor"),
            P("section", "tensor", "dp"),
            P("section", "dp"),
            P("section", "dp", "tensor"),
            P("section", "tensor"),
            P("section", "tensor", "dp"),
        ),
        check_vma=False,
    )
```

```python
import functools

import jax
import jax.numpy as jnp
from jax import lax
from jax.experimental import pallas as pl
from jax.experimental.pallas import tpu as pltpu
from jax.sharding import PartitionSpec as P

MESH = pl.DeviceIdType.MESH
ANY = pl.ANY
F32 = jnp.float32
BF16 = jnp.bfloat16

HEAD_DIM = 64
EPS = 1e-06
LENGTH = 866
ROWS = 896
BLOCK = 224
D = 768
PAIRS = 6
Q_BLOCKS = ((0, 256), (256, 256), (512, 384))
VMEM_BYTES = 60 * 1024 * 1024

CHUNK = 768


def call(body, out_shape, in_specs, out_specs, grid=(), scratch=(), flops=0, moved=0, **more):
    return pl.pallas_call(
        body,
        out_shape=out_shape,
        grid=grid,
        in_specs=in_specs,
        out_specs=out_specs,
        scratch_shapes=scratch,
        cost_estimate=pl.CostEstimate(flops=flops, bytes_accessed=moved, transcendentals=0),
        compiler_params=pltpu.CompilerParams(vmem_limit_bytes=VMEM_BYTES, **more),
    )


def shape(dims, dtype):
    return jax.ShapeDtypeStruct(dims, dtype)


def whole(*dims):
    return pl.BlockSpec(dims, lambda *_: (0,) * len(dims), pipeline_mode=pl.Buffered(1))


def rows_of(width):
    return pl.BlockSpec((BLOCK, width), lambda i: (i, 0))


def dot(a, b, ca=1, cb=0):
    return lax.dot_general(a, b, (((ca,), (cb,)), ((), ())), preferred_element_type=F32)


def normalized(h):
    average = jnp.mean(h, axis=-1, keepdims=True)
    centred = h - average
    spread = jnp.mean(centred * centred, axis=-1, keepdims=True)
    r = lax.rsqrt(spread + EPS)
    return centred * r, r


def norm_back(g, h, gain, grad_normed):
    xhat, r = normalized(h)
    t = grad_normed * gain
    t_mean = jnp.mean(t, axis=-1, keepdims=True)
    tx_mean = jnp.mean(t * xhat, axis=-1, keepdims=True)
    return g + r * (t - t_mean - xhat * tx_mean), xhat


def block(i):
    return pl.ds(pl.multiple_of(i * BLOCK, 32), BLOCK)


def gelu_and_slope(x):
    phi = 0.5 * (1.0 + lax.erf(x * 0.7071067811865476))
    density = jnp.exp(-0.5 * x * x) * 0.3989422804014327
    return (x * phi).astype(BF16), phi + x * density


def qkv_block(h, gain, shift, w_ref, bias, q_ref, k_ref, v_ref, r):
    xhat, _ = normalized(h)
    normed = (xhat * gain + shift).astype(BF16)
    for c in range(0, 2304, 768):
        part = (dot(normed, w_ref[:, c : c + 768]) + bias[:, c : c + 768]).astype(BF16)
        for n in range(c // 128, c // 128 + 6):
            lanes = part[:, n * 128 - c : n * 128 - c + 128]
            pair = n // 9 * 3 + n % 3
            kind = n % 9 // 3
            if kind == 0:
                q_ref[pair, r, :] = (lanes.astype(F32) * 0.125).astype(BF16)
            elif kind == 1:
                k_ref[pair, r, :] = lanes
            else:
                v_ref[pair, r, :] = lanes
    return normed


def joined(ref, r):
    return jnp.concatenate([ref[j, r, :] for j in range(PAIRS)], axis=1)


def mixed_back_block(g, w_out_ref, gm_ref, r):
    gb = g.astype(BF16)
    gm = dot(gb, w_out_ref[...], 1, 1).astype(BF16)
    for j in range(PAIRS):
        gm_ref[j, r, :] = gm[:, j * 128 : j * 128 + 128]
    return gb


def add_row(vec_ref, at, values):
    vec_ref[at : at + 1, :] += jnp.sum(values, axis=0, keepdims=True)


def qkv_back_block(g, h, gain, gq_ref, gk_ref, gv_ref, w_ref, vec_ref, r):
    grad_normed = jnp.zeros((BLOCK, D), F32)
    for half in range(2):
        parts = [ref[half * 3 + j, r, :] for ref in (gq_ref, gk_ref, gv_ref) for j in range(3)]
        part = jnp.concatenate(parts, axis=1)
        grad_normed = grad_normed + dot(part, w_ref[:, half * 1152 : half * 1152 + 1152], 1, 1)
    out, xhat = norm_back(g, h, gain, grad_normed)
    add_row(vec_ref, 0, grad_normed * xhat)
    add_row(vec_ref, 1, grad_normed)
    add_row(vec_ref, 2, g.astype(BF16).astype(F32))
    add_row(vec_ref, 3, joined(gq_ref, r).astype(F32))
    add_row(vec_ref, 4, joined(gv_ref, r).astype(F32))
    return out


def head_mask(dims, axis, head):
    at = lax.broadcasted_iota(jnp.int32, dims, axis)
    return at < HEAD_DIM if head == 0 else at >= HEAD_DIM


def key_masked(s):
    cut = 864
    tail = s[cut:, :]
    at = lax.broadcasted_iota(jnp.int32, tail.shape, 0)
    tail = jnp.where(at < LENGTH - cut, tail, -1e30)
    return jnp.concatenate([s[:cut, :], tail], axis=0)


def attend_body(q_ref, k_ref, v_ref, o_ref, lse_ref):
    k = k_ref[0]
    v_t = v_ref[0].T
    lse_ref[...] = jnp.zeros_like(lse_ref)
    v_heads = [jnp.where(head_mask(v_t.shape, 0, head), v_t, 0) for head in range(2)]
    for start, size in Q_BLOCKS:
        rows = slice(start, start + size)
        q = q_ref[0, rows, :]
        out = jnp.zeros((128, size), F32)
        for head in range(2):
            q_head = jnp.where(head_mask(q.shape, 1, head), q, 0)
            s = key_masked(dot(k, q_head, 1, 1))
            top = jnp.max(s, axis=0, keepdims=True)
            e = jnp.exp(s - top)
            total = jnp.sum(e, axis=0, keepdims=True)
            p = (e * (1.0 / total)).astype(BF16)
            out = out + dot(v_heads[head], p)
            lse_ref[0, head : head + 1, rows] = top + jnp.log(total)
        o_ref[0, rows, :] = out.T.astype(BF16)


PAIR = pl.BlockSpec((1, ROWS, 128), lambda j: (j, 0, 0))
PAIR_ROW = pl.BlockSpec((1, 8, ROWS), lambda j: (j, 0, 0))


def attend(q, k, v):
    return call(
        attend_body,
        (shape((PAIRS, ROWS, 128), BF16), shape((PAIRS, 8, ROWS), F32)),
        [PAIR] * 3,
        (PAIR, PAIR_ROW),
        grid=(PAIRS,),
    )(q, k, v)


def attend_back_body(q_ref, k_ref, v_ref, o_ref, gm_ref, lse_ref, gq_ref, gk_ref, gv_ref):
    k, v = k_ref[0], v_ref[0]
    k_t = k.T
    k_heads = [jnp.where(head_mask(k_t.shape, 0, head), k_t, 0) for head in range(2)]
    grad_k = jnp.zeros((ROWS, 128), F32)
    grad_v = jnp.zeros((ROWS, 128), F32)
    for start, size in Q_BLOCKS:
        rows = slice(start, start + size)
        q, gm = q_ref[0, rows, :], gm_ref[0, rows, :]
        product = gm.astype(F32) * o_ref[0, rows, :].astype(F32)
        grad_q = jnp.zeros((128, size), F32)
        for head in range(2):
            q_head = jnp.where(head_mask(q.shape, 1, head), q, 0)
            gm_head = jnp.where(head_mask(gm.shape, 1, head), gm, 0)
            ones = jnp.where(head_mask((8, 128), 1, head), 1.0, 0.0)
            inner = lax.dot_general(
                ones, product, (((1,), (1,)), ((), ())),
                precision=lax.Precision.HIGHEST, preferred_element_type=F32,
            )[0:1, :]
            s = key_masked(dot(k, q_head, 1, 1))
            p = jnp.exp(s - lse_ref[0, head : head + 1, rows])
            gp = dot(v, gm_head, 1, 1)
            gs = (p * (gp - inner)).astype(BF16)
            grad_v = grad_v + dot(p.astype(BF16), gm_head)
            grad_k = grad_k + dot(gs, q_head)
            grad_q = grad_q + dot(k_heads[head], gs)
        gq_ref[0, rows, :] = (grad_q.T * 0.125).astype(BF16)
    gk_ref[0] = grad_k.astype(BF16)
    gv_ref[0] = grad_v.astype(BF16)


def attend_back(q, k, v, o, gm, lse):
    return call(
        attend_back_body,
        (shape((PAIRS, ROWS, 128), BF16),) * 3,
        [PAIR] * 5 + [PAIR_ROW],
        (PAIR,) * 3,
        grid=(PAIRS,),
    )(q, k, v, o, gm, lse)


def pair_rows():
    return pl.BlockSpec((PAIRS, BLOCK, 128), lambda i: (0, i, 0))


def first_qkv_body(h_ref, gain_ref, shift_ref, w_ref, bias_ref, q_ref, k_ref, v_ref, normed_ref):
    normed_ref[...] = qkv_block(
        h_ref[...], gain_ref[...], shift_ref[...], w_ref, bias_ref, q_ref, k_ref, v_ref,
        slice(None))


def first_qkv(h, gain, shift, w, bias):
    return call(
        first_qkv_body,
        (shape((PAIRS, ROWS, 128), BF16),) * 3 + (shape((ROWS, D), BF16),),
        [rows_of(D), whole(1, D), whole(1, D), whole(D, 2304), whole(1, 2304)],
        (pair_rows(), pair_rows(), pair_rows(), rows_of(D)),
        grid=(ROWS // BLOCK,),
    )(h, gain, shift, w, bias)


def last_qkv_back_body(g_ref, h_ref, gain_ref, gq_ref, gk_ref, gv_ref, w_ref, out_ref, vec_ref):
    @pl.when(pl.program_id(0) == 0)
    def _():
        vec_ref[...] = jnp.zeros_like(vec_ref)

    out_ref[...] = qkv_back_block(
        g_ref[...], h_ref[...], gain_ref[...], gq_ref, gk_ref, gv_ref, w_ref, vec_ref,
        slice(None))


def last_qkv_back(g, h, gain, gq, gk, gv, w):
    return call(
        last_qkv_back_body,
        (shape((ROWS, D), F32), shape((8, D), F32)),
        [rows_of(D), rows_of(D), whole(1, D), pair_rows(), pair_rows(), pair_rows(),
         whole(D, 2304)],
        (rows_of(D), whole(8, D)),
        grid=(ROWS // BLOCK,),
    )(g, h, gain, gq, gk, gv, w)


def weight_grad_body(first_blocks, normed_ref, gb_ref, x1_ref, x2_ref, out_ref, normed_t, gb_t):
    half, n = pl.program_id(0), pl.program_id(1)

    @pl.when((half == 0) & (n == 0))
    def _():
        normed_t[...] = normed_ref[...].T
        gb_t[...] = gb_ref[...].T

    @pl.when(n < first_blocks)
    def _():
        out_ref[0] = dot(normed_t[...], x1_ref[...])

    @pl.when(n >= first_blocks)
    def _():
        out_ref[0] = dot(gb_t[...], x2_ref[...])


def ff_weight_grads(normed, gb, x1, x2):
    return call(
        functools.partial(weight_grad_body, 2),
        shape((2, D, 3072), F32),
        [whole(ROWS, D), whole(ROWS, D),
         pl.BlockSpec((ROWS, 768), lambda h, n: (0, h * 2 + jnp.minimum(n, 1))),
         pl.BlockSpec((ROWS, 768), lambda h, n: (0, h * 2 + jnp.maximum(n - 2, 0)))],
        pl.BlockSpec((1, D, 768), lambda h, n: (h, 0, n)),
        grid=(2, 4),
        scratch=[pltpu.VMEM((D, ROWS), BF16), pltpu.VMEM((D, ROWS), BF16)],
    )(normed, gb, x1, x2)


def attn_weight_grad_body(normed_ref, gb_ref, gq_ref, gk_ref, gv_ref, o_ref, out_ref,
                          normed_t, gb_t):
    @pl.when(pl.program_id(0) == 0)
    def _():
        normed_t[...] = normed_ref[...].T
        gb_t[...] = gb_ref[...].T

    for n, ref in enumerate((gq_ref, gk_ref, gv_ref, o_ref)):
        x = jnp.concatenate([ref[j] for j in range(3)], axis=1)
        left = gb_t if n == 3 else normed_t
        out_ref[0, :, n * 384 : n * 384 + 384] = dot(left[...], x)


def attn_weight_grads(normed, gb, gq, gk, gv, o):
    pairs = pl.BlockSpec((3, ROWS, 128), lambda h: (h, 0, 0))
    return call(
        attn_weight_grad_body,
        shape((2, D, 1536), F32),
        [whole(ROWS, D), whole(ROWS, D)] + [pairs] * 4,
        pl.BlockSpec((1, D, 1536), lambda h: (h, 0, 0)),
        grid=(2,),
        scratch=[pltpu.VMEM((D, ROWS), BF16), pltpu.VMEM((D, ROWS), BF16)],
    )(normed, gb, gq, gk, gv, o)


def attn_weights_body(qkv_ref, qkv_o_ref, out_ref, out_o_ref, w_ref, w_out_ref):
    for t in range(3):
        w_ref[:, t * 384 : t * 384 + 384] = qkv_ref[t]
        w_ref[:, 1152 + t * 384 : 1536 + t * 384] = qkv_o_ref[t].astype(BF16)
    w_out_ref[0:384, :] = out_ref[...]
    w_out_ref[384:768, :] = out_o_ref[...].astype(BF16)


def attn_weights(qkv, qkv_o, out, out_o):
    vmem = pl.BlockSpec(memory_space=pltpu.VMEM)
    return call(
        attn_weights_body,
        (shape((D, 2304), BF16), shape((D, D), BF16)),
        [vmem] * 4,
        (vmem, vmem),
    )(qkv, qkv_o, out, out_o)


def ff_weights_body(up_ref, up_o_ref, down_ref, down_o_ref, w_up_ref, w_down_ref):
    half = pl.program_id(0)

    @pl.when(half == 0)
    def _():
        w_up_ref[...] = up_ref[...]
        w_down_ref[...] = down_ref[...]

    @pl.when(half == 1)
    def _():
        w_up_ref[...] = up_o_ref[...].astype(BF16)
        w_down_ref[...] = down_o_ref[...].astype(BF16)


def ff_weights(up, up_o, down, down_o):
    return call(
        ff_weights_body,
        (shape((D, 3072), BF16), shape((3072, D), BF16)),
        [whole(D, 1536), whole(D, 1536), whole(1536, D), whole(1536, D)],
        (pl.BlockSpec((D, 1536), lambda h: (0, h)), pl.BlockSpec((1536, D), lambda h: (h, 0))),
        grid=(2,),
    )(up, up_o, down, down_o)


def place():
    s, r, p = lax.axis_index("section"), lax.axis_index("dp"), lax.axis_index("tensor")
    return s, r, p, r // 4, r % 4


def on_dp(y, z):
    return {"dp": y * 4 + z}


def greet(peers):
    barrier = pltpu.get_barrier_semaphore()
    for peer in peers:
        pl.semaphore_signal(barrier, inc=1, device_id=peer, device_id_type=MESH)
    pl.semaphore_wait(barrier, len(peers))


def remote(src, dst, send, recv, device):
    return pltpu.make_async_remote_copy(
        src_ref=src, dst_ref=dst, send_sem=send, recv_sem=recv, device_id=device,
        device_id_type=MESH,
    )


def gather_body(qkv_in, out_in, up_in, down_in, qvb_in, upb_in,
                qkv, out, up, down, qvb, upb, send0, recv0, send1, recv1, send2, recv2, gate):
    s, r, p, y, z = place()
    partner = {"tensor": 1 - p}
    z_peers = [on_dp(y, (z + d) % 4) for d in range(1, 4)]
    y_peers = [on_dp((y + d) % 4, z) for d in range(1, 4)]
    attn = s % 2 == 0
    barrier = pltpu.get_barrier_semaphore()
    for peer in [partner] + z_peers + y_peers:
        pl.semaphore_signal(barrier, inc=1, device_id=peer, device_id_type=MESH)

    @pl.when(attn)
    def _():
        pl.semaphore_wait(barrier, 8)

    @pl.when(jnp.logical_not(attn))
    def _():
        pl.semaphore_signal(barrier, inc=1, device_id={"section": s - 1}, device_id_type=MESH)
        pl.semaphore_wait(barrier, 7)

    def run(whole_pair, z_first, y_first, gated):
        pieces = [(src, view, True) for src, view in z_first]
        pieces += [(src, view, False) for src, view in y_first]
        copies0 = [
            remote(src, view(y, z), send0.at[i], recv0.at[i], partner)
            for i, (src, view, _) in enumerate(pieces)
        ]
        bias = remote(whole_pair[0], whole_pair[1], send0.at[3], recv0.at[3], partner)
        for copy in copies0:
            copy.start()
        bias.start()
        if gated:
            pl.semaphore_wait(gate, 1)
        copies1 = []
        for i, (src, view, along_z) in enumerate(pieces):
            copies0[i].wait_recv()
            part = view(y, z)
            copies1.append([
                remote(part, part, send1.at[i, d], recv1.at[i, d],
                       z_peers[d] if along_z else y_peers[d])
                for d in range(3)
            ])
            for copy in copies1[-1]:
                copy.start()
        copies2 = []
        for i, (src, view, along_z) in enumerate(pieces):
            for copy in copies1[i]:
                copy.wait_recv()
            part = view(y, slice(None)) if along_z else view(slice(None), z)
            copies2.append([
                remote(part, part, send2.at[i, d], recv2.at[i, d],
                       y_peers[d] if along_z else z_peers[d])
                for d in range(3)
            ])
            for copy in copies2[-1]:
                copy.start()
        for group in copies2:
            for copy in group:
                copy.wait_recv()
        bias.wait_recv()
        if not gated:
            pl.semaphore_signal(gate, inc=1, device_id={"section": s + 1}, device_id_type=MESH)
        for copy in copies0 + [bias]:
            copy.wait_send()
        for group in copies1 + copies2:
            for copy in group:
                copy.wait_send()

    @pl.when(attn)
    def _():
        run(
            (qvb_in, qvb),
            [(qkv_in.at[0:2], lambda a, b: qkv.at[0:2, a, b])],
            [(qkv_in.at[2], lambda a, b: qkv.at[2, a, b]), (out_in, lambda a, b: out.at[a, b])],
            False,
        )

    @pl.when(jnp.logical_not(attn))
    def _():
        run(
            (upb_in, upb),
            [(up_in, lambda a, b: up.at[a, b])],
            [(down_in, lambda a, b: down.at[a, b])],
            True,
        )


def gather_halves(qkv, out, up, down, qv_bias, up_bias):
    dma = pltpu.SemaphoreType.DMA
    any_spec = pl.BlockSpec(memory_space=ANY)
    return call(
        gather_body,
        (shape((3, 4, 4, 48, 384), F32), shape((4, 4, 24, D), F32), shape((4, 4, 48, 1536), F32),
         shape((4, 4, 96, D), F32), shape((2, 384), F32), shape((1, 1536), F32)),
        [any_spec] * 6,
        (any_spec,) * 6,
        scratch=[dma((4,)), dma((4,)), dma((3, 3)), dma((3, 3)), dma((3, 3)), dma((3, 3)),
                 pltpu.SemaphoreType.REGULAR],
        collective_id=1,
        has_side_effects=True,
    )(qkv, out, up, down, qv_bias, up_bias)


def local(src, dst, sem):
    return pltpu.make_async_copy(src, dst, sem)


def start_all(copies):
    for copy in copies:
        copy.start()


def wait_all(copies):
    for copy in copies:
        copy.wait()


BLOCKS = ROWS // BLOCK


class Link:
    def __init__(self, src, dst, send, recv):
        self.src, self.dst, self.sems = src, dst, (send, recv)

    def copy(self, i, device):
        r = block(i)
        return remote(self.src.at[r], self.dst.at[r], self.sems[0].at[i], self.sems[1].at[i], device)

    def expect_from(self, device):
        pl.semaphore_signal(
            pltpu.get_barrier_semaphore(), inc=1, device_id=device, device_id_type=MESH)

    def ready(self):
        pl.semaphore_wait(pltpu.get_barrier_semaphore(), 1)

    def arrived(self, i, device):
        self.copy(i, device).wait_recv()

    def sent(self, device):
        for i in range(BLOCKS):
            self.copy(i, device).wait_send()


def stores(pairs, sems):
    def of(i):
        r = block(i)
        found = []
        for n, (src, dst) in enumerate(pairs):
            if len(src.shape) == 3:
                found.append(local(src.at[:, r], dst.at[:, r], sems.at[n, i]))
            else:
                found.append(local(src.at[r], dst.at[r], sems.at[n, i]))
        return found

    return of


def every_block(step):
    def body(i, carry):
        step(i, block(i))
        return carry

    lax.fori_loop(0, BLOCKS, body, 0)


def out_proj_rows(o_v, h_v, w_out_v, end, hout, r):
    hout[r, :] = h_v[r, :] + (dot(joined(o_v, r), w_out_v[...]) + end)


def forward_body(o, h0, w_out, up, down, w, gain, shift, end, upb, qkvb,
                 h_out, h_in, act, slope, normed, q, k, v,
                 hin, hout, up_v, down_v, act_v, slope_v, normed_v, o_v, w_out_v, w_v, q_v, k_v,
                 v_v, ld, st, send, recv):
    s, _, p, _, _ = place()
    link = Link(hout, hin, send, recv)

    @pl.when(s == 0)
    def _():
        target = {"section": 1}
        loads = [local(o, o_v, ld.at[0]), local(h0, hin, ld.at[1]), local(w_out, w_out_v, ld.at[2])]
        start_all(loads)
        link.ready()
        wait_all(loads)
        out = stores([(hout, h_out)], st)

        def step(i, r):
            out_proj_rows(o_v, hin, w_out_v, end[...], hout, r)
            link.copy(i, target).start()
            start_all(out(i))

        every_block(step)
        link.sent(target)
        for i in range(BLOCKS):
            wait_all(out(i))

    @pl.when(s == 1)
    def _():
        source, target = {"section": 0}, {"section": 2, "tensor": 1 - p}
        loads = [local(up, up_v, ld.at[0]), local(down, down_v, ld.at[1])]
        start_all(loads)
        link.expect_from(source)
        link.ready()
        wait_all(loads)
        out = stores([(hout, h_out), (hin, h_in), (act_v, act), (slope_v, slope),
                      (normed_v, normed)], st)

        def step(i, r):
            link.arrived(i, source)
            h = hin[r, :]
            xhat, _ = normalized(h)
            low = (xhat * gain[...] + shift[...]).astype(BF16)
            normed_v[r, :] = low
            total = h + end[...]
            for c in range(0, 3072, 768):
                cols = slice(c, c + 768)
                x = dot(low, up_v[:, cols]) + upb[:, cols]
                active, steep = gelu_and_slope(x)
                act_v[r, cols] = active
                slope_v[r, cols] = steep
                total = total + dot(active, down_v[cols, :])
            hout[r, :] = total
            link.copy(i, target).start()
            start_all(out(i))

        every_block(step)
        link.sent(target)
        for i in range(BLOCKS):
            wait_all(out(i))

    @pl.when(s == 2)
    def _():
        source = {"section": 1, "tensor": 1 - p}
        load = local(w, w_v, ld.at[0])
        load.start()
        link.expect_from(source)
        load.wait()
        out = stores([(hin, h_in), (normed_v, normed), (q_v, q), (k_v, k), (v_v, v)], st)

        def step(i, r):
            link.arrived(i, source)
            normed_v[r, :] = qkv_block(
                hin[r, :], gain[...], shift[...], w_v, qkvb, q_v, k_v, v_v, r)
            start_all(out(i))

        every_block(step)
        for i in range(BLOCKS):
            wait_all(out(i))


def staged(body, outs, operands, small, scratch, stored, collective_id):
    dma = pltpu.SemaphoreType.DMA
    any_spec = pl.BlockSpec(memory_space=ANY)
    vmem = pl.BlockSpec(memory_space=pltpu.VMEM)
    return call(
        body,
        tuple(shape(*o) for o in outs),
        [any_spec] * len(operands) + [vmem] * len(small),
        (any_spec,) * len(outs),
        scratch=[pltpu.VMEM(*x) for x in scratch]
        + [dma((8,)), dma((stored, BLOCKS))] + [dma((BLOCKS,))] * 4,
        collective_id=collective_id,
        has_side_effects=True,
    )(*operands, *small)


WIDE = (ROWS, D)
HIDDEN = (ROWS, 3072)
PAIRED = (PAIRS, ROWS, 128)


def forward(o, h0, w_out, up, down, w, gain, shift, end, upb, qkvb):
    def body(*refs):
        return forward_body(*refs[:-2])

    return staged(
        body,
        [(WIDE, F32), (WIDE, F32), (HIDDEN, BF16), (HIDDEN, F32), (WIDE, BF16), (PAIRED, BF16),
         (PAIRED, BF16), (PAIRED, BF16)],
        (o, h0, w_out, up, down, w),
        (gain, shift, end, upb, qkvb),
        [(WIDE, F32), (WIDE, F32), ((D, 3072), BF16), ((3072, D), BF16), (HIDDEN, BF16),
         (HIDDEN, F32), (WIDE, BF16), (PAIRED, BF16), ((D, D), BF16), ((D, 2304), BF16),
         (PAIRED, BF16), (PAIRED, BF16), (PAIRED, BF16)],
        5,
        2,
    )


def middle_body(o, h2, w_out, up, down, cot, gain, shift, end, upb,
                h_out, h_in, act, gr, gb, normed, g_in, gm, g_out, vec,
                hin, hout, gin, gout, act_v, gr_v, gb_v, normed_v, up_v, down_v, o_v, w_out_v, gm_v,
                vec_v, ups_v, ld, st, send, recv, back_send, back_recv):
    s, _, _, _, _ = place()
    link = Link(hout, hin, send, recv)
    back = Link(gout, gin, back_send, back_recv)

    @pl.when(s == 2)
    def _():
        other = {"section": 3}
        loads = [local(o, o_v, ld.at[0]), local(h2, hin, ld.at[1]), local(w_out, w_out_v, ld.at[2])]
        start_all(loads)
        back.expect_from(other)
        link.ready()
        wait_all(loads)
        out = stores([(hout, h_out)], st)
        back_out = stores([(hout, h_out), (gin, g_in), (gb_v, gb), (gm_v, gm)], st)

        def step(i, r):
            out_proj_rows(o_v, hin, w_out_v, end[...], hout, r)
            link.copy(i, other).start()
            start_all(out(i))

        every_block(step)

        def back_step(i, r):
            back.arrived(i, other)
            gb_v[r, :] = mixed_back_block(gin[r, :], w_out_v, gm_v, r)
            start_all(back_out(i)[1:])

        every_block(back_step)
        link.sent(other)
        for i in range(BLOCKS):
            wait_all(back_out(i))

    @pl.when(s == 3)
    def _():
        other = {"section": 2}
        loads = [local(up, up_v, ld.at[0]), local(down, down_v, ld.at[1]),
                 local(cot, gin, ld.at[2])]
        start_all(loads)
        link.expect_from(other)
        back.ready()
        wait_all(loads)
        vec_v[...] = jnp.zeros_like(vec_v)
        ups_v[...] = jnp.zeros_like(ups_v)
        out = stores([(hout, h_out), (hin, h_in), (act_v, act), (gr_v, gr), (gb_v, gb),
                      (normed_v, normed), (gout, g_out)], st)

        def step(i, r):
            link.arrived(i, other)
            h, g = hin[r, :], gin[r, :]
            xhat, _ = normalized(h)
            low = (xhat * gain[...] + shift[...]).astype(BF16)
            normed_v[r, :] = low
            g_low = g.astype(BF16)
            gb_v[r, :] = g_low
            total = h + end[...]
            grad_normed = jnp.zeros((BLOCK, D), F32)
            for c in range(0, 3072, 768):
                cols = slice(c, c + 768)
                x = dot(low, up_v[:, cols]) + upb[:, cols]
                active, steep = gelu_and_slope(x)
                act_v[r, cols] = active
                total = total + dot(active, down_v[cols, :])
                raised = (dot(g_low, down_v[cols, :], 1, 1) * steep).astype(BF16)
                gr_v[r, cols] = raised
                ups_v[:, cols] += jnp.sum(raised.astype(F32), axis=0, keepdims=True)
                grad_normed = grad_normed + dot(raised, up_v[:, cols], 1, 1)
            hout[r, :] = total
            result, xhat = norm_back(g, h, gain[...], grad_normed)
            gout[r, :] = result
            back.copy(i, other).start()
            add_row(vec_v, 0, grad_normed * xhat)
            add_row(vec_v, 1, grad_normed)
            add_row(vec_v, 2, g_low.astype(F32))
            start_all(out(i))

        every_block(step)
        for c in range(4):
            vec_v[3 + c : 4 + c, :] = ups_v[:, c * D : c * D + D]
        last = local(vec_v, vec, ld.at[3])
        last.start()
        back.sent(other)
        for i in range(BLOCKS):
            wait_all(out(i))
        last.wait()


def middle(o, h2, w_out, up, down, cot, gain, shift, end, upb):
    return staged(
        middle_body,
        [(WIDE, F32), (WIDE, F32), (HIDDEN, BF16), (HIDDEN, BF16), (WIDE, BF16), (WIDE, BF16),
         (WIDE, F32), (PAIRED, BF16), (WIDE, F32), ((8, D), F32)],
        (o, h2, w_out, up, down, cot),
        (gain, shift, end, upb),
        [(WIDE, F32)] * 4
        + [(HIDDEN, BF16), (HIDDEN, BF16), (WIDE, BF16), (WIDE, BF16), ((D, 3072), BF16),
           ((3072, D), BF16), (PAIRED, BF16), ((D, D), BF16), (PAIRED, BF16), ((8, D), F32),
           ((1, 3072), F32)],
        7,
        3,
    )


def backward_body(g2, h, gq, gk, gv, w, up, down, slope, w_out, gain,
                  g_out, g_in, gr, gb, gm, vec,
                  gin, gout, h_v, slope_v, gr_v, gb_v, up_v, down_v, gq_v, gk_v, gv_v, w_v, w_out_v,
                  gm_v, vec_v, ups_v, ld, st, send, recv, next_send, next_recv):
    s, _, p, _, _ = place()
    first = Link(gout, gin, send, recv)
    second = Link(gout, gin, next_send, next_recv)

    @pl.when(s == 2)
    def _():
        target = {"section": 1, "tensor": 1 - p}
        loads = [local(a, b, ld.at[n]) for n, (a, b) in enumerate(
            ((g2, gin), (h, h_v), (gq, gq_v), (gk, gk_v), (gv, gv_v), (w, w_v)))]
        start_all(loads)
        first.ready()
        wait_all(loads)
        vec_v[...] = jnp.zeros_like(vec_v)
        out = stores([(gout, g_out)], st)

        def step(i, r):
            gout[r, :] = qkv_back_block(
                gin[r, :], h_v[r, :], gain[...], gq_v, gk_v, gv_v, w_v, vec_v, r)
            first.copy(i, target).start()
            start_all(out(i))

        every_block(step)
        last = local(vec_v, vec, ld.at[6])
        last.start()
        first.sent(target)
        for i in range(BLOCKS):
            wait_all(out(i))
        last.wait()

    @pl.when(s == 1)
    def _():
        source, target = {"section": 2, "tensor": 1 - p}, {"section": 0}
        loads = [local(a, b, ld.at[n]) for n, (a, b) in enumerate(
            ((up, up_v), (down, down_v), (slope, slope_v), (h, h_v)))]
        start_all(loads)
        first.expect_from(source)
        second.ready()
        wait_all(loads)
        vec_v[...] = jnp.zeros_like(vec_v)
        ups_v[...] = jnp.zeros_like(ups_v)
        out = stores([(gout, g_out), (gr_v, gr), (gb_v, gb)], st)

        def step(i, r):
            first.arrived(i, source)
            g = gin[r, :]
            g_low = g.astype(BF16)
            gb_v[r, :] = g_low
            grad_normed = jnp.zeros((BLOCK, D), F32)
            for c in range(0, 3072, 768):
                cols = slice(c, c + 768)
                raised = (dot(g_low, down_v[cols, :], 1, 1) * slope_v[r, cols]).astype(BF16)
                gr_v[r, cols] = raised
                ups_v[:, cols] += jnp.sum(raised.astype(F32), axis=0, keepdims=True)
                grad_normed = grad_normed + dot(raised, up_v[:, cols], 1, 1)
            result, xhat = norm_back(g, h_v[r, :], gain[...], grad_normed)
            gout[r, :] = result
            second.copy(i, target).start()
            add_row(vec_v, 0, grad_normed * xhat)
            add_row(vec_v, 1, grad_normed)
            add_row(vec_v, 2, g_low.astype(F32))
            start_all(out(i))

        every_block(step)
        for c in range(4):
            vec_v[3 + c : 4 + c, :] = ups_v[:, c * D : c * D + D]
        last = local(vec_v, vec, ld.at[6])
        last.start()
        second.sent(target)
        for i in range(BLOCKS):
            wait_all(out(i))
        last.wait()

    @pl.when(s == 0)
    def _():
        source = {"section": 1}
        load = local(w_out, w_out_v, ld.at[0])
        load.start()
        second.expect_from(source)
        load.wait()
        out = stores([(gin, g_in), (gb_v, gb), (gm_v, gm)], st)

        def step(i, r):
            second.arrived(i, source)
            gb_v[r, :] = mixed_back_block(gin[r, :], w_out_v, gm_v, r)
            start_all(out(i))

        every_block(step)
        for i in range(BLOCKS):
            wait_all(out(i))


def backward(g2, h, gq, gk, gv, w, up, down, slope, w_out, gain):
    return staged(
        backward_body,
        [(WIDE, F32), (WIDE, F32), (HIDDEN, BF16), (WIDE, BF16), (PAIRED, BF16), ((8, D), F32)],
        (g2, h, gq, gk, gv, w, up, down, slope, w_out),
        (gain,),
        [(WIDE, F32)] * 3
        + [(HIDDEN, F32), (HIDDEN, BF16), (WIDE, BF16), ((D, 3072), BF16), ((3072, D), BF16),
           (PAIRED, BF16), (PAIRED, BF16), (PAIRED, BF16), ((D, 2304), BF16), ((D, D), BF16),
           (PAIRED, BF16), ((8, D), F32), ((1, 3072), F32)],
        3,
        4,
    )


def exchange_body(h, theirs, send, recv):
    s, _, p, _, _ = place()

    @pl.when(s < 2)
    def _():
        partner = {"tensor": 1 - p}
        greet([partner])
        copy = remote(h, theirs, send, recv, partner)
        copy.start()
        copy.wait()


def exchange(h):
    dma = pltpu.SemaphoreType.DMA
    any_spec = pl.BlockSpec(memory_space=ANY)
    return call(
        exchange_body, shape(WIDE, F32), [any_spec], any_spec,
        scratch=[dma, dma], collective_id=5, has_side_effects=True,
    )(h)


def finish_body(hm, g0, gb, gm, w0, w1, w2, w3, v0, vb, vm,
                h_theirs, g_theirs, out, vec,
                acc, r1, r2, fin, r3, va, v1r, v2r,
                own, s1, q1, s2, q2, s3, q3, xs, xr, vs, vr, vo):
    s, r, p, y, z = place()
    partner = {"tensor": 1 - p}
    z_peers = [on_dp(y, (z + d) % 4) for d in range(1, 4)]
    y_peers = [on_dp((y + d) % 4, z) for d in range(1, 4)]
    greet([partner] + z_peers + y_peers)

    def run(h, g, w, v, chunks):
        jobs = [(c * CHUNK, c < chunks // 2) for c in range(chunks)]
        first, second, third = [], [], []
        vload = pltpu.make_async_copy(v, va, vo.at[0])
        vload.start()
        for j, (c, z_first) in enumerate(jobs):
            cols = pl.ds(c, CHUNK)
            if z_first:
                here = w.at[:, :, z, :, cols]
                there = [w.at[:, :, (z + d) % 4, :, cols] for d in range(1, 4)]
                peers = z_peers
            else:
                here = w.at[:, y, :, :, cols]
                there = [w.at[:, (y + d) % 4, :, :, cols] for d in range(1, 4)]
                peers = y_peers
            load = pltpu.make_async_copy(here, acc.at[j], own.at[j])
            load.start()
            group = [
                remote(there[d], r1.at[j, d], s1.at[j, d], q1.at[j, d], peers[d]) for d in range(3)
            ]
            for copy in group:
                copy.start()
            first.append((load, group))
        vload.wait()
        vgroup = [remote(va, v1r.at[d], vs.at[d], vr.at[d], z_peers[d]) for d in range(3)]
        for copy in vgroup:
            copy.start()
        swap = [remote(g, g_theirs, xs.at[0], xr.at[0], partner)]
        if h is not None:
            swap.append(remote(h, h_theirs, xs.at[1], xr.at[1], partner))
        start_all(swap)

        for j, (c, z_first) in enumerate(jobs):
            load, group = first[j]
            load.wait()
            for copy in group:
                copy.wait_recv()

            def total(i, carry, j=j):
                a, b = i // 4, i % 4
                acc[j, a, b] += r1[j, 0, a, b] + r1[j, 1, a, b] + r1[j, 2, a, b]
                return carry

            lax.fori_loop(0, 8, total, 0)
            peers = y_peers if z_first else z_peers
            mine = y if z_first else z
            group = [
                remote(acc.at[j, :, (mine + d + 1) % 4], r2.at[j, d], s2.at[j, d], q2.at[j, d],
                       peers[d])
                for d in range(3)
            ]
            for copy in group:
                copy.start()
            second.append(group)
        for copy in vgroup:
            copy.wait()
        va[...] = va[...] + v1r[0] + v1r[1] + v1r[2]
        vgroup = [remote(va, v2r.at[d], vs.at[3 + d], vr.at[3 + d], y_peers[d]) for d in range(3)]
        for copy in vgroup:
            copy.start()
        for j, (c, z_first) in enumerate(jobs):
            for copy in second[j]:
                copy.wait_recv()
            mine = y if z_first else z
            for a in range(2):
                fin[j, a] = acc[j, a, mine] + r2[j, 0, a] + r2[j, 1, a] + r2[j, 2, a]
            copy = remote(fin.at[j, 1], r3.at[j], s3.at[j], q3.at[j], partner)
            copy.start()
            third.append(copy)
        for copy in vgroup:
            copy.wait()
        vec[0] = va[...] + v2r[0] + v2r[1] + v2r[2]
        vlast = remote(vec.at[0], vec.at[1], vs.at[6], vr.at[6], partner)
        vlast.start()
        for j, (c, _) in enumerate(jobs):
            third[j].wait_recv()
            out[:, c : c + CHUNK] = fin[j, 0] + r3[j]
        vlast.wait()
        wait_all(swap)
        for copy in third:
            copy.wait_send()
        for _, group in first:
            for copy in group:
                copy.wait_send()
        for group in second:
            for copy in group:
                copy.wait_send()

    pl.when(s == 0)(lambda: run(None, g0, w0, v0, 2))
    pl.when(s == 1)(lambda: run(None, gb, w1, vb, 4))
    pl.when(s == 2)(lambda: run(hm, gb, w2, vb, 2))
    pl.when(s == 3)(lambda: run(hm, gm, w3, vm, 4))


def finish(hm, gs, ws, vs):
    dma = pltpu.SemaphoreType.DMA
    any_spec = pl.BlockSpec(memory_space=ANY)
    vmem = pl.BlockSpec(memory_space=pltpu.VMEM)
    return call(
        finish_body,
        (shape(WIDE, F32), shape(WIDE, F32), shape((48, 3072), F32),
         shape((2, 8, D), F32)),
        [any_spec] * 11,
        (any_spec, any_spec, vmem, vmem),
        scratch=[
            pltpu.VMEM((4, 2, 4, 48, CHUNK), F32),
            pltpu.VMEM((4, 3, 2, 4, 48, CHUNK), F32),
            pltpu.VMEM((4, 3, 2, 48, CHUNK), F32),
            pltpu.VMEM((4, 2, 48, CHUNK), F32),
            pltpu.VMEM((4, 48, CHUNK), F32),
            pltpu.VMEM((8, D), F32),
            pltpu.VMEM((3, 8, D), F32),
            pltpu.VMEM((3, 8, D), F32),
            dma((4,)), dma((4, 3)), dma((4, 3)), dma((4, 3)), dma((4, 3)), dma((4,)), dma((4,)),
            dma((2,)), dma((2,)), dma((7,)), dma((7,)), dma((1,)),
        ],
        collective_id=20,
        has_side_effects=True,
    )(hm, *gs, *ws, *vs)


def assemble_body(hf, hm, h_early, h_late, g0, gb, gm, g_late, hid, gin, h_v, g_v, sems):
    s, _, p, _, _ = place()
    step = pl.program_id(0)
    clip = jnp.where(s < 2, p, 1 - p)

    def at(index, n, h, g):
        return [local(h, h_v.at[index], sems.at[n, 0]), local(g, g_v.at[index], sems.at[n, 1])]

    @pl.when(step == 0)
    def _():
        mine = ((s == 0, hf, g0), (s == 1, hf, gb), (s == 2, hm, gb), (s == 3, hm, gm))
        for active, h, g in mine:
            pl.when(active)(functools.partial(lambda h, g: start_all(at(clip, 0, h, g)), h, g))
        pl.when(s < 2)(lambda: start_all(at(1 - clip, 1, h_early, g_late)))
        pl.when(s >= 2)(lambda: start_all(at(1 - clip, 1, h_late, g_late)))

    pl.when(step == clip)(lambda: wait_all(at(clip, 0, hf, g0)))
    pl.when(step != clip)(lambda: wait_all(at(1 - clip, 1, h_late, g_late)))
    hid[0, 0] = h_v[step, 0:LENGTH, :]
    gin[0, 0] = g_v[step, 0:LENGTH, :]


def assemble(*operands):
    any_spec = pl.BlockSpec(memory_space=ANY)
    out = pl.BlockSpec((1, 1, LENGTH, D), lambda c: (0, c, 0, 0))
    return call(
        assemble_body,
        (shape((1, 2, LENGTH, D), F32),) * 2,
        [any_spec] * 8,
        (out, out),
        grid=(2,),
        scratch=[pltpu.VMEM((2, ROWS, D), F32), pltpu.VMEM((2, ROWS, D), F32),
                 pltpu.SemaphoreType.DMA((2, 2))],
    )(*operands)


def unwritten(shapes):
    any_spec = pl.BlockSpec(memory_space=ANY)
    return pl.pallas_call(
        lambda *refs: None,
        out_shape=tuple(shapes),
        out_specs=(any_spec,) * len(shapes),
    )()


def only_at(active, run, operands):
    like = jax.eval_shape(run, *operands)
    leaves, tree = jax.tree.flatten(like)

    def skip(*_):
        return jax.tree.unflatten(tree, unwritten([shape(x.shape, x.dtype) for x in leaves]))

    return lax.cond(active, run, skip, *operands)


def pad_rows(x):
    return jnp.pad(x.astype(F32), ((0, ROWS - LENGTH), (0, 0)))


def per_device(inputs, cotangent, norm_gain, norm_bias, qkv_weight, qv_bias, out_weight, end_bias,
               up_weight, up_bias, down_weight):
    s, r, p = lax.axis_index("section"), lax.axis_index("dp"), lax.axis_index("tensor")
    clip = jnp.where(s < 2, p, 1 - p)
    qkv, out_w, up, down = qkv_weight[0], out_weight[0], up_weight[0], down_weight[0]

    def slice_of(x, axis, size):
        return lax.dynamic_slice_in_dim(x, r * size, size, axis).astype(F32)

    qkv_o, out_o, up_o, down_o, qvb_o, upb_o = gather_halves(
        slice_of(qkv, 1, 48), slice_of(out_w, 0, 24), slice_of(up, 0, 48), slice_of(down, 0, 96),
        qv_bias[0], up_bias,
    )

    attn = s % 2 == 0
    w, w_out = only_at(attn, attn_weights, (
        qkv, qkv_o.reshape(3, D, 384), out_w, out_o.reshape(384, D)))
    w_up, w_down = only_at(~attn, ff_weights, (
        up, up_o.reshape(D, 1536), down, down_o.reshape(1536, D)))
    upb = jnp.concatenate([up_bias, upb_o], axis=1)
    none = jnp.zeros((384,), F32)
    qkvb = jnp.concatenate(
        [qv_bias[0, 0], none, qv_bias[0, 1], qvb_o[0], none, qvb_o[1]])[None]
    gain, shift, end = norm_gain, norm_bias, end_bias

    def start(h):
        q, k, v, normed = first_qkv(h, gain, shift, w, qkvb)
        o, lse = attend(q, k, v)
        return q, k, v, normed, o, lse

    h0 = pad_rows(lax.dynamic_index_in_dim(inputs, clip, 0, keepdims=False))
    cot = pad_rows(lax.dynamic_index_in_dim(cotangent, clip, 0, keepdims=False))
    q0, k0, v0, normed0, o0, lse0 = only_at(s == 0, start, (h0,))
    hf, h_in, act1, slope1, normed_f, q2, k2, v2 = forward(
        o0, h0, w_out, w_up, w_down, w, gain, shift, end, upb, qkvb)
    h_early = exchange(hf)
    o2, lse2 = only_at(s == 2, attend, (q2, k2, v2))
    o2, h_early = lax.optimization_barrier((o2, h_early))
    hm, _, act3, gr3, gb_m, normed3, g2, gm2, g_m, vec_m = middle(
        o2, h_in, w_out, w_up, w_down, cot, gain, shift, end, upb)
    gq2, gk2, gv2 = only_at(s == 2, attend_back, (q2, k2, v2, o2, gm2, lse2))
    g_b, g_in0, gr1, gb_b, gm0, vec_b = backward(
        g2, h_in, gq2, gk2, gv2, w, w_up, w_down, slope1, w_out, gain)

    def end_back(q, k, v, o, gm, lse, g, h):
        gq, gk, gv = attend_back(q, k, v, o, gm, lse)
        return last_qkv_back(g, h, gain, gq, gk, gv, w) + (gq, gk, gv)

    g_0, vec_0, gq0, gk0, gv0 = only_at(s == 0, end_back, (q0, k0, v0, o0, gm0, lse0, g_in0, h0))
    gb_m, vec_b = lax.optimization_barrier((gb_m, vec_b))
    w3 = only_at(s == 3, ff_weight_grads, (normed3, gb_m, gr3, act3))
    w2 = only_at(s == 2, attn_weight_grads, (normed_f, gb_m, gq2, gk2, gv2, o2))
    w1 = only_at(s == 1, ff_weight_grads, (normed_f, gb_b, gr1, act1))
    w0 = only_at(s == 0, attn_weight_grads, (normed0, gb_b, gq0, gk0, gv0, o0))
    split = [x.reshape(2, 4, 4, 48, x.shape[2]) for x in (w0, w1, w2, w3)]
    h_late, g_late, sums, vec = finish(hm, (g_0, g_b, g_m), split, (vec_0, vec_b, vec_m))
    hid, gin = assemble(hf, hm, h_early, h_late, g_0, g_b, g_m, g_late)

    both = vec[0] + vec[1]

    def mine(row):
        return lax.dynamic_slice_in_dim(both[row], r * 48, 48)[None]

    def when(flag, x):
        return jnp.where(flag, x, 0.0)[None]

    qkv_grad = jnp.transpose(sums[:, :1152].reshape(48, 3, 384), (1, 0, 2))
    qv_grad = vec[0, 3:5, :384] + vec[1, 3:5, 384:]
    up_bias_grad = (vec[0, 3:5] + vec[1, 5:7]).reshape(1536)
    return (
        hid,
        gin,
        mine(0),
        mine(1),
        when(attn, qkv_grad),
        when(attn, qv_grad),
        when(attn, sums[:, 1152:1536].T),
        mine(2),
        when(~attn, sums[:, :1536]),
        when(~attn, up_bias_grad),
        when(~attn, sums[:, 1536:].T),
    )


def solution(mesh):
    return jax.shard_map(
        per_device,
        mesh=mesh,
        in_specs=(
            P("dp", None, None),
            P("dp", None, None),
            P("section", None),
            P("section", None),
            P("section", None, None, "tensor"),
            P("section", None, "tensor"),
            P("section", "tensor", None),
            P("section", None),
            P("section", None, "tensor"),
            P("section", "tensor"),
            P("section", "tensor", None),
        ),
        out_specs=(
            P("section", "dp", None, None),
            P("section", "dp", None, None),
            P("section", "dp"),
            P("section", "dp"),
            P("section", None, "dp", "tensor"),
            P("section", None, "tensor"),
            P("section", "tensor", "dp"),
            P("section", "dp"),
            P("section", "dp", "tensor"),
            P("section", "tensor"),
            P("section", "tensor", "dp"),
        ),
        check_vma=False,
    )
```

```python
import functools

import jax
import jax.numpy as jnp
from jax import lax
from jax.experimental import pallas as pl
from jax.experimental.pallas import tpu as pltpu
from jax.sharding import PartitionSpec as P

MESH = pl.DeviceIdType.MESH
ANY = pl.ANY
F32 = jnp.float32
BF16 = jnp.bfloat16

HEAD_DIM = 64
EPS = 1e-06
LENGTH = 866
ROWS = 896
BLOCK = 224
D = 768
PAIRS = 6
Q_BLOCKS = ((0, 256), (256, 256), (512, 384))
VMEM_BYTES = 60 * 1024 * 1024

CHUNK = 768


def call(body, out_shape, in_specs, out_specs, grid=(), scratch=(), aliases={}, **more):
    return pl.pallas_call(
        body,
        out_shape=out_shape,
        grid=grid,
        in_specs=in_specs,
        out_specs=out_specs,
        scratch_shapes=scratch,
        input_output_aliases=aliases,
        compiler_params=pltpu.CompilerParams(vmem_limit_bytes=VMEM_BYTES, **more),
    )


def shape(dims, dtype):
    return jax.ShapeDtypeStruct(dims, dtype)


def whole(*dims):
    return pl.BlockSpec(dims, lambda *_: (0,) * len(dims), pipeline_mode=pl.Buffered(1))


def rows_of(width):
    return pl.BlockSpec((BLOCK, width), lambda i: (i, 0))


def dot(a, b, ca=1, cb=0):
    return lax.dot_general(a, b, (((ca,), (cb,)), ((), ())), preferred_element_type=F32)


def normalized(h):
    average = jnp.mean(h, axis=-1, keepdims=True)
    centred = h - average
    spread = jnp.mean(centred * centred, axis=-1, keepdims=True)
    r = lax.rsqrt(spread + EPS)
    return centred * r, r


def norm_back(g, h, gain, grad_normed):
    xhat, r = normalized(h)
    t = grad_normed * gain
    t_mean = jnp.mean(t, axis=-1, keepdims=True)
    tx_mean = jnp.mean(t * xhat, axis=-1, keepdims=True)
    return g + r * (t - t_mean - xhat * tx_mean), xhat


def block(i):
    return pl.ds(pl.multiple_of(i * BLOCK, 32), BLOCK)


def gelu_and_slope(x):
    phi = 0.5 * (1.0 + lax.erf(x * 0.7071067811865476))
    density = jnp.exp(-0.5 * x * x) * 0.3989422804014327
    return (x * phi).astype(BF16), phi + x * density


def qkv_block(h, gain, shift, w_ref, bias, q_ref, k_ref, v_ref, r):
    xhat, _ = normalized(h)
    normed = (xhat * gain + shift).astype(BF16)
    for c in range(0, 2304, 768):
        part = (dot(normed, w_ref[:, c : c + 768]) + bias[:, c : c + 768]).astype(BF16)
        for n in range(c // 128, c // 128 + 6):
            lanes = part[:, n * 128 - c : n * 128 - c + 128]
            pair = n // 9 * 3 + n % 3
            kind = n % 9 // 3
            if kind == 0:
                q_ref[pair, r, :] = (lanes.astype(F32) * 0.125).astype(BF16)
            elif kind == 1:
                k_ref[pair, r, :] = lanes
            else:
                v_ref[pair, r, :] = lanes
    return normed


def joined(ref, r):
    return jnp.concatenate([ref[j, r, :] for j in range(PAIRS)], axis=1)


def mixed_back_block(g, w_out_ref, gm_ref, r):
    gb = g.astype(BF16)
    gm = dot(gb, w_out_ref[...], 1, 1).astype(BF16)
    for j in range(PAIRS):
        gm_ref[j, r, :] = gm[:, j * 128 : j * 128 + 128]
    return gb


def add_row(vec_ref, at, values):
    vec_ref[at : at + 1, :] += jnp.sum(values, axis=0, keepdims=True)


def qkv_back_rows(g, h, gain, parts, w_ref, vec_ref):
    grad_normed = jnp.zeros((BLOCK, D), F32)
    for half, (qk, v) in enumerate(parts):
        part = jnp.concatenate([qk, v], axis=1)
        grad_normed = grad_normed + dot(part, w_ref[:, half * 1152 : half * 1152 + 1152], 1, 1)
    out, xhat = norm_back(g, h, gain, grad_normed)
    add_row(vec_ref, 0, grad_normed * xhat)
    add_row(vec_ref, 1, grad_normed)
    add_row(vec_ref, 2, g.astype(BF16).astype(F32))
    add_row(vec_ref, 3, jnp.concatenate([qk[:, :384] for qk, _ in parts], axis=1).astype(F32))
    add_row(vec_ref, 4, jnp.concatenate([v for _, v in parts], axis=1).astype(F32))
    return out


def pairs_of(refs, half, r):
    return jnp.concatenate([ref[half * 3 + i, r, :] for ref in refs for i in range(3)], axis=1)


def head_mask(dims, axis, head):
    at = lax.broadcasted_iota(jnp.int32, dims, axis)
    return at < HEAD_DIM if head == 0 else at >= HEAD_DIM


def key_masked(s):
    cut = 864
    tail = s[cut:, :]
    at = lax.broadcasted_iota(jnp.int32, tail.shape, 0)
    tail = jnp.where(at < LENGTH - cut, tail, -1e30)
    return jnp.concatenate([s[:cut, :], tail], axis=0)


def attend_pair(q_ref, k_ref, v_ref, o_ref, lse_ref, j):
    k = k_ref[j]
    v_t = v_ref[j].T
    lse_ref[j] = jnp.zeros((8, ROWS), F32)
    v_heads = [jnp.where(head_mask(v_t.shape, 0, head), v_t, 0) for head in range(2)]
    for start, size in Q_BLOCKS:
        rows = slice(start, start + size)
        q = q_ref[j, rows, :]
        out = jnp.zeros((128, size), F32)
        for head in range(2):
            q_head = jnp.where(head_mask(q.shape, 1, head), q, 0)
            s = key_masked(dot(k, q_head, 1, 1))
            top = jnp.max(s, axis=0, keepdims=True)
            e = jnp.exp(s - top)
            total = jnp.sum(e, axis=0, keepdims=True)
            p = (e * (1.0 / total)).astype(BF16)
            out = out + dot(v_heads[head], p)
            lse_ref[j, head : head + 1, rows] = top + jnp.log(total)
        o_ref[j, rows, :] = out.T.astype(BF16)


def attend_body(q_ref, k_ref, v_ref, o_ref, lse_ref):
    attend_pair(q_ref, k_ref, v_ref, o_ref, lse_ref, 0)


PAIR = pl.BlockSpec((1, ROWS, 128), lambda j: (j, 0, 0))
PAIR_ROW = pl.BlockSpec((1, 8, ROWS), lambda j: (j, 0, 0))


def attend(q, k, v):
    return call(
        attend_body,
        (shape((PAIRS, ROWS, 128), BF16), shape((PAIRS, 8, ROWS), F32)),
        [PAIR] * 3,
        (PAIR, PAIR_ROW),
        grid=(PAIRS,),
    )(q, k, v)


def attend_back_body(q_ref, k_ref, v_ref, o_ref, gm_ref, lse_ref, gq_ref, gk_ref, gv_ref):
    k, v = k_ref[0], v_ref[0]
    k_t = k.T
    k_heads = [jnp.where(head_mask(k_t.shape, 0, head), k_t, 0) for head in range(2)]
    grad_k = jnp.zeros((ROWS, 128), F32)
    grad_v = jnp.zeros((ROWS, 128), F32)
    for start, size in Q_BLOCKS:
        rows = slice(start, start + size)
        q, gm = q_ref[0, rows, :], gm_ref[0, rows, :]
        product = gm.astype(F32) * o_ref[0, rows, :].astype(F32)
        grad_q = jnp.zeros((128, size), F32)
        for head in range(2):
            q_head = jnp.where(head_mask(q.shape, 1, head), q, 0)
            gm_head = jnp.where(head_mask(gm.shape, 1, head), gm, 0)
            ones = jnp.where(head_mask((8, 128), 1, head), 1.0, 0.0)
            inner = lax.dot_general(
                ones, product, (((1,), (1,)), ((), ())),
                precision=lax.Precision.HIGHEST, preferred_element_type=F32,
            )[0:1, :]
            s = key_masked(dot(k, q_head, 1, 1))
            p = jnp.exp(s - lse_ref[0, head : head + 1, rows])
            gp = dot(v, gm_head, 1, 1)
            gs = (p * (gp - inner)).astype(BF16)
            grad_v = grad_v + dot(p.astype(BF16), gm_head)
            grad_k = grad_k + dot(gs, q_head)
            grad_q = grad_q + dot(k_heads[head], gs)
        gq_ref[0, rows, :] = (grad_q.T * 0.125).astype(BF16)
    gk_ref[0] = grad_k.astype(BF16)
    gv_ref[0] = grad_v.astype(BF16)


def attend_back(q, k, v, o, gm, lse):
    return call(
        attend_back_body,
        (shape((PAIRS, ROWS, 128), BF16),) * 3,
        [PAIR] * 5 + [PAIR_ROW],
        (PAIR,) * 3,
        grid=(PAIRS,),
    )(q, k, v, o, gm, lse)


def extract_body(x_ref, out_ref):
    s, p = lax.axis_index("section"), lax.axis_index("tensor")
    clip = jnp.where(s < 2, p, 1 - p)
    x = x_ref[...].astype(F32)
    x = jnp.where(clip == 0, x[:, 0, :], x[:, 1, :])
    at = lax.broadcasted_iota(jnp.int32, x.shape, 0) + pl.program_id(0) * BLOCK
    out_ref[...] = jnp.where(at < LENGTH, x, 0.0)


def extract(x):
    return call(
        extract_body,
        shape((ROWS, D), F32),
        [pl.BlockSpec((BLOCK, 2, D), lambda i: (i, 0, 0))],
        rows_of(D),
        grid=(ROWS // BLOCK,),
    )(x)


def place():
    s, r, p = lax.axis_index("section"), lax.axis_index("dp"), lax.axis_index("tensor")
    return s, r, p, r // 4, r % 4


def on_dp(y, z):
    return {"dp": y * 4 + z}


def greet(peers):
    barrier = pltpu.get_barrier_semaphore()
    for peer in peers:
        pl.semaphore_signal(barrier, inc=1, device_id=peer, device_id_type=MESH)
    pl.semaphore_wait(barrier, len(peers))


def remote(src, dst, send, recv, device):
    return pltpu.make_async_remote_copy(
        src_ref=src, dst_ref=dst, send_sem=send, recv_sem=recv, device_id=device,
        device_id_type=MESH,
    )


def local(src, dst, sem):
    return pltpu.make_async_copy(src, dst, sem)


def start_all(copies):
    for copy in copies:
        copy.start()


def wait_all(copies):
    for copy in copies:
        copy.wait()


BLOCKS = ROWS // BLOCK


class Piece:
    def __init__(self, n, source, view, halves, z_first, sems):
        self.n, self.source, self.view, self.halves, self.z_first = n, source, view, halves, z_first
        self.send, self.recv = sems
        _, _, p, self.y, self.z = place()
        self.partner = {"tensor": 1 - p}

    def copies(self, stage):
        y, z, view = self.y, self.z, self.view
        along_z = [on_dp(y, (z + d) % 4) for d in (1, 3)]
        along_y = [on_dp((y + d) % 4, z) for d in (1, 3)]

        def copy(n, src, dst, device):
            return remote(src, dst, self.send.at[self.n, stage, n], self.recv.at[self.n, stage, n],
                          device)

        def both(refs, peers):
            return [copy(n, refs[n], refs[n], peers[n]) for n in range(2)]

        everything = slice(0, 4)
        if self.z_first:
            ring, ring2 = along_z, along_y
            one = lambda d: view(y, (z + d) % 4)
            group = lambda d, part=everything: view((y + d) % 4, part)
        else:
            ring, ring2 = along_y, along_z
            one = lambda d: view((y + d) % 4, z)
            group = lambda d, part=everything: view(part, (z + d) % 4)
        if stage == 0:
            return [copy(0, self.source, view(y, z), self.partner)]
        if stage == 1:
            return both([one(0), one(0)], ring)
        if stage == 2:
            return both([self.halves(one(3))[0], self.halves(one(1))[1]], ring)
        if stage == 3:
            return both([group(0), group(0)], ring2)
        return both([group(3, slice(0, 2)), group(1, slice(2, 4))], ring2)


def advance(pieces, stage):
    for piece in pieces:
        if stage > 0:
            for copy in piece.copies(stage - 1):
                copy.wait_recv()
        if stage < 5:
            start_all(piece.copies(stage))


def all_sent(pieces):
    for piece in pieces:
        for stage in range(5):
            for copy in piece.copies(stage):
                copy.wait_send()


def opening_body(qkv, out_w, up, down, x, qvb, upb, gain, shift,
                 w, w_out, w_up, w_down, h0, normed, q, k, v, o, lse, qkvb, upb_all,
                 w_v, w_out_v, up_v, down_v, fq, fo, fu, fd, lq, lo, lu, ldn, qvb_o, upb_o,
                 x_v, h_v, normed_v, q_v, k_v, v_v, o_v, lse_v, ld, st, send, recv, bsend, brecv,
                 gate):
    s, r, p, y, z = place()
    partner = {"tensor": 1 - p}
    attn = s % 2 == 0
    peers = [partner] + [on_dp(y, (z + d) % 4) for d in (1, 3)] \
        + [on_dp((y + d) % 4, z) for d in (1, 3)]
    barrier = pltpu.get_barrier_semaphore()
    for peer in peers:
        pl.semaphore_signal(barrier, inc=1, device_id=peer, device_id_type=MESH)

    def rows_at(n):
        return pl.ds(pl.multiple_of(r * n, n), n)

    def qkv_half(half):
        cols = slice(half * 1152, half * 1152 + 1152)

        def step(i, carry):
            rows = block(i)
            if half == 0:
                x0 = x_v[rows].astype(F32)
                h = jnp.where(p == 0, x0[:, 0, :], x0[:, 1, :])
                at = lax.broadcasted_iota(jnp.int32, h.shape, 0) + i * BLOCK
                h = jnp.where(at < LENGTH, h, 0.0)
                h_v[rows, :] = h
                xhat, _ = normalized(h)
                normed_v[rows, :] = (xhat * gain[...] + shift[...]).astype(BF16)
            part = (dot(normed_v[rows, :], w_v[:, cols]) + qkvb[:, cols]).astype(BF16)
            for n in range(9):
                lanes = part[:, n * 128 : n * 128 + 128]
                pair = half * 3 + n % 3
                if n < 3:
                    q_v[pair, rows, :] = (lanes.astype(F32) * 0.125).astype(BF16)
                elif n < 6:
                    k_v[pair, rows, :] = lanes
                else:
                    v_v[pair, rows, :] = lanes
            return carry

        lax.fori_loop(0, BLOCKS, step, 0)

    @pl.when(attn)
    def _():
        loads = [local(qkv.at[t], w_v.at[:, pl.ds(t * 384, 384)], ld.at[t]) for t in range(3)]
        loads.append(local(out_w, w_out_v.at[pl.ds(0, 384)], ld.at[3]))
        clips = local(x, x_v.at[pl.ds(0, LENGTH)], ld.at[4])
        start_all(loads)
        pl.when(s == 0)(clips.start)
        sems = send, recv
        pieces = [
            Piece(0, fq.at[0:2], lambda a, b: lq.at[0:2, a, b],
                  lambda ref: (ref.at[0], ref.at[1]), True, sems),
            Piece(1, fq.at[2], lambda a, b: lq.at[2, a, b],
                  lambda ref: (ref.at[pl.ds(0, 24)], ref.at[pl.ds(24, 24)]), False, sems),
            Piece(2, fo.at[pl.ds(pl.multiple_of(r * 24, 8), 24)], lambda a, b: lo.at[a, b],
                  lambda ref: (ref.at[:, pl.ds(0, 384)], ref.at[:, pl.ds(384, 384)]), False, sems),
        ]
        bias = remote(qvb, qvb_o, bsend, brecv, partner)
        qkvb[:, 0:384] = qvb[0:1, :]
        qkvb[:, 384:768] = jnp.zeros((1, 384), F32)
        qkvb[:, 768:1152] = qvb[1:2, :]
        wait_all(loads)
        for t in range(3):
            fq[t] = w_v[rows_at(48), t * 384 : t * 384 + 384].astype(F32)
        fo[...] = w_out_v[0:384, :].astype(F32)
        pl.semaphore_wait(barrier, 6)
        advance(pieces, 0)
        bias.start()

        @pl.when(s == 0)
        def _():
            clips.wait()
            qkv_half(0)

        advance(pieces, 1)
        stored = [local(w_v, w, st.at[0]), local(w_out_v, w_out, st.at[1])]

        def gathered():
            advance(pieces, 4)
            bias.wait()
            advance(pieces, 5)
            for t in range(3):
                at = 1152 + t * 384

                def widen(i, carry, t=t, at=at):
                    w_v[pl.ds(pl.multiple_of(i * 192, 192), 192), at : at + 384] = \
                        lq[t, i].reshape(192, 384).astype(BF16)
                    return carry

                lax.fori_loop(0, 4, widen, 0)
            for i in range(4):
                w_out_v[384 + i * 96 : 480 + i * 96, :] = lo[i].reshape(96, D).astype(BF16)
            qkvb[:, 1152:1536] = qvb_o[0:1, :]
            qkvb[:, 1536:1920] = jnp.zeros((1, 384), F32)
            qkvb[:, 1920:2304] = qvb_o[1:2, :]
            start_all(stored)
            pl.when(s == 0)(functools.partial(qkv_half, 1))

        def pair_step(i, carry):
            pl.when(s == 0)(lambda: attend_pair(q_v, k_v, v_v, o_v, lse_v, i))
            pl.when(i == 0)(lambda: advance(pieces, 2))

            @pl.when(i == 1)
            def _():
                advance(pieces, 3)
                pl.semaphore_signal(gate, inc=1, device_id={"section": s + 1}, device_id_type=MESH)

            pl.when(i == 2)(gathered)
            return carry

        lax.fori_loop(0, PAIRS, pair_step, 0)

        @pl.when(s == 0)
        def _():
            kept = [local(a, b, st.at[2 + n]) for n, (a, b) in enumerate(
                ((h_v, h0), (normed_v, normed), (q_v, q), (k_v, k), (v_v, v), (o_v, o),
                 (lse_v, lse)))]
            start_all(kept)
            wait_all(kept)

        all_sent(pieces)
        wait_all(stored)

    @pl.when(jnp.logical_not(attn))
    def _():
        pl.semaphore_signal(barrier, inc=1, device_id={"section": s - 1}, device_id_type=MESH)
        loads = [local(up, up_v.at[:, pl.ds(0, 1536)], ld.at[0]),
                 local(down, down_v.at[pl.ds(0, 1536)], ld.at[1])]
        start_all(loads)
        sems = send, recv
        pieces = [
            Piece(0, fu, lambda a, b: lu.at[a, b],
                  lambda ref: (ref.at[pl.ds(0, 24)], ref.at[pl.ds(24, 24)]), True, sems),
            Piece(1, fd, lambda a, b: ldn.at[a, b],
                  lambda ref: (ref.at[pl.ds(0, 48)], ref.at[pl.ds(48, 48)]), False, sems),
        ]
        bias = remote(upb, upb_o, bsend, brecv, partner)
        upb_all[:, 0:1536] = upb[...]
        wait_all(loads)
        fu[...] = up_v[rows_at(48), 0:1536].astype(F32)
        fd[...] = down_v[rows_at(96), :].astype(F32)
        pl.semaphore_wait(barrier, 5)
        advance(pieces, 0)
        bias.start()
        pl.semaphore_wait(gate, 1)
        for stage in range(1, 5):
            advance(pieces, stage)
        bias.wait()
        upb_all[:, 1536:3072] = upb_o[...]
        advance(pieces, 5)

        def widen(i, carry):
            up_v[pl.ds(pl.multiple_of(i * 192, 192), 192), 1536:3072] = \
                lu[i].reshape(192, 1536).astype(BF16)
            down_v[pl.ds(pl.multiple_of(1536 + i * 384, 384), 384), :] = \
                ldn[i].reshape(384, D).astype(BF16)
            return carry

        lax.fori_loop(0, 4, widen, 0)
        stored = [local(up_v, w_up, st.at[0]), local(down_v, w_down, st.at[1])]
        start_all(stored)
        all_sent(pieces)
        wait_all(stored)


def opening(qkv, out_w, up, down, x, qvb, upb, gain, shift):
    dma = pltpu.SemaphoreType.DMA
    any_spec = pl.BlockSpec(memory_space=ANY)
    vmem = pl.BlockSpec(memory_space=pltpu.VMEM)
    paired, lse = (PAIRS, ROWS, 128), (PAIRS, 8, ROWS)
    return call(
        opening_body,
        (shape((D, 2304), BF16), shape((D, D), BF16), shape((D, 3072), BF16),
         shape((3072, D), BF16), shape((ROWS, D), F32), shape((ROWS, D), BF16),
         shape(paired, BF16), shape(paired, BF16), shape(paired, BF16), shape(paired, BF16),
         shape(lse, F32), shape((1, 2304), F32), shape((1, 3072), F32)),
        [any_spec] * 5 + [vmem] * 4,
        (any_spec,) * 11 + (vmem, vmem),
        scratch=[
            pltpu.VMEM((D, 2304), BF16), pltpu.VMEM((D, D), BF16), pltpu.VMEM((D, 3072), BF16),
            pltpu.VMEM((3072, D), BF16), pltpu.VMEM((3, 48, 384), F32), pltpu.VMEM((384, D), F32),
            pltpu.VMEM((48, 1536), F32), pltpu.VMEM((96, D), F32),
            pltpu.VMEM((3, 4, 4, 48, 384), F32), pltpu.VMEM((4, 4, 24, D), F32),
            pltpu.VMEM((4, 4, 48, 1536), F32), pltpu.VMEM((4, 4, 96, D), F32),
            pltpu.VMEM((2, 384), F32), pltpu.VMEM((1, 1536), F32),
            pltpu.VMEM((ROWS, 2, D), BF16), pltpu.VMEM((ROWS, D), F32),
            pltpu.VMEM((ROWS, D), BF16), pltpu.VMEM(paired, BF16), pltpu.VMEM(paired, BF16),
            pltpu.VMEM(paired, BF16), pltpu.VMEM(paired, BF16), pltpu.VMEM(lse, F32),
            dma((5,)), dma((9,)), dma((3, 5, 2)), dma((3, 5, 2)), dma, dma,
            pltpu.SemaphoreType.REGULAR,
        ],
        collective_id=1,
        has_side_effects=True,
    )(qkv, out_w, up, down, x, qvb, upb, gain, shift)


class Link:
    def __init__(self, src, dst, send, recv):
        self.src, self.dst, self.sems = src, dst, (send, recv)

    def copy(self, i, device):
        r = block(i)
        return remote(self.src.at[r], self.dst.at[r], self.sems[0].at[i], self.sems[1].at[i], device)

    def expect_from(self, device):
        pl.semaphore_signal(
            pltpu.get_barrier_semaphore(), inc=1, device_id=device, device_id_type=MESH)

    def ready(self):
        pl.semaphore_wait(pltpu.get_barrier_semaphore(), 1)

    def arrived(self, i, device):
        self.copy(i, device).wait_recv()

    def sent(self, device):
        for i in range(BLOCKS):
            self.copy(i, device).wait_send()

    def both_ways(self, device):
        for i in range(BLOCKS):
            self.copy(i, device).wait()


def stores(pairs, sems):
    def of(i):
        r = block(i)
        found = []
        for n, (src, dst) in enumerate(pairs):
            if len(src.shape) == 3:
                found.append(local(src.at[:, r], dst.at[:, r], sems.at[n, i]))
            else:
                found.append(local(src.at[r], dst.at[r], sems.at[n, i]))
        return found

    return of


def every_block(step):
    def body(i, carry):
        step(i, block(i))
        return carry

    lax.fori_loop(0, BLOCKS, body, 0)


def out_proj_rows(o_v, h_v, w_out_v, end, hout, r):
    hout[r, :] = h_v[r, :] + (dot(joined(o_v, r), w_out_v[...]) + end)


def forward_body(o, h0, w_out, up, down, w, gain, shift, end, upb, qkvb,
                 h_out, h_in, act, slope, normed, q, k, v,
                 hin, hout, up_v, down_v, act_v, slope_v, normed_v, o_v, w_out_v, w_v, q_v, k_v,
                 v_v, ld, st, send, recv):
    s, _, p, _, _ = place()
    link = Link(hout, hin, send, recv)

    @pl.when(s == 0)
    def _():
        target = {"section": 1}
        loads = [local(o, o_v, ld.at[0]), local(h0, hin, ld.at[1]), local(w_out, w_out_v, ld.at[2])]
        start_all(loads)
        link.ready()
        wait_all(loads)
        out = stores([(hout, h_out)], st)

        def step(i, r):
            out_proj_rows(o_v, hin, w_out_v, end[...], hout, r)
            link.copy(i, target).start()
            start_all(out(i))

        every_block(step)
        link.sent(target)
        for i in range(BLOCKS):
            wait_all(out(i))

    @pl.when(s == 1)
    def _():
        source, target = {"section": 0}, {"section": 2, "tensor": 1 - p}
        loads = [local(up, up_v, ld.at[0]), local(down, down_v, ld.at[1])]
        start_all(loads)
        link.expect_from(source)
        link.ready()
        wait_all(loads)
        out = stores([(hout, h_out), (hin, h_in), (act_v, act), (slope_v, slope),
                      (normed_v, normed)], st)

        def step(i, r):
            link.arrived(i, source)
            h = hin[r, :]
            xhat, _ = normalized(h)
            low = (xhat * gain[...] + shift[...]).astype(BF16)
            normed_v[r, :] = low
            total = h + end[...]
            for c in range(0, 3072, 768):
                cols = slice(c, c + 768)
                x = dot(low, up_v[:, cols]) + upb[:, cols]
                active, steep = gelu_and_slope(x)
                act_v[r, cols] = active
                slope_v[r, cols] = steep
                total = total + dot(active, down_v[cols, :])
            hout[r, :] = total
            link.copy(i, target).start()
            start_all(out(i))

        every_block(step)
        link.sent(target)
        for i in range(BLOCKS):
            wait_all(out(i))

    @pl.when(s == 2)
    def _():
        source = {"section": 1, "tensor": 1 - p}
        load = local(w, w_v, ld.at[0])
        load.start()
        link.expect_from(source)
        load.wait()
        out = stores([(hin, h_in), (normed_v, normed), (q_v, q), (k_v, k), (v_v, v)], st)

        def step(i, r):
            link.arrived(i, source)
            normed_v[r, :] = qkv_block(
                hin[r, :], gain[...], shift[...], w_v, qkvb, q_v, k_v, v_v, r)
            start_all(out(i))

        every_block(step)
        for i in range(BLOCKS):
            wait_all(out(i))


def staged(body, outs, operands, small, scratch, stored, collective_id):
    dma = pltpu.SemaphoreType.DMA
    any_spec = pl.BlockSpec(memory_space=ANY)
    vmem = pl.BlockSpec(memory_space=pltpu.VMEM)
    return call(
        body,
        tuple(shape(*o) for o in outs),
        [any_spec] * len(operands) + [vmem] * len(small),
        (any_spec,) * len(outs),
        scratch=[pltpu.VMEM(*x) for x in scratch]
        + [dma((8,)), dma((stored, BLOCKS))] + [dma((BLOCKS,))] * 4 + [dma((2 * BLOCKS,))] * 2,
        collective_id=collective_id,
        has_side_effects=True,
    )(*operands, *small)


WIDE = (ROWS, D)
HIDDEN = (ROWS, 3072)
PAIRED = (PAIRS, ROWS, 128)


def forward(o, h0, w_out, up, down, w, gain, shift, end, upb, qkvb):
    def body(*refs):
        return forward_body(*refs[:-4])

    return staged(
        body,
        [(WIDE, F32), (WIDE, F32), (HIDDEN, BF16), (HIDDEN, F32), (WIDE, BF16), (PAIRED, BF16),
         (PAIRED, BF16), (PAIRED, BF16)],
        (o, h0, w_out, up, down, w),
        (gain, shift, end, upb, qkvb),
        [(WIDE, F32), (WIDE, F32), ((D, 3072), BF16), ((3072, D), BF16), (HIDDEN, BF16),
         (HIDDEN, F32), (WIDE, BF16), (PAIRED, BF16), ((D, D), BF16), ((D, 2304), BF16),
         (PAIRED, BF16), (PAIRED, BF16), (PAIRED, BF16)],
        5,
        2,
    )


def middle_body(o, h2, w_out, up, down, cot, gain, shift, end, upb,
                h_out, h_in, act, gr, gb, normed, g_in, gm, g_out, vec, h_theirs, g_theirs,
                hin, hout, gin, gout, act_v, gr_v, gb_v, normed_v, up_v, down_v, o_v, w_out_v, gm_v,
                vec_v, ups_v, ld, st, send, recv, back_send, back_recv, x_send, x_recv):
    s, _, p, _, _ = place()
    theirs = {"tensor": 1 - p}
    h_link = Link(hout, h_theirs, x_send, x_recv)
    g_link = Link(gout, g_theirs, x_send.at[pl.ds(BLOCKS, BLOCKS)], x_recv.at[pl.ds(BLOCKS, BLOCKS)])
    link = Link(hout, hin, send, recv)
    back = Link(gout, gin, back_send, back_recv)

    @pl.when(s == 2)
    def _():
        other = {"section": 3}
        loads = [local(o, o_v, ld.at[0]), local(h2, hin, ld.at[1]), local(w_out, w_out_v, ld.at[2])]
        start_all(loads)
        back.expect_from(other)
        link.ready()
        wait_all(loads)
        out = stores([(hout, h_out)], st)
        back_out = stores([(hout, h_out), (gin, g_in), (gb_v, gb), (gm_v, gm)], st)

        def step(i, r):
            out_proj_rows(o_v, hin, w_out_v, end[...], hout, r)
            link.copy(i, other).start()
            start_all(out(i))

        every_block(step)

        def back_step(i, r):
            back.arrived(i, other)
            gb_v[r, :] = mixed_back_block(gin[r, :], w_out_v, gm_v, r)
            start_all(back_out(i)[1:])

        every_block(back_step)
        link.sent(other)
        for i in range(BLOCKS):
            wait_all(back_out(i))

    @pl.when(s == 3)
    def _():
        other = {"section": 2}
        loads = [local(up, up_v, ld.at[0]), local(down, down_v, ld.at[1]),
                 local(cot, gin, ld.at[2])]
        start_all(loads)
        link.expect_from(other)
        pl.semaphore_signal(
            pltpu.get_barrier_semaphore(), inc=1, device_id=theirs, device_id_type=MESH)
        pl.semaphore_wait(pltpu.get_barrier_semaphore(), 2)
        wait_all(loads)
        vec_v[...] = jnp.zeros_like(vec_v)
        ups_v[...] = jnp.zeros_like(ups_v)
        out = stores([(hout, h_out), (hin, h_in), (act_v, act), (gr_v, gr), (gb_v, gb),
                      (normed_v, normed), (gout, g_out)], st)

        def step(i, r):
            link.arrived(i, other)
            h, g = hin[r, :], gin[r, :]
            xhat, _ = normalized(h)
            low = (xhat * gain[...] + shift[...]).astype(BF16)
            normed_v[r, :] = low
            g_low = g.astype(BF16)
            gb_v[r, :] = g_low
            total = h + end[...]
            grad_normed = jnp.zeros((BLOCK, D), F32)
            for c in range(0, 3072, 768):
                cols = slice(c, c + 768)
                x = dot(low, up_v[:, cols]) + upb[:, cols]
                active, steep = gelu_and_slope(x)
                act_v[r, cols] = active
                total = total + dot(active, down_v[cols, :])
                raised = (dot(g_low, down_v[cols, :], 1, 1) * steep).astype(BF16)
                gr_v[r, cols] = raised
                ups_v[:, cols] += jnp.sum(raised.astype(F32), axis=0, keepdims=True)
                grad_normed = grad_normed + dot(raised, up_v[:, cols], 1, 1)
            hout[r, :] = total
            result, xhat = norm_back(g, h, gain[...], grad_normed)
            gout[r, :] = result
            back.copy(i, other).start()
            h_link.copy(i, theirs).start()
            g_link.copy(i, theirs).start()
            add_row(vec_v, 0, grad_normed * xhat)
            add_row(vec_v, 1, grad_normed)
            add_row(vec_v, 2, g_low.astype(F32))
            start_all(out(i))

        every_block(step)
        for c in range(4):
            vec_v[3 + c : 4 + c, :] = ups_v[:, c * D : c * D + D]
        last = local(vec_v, vec, ld.at[3])
        last.start()
        back.sent(other)
        h_link.both_ways(theirs)
        g_link.both_ways(theirs)
        for i in range(BLOCKS):
            wait_all(out(i))
        last.wait()


def middle(o, h2, w_out, up, down, cot, gain, shift, end, upb):
    return staged(
        middle_body,
        [(WIDE, F32), (WIDE, F32), (HIDDEN, BF16), (HIDDEN, BF16), (WIDE, BF16), (WIDE, BF16),
         (WIDE, F32), (PAIRED, BF16), (WIDE, F32), ((8, D), F32), (WIDE, F32), (WIDE, F32)],
        (o, h2, w_out, up, down, cot),
        (gain, shift, end, upb),
        [(WIDE, F32)] * 4
        + [(HIDDEN, BF16), (HIDDEN, BF16), (WIDE, BF16), (WIDE, BF16), ((D, 3072), BF16),
           ((3072, D), BF16), (PAIRED, BF16), ((D, D), BF16), (PAIRED, BF16), ((8, D), F32),
           ((1, 3072), F32)],
        7,
        3,
    )


def backward_body(g2, h, gq, gk, gv, w, up, down, slope, w_out, h_made, gain,
                  g_out, g_in, gr, gb, gm, vec, h_theirs, g_theirs,
                  gin, gout, h_v, slope_v, gr_v, gb_v, up_v, down_v, gq_v, gk_v, gv_v, w_v, w_out_v,
                  gm_v, vec_v, ups_v, ld, st, send, recv, next_send, next_recv, x_send, x_recv):
    s, _, p, _, _ = place()
    theirs = {"tensor": 1 - p}
    partner = Link(gout, g_theirs, x_send, x_recv)
    made = remote(h_made, h_theirs, x_send.at[BLOCKS], x_recv.at[BLOCKS], theirs)
    first = Link(gout, gin, send, recv)
    second = Link(gout, gin, next_send, next_recv)

    @pl.when(s == 2)
    def _():
        target = {"section": 1, "tensor": 1 - p}
        loads = [local(a, b, ld.at[n]) for n, (a, b) in enumerate(
            ((g2, gin), (h, h_v), (gq, gq_v), (gk, gk_v), (gv, gv_v), (w, w_v)))]
        start_all(loads)
        pl.semaphore_signal(
            pltpu.get_barrier_semaphore(), inc=1, device_id=theirs, device_id_type=MESH)
        pl.semaphore_wait(pltpu.get_barrier_semaphore(), 2)
        made.start()
        wait_all(loads)
        vec_v[...] = jnp.zeros_like(vec_v)
        out = stores([(gout, g_out)], st)

        def step(i, r):
            parts = [(pairs_of((gq_v, gk_v), half, r), pairs_of((gv_v,), half, r))
                     for half in range(2)]
            gout[r, :] = qkv_back_rows(gin[r, :], h_v[r, :], gain[...], parts, w_v, vec_v)
            first.copy(i, target).start()
            partner.copy(i, theirs).start()
            start_all(out(i))

        every_block(step)
        last = local(vec_v, vec, ld.at[6])
        last.start()
        first.sent(target)
        partner.both_ways(theirs)
        made.wait()
        for i in range(BLOCKS):
            wait_all(out(i))
        last.wait()

    @pl.when(s == 1)
    def _():
        source, target = {"section": 2, "tensor": 1 - p}, {"section": 0}
        loads = [local(a, b, ld.at[n]) for n, (a, b) in enumerate(
            ((up, up_v), (down, down_v), (slope, slope_v), (h, h_v)))]
        start_all(loads)
        first.expect_from(source)
        second.ready()
        wait_all(loads)
        vec_v[...] = jnp.zeros_like(vec_v)
        ups_v[...] = jnp.zeros_like(ups_v)
        out = stores([(gout, g_out), (gr_v, gr), (gb_v, gb)], st)

        def step(i, r):
            first.arrived(i, source)
            g = gin[r, :]
            g_low = g.astype(BF16)
            gb_v[r, :] = g_low
            grad_normed = jnp.zeros((BLOCK, D), F32)
            for c in range(0, 3072, 768):
                cols = slice(c, c + 768)
                raised = (dot(g_low, down_v[cols, :], 1, 1) * slope_v[r, cols]).astype(BF16)
                gr_v[r, cols] = raised
                ups_v[:, cols] += jnp.sum(raised.astype(F32), axis=0, keepdims=True)
                grad_normed = grad_normed + dot(raised, up_v[:, cols], 1, 1)
            result, xhat = norm_back(g, h_v[r, :], gain[...], grad_normed)
            gout[r, :] = result
            second.copy(i, target).start()
            add_row(vec_v, 0, grad_normed * xhat)
            add_row(vec_v, 1, grad_normed)
            add_row(vec_v, 2, g_low.astype(F32))
            start_all(out(i))

        every_block(step)
        for c in range(4):
            vec_v[3 + c : 4 + c, :] = ups_v[:, c * D : c * D + D]
        last = local(vec_v, vec, ld.at[6])
        last.start()
        second.sent(target)
        for i in range(BLOCKS):
            wait_all(out(i))
        last.wait()

    @pl.when(s == 0)
    def _():
        source = {"section": 1}
        load = local(w_out, w_out_v, ld.at[0])
        load.start()
        second.expect_from(source)
        load.wait()
        out = stores([(gin, g_in), (gb_v, gb), (gm_v, gm)], st)

        def step(i, r):
            second.arrived(i, source)
            gb_v[r, :] = mixed_back_block(gin[r, :], w_out_v, gm_v, r)
            start_all(out(i))

        every_block(step)
        for i in range(BLOCKS):
            wait_all(out(i))


def backward(g2, h, gq, gk, gv, w, up, down, slope, w_out, h_made, gain):
    return staged(
        backward_body,
        [(WIDE, F32), (WIDE, F32), (HIDDEN, BF16), (WIDE, BF16), (PAIRED, BF16), ((8, D), F32),
         (WIDE, F32), (WIDE, F32)],
        (g2, h, gq, gk, gv, w, up, down, slope, w_out, h_made),
        (gain,),
        [(WIDE, F32)] * 3
        + [(HIDDEN, F32), (HIDDEN, BF16), (WIDE, BF16), ((D, 3072), BF16), ((3072, D), BF16),
           (PAIRED, BF16), (PAIRED, BF16), (PAIRED, BF16), ((D, 2304), BF16), ((D, D), BF16),
           (PAIRED, BF16), ((8, D), F32), ((1, 3072), F32)],
        3,
        4,
    )


def exchange_body(h, theirs, send, recv):
    s, _, p, _, _ = place()

    @pl.when(s < 2)
    def _():
        partner = {"tensor": 1 - p}
        greet([partner])
        copy = remote(h, theirs, send, recv, partner)
        copy.start()
        copy.wait()


def exchange(h):
    dma = pltpu.SemaphoreType.DMA
    any_spec = pl.BlockSpec(memory_space=ANY)
    return call(
        exchange_body, shape(WIDE, F32), [any_spec], any_spec,
        scratch=[dma, dma], collective_id=5, has_side_effects=True,
    )(h)


JOB = (2, 4, 4, 48, CHUNK)


class Reduction:
    def __init__(self, acc, far, near, far2, near2, last, fin, sems):
        self.acc, self.far, self.near, self.far2, self.near2 = acc, far, near, far2, near2
        self.last, self.fin = last, fin
        self.send, self.recv = sems
        _, _, p, self.y, self.z = place()
        self.partner = {"tensor": 1 - p}

    def at(self, j, z_first):
        y, z = self.y, self.z
        along_z = [on_dp(y, (z + d) % 4) for d in (1, 3)]
        along_y = [on_dp((y + d) % 4, z) for d in (1, 3)]
        if z_first:
            return z, y, along_z, along_y, lambda h, i: self.acc.at[j, h, :, i], \
                lambda h, i: self.acc.at[j, h, i, z]
        return y, z, along_y, along_z, lambda h, i: self.acc.at[j, h, i], \
            lambda h, i: self.acc.at[j, h, y, i]

    def copies(self, j, z_first, stage):
        here, there, ring, ring2, part, part2 = self.at(j, z_first)
        both = slice(0, 2)

        def pair(sources, target, peers):
            return [
                remote(sources[n], target.at[j, n], self.send.at[j, stage, n],
                       self.recv.at[j, stage, n], peers[n])
                for n in range(2)
            ]

        if stage == 0:
            return pair([part(0, (here + 2) % 4), part(1, (here + 2) % 4)], self.far, ring)
        if stage == 1:
            return pair([part(both, (here + 1) % 4), part(both, (here + 3) % 4)], self.near, ring)
        if stage == 2:
            return pair([part2(0, (there + 2) % 4), part2(1, (there + 2) % 4)], self.far2, ring2)
        if stage == 3:
            return pair([part2(both, (there + 1) % 4), part2(both, (there + 3) % 4)], self.near2,
                        ring2)
        return [remote(self.fin.at[j, 1], self.last.at[j], self.send.at[j, 4, 0],
                       self.recv.at[j, 4, 0], self.partner)]

    def step(self, j, z_first, stage, out, column):
        here, there, _, _, part, part2 = self.at(j, z_first)
        if stage > 0:
            for copy in self.copies(j, z_first, stage - 1):
                copy.wait_recv()
        if stage == 1:
            def add_far(i, carry):
                for n, d in ((0, 1), (1, 3)):
                    ref = part(n, (here + d) % 4)
                    ref[i] = ref[i] + self.far[j, n, i]
                return carry

            lax.fori_loop(0, 4, add_far, 0)
        if stage == 2:
            def add_near(i, carry):
                for h in range(2):
                    ref = part(h, here)
                    ref[i] = ref[i] + (self.near[j, 0, h, i] + self.near[j, 1, h, i])
                return carry

            lax.fori_loop(0, 4, add_near, 0)
        if stage == 3:
            for n, d in ((0, 1), (1, 3)):
                ref = part2(n, (there + d) % 4)
                ref[...] = ref[...] + self.far2[j, n]
        if stage == 4:
            for h in range(2):
                ref = part2(h, there)
                self.fin[j, h] = ref[...] + (self.near2[j, 0, h] + self.near2[j, 1, h])
        if stage == 5:
            out[:, column : column + CHUNK] = self.fin[j, 0] + self.last[j]
        else:
            start_all(self.copies(j, z_first, stage))

    def sent(self, j, z_first):
        for stage in range(5):
            for copy in self.copies(j, z_first, stage):
                copy.wait_send()


def reduction_scratch(jobs):
    dma = pltpu.SemaphoreType.DMA
    return [
        pltpu.VMEM((jobs,) + JOB, F32),
        pltpu.VMEM((jobs, 2, 4, 48, CHUNK), F32),
        pltpu.VMEM((jobs, 2, 2, 4, 48, CHUNK), F32),
        pltpu.VMEM((jobs, 2, 48, CHUNK), F32),
        pltpu.VMEM((jobs, 2, 2, 48, CHUNK), F32),
        pltpu.VMEM((jobs, 48, CHUNK), F32),
        pltpu.VMEM((jobs, 2, 48, CHUNK), F32),
        dma((jobs, 5, 2)),
        dma((jobs, 5, 2)),
    ]


class Sums:
    def __init__(self, va, v1, v2, vec, send, recv):
        self.va, self.v1, self.v2, self.vec, self.send, self.recv = va, v1, v2, vec, send, recv
        _, _, p, y, z = place()
        self.partner = {"tensor": 1 - p}
        self.peers = [on_dp(y, (z + d) % 4) for d in range(1, 4)], \
            [on_dp((y + d) % 4, z) for d in range(1, 4)]

    def copies(self, stage):
        if stage == 2:
            return [remote(self.vec.at[0], self.vec.at[1], self.send.at[6], self.recv.at[6],
                           self.partner)]
        held = self.v1 if stage == 0 else self.v2
        return [
            remote(self.va.at[stage], held.at[d], self.send.at[3 * stage + d],
                   self.recv.at[3 * stage + d], self.peers[stage][d])
            for d in range(3)
        ]

    def step(self, stage):
        if stage > 0:
            for copy in self.copies(stage - 1):
                copy.wait()
        if stage == 1:
            self.va[1] = self.va[0] + (self.v1[0] + self.v1[1] + self.v1[2])
        if stage == 2:
            self.vec[0] = self.va[1] + (self.v2[0] + self.v2[1] + self.v2[2])
        if stage < 3:
            start_all(self.copies(stage))


def sums_scratch():
    dma = pltpu.SemaphoreType.DMA
    return [pltpu.VMEM((2, 8, D), F32), pltpu.VMEM((3, 8, D), F32), pltpu.VMEM((3, 8, D), F32),
            dma((7,)), dma((7,))]


def greet_all():
    _, _, p, y, z = place()
    peers = [{"tensor": 1 - p}]
    peers += [on_dp(y, (z + d) % 4) for d in range(1, 4)]
    peers += [on_dp((y + d) % 4, z) for d in range(1, 4)]
    greet(peers)


def job_terms(acc, j, lefts, left_t, x_of):
    width = CHUNK // len(lefts)

    def step(i, carry):
        half, y = i // 4, i % 4
        rows = pl.ds(pl.multiple_of(y * 192, 192), 192)
        for n, left in enumerate(lefts):
            cols = slice(n * width, n * width + width)
            term = dot(left_t[left, rows, :], x_of(half)[:, cols])
            acc[j, half, y, :, :, cols] = term.reshape(4, 48, width)
        return carry

    lax.fori_loop(0, 8, step, 0)


def attn_finish_body(gq0, gk0, gv0, o0, gb0, n0, gq2, gk2, gv2, o2, gb2, n2, g_in, h, w, v2,
                     gain,
                     g_theirs, g_own, out, vec,
                     *scratch):
    red = Reduction(*scratch[:7], scratch[7:9])
    sums = Sums(*scratch[9:12], vec, *scratch[12:14])
    x_v, low_v, left_t, gin_v, h_v, gout, w_v, xl, ld, st, send, recv = scratch[14:]
    s, _, p, _, _ = place()
    partner = {"tensor": 1 - p}
    jobs = ((True, 0), (False, CHUNK))
    vec_ref = sums.va.at[0]

    def loads(gq, gk, gv, o, normed, gb):
        found = [local(normed, low_v.at[0], ld.at[0]), local(gb, low_v.at[1], ld.at[1])]
        for j, refs in enumerate(((gq, gk), (gv, o))):
            for n, ref in enumerate(refs):
                for pair in range(PAIRS):
                    half, i = pair // 3, pair % 3
                    found.append(local(
                        ref.at[pair],
                        x_v.at[j, half, :, pl.ds(n * 384 + i * 128, 128)],
                        xl.at[j, n, pair]))
        return found

    def more_loads():
        return [local(g_in, gin_v, ld.at[2]), local(h, h_v, ld.at[3]), local(w, w_v, ld.at[4])]

    def early_sums():
        return local(v2, vec_ref, ld.at[5])

    first = loads(gq0, gk0, gv0, o0, n0, gb0)

    @pl.when(s == 0)
    def _():
        start_all(first)
        start_all(more_loads())

    @pl.when(s == 2)
    def _():
        start_all(loads(gq2, gk2, gv2, o2, n2, gb2))
        early_sums().start()

    def swap(i):
        r = block(i)
        return remote(gout.at[r], g_theirs.at[r], send.at[i], recv.at[i], partner)

    def keep(i):
        r = block(i)
        return local(gout.at[r], g_own.at[r], st.at[i])

    def rows(start):
        def step(i, carry):
            r = block(i)
            parts = [(x_v[0, half, r, :], x_v[1, half, r, 0:384]) for half in range(2)]
            gout[r, :] = qkv_back_rows(gin_v[r, :], h_v[r, :], gain[...], parts, w_v, vec_ref)
            swap(i).start()
            keep(i).start()
            return carry

        lax.fori_loop(start, start + 2, step, 0)

    @pl.when(s % 2 == 0)
    def _():
        for n in range(2):
            first[n].wait()
            left_t[n] = low_v[n].T
        wait_all(first[2:])
        greet_all()

        @pl.when(s == 0)
        def _():
            sums.va[0] = jnp.zeros((8, D), F32)

        @pl.when(s == 2)
        def _():
            early_sums().wait()

        for t in range(7):
            if t < 2:
                job_terms(red.acc, t, (0, t), left_t, lambda half, t=t: x_v.at[t, half])
                red.step(t, jobs[t][0], 0, out, jobs[t][1])
            if t == 1:
                @pl.when(s == 0)
                def _():
                    wait_all(more_loads())
                    rows(0)
            if t == 2:
                @pl.when(s == 0)
                def _():
                    rows(2)
            if t >= 2 and t < 5:
                sums.step(t - 2)
            for stage in range(1, 6):
                if 0 <= t - stage < 2:
                    j = t - stage
                    red.step(j, jobs[j][0], stage, out, jobs[j][1])
        sums.step(3)
        for j in range(2):
            red.sent(j, jobs[j][0])

        @pl.when(s == 0)
        def _():
            for i in range(BLOCKS):
                swap(i).wait()
                keep(i).wait()


def attn_finish(first, last, rest, gain):
    dma = pltpu.SemaphoreType.DMA
    any_spec = pl.BlockSpec(memory_space=ANY)
    vmem = pl.BlockSpec(memory_space=pltpu.VMEM)
    return call(
        attn_finish_body,
        (shape(WIDE, F32), shape(WIDE, F32), shape((48, 2 * CHUNK), F32), shape((2, 8, D), F32)),
        [any_spec] * 16 + [vmem],
        (any_spec, any_spec, vmem, vmem),
        scratch=reduction_scratch(2) + sums_scratch() + [
            pltpu.VMEM((2, 2, ROWS, CHUNK), BF16), pltpu.VMEM((2,) + WIDE, BF16),
            pltpu.VMEM((2, D, ROWS), BF16), pltpu.VMEM(WIDE, F32), pltpu.VMEM(WIDE, F32),
            pltpu.VMEM(WIDE, F32), pltpu.VMEM((D, 2304), BF16),
            dma((2, 2, PAIRS)), dma((6,)), dma((BLOCKS,)), dma((BLOCKS,)), dma((BLOCKS,)),
        ],
        collective_id=20,
        has_side_effects=True,
    )(*first, *last, *rest, gain)


def ff_finish_body(gr1, act1, gb1, n1, gr3, act3, gb3, n3, g1, v1, v3,
                   g_theirs, out, vec,
                   *scratch):
    red = Reduction(*scratch[:7], scratch[7:9])
    sums = Sums(*scratch[9:12], vec, *scratch[12:14])
    x_v, low_v, left_t, ld, xs, xr, vl = scratch[14:]
    s, _, p, _, _ = place()
    partner = {"tensor": 1 - p}
    jobs = ((True, 0), (False, 2 * CHUNK), (True, CHUNK), (False, 3 * CHUNK))

    def load(t, gr, act):
        z_first, column = jobs[t]
        x = gr if z_first else act
        at = column % (2 * CHUNK)
        return [
            local(x.at[:, half * 2 * CHUNK + at : half * 2 * CHUNK + at + CHUNK],
                  x_v.at[t % 2, half], ld.at[t % 2, half])
            for half in range(2)
        ]

    def start_load(t):
        pl.when(s == 1)(lambda: start_all(load(t, gr1, act1)))
        pl.when(s == 3)(lambda: start_all(load(t, gr3, act3)))

    def small(normed, gb, vecs):
        return [local(normed, low_v.at[0], vl.at[0]), local(gb, low_v.at[1], vl.at[1]),
                local(vecs, sums.va.at[0], vl.at[2])]

    swap = remote(g1, g_theirs, xs, xr, partner)

    @pl.when(s % 2 == 1)
    def _():
        pl.when(s == 1)(lambda: start_all(small(n1, gb1, v1)))
        pl.when(s == 3)(lambda: start_all(small(n3, gb3, v3)))
        start_load(0)
        start_load(1)
        smalls = small(n1, gb1, v1)
        for n in range(2):
            smalls[n].wait()
            left_t[n] = low_v[n].T
        greet_all()
        pl.when(s == 1)(swap.start)
        smalls[2].wait()
        for t in range(9):
            if t < 4:
                wait_all(load(t, gr1, act1))
                job_terms(red.acc, t, (t % 2,), left_t, lambda half, t=t: x_v.at[t % 2, half])
                if t + 2 < 4:
                    start_load(t + 2)
                red.step(t, jobs[t][0], 0, out, jobs[t][1])
            if t < 3:
                sums.step(t)
            for stage in range(1, 6):
                if 0 <= t - stage < 4:
                    j = t - stage
                    red.step(j, jobs[j][0], stage, out, jobs[j][1])
        sums.step(3)
        for j in range(4):
            red.sent(j, jobs[j][0])
        pl.when(s == 1)(swap.wait)


def ff_finish(first, last, rest):
    dma = pltpu.SemaphoreType.DMA
    any_spec = pl.BlockSpec(memory_space=ANY)
    vmem = pl.BlockSpec(memory_space=pltpu.VMEM)
    return call(
        ff_finish_body,
        (shape(WIDE, F32), shape((48, 4 * CHUNK), F32), shape((2, 8, D), F32)),
        [any_spec] * 11,
        (any_spec, vmem, vmem),
        scratch=reduction_scratch(4) + sums_scratch() + [
            pltpu.VMEM((2, 2, ROWS, CHUNK), BF16), pltpu.VMEM((2,) + WIDE, BF16),
            pltpu.VMEM((2, D, ROWS), BF16),
            dma((2, 2)), dma, dma, dma((3,)),
        ],
        collective_id=21,
        has_side_effects=True,
    )(*first, *last, *rest)


def interleave(a_ref, b_ref, out_ref, first):
    def step(i, carry):
        r = block(i)
        a, b = a_ref[r, :], b_ref[r, :]
        out_ref[r, 0, :] = jnp.where(first, a, b)
        out_ref[r, 1, :] = jnp.where(first, b, a)
        return carry

    lax.fori_loop(0, BLOCKS - 1, step, 0)
    at = (BLOCKS - 1) * BLOCK
    a, b = a_ref[at:LENGTH, :], b_ref[at:LENGTH, :]
    out_ref[at:LENGTH, 0, :] = jnp.where(first, a, b)
    out_ref[at:LENGTH, 1, :] = jnp.where(first, b, a)


def early_body(hf, h_theirs, out, a_v, b_v, o_v, sems):
    s, _, p, _, _ = place()

    @pl.when(s < 2)
    def _():
        loads = [local(hf, a_v, sems.at[0]), local(h_theirs, b_v, sems.at[1])]
        start_all(loads)
        wait_all(loads)
        interleave(a_v, b_v, o_v, p == 0)
        store = local(o_v, out, sems.at[2])
        store.start()
        store.wait()


BOTH = (LENGTH, 2, D)


def early(hf, h_theirs):
    any_spec = pl.BlockSpec(memory_space=ANY)
    return call(
        early_body,
        shape(BOTH, F32),
        [any_spec] * 2,
        any_spec,
        scratch=[pltpu.VMEM(WIDE, F32), pltpu.VMEM(WIDE, F32), pltpu.VMEM(BOTH, F32),
                 pltpu.SemaphoreType.DMA((3,))],
    )(hf, h_theirs)


def assemble_body(hid_in, hm, h2, h3, g0, gb, gm, ga, gf, g2, g3, hid, gin, a_v, b_v, o_v, sems):
    s, _, p, _, _ = place()
    clip = jnp.where(s < 2, p, 1 - p)

    def loads(mine, theirs, n):
        return [local(mine, a_v.at[n], sems.at[n, 0]), local(theirs, b_v.at[n], sems.at[n, 1])]

    for at, mine, theirs in ((0, g0, ga), (1, gb, gf), (2, gb, g2), (3, gm, g3)):
        pl.when(s == at)(functools.partial(lambda a, b: start_all(loads(a, b, 0)), mine, theirs))
    for at, mine, theirs in ((2, hm, h2), (3, hm, h3)):
        pl.when(s == at)(functools.partial(lambda a, b: start_all(loads(a, b, 1)), mine, theirs))

    def put(n, out):
        wait_all(loads(hm, h2, n))
        interleave(a_v.at[n], b_v.at[n], o_v.at[n], clip == 0)
        local(o_v.at[n], out, sems.at[n, 2]).start()

    def done(n, out):
        local(o_v.at[n], out, sems.at[n, 2]).wait()

    put(0, gin)
    pl.when(s >= 2)(functools.partial(put, 1, hid))
    pl.when(s >= 2)(functools.partial(done, 1, hid))
    done(0, gin)


def assemble(*operands):
    any_spec = pl.BlockSpec(memory_space=ANY)
    return call(
        assemble_body,
        (shape(BOTH, F32),) * 2,
        [any_spec] * 11,
        (any_spec, any_spec),
        scratch=[pltpu.VMEM((2,) + WIDE, F32), pltpu.VMEM((2,) + WIDE, F32),
                 pltpu.VMEM((2,) + BOTH, F32), pltpu.SemaphoreType.DMA((2, 3))],
        aliases={0: 0},
    )(*operands)


def unwritten(shapes):
    any_spec = pl.BlockSpec(memory_space=ANY)
    return pl.pallas_call(
        lambda *refs: None,
        out_shape=tuple(shapes),
        out_specs=(any_spec,) * len(shapes),
    )()


def only_at(active, run, operands):
    like = jax.eval_shape(run, *operands)
    leaves, tree = jax.tree.flatten(like)

    def skip(*_):
        return jax.tree.unflatten(tree, unwritten([shape(x.shape, x.dtype) for x in leaves]))

    return lax.cond(active, run, skip, *operands)


def per_device(inputs, cotangent, norm_gain, norm_bias, qkv_weight, qv_bias, out_weight, end_bias,
               up_weight, up_bias, down_weight):
    s, r, p = lax.axis_index("section"), lax.axis_index("dp"), lax.axis_index("tensor")
    qkv, out_w, up, down = qkv_weight[0], out_weight[0], up_weight[0], down_weight[0]

    gain, shift, end = norm_gain, norm_bias, end_bias
    attn = s % 2 == 0
    by_row = [jnp.transpose(x, (1, 0, 2)) for x in (inputs, cotangent)]
    w, w_out, w_up, w_down, h0, normed0, q0, k0, v0, o0, lse0, qkvb, upb = opening(
        qkv, out_w, up, down, by_row[0], qv_bias[0], up_bias, gain, shift)
    cot = only_at(s == 3, lambda x: (extract(x),), (by_row[1],))[0]
    hf, h_in, act1, slope1, normed_f, q2, k2, v2 = forward(
        o0, h0, w_out, w_up, w_down, w, gain, shift, end, upb, qkvb)
    h_early = exchange(hf)
    o2, lse2 = only_at(s == 2, attend, (q2, k2, v2))
    hid_early = early(hf, h_early)
    o2, hid_early = lax.optimization_barrier((o2, hid_early))
    hm, _, act3, gr3, gb_m, normed3, g2, gm2, g_m, vec_m, h3_theirs, g3_theirs = middle(
        o2, h_in, w_out, w_up, w_down, cot, gain, shift, end, upb)
    gq2, gk2, gv2 = only_at(s == 2, attend_back, (q2, k2, v2, o2, gm2, lse2))
    g_b, g_in0, gr1, gb_b, gm0, vec_b, h2_theirs, g2_theirs = backward(
        g2, h_in, gq2, gk2, gv2, w, w_up, w_down, slope1, w_out, hm, gain)

    gq0, gk0, gv0 = only_at(s == 0, attend_back, (q0, k0, v0, o0, gm0, lse0))
    gb_m, vec_b = lax.optimization_barrier((gb_m, vec_b))
    g1_theirs, ff_sums, ff_vec = ff_finish(
        (gr1, act1, gb_b, normed_f), (gr3, act3, gb_m, normed3), (g_b, vec_b, vec_m))
    g0_theirs, g_0, attn_sums, attn_vec = attn_finish(
        (gq0, gk0, gv0, o0, gb_b, normed0), (gq2, gk2, gv2, o2, gb_m, normed_f),
        (g_in0, h0, w, vec_b), gain)
    hid, gin = assemble(
        hid_early, hm, h2_theirs, h3_theirs, g_0, g_b, g_m, g0_theirs, g1_theirs, g2_theirs,
        g3_theirs)
    hid, gin = [jnp.transpose(x, (1, 0, 2))[None] for x in (hid, gin)]
    vec = jnp.where(attn, attn_vec, ff_vec)

    both = vec[0] + vec[1]

    def mine(row):
        return lax.dynamic_slice_in_dim(both[row], r * 48, 48)[None]

    def when(flag, x):
        return jnp.where(flag, x, 0.0)[None]

    qkv_grad = jnp.transpose(attn_sums[:, :1152].reshape(48, 3, 384), (1, 0, 2))
    qv_grad = vec[0, 3:5, :384] + vec[1, 3:5, 384:]
    up_bias_grad = (vec[0, 3:5] + vec[1, 5:7]).reshape(1536)
    return (
        hid,
        gin,
        mine(0),
        mine(1),
        when(attn, qkv_grad),
        when(attn, qv_grad),
        when(attn, attn_sums[:, 1152:].T),
        mine(2),
        when(~attn, ff_sums[:, :1536]),
        when(~attn, up_bias_grad),
        when(~attn, ff_sums[:, 1536:].T),
    )


def solution(mesh):
    return jax.shard_map(
        per_device,
        mesh=mesh,
        in_specs=(
            P("dp", None, None),
            P("dp", None, None),
            P("section", None),
            P("section", None),
            P("section", None, None, "tensor"),
            P("section", None, "tensor"),
            P("section", "tensor", None),
            P("section", None),
            P("section", None, "tensor"),
            P("section", "tensor"),
            P("section", "tensor", None),
        ),
        out_specs=(
            P("section", "dp", None, None),
            P("section", "dp", None, None),
            P("section", "dp"),
            P("section", "dp"),
            P("section", None, "dp", "tensor"),
            P("section", None, "tensor"),
            P("section", "tensor", "dp"),
            P("section", "dp"),
            P("section", "dp", "tensor"),
            P("section", "tensor"),
            P("section", "tensor", "dp"),
        ),
        check_vma=False,
    )
```

```python
import functools

import jax
import jax.numpy as jnp
from jax import lax
from jax.experimental import pallas as pl
from jax.experimental.pallas import tpu as pltpu
from jax.sharding import PartitionSpec as P

MESH = pl.DeviceIdType.MESH
ANY = pl.ANY
F32 = jnp.float32
BF16 = jnp.bfloat16

HEAD_DIM = 64
EPS = 1e-06
LENGTH = 866
ROWS = 896
BLOCK = 224
D = 768
PAIRS = 6
Q_BLOCKS = ((0, 384), (384, 512))
VMEM_BYTES = 60 * 1024 * 1024

CHUNK = 768


def call(body, out_shape, in_specs, out_specs, grid=(), scratch=(), aliases={}, **more):
    return pl.pallas_call(
        body,
        out_shape=out_shape,
        grid=grid,
        in_specs=in_specs,
        out_specs=out_specs,
        scratch_shapes=scratch,
        input_output_aliases=aliases,
        compiler_params=pltpu.CompilerParams(vmem_limit_bytes=VMEM_BYTES, **more),
    )


def shape(dims, dtype):
    return jax.ShapeDtypeStruct(dims, dtype)


def whole(*dims):
    return pl.BlockSpec(dims, lambda *_: (0,) * len(dims), pipeline_mode=pl.Buffered(1))


def rows_of(width):
    return pl.BlockSpec((BLOCK, width), lambda i: (i, 0))


def dot(a, b, ca=1, cb=0):
    return lax.dot_general(a, b, (((ca,), (cb,)), ((), ())), preferred_element_type=F32)


def normalized(h):
    average = jnp.mean(h, axis=-1, keepdims=True)
    centred = h - average
    spread = jnp.mean(centred * centred, axis=-1, keepdims=True)
    r = lax.rsqrt(spread + EPS)
    return centred * r, r


def norm_back(g, h, gain, grad_normed):
    xhat, r = normalized(h)
    t = grad_normed * gain
    t_mean = jnp.mean(t, axis=-1, keepdims=True)
    tx_mean = jnp.mean(t * xhat, axis=-1, keepdims=True)
    return g + r * (t - t_mean - xhat * tx_mean), xhat


def block(i):
    return pl.ds(pl.multiple_of(i * BLOCK, 32), BLOCK)


def gelu_and_slope(x):
    phi = 0.5 * (1.0 + lax.erf(x * 0.7071067811865476))
    density = jnp.exp(-0.5 * x * x) * 0.3989422804014327
    return (x * phi).astype(BF16), phi + x * density


def qkv_block(h, gain, shift, w_ref, bias, q_ref, k_ref, v_ref, normed_ref, r):
    xhat, _ = normalized(h)
    normed_ref[r, :] = (xhat * gain + shift).astype(BF16)

    def half_step(half, carry):
        cols = pl.ds(pl.multiple_of(half * 1152, 128), 1152)
        part = (dot(normed_ref[r, :], w_ref[:, cols]) + bias[:, cols]).astype(BF16)
        for n in range(9):
            lanes = part[:, n * 128 : n * 128 + 128]
            pair = half * 3 + n % 3
            if n < 3:
                q_ref[pair, r, :] = (lanes.astype(F32) * 0.125).astype(BF16)
            elif n < 6:
                k_ref[pair, r, :] = lanes
            else:
                v_ref[pair, r, :] = lanes
        return carry

    lax.fori_loop(0, 2, half_step, 0)


def joined(ref, r):
    return jnp.concatenate([ref[j, r, :] for j in range(PAIRS)], axis=1)


def mixed_back_block(g, w_out_ref, gm_ref, r):
    gb = g.astype(BF16)
    gm = dot(gb, w_out_ref[...], 1, 1).astype(BF16)
    for j in range(PAIRS):
        gm_ref[j, r, :] = gm[:, j * 128 : j * 128 + 128]
    return gb


def add_row(vec_ref, at, values):
    vec_ref[at : at + 1, :] += jnp.sum(values, axis=0, keepdims=True)


def qkv_back_rows(g, h, gain, parts, w_ref, vec_ref):
    grad_normed = jnp.zeros((BLOCK, D), F32)
    for half, (qk, v) in enumerate(parts):
        part = jnp.concatenate([qk, v], axis=1)
        grad_normed = grad_normed + dot(part, w_ref[:, half * 1152 : half * 1152 + 1152], 1, 1)
    out, xhat = norm_back(g, h, gain, grad_normed)
    add_row(vec_ref, 0, grad_normed * xhat)
    add_row(vec_ref, 1, grad_normed)
    add_row(vec_ref, 2, g.astype(BF16).astype(F32))
    add_row(vec_ref, 3, jnp.concatenate([qk[:, :384] for qk, _ in parts], axis=1).astype(F32))
    add_row(vec_ref, 4, jnp.concatenate([v for _, v in parts], axis=1).astype(F32))
    return out


def pairs_of(refs, half, r):
    return jnp.concatenate([ref[half * 3 + i, r, :] for ref in refs for i in range(3)], axis=1)


def head_mask(dims, axis, head):
    at = lax.broadcasted_iota(jnp.int32, dims, axis)
    return at < HEAD_DIM if head == 0 else at >= HEAD_DIM


def with_lanes(x, head, columns):
    lane = lax.broadcasted_iota(jnp.int32, x.shape, 1)
    own, spare = (lane < HEAD_DIM, HEAD_DIM) if head == 0 else (lane >= HEAD_DIM, 0)
    out = jnp.where(own, x, 0)
    for n, column in enumerate(columns):
        out = jnp.where(lane == spare + n, column, out)
    return out


def in_pieces(x):
    high = x.astype(BF16)
    rest = x - high.astype(F32)
    middle = rest.astype(BF16)
    return [high, middle, (rest - middle.astype(F32)).astype(BF16)]


def key_bias():
    row = lax.broadcasted_iota(jnp.int32, (ROWS, 1), 0)
    return jnp.where(row < LENGTH, 0.0, -1e30).astype(BF16)


def attend_pair(q_ref, k_ref, v_ref, o_ref, lse_ref, j):
    one = jnp.ones((1, 1), BF16)
    q, k, v_t = q_ref[j], k_ref[j], v_ref[j].T
    out = jnp.zeros((128, ROWS), F32)
    rows = []
    for head in range(2):
        s = dot(with_lanes(k, head, [key_bias()]), with_lanes(q, head, [one]), 1, 1)
        top = jnp.max(s, axis=0, keepdims=True)
        e = jnp.exp(s - top)
        total = jnp.sum(e, axis=0, keepdims=True)
        p = (e * (1.0 / total)).astype(BF16)
        out = out + dot(jnp.where(head_mask(v_t.shape, 0, head), v_t, 0), p)
        rows.append(top + jnp.log(total))
    o_ref[j] = out.T.astype(BF16)
    lse_ref[j] = jnp.concatenate(rows + [jnp.zeros((6, ROWS), F32)], axis=0)


def attend_back_pair(q_ref, k_ref, v_ref, gm_ref, lse_ref, gq_ref, gk_ref, gv_ref, j):
    one = jnp.ones((1, 1), BF16)
    k, v = k_ref[j], v_ref[j]
    k_t = k.T
    k_heads = [jnp.where(head_mask(k_t.shape, 0, head), k_t, 0) for head in range(2)]
    k_lanes = [with_lanes(k, head, [one, one, one, key_bias()]) for head in range(2)]
    lse_columns = lse_ref[j].T
    grad_k = jnp.zeros((ROWS, 128), F32)
    grad_v = jnp.zeros((ROWS, 128), F32)
    for start, size in Q_BLOCKS:
        rows = slice(start, start + size)
        q, gm, lse = q_ref[j, rows, :], gm_ref[j, rows, :], lse_columns[rows, :]
        grad_q = jnp.zeros((128, size), F32)
        for head in range(2):
            q_lanes = with_lanes(q, head, in_pieces(-lse[:, head : head + 1]) + [one])
            q_head, gm_head = with_lanes(q, head, []), with_lanes(gm, head, [])
            p = jnp.exp(dot(k_lanes[head], q_lanes, 1, 1))
            gp = dot(v, gm_head, 1, 1)
            inner = jnp.sum(p * gp, axis=0, keepdims=True)
            gs = (p * (gp - inner)).astype(BF16)
            grad_v = grad_v + dot(p.astype(BF16), gm_head)
            grad_k = grad_k + dot(gs, q_head)
            grad_q = grad_q + dot(k_heads[head], gs)
        gq_ref[j, rows, :] = (grad_q.T * 0.125).astype(BF16)
    gk_ref[j] = grad_k.astype(BF16)
    gv_ref[j] = grad_v.astype(BF16)


def extract_body(x_ref, out_ref):
    s, p = lax.axis_index("section"), lax.axis_index("tensor")
    clip = jnp.where(s < 2, p, 1 - p)
    x = x_ref[...].astype(F32)
    x = jnp.where(clip == 0, x[:, 0, :], x[:, 1, :])
    at = lax.broadcasted_iota(jnp.int32, x.shape, 0) + pl.program_id(0) * BLOCK
    out_ref[...] = jnp.where(at < LENGTH, x, 0.0)


def extract(x):
    return call(
        extract_body,
        shape((ROWS, D), F32),
        [pl.BlockSpec((BLOCK, 2, D), lambda i: (i, 0, 0))],
        rows_of(D),
        grid=(ROWS // BLOCK,),
    )(x)


def place():
    s, r, p = lax.axis_index("section"), lax.axis_index("dp"), lax.axis_index("tensor")
    return s, r, p, r // 4, r % 4


def on_dp(y, z):
    return {"dp": y * 4 + z}


def greet(peers):
    barrier = pltpu.get_barrier_semaphore()
    for peer in peers:
        pl.semaphore_signal(barrier, inc=1, device_id=peer, device_id_type=MESH)
    pl.semaphore_wait(barrier, len(peers))


def remote(src, dst, send, recv, device):
    return pltpu.make_async_remote_copy(
        src_ref=src, dst_ref=dst, send_sem=send, recv_sem=recv, device_id=device,
        device_id_type=MESH,
    )


def local(src, dst, sem):
    return pltpu.make_async_copy(src, dst, sem)


def start_all(copies):
    for copy in copies:
        copy.start()


def wait_all(copies):
    for copy in copies:
        copy.wait()


BLOCKS = ROWS // BLOCK


class Piece:
    def __init__(self, n, source, view, halves, z_first, sems):
        self.n, self.source, self.view, self.halves, self.z_first = n, source, view, halves, z_first
        self.send, self.recv = sems
        _, _, p, self.y, self.z = place()
        self.partner = {"tensor": 1 - p}

    def copies(self, stage):
        y, z, view = self.y, self.z, self.view
        along_z = [on_dp(y, (z + d) % 4) for d in (1, 3)]
        along_y = [on_dp((y + d) % 4, z) for d in (1, 3)]

        def copy(n, src, dst, device):
            return remote(src, dst, self.send.at[self.n, stage, n], self.recv.at[self.n, stage, n],
                          device)

        def both(refs, peers):
            return [copy(n, refs[n], refs[n], peers[n]) for n in range(2)]

        everything = slice(0, 4)
        if self.z_first:
            ring, ring2 = along_z, along_y
            one = lambda d: view(y, (z + d) % 4)
            group = lambda d, part=everything: view((y + d) % 4, part)
        else:
            ring, ring2 = along_y, along_z
            one = lambda d: view((y + d) % 4, z)
            group = lambda d, part=everything: view(part, (z + d) % 4)
        if stage == 0:
            return [copy(0, self.source, view(y, z), self.partner)]
        if stage == 1:
            return both([one(0), one(0)], ring)
        if stage == 2:
            return both([self.halves(one(3))[0], self.halves(one(1))[1]], ring)
        if stage == 3:
            return both([group(0), group(0)], ring2)
        return both([group(3, slice(0, 2)), group(1, slice(2, 4))], ring2)


def advance(pieces, stage):
    for piece in pieces:
        if stage > 0:
            for copy in piece.copies(stage - 1):
                copy.wait_recv()
        if stage < 5:
            start_all(piece.copies(stage))


def all_sent(pieces):
    for piece in pieces:
        for stage in range(5):
            for copy in piece.copies(stage):
                copy.wait_send()


def opening_body(qkv, out_w, up, down, x, qvb, upb, gain, shift,
                 w, w_out, w_up, w_down, h0, normed, q, k, v, o, lse, qkvb, upb_all,
                 w_v, w_out_v, up_v, down_v, fq, fo, fu, fd, lq, lo, lu, ldn, qvb_o, upb_o,
                 x_v, h_v, normed_v, q_v, k_v, v_v, o_v, lse_v, ld, st, send, recv, bsend, brecv,
                 gate):
    s, r, p, y, z = place()
    partner = {"tensor": 1 - p}
    attn = s % 2 == 0
    peers = [partner] + [on_dp(y, (z + d) % 4) for d in (1, 3)] \
        + [on_dp((y + d) % 4, z) for d in (1, 3)]
    barrier = pltpu.get_barrier_semaphore()
    for peer in peers:
        pl.semaphore_signal(barrier, inc=1, device_id=peer, device_id_type=MESH)

    def rows_at(n):
        return pl.ds(pl.multiple_of(r * n, n), n)

    def qkv_half(half):
        cols = pl.ds(pl.multiple_of(half * 1152, 128), 1152)

        def step(i, carry):
            rows = block(i)

            @pl.when(half == 0)
            def _():
                x0 = x_v[rows].astype(F32)
                h = jnp.where(p == 0, x0[:, 0, :], x0[:, 1, :])
                at = lax.broadcasted_iota(jnp.int32, h.shape, 0) + i * BLOCK
                h = jnp.where(at < LENGTH, h, 0.0)
                h_v[rows, :] = h
                xhat, _ = normalized(h)
                normed_v[rows, :] = (xhat * gain[...] + shift[...]).astype(BF16)

            part = (dot(normed_v[rows, :], w_v[:, cols]) + qkvb[:, cols]).astype(BF16)
            for n in range(9):
                lanes = part[:, n * 128 : n * 128 + 128]
                pair = half * 3 + n % 3
                if n < 3:
                    q_v[pair, rows, :] = (lanes.astype(F32) * 0.125).astype(BF16)
                elif n < 6:
                    k_v[pair, rows, :] = lanes
                else:
                    v_v[pair, rows, :] = lanes
            return carry

        lax.fori_loop(0, BLOCKS, step, 0)

    @pl.when(attn)
    def _():
        loads = [local(qkv.at[t], w_v.at[:, pl.ds(t * 384, 384)], ld.at[t]) for t in range(3)]
        loads.append(local(out_w, w_out_v.at[pl.ds(0, 384)], ld.at[3]))
        clips = local(x, x_v.at[pl.ds(0, LENGTH)], ld.at[4])
        start_all(loads)
        pl.when(s == 0)(clips.start)
        sems = send, recv
        pieces = [
            Piece(0, fq.at[0:2], lambda a, b: lq.at[0:2, a, b],
                  lambda ref: (ref.at[0], ref.at[1]), True, sems),
            Piece(1, fq.at[2], lambda a, b: lq.at[2, a, b],
                  lambda ref: (ref.at[pl.ds(0, 24)], ref.at[pl.ds(24, 24)]), False, sems),
            Piece(2, fo.at[pl.ds(pl.multiple_of(r * 24, 8), 24)], lambda a, b: lo.at[a, b],
                  lambda ref: (ref.at[:, pl.ds(0, 384)], ref.at[:, pl.ds(384, 384)]), False, sems),
        ]
        bias = remote(qvb, qvb_o, bsend, brecv, partner)
        qkvb[:, 0:384] = qvb[0:1, :]
        qkvb[:, 384:768] = jnp.zeros((1, 384), F32)
        qkvb[:, 768:1152] = qvb[1:2, :]
        wait_all(loads)
        for t in range(3):
            fq[t] = w_v[rows_at(48), t * 384 : t * 384 + 384].astype(F32)
        fo[...] = w_out_v[0:384, :].astype(F32)
        pl.semaphore_wait(barrier, 6)
        advance(pieces, 0)
        bias.start()

        pl.when(s == 0)(clips.wait)
        stored = [local(w_v, w, st.at[0]), local(w_out_v, w_out, st.at[1])]

        def gathered():
            advance(pieces, 4)
            bias.wait()
            advance(pieces, 5)
            for t in range(3):
                at = 1152 + t * 384

                def widen(i, carry, t=t, at=at):
                    w_v[pl.ds(pl.multiple_of(i * 192, 192), 192), at : at + 384] = \
                        lq[t, i].reshape(192, 384).astype(BF16)
                    return carry

                lax.fori_loop(0, 4, widen, 0)
            for i in range(4):
                w_out_v[384 + i * 96 : 480 + i * 96, :] = lo[i].reshape(96, D).astype(BF16)
            qkvb[:, 1152:1536] = qvb_o[0:1, :]
            qkvb[:, 1536:1920] = jnp.zeros((1, 384), F32)
            qkvb[:, 1920:2304] = qvb_o[1:2, :]
            start_all(stored)

        def pair_step(i, carry):
            pl.when((s == 0) & (i % 3 == 0))(lambda: qkv_half(i // 3))
            pl.when(i == 0)(lambda: advance(pieces, 1))
            pl.when(s == 0)(lambda: attend_pair(q_v, k_v, v_v, o_v, lse_v, i))
            pl.when(i == 0)(lambda: advance(pieces, 2))

            @pl.when(i == 1)
            def _():
                advance(pieces, 3)
                pl.semaphore_signal(gate, inc=1, device_id={"section": s + 1}, device_id_type=MESH)

            pl.when(i == 2)(gathered)
            return carry

        lax.fori_loop(0, PAIRS, pair_step, 0)

        @pl.when(s == 0)
        def _():
            kept = [local(a, b, st.at[2 + n]) for n, (a, b) in enumerate(
                ((h_v, h0), (normed_v, normed), (q_v, q), (k_v, k), (v_v, v), (o_v, o),
                 (lse_v, lse)))]
            start_all(kept)
            wait_all(kept)

        all_sent(pieces)
        wait_all(stored)

    @pl.when(jnp.logical_not(attn))
    def _():
        pl.semaphore_signal(barrier, inc=1, device_id={"section": s - 1}, device_id_type=MESH)
        loads = [local(up, up_v.at[:, pl.ds(0, 1536)], ld.at[0]),
                 local(down, down_v.at[pl.ds(0, 1536)], ld.at[1])]
        start_all(loads)
        sems = send, recv
        pieces = [
            Piece(0, fu, lambda a, b: lu.at[a, b],
                  lambda ref: (ref.at[pl.ds(0, 24)], ref.at[pl.ds(24, 24)]), True, sems),
            Piece(1, fd, lambda a, b: ldn.at[a, b],
                  lambda ref: (ref.at[pl.ds(0, 48)], ref.at[pl.ds(48, 48)]), False, sems),
        ]
        bias = remote(upb, upb_o, bsend, brecv, partner)
        upb_all[:, 0:1536] = upb[...]
        wait_all(loads)
        fu[...] = up_v[rows_at(48), 0:1536].astype(F32)
        fd[...] = down_v[rows_at(96), :].astype(F32)
        pl.semaphore_wait(barrier, 5)
        advance(pieces, 0)
        bias.start()
        pl.semaphore_wait(gate, 1)
        for stage in range(1, 5):
            advance(pieces, stage)
        bias.wait()
        upb_all[:, 1536:3072] = upb_o[...]
        advance(pieces, 5)

        def widen(i, carry):
            up_v[pl.ds(pl.multiple_of(i * 192, 192), 192), 1536:3072] = \
                lu[i].reshape(192, 1536).astype(BF16)
            down_v[pl.ds(pl.multiple_of(1536 + i * 384, 384), 384), :] = \
                ldn[i].reshape(384, D).astype(BF16)
            return carry

        lax.fori_loop(0, 4, widen, 0)
        stored = [local(up_v, w_up, st.at[0]), local(down_v, w_down, st.at[1])]
        start_all(stored)
        all_sent(pieces)
        wait_all(stored)


def opening(qkv, out_w, up, down, x, qvb, upb, gain, shift):
    dma = pltpu.SemaphoreType.DMA
    any_spec = pl.BlockSpec(memory_space=ANY)
    vmem = pl.BlockSpec(memory_space=pltpu.VMEM)
    paired, lse = (PAIRS, ROWS, 128), (PAIRS, 8, ROWS)
    return call(
        opening_body,
        (shape((D, 2304), BF16), shape((D, D), BF16), shape((D, 3072), BF16),
         shape((3072, D), BF16), shape((ROWS, D), F32), shape((ROWS, D), BF16),
         shape(paired, BF16), shape(paired, BF16), shape(paired, BF16), shape(paired, BF16),
         shape(lse, F32), shape((1, 2304), F32), shape((1, 3072), F32)),
        [any_spec] * 5 + [vmem] * 4,
        (any_spec,) * 11 + (vmem, vmem),
        scratch=[
            pltpu.VMEM((D, 2304), BF16), pltpu.VMEM((D, D), BF16), pltpu.VMEM((D, 3072), BF16),
            pltpu.VMEM((3072, D), BF16), pltpu.VMEM((3, 48, 384), F32), pltpu.VMEM((384, D), F32),
            pltpu.VMEM((48, 1536), F32), pltpu.VMEM((96, D), F32),
            pltpu.VMEM((3, 4, 4, 48, 384), F32), pltpu.VMEM((4, 4, 24, D), F32),
            pltpu.VMEM((4, 4, 48, 1536), F32), pltpu.VMEM((4, 4, 96, D), F32),
            pltpu.VMEM((2, 384), F32), pltpu.VMEM((1, 1536), F32),
            pltpu.VMEM((ROWS, 2, D), BF16), pltpu.VMEM((ROWS, D), F32),
            pltpu.VMEM((ROWS, D), BF16), pltpu.VMEM(paired, BF16), pltpu.VMEM(paired, BF16),
            pltpu.VMEM(paired, BF16), pltpu.VMEM(paired, BF16), pltpu.VMEM(lse, F32),
            dma((5,)), dma((9,)), dma((3, 5, 2)), dma((3, 5, 2)), dma, dma,
            pltpu.SemaphoreType.REGULAR,
        ],
        collective_id=1,
        has_side_effects=True,
    )(qkv, out_w, up, down, x, qvb, upb, gain, shift)


class Link:
    def __init__(self, src, dst, send, recv):
        self.src, self.dst, self.sems = src, dst, (send, recv)

    def copy(self, i, device):
        r = block(i)
        return remote(self.src.at[r], self.dst.at[r], self.sems[0].at[i], self.sems[1].at[i], device)

    def expect_from(self, device):
        pl.semaphore_signal(
            pltpu.get_barrier_semaphore(), inc=1, device_id=device, device_id_type=MESH)

    def ready(self):
        pl.semaphore_wait(pltpu.get_barrier_semaphore(), 1)

    def arrived(self, i, device):
        self.copy(i, device).wait_recv()

    def sent(self, device):
        for i in range(BLOCKS):
            self.copy(i, device).wait_send()

    def both_ways(self, device):
        for i in range(BLOCKS):
            self.copy(i, device).wait()


def stores(pairs, sems):
    def of(i):
        r = block(i)
        found = []
        for n, (src, dst) in enumerate(pairs):
            if len(src.shape) == 3:
                found.append(local(src.at[:, r], dst.at[:, r], sems.at[n, i]))
            else:
                found.append(local(src.at[r], dst.at[r], sems.at[n, i]))
        return found

    return of


def every_block(step):
    def body(i, carry):
        step(i, block(i))
        return carry

    lax.fori_loop(0, BLOCKS, body, 0)


def out_proj_rows(o_v, h_v, w_out_v, end, hout, r):
    hout[r, :] = h_v[r, :] + (dot(joined(o_v, r), w_out_v[...]) + end)


def forward_body(o, h0, w_out, up, down, w, gain, shift, end, upb, qkvb,
                 h_out, h_in, act, slope, normed, q, k, v, o2, lse2,
                 hin, hout, up_v, down_v, act_v, slope_v, normed_v, o_v, w_out_v, w_v, q_v, k_v,
                 v_v, lse_v, ld, st, send, recv):
    s, _, p, _, _ = place()
    link = Link(hout, hin, send, recv)

    @pl.when(s == 0)
    def _():
        target = {"section": 1}
        loads = [local(o, o_v, ld.at[0]), local(h0, hin, ld.at[1]), local(w_out, w_out_v, ld.at[2])]
        start_all(loads)
        link.ready()
        wait_all(loads)
        out = stores([(hout, h_out)], st)

        def step(i, r):
            out_proj_rows(o_v, hin, w_out_v, end[...], hout, r)
            link.copy(i, target).start()
            start_all(out(i))

        every_block(step)
        link.sent(target)
        for i in range(BLOCKS):
            wait_all(out(i))

    @pl.when(s == 1)
    def _():
        source, target = {"section": 0}, {"section": 2, "tensor": 1 - p}
        loads = [local(up, up_v, ld.at[0]), local(down, down_v, ld.at[1])]
        start_all(loads)
        link.expect_from(source)
        link.ready()
        wait_all(loads)
        out = stores([(hout, h_out), (hin, h_in), (act_v, act), (slope_v, slope),
                      (normed_v, normed)], st)

        def step(i, r):
            link.arrived(i, source)
            h = hin[r, :]
            xhat, _ = normalized(h)
            low = (xhat * gain[...] + shift[...]).astype(BF16)
            normed_v[r, :] = low
            hout[r, :] = h + end[...]

            def chunk(c, carry):
                cols = pl.ds(pl.multiple_of(c * 768, 768), 768)
                x = dot(low, up_v[:, cols]) + upb[:, cols]
                active, steep = gelu_and_slope(x)
                act_v[r, cols] = active
                slope_v[r, cols] = steep
                hout[r, :] += dot(active, down_v[cols, :])
                return carry

            lax.fori_loop(0, 4, chunk, 0)
            link.copy(i, target).start()
            start_all(out(i))

        every_block(step)
        link.sent(target)
        for i in range(BLOCKS):
            wait_all(out(i))

    @pl.when(s == 2)
    def _():
        source = {"section": 1, "tensor": 1 - p}
        load = local(w, w_v, ld.at[0])
        load.start()
        link.expect_from(source)
        load.wait()
        out = stores([(hin, h_in), (normed_v, normed), (q_v, q), (k_v, k), (v_v, v)], st)

        def step(i, r):
            link.arrived(i, source)
            qkv_block(hin[r, :], gain[...], shift[...], w_v, qkvb, q_v, k_v, v_v, normed_v, r)
            start_all(out(i))

        every_block(step)

        def attend_step(i, carry):
            attend_pair(q_v, k_v, v_v, o_v, lse_v, i)
            return carry

        lax.fori_loop(0, PAIRS, attend_step, 0)
        kept = [local(o_v, o2, ld.at[1]), local(lse_v, lse2, ld.at[2])]
        start_all(kept)
        for i in range(BLOCKS):
            wait_all(out(i))
        wait_all(kept)


def staged(body, outs, operands, small, scratch, stored, collective_id):
    dma = pltpu.SemaphoreType.DMA
    any_spec = pl.BlockSpec(memory_space=ANY)
    vmem = pl.BlockSpec(memory_space=pltpu.VMEM)
    return call(
        body,
        tuple(shape(*o) for o in outs),
        [any_spec] * len(operands) + [vmem] * len(small),
        (any_spec,) * len(outs),
        scratch=[pltpu.VMEM(*x) for x in scratch]
        + [dma((8,)), dma((stored, BLOCKS))] + [dma((BLOCKS,))] * 4 + [dma((2 * BLOCKS,))] * 2,
        collective_id=collective_id,
        has_side_effects=True,
    )(*operands, *small)


WIDE = (ROWS, D)
HIDDEN = (ROWS, 3072)
PAIRED = (PAIRS, ROWS, 128)
LSE = (PAIRS, 8, ROWS)


def forward(o, h0, w_out, up, down, w, gain, shift, end, upb, qkvb):
    def body(*refs):
        return forward_body(*refs[:-4])

    return staged(
        body,
        [(WIDE, F32), (WIDE, F32), (HIDDEN, BF16), (HIDDEN, F32), (WIDE, BF16), (PAIRED, BF16),
         (PAIRED, BF16), (PAIRED, BF16), (PAIRED, BF16), (LSE, F32)],
        (o, h0, w_out, up, down, w),
        (gain, shift, end, upb, qkvb),
        [(WIDE, F32), (WIDE, F32), ((D, 3072), BF16), ((3072, D), BF16), (HIDDEN, BF16),
         (HIDDEN, F32), (WIDE, BF16), (PAIRED, BF16), ((D, D), BF16), ((D, 2304), BF16),
         (PAIRED, BF16), (PAIRED, BF16), (PAIRED, BF16), (LSE, F32)],
        5,
        2,
    )


def middle_body(o, h2, w_out, up, down, cot, gain, shift, end, upb,
                h_out, h_in, act, gr, gb, normed, g_in, gm, g_out, vec, h_theirs,
                hin, hout, gin, gout, act_v, gr_v, gb_v, normed_v, up_v, down_v, o_v, w_out_v, gm_v,
                vec_v, ups_v, ld, st, send, recv, back_send, back_recv, x_send, x_recv):
    s, _, p, _, _ = place()
    theirs = {"tensor": 1 - p}
    h_link = Link(hout, h_theirs, x_send, x_recv)
    link = Link(hout, hin, send, recv)
    back = Link(gout, gin, back_send, back_recv)

    @pl.when(s == 2)
    def _():
        other = {"section": 3}
        loads = [local(o, o_v, ld.at[0]), local(h2, hin, ld.at[1]), local(w_out, w_out_v, ld.at[2])]
        start_all(loads)
        back.expect_from(other)
        link.ready()
        wait_all(loads)
        out = stores([(hout, h_out)], st)
        back_out = stores([(hout, h_out), (gin, g_in), (gb_v, gb), (gm_v, gm)], st)

        def step(i, r):
            out_proj_rows(o_v, hin, w_out_v, end[...], hout, r)
            link.copy(i, other).start()
            start_all(out(i))

        every_block(step)

        def back_step(i, r):
            back.arrived(i, other)
            gb_v[r, :] = mixed_back_block(gin[r, :], w_out_v, gm_v, r)
            start_all(back_out(i)[1:])

        every_block(back_step)
        link.sent(other)
        for i in range(BLOCKS):
            wait_all(back_out(i))

    @pl.when(s == 3)
    def _():
        other = {"section": 2}
        loads = [local(up, up_v, ld.at[0]), local(down, down_v, ld.at[1]),
                 local(cot, gin, ld.at[2])]
        start_all(loads)
        link.expect_from(other)
        pl.semaphore_signal(
            pltpu.get_barrier_semaphore(), inc=1, device_id=theirs, device_id_type=MESH)
        pl.semaphore_wait(pltpu.get_barrier_semaphore(), 2)
        wait_all(loads)
        vec_v[...] = jnp.zeros_like(vec_v)
        ups_v[...] = jnp.zeros_like(ups_v)
        out = stores([(hout, h_out), (hin, h_in), (act_v, act), (gr_v, gr), (gb_v, gb),
                      (normed_v, normed), (gout, g_out)], st)

        def step(i, r):
            link.arrived(i, other)
            h, g = hin[r, :], gin[r, :]
            xhat, _ = normalized(h)
            low = (xhat * gain[...] + shift[...]).astype(BF16)
            normed_v[r, :] = low
            g_low = g.astype(BF16)
            gb_v[r, :] = g_low
            total = h + end[...]
            grad_normed = jnp.zeros((BLOCK, D), F32)
            for c in range(0, 3072, 768):
                cols = slice(c, c + 768)
                x = dot(low, up_v[:, cols]) + upb[:, cols]
                active, steep = gelu_and_slope(x)
                act_v[r, cols] = active
                total = total + dot(active, down_v[cols, :])
                raised = (dot(g_low, down_v[cols, :], 1, 1) * steep).astype(BF16)
                gr_v[r, cols] = raised
                ups_v[:, cols] += jnp.sum(raised.astype(F32), axis=0, keepdims=True)
                grad_normed = grad_normed + dot(raised, up_v[:, cols], 1, 1)
            hout[r, :] = total
            result, xhat = norm_back(g, h, gain[...], grad_normed)
            gout[r, :] = result
            back.copy(i, other).start()
            h_link.copy(i, theirs).start()
            add_row(vec_v, 0, grad_normed * xhat)
            add_row(vec_v, 1, grad_normed)
            add_row(vec_v, 2, g_low.astype(F32))
            start_all(out(i))

        every_block(step)
        for c in range(4):
            vec_v[3 + c : 4 + c, :] = ups_v[:, c * D : c * D + D]
        last = local(vec_v, vec, ld.at[3])
        last.start()
        back.sent(other)
        h_link.both_ways(theirs)
        for i in range(BLOCKS):
            wait_all(out(i))
        last.wait()


def middle(o, h2, w_out, up, down, cot, gain, shift, end, upb):
    return staged(
        middle_body,
        [(WIDE, F32), (WIDE, F32), (HIDDEN, BF16), (HIDDEN, BF16), (WIDE, BF16), (WIDE, BF16),
         (WIDE, F32), (PAIRED, BF16), (WIDE, F32), ((8, D), F32), (WIDE, F32)],
        (o, h2, w_out, up, down, cot),
        (gain, shift, end, upb),
        [(WIDE, F32)] * 4
        + [(HIDDEN, BF16), (HIDDEN, BF16), (WIDE, BF16), (WIDE, BF16), ((D, 3072), BF16),
           ((3072, D), BF16), (PAIRED, BF16), ((D, D), BF16), (PAIRED, BF16), ((8, D), F32),
           ((1, 3072), F32)],
        7,
        3,
    )


def backward_body(g2, h, q, k, v, gm2, lse, w, up, down, slope, w_out, h_made, gain,
                  g_out, g_in, gr, gb, gm, vec, h_theirs, g_theirs, gq, gk, gv,
                  gin, gout, h_v, slope_v, gr_v, gb_v, up_v, down_v, gq_v, gk_v, gv_v, w_v, w_out_v,
                  gm_v, vec_v, ups_v, q_v, k_v, v_v, lse_v, ld, st, send, recv, next_send, next_recv,
                  x_send, x_recv):
    s, _, p, _, _ = place()
    theirs = {"tensor": 1 - p}
    partner = Link(gout, g_theirs, x_send, x_recv)
    made = remote(h_made, h_theirs, x_send.at[BLOCKS], x_recv.at[BLOCKS], theirs)
    first = Link(gout, gin, send, recv)
    second = Link(gout, gin, next_send, next_recv)

    @pl.when(s == 2)
    def _():
        target = {"section": 1, "tensor": 1 - p}
        loads = [local(a, b, ld.at[n]) for n, (a, b) in enumerate(
            ((q, q_v), (k, k_v), (v, v_v), (gm2, gm_v), (lse, lse_v), (g2, gin), (h, h_v),
             (w, w_v)))]
        start_all(loads)
        pl.semaphore_signal(
            pltpu.get_barrier_semaphore(), inc=1, device_id=theirs, device_id_type=MESH)
        pl.semaphore_wait(pltpu.get_barrier_semaphore(), 2)
        made.start()
        wait_all(loads[:5])

        def attend_step(i, carry):
            attend_back_pair(q_v, k_v, v_v, gm_v, lse_v, gq_v, gk_v, gv_v, i)
            return carry

        lax.fori_loop(0, PAIRS, attend_step, 0)
        kept = [local(a, b, ld.at[n]) for n, (a, b) in enumerate(
            ((gq_v, gq), (gk_v, gk), (gv_v, gv)))]
        start_all(kept)
        wait_all(loads[5:])
        vec_v[...] = jnp.zeros_like(vec_v)
        out = stores([(gout, g_out)], st)

        def step(i, r):
            parts = [(pairs_of((gq_v, gk_v), half, r), pairs_of((gv_v,), half, r))
                     for half in range(2)]
            gout[r, :] = qkv_back_rows(gin[r, :], h_v[r, :], gain[...], parts, w_v, vec_v)
            first.copy(i, target).start()
            start_all(out(i))

        every_block(step)
        last = local(vec_v, vec, ld.at[6])
        last.start()
        first.sent(target)
        made.wait()
        wait_all(kept)
        for i in range(BLOCKS):
            wait_all(out(i))
        last.wait()

    @pl.when(s == 1)
    def _():
        source, target = {"section": 2, "tensor": 1 - p}, {"section": 0}
        loads = [local(a, b, ld.at[n]) for n, (a, b) in enumerate(
            ((up, up_v), (down, down_v), (slope, slope_v), (h, h_v)))]
        start_all(loads)
        first.expect_from(source)
        pl.semaphore_signal(
            pltpu.get_barrier_semaphore(), inc=1, device_id=theirs, device_id_type=MESH)
        pl.semaphore_wait(pltpu.get_barrier_semaphore(), 2)
        wait_all(loads)
        vec_v[...] = jnp.zeros_like(vec_v)
        ups_v[...] = jnp.zeros_like(ups_v)
        out = stores([(gout, g_out), (gr_v, gr), (gb_v, gb)], st)

        def step(i, r):
            first.arrived(i, source)
            g = gin[r, :]
            g_low = g.astype(BF16)
            gb_v[r, :] = g_low
            gout[r, :] = jnp.zeros((BLOCK, D), F32)

            def chunk(c, carry):
                cols = pl.ds(pl.multiple_of(c * 768, 768), 768)
                raised = (dot(g_low, down_v[cols, :], 1, 1) * slope_v[r, cols]).astype(BF16)
                gr_v[r, cols] = raised
                ups_v[:, cols] += jnp.sum(raised.astype(F32), axis=0, keepdims=True)
                gout[r, :] += dot(raised, up_v[:, cols], 1, 1)
                return carry

            lax.fori_loop(0, 4, chunk, 0)
            grad_normed = gout[r, :]
            result, xhat = norm_back(g, h_v[r, :], gain[...], grad_normed)
            gout[r, :] = result
            second.copy(i, target).start()
            pl.when(i < BLOCKS - 1)(lambda: partner.copy(i, theirs).start())
            add_row(vec_v, 0, grad_normed * xhat)
            add_row(vec_v, 1, grad_normed)
            add_row(vec_v, 2, g_low.astype(F32))
            start_all(out(i))

        every_block(step)
        for c in range(4):
            vec_v[3 + c : 4 + c, :] = ups_v[:, c * D : c * D + D]
        last = local(vec_v, vec, ld.at[6])
        last.start()
        second.sent(target)
        for i in range(BLOCKS - 1):
            partner.copy(i, theirs).wait()
        for i in range(BLOCKS):
            wait_all(out(i))
        last.wait()

    @pl.when(s == 0)
    def _():
        source = {"section": 1}
        load = local(w_out, w_out_v, ld.at[0])
        load.start()
        second.expect_from(source)
        load.wait()
        out = stores([(gin, g_in), (gb_v, gb), (gm_v, gm)], st)

        def step(i, r):
            second.arrived(i, source)
            gb_v[r, :] = mixed_back_block(gin[r, :], w_out_v, gm_v, r)
            start_all(out(i))

        every_block(step)
        for i in range(BLOCKS):
            wait_all(out(i))


def backward(g2, h, q, k, v, gm, lse, w, up, down, slope, w_out, h_made, gain):
    return staged(
        backward_body,
        [(WIDE, F32), (WIDE, F32), (HIDDEN, BF16), (WIDE, BF16), (PAIRED, BF16), ((8, D), F32),
         (WIDE, F32), (WIDE, F32), (PAIRED, BF16), (PAIRED, BF16), (PAIRED, BF16)],
        (g2, h, q, k, v, gm, lse, w, up, down, slope, w_out, h_made),
        (gain,),
        [(WIDE, F32)] * 3
        + [(HIDDEN, F32), (HIDDEN, BF16), (WIDE, BF16), ((D, 3072), BF16), ((3072, D), BF16),
           (PAIRED, BF16), (PAIRED, BF16), (PAIRED, BF16), ((D, 2304), BF16), ((D, D), BF16),
           (PAIRED, BF16), ((8, D), F32), ((1, 3072), F32), (PAIRED, BF16), (PAIRED, BF16),
           (PAIRED, BF16), (LSE, F32)],
        3,
        4,
    )


def exchange_body(h, theirs, send, recv):
    s, _, p, _, _ = place()

    @pl.when(s < 2)
    def _():
        partner = {"tensor": 1 - p}
        greet([partner])
        copy = remote(h, theirs, send, recv, partner)
        copy.start()
        copy.wait()


def exchange(h):
    dma = pltpu.SemaphoreType.DMA
    any_spec = pl.BlockSpec(memory_space=ANY)
    return call(
        exchange_body, shape(WIDE, F32), [any_spec], any_spec,
        scratch=[dma, dma], collective_id=5, has_side_effects=True,
    )(h)


class Reduction:
    def __init__(self, acc, far, near, far2, near2, last, fin, sems):
        self.acc, self.far, self.near, self.far2, self.near2 = acc, far, near, far2, near2
        self.last, self.fin = last, fin
        self.send, self.recv = sems
        _, _, p, self.y, self.z = place()
        self.partner = {"tensor": 1 - p}

    def at(self, j, z_first):
        y, z = self.y, self.z
        along_z = [on_dp(y, (z + d) % 4) for d in (1, 3)]
        along_y = [on_dp((y + d) % 4, z) for d in (1, 3)]
        if z_first:
            return z, y, along_z, along_y, lambda h, i: self.acc.at[j, h, :, i], \
                lambda h, i: self.acc.at[j, h, i, z]
        return y, z, along_y, along_z, lambda h, i: self.acc.at[j, h, i], \
            lambda h, i: self.acc.at[j, h, y, i]

    def copies(self, j, z_first, stage):
        here, there, ring, ring2, part, part2 = self.at(j, z_first)
        both = slice(0, 2)

        def pair(sources, target, peers):
            return [
                remote(sources[n], target.at[j, n], self.send.at[j, stage, n],
                       self.recv.at[j, stage, n], peers[n])
                for n in range(2)
            ]

        if stage == 0:
            return pair([part(0, (here + 2) % 4), part(1, (here + 2) % 4)], self.far, ring)
        if stage == 1:
            return pair([part(both, (here + 1) % 4), part(both, (here + 3) % 4)], self.near, ring)
        if stage == 2:
            return pair([part2(0, (there + 2) % 4), part2(1, (there + 2) % 4)], self.far2, ring2)
        if stage == 3:
            return pair([part2(both, (there + 1) % 4), part2(both, (there + 3) % 4)], self.near2,
                        ring2)
        return [remote(self.fin.at[j, 1], self.last.at[j], self.send.at[j, 4, 0],
                       self.recv.at[j, 4, 0], self.partner)]

    def step(self, j, z_first, stage, put):
        here, there, _, _, part, part2 = self.at(j, z_first)
        if stage > 0:
            for copy in self.copies(j, z_first, stage - 1):
                copy.wait_recv()
        if stage == 1:
            def add_far(i, carry):
                for n, d in ((0, 1), (1, 3)):
                    ref = part(n, (here + d) % 4)
                    ref[i] = ref[i] + self.far[j, n, i]
                return carry

            lax.fori_loop(0, 4, add_far, 0)
        if stage == 2:
            def add_near(i, carry):
                for h in range(2):
                    ref = part(h, here)
                    ref[i] = ref[i] + (self.near[j, 0, h, i] + self.near[j, 1, h, i])
                return carry

            lax.fori_loop(0, 4, add_near, 0)
        if stage == 3:
            for n, d in ((0, 1), (1, 3)):
                ref = part2(n, (there + d) % 4)
                ref[...] = ref[...] + self.far2[j, n]
        if stage == 4:
            for h in range(2):
                ref = part2(h, there)
                self.fin[j, h] = ref[...] + (self.near2[j, 0, h] + self.near2[j, 1, h])
        if stage == 5:
            put(j, self.fin[j, 0] + self.last[j])
        else:
            start_all(self.copies(j, z_first, stage))

    def sent(self, j, z_first):
        for stage in range(5):
            for copy in self.copies(j, z_first, stage):
                copy.wait_send()


def reduction_scratch(jobs, width):
    dma = pltpu.SemaphoreType.DMA
    return [
        pltpu.VMEM((jobs, 2, 4, 4, 48, width), F32),
        pltpu.VMEM((jobs, 2, 4, 48, width), F32),
        pltpu.VMEM((jobs, 2, 2, 4, 48, width), F32),
        pltpu.VMEM((jobs, 2, 48, width), F32),
        pltpu.VMEM((jobs, 2, 2, 48, width), F32),
        pltpu.VMEM((jobs, 48, width), F32),
        pltpu.VMEM((jobs, 2, 48, width), F32),
        dma((jobs, 5, 2)),
        dma((jobs, 5, 2)),
    ]


class Sums:
    def __init__(self, va, v1, v2, vec, send, recv):
        self.va, self.v1, self.v2, self.vec, self.send, self.recv = va, v1, v2, vec, send, recv
        _, _, p, y, z = place()
        self.partner = {"tensor": 1 - p}
        self.peers = [on_dp(y, (z + d) % 4) for d in range(1, 4)], \
            [on_dp((y + d) % 4, z) for d in range(1, 4)]

    def copies(self, stage):
        if stage == 2:
            return [remote(self.vec.at[0], self.vec.at[1], self.send.at[6], self.recv.at[6],
                           self.partner)]
        held = self.v1 if stage == 0 else self.v2
        return [
            remote(self.va.at[stage], held.at[d], self.send.at[3 * stage + d],
                   self.recv.at[3 * stage + d], self.peers[stage][d])
            for d in range(3)
        ]

    def step(self, stage):
        if stage > 0:
            for copy in self.copies(stage - 1):
                copy.wait()
        if stage == 1:
            self.va[1] = self.va[0] + (self.v1[0] + self.v1[1] + self.v1[2])
        if stage == 2:
            self.vec[0] = self.va[1] + (self.v2[0] + self.v2[1] + self.v2[2])
        if stage < 3:
            start_all(self.copies(stage))


def sums_scratch():
    dma = pltpu.SemaphoreType.DMA
    return [pltpu.VMEM((2, 8, D), F32), pltpu.VMEM((3, 8, D), F32), pltpu.VMEM((3, 8, D), F32),
            dma((7,)), dma((7,))]


def greet_all():
    _, _, p, y, z = place()
    peers = [{"tensor": 1 - p}]
    peers += [on_dp(y, (z + d) % 4) for d in range(1, 4)]
    peers += [on_dp((y + d) % 4, z) for d in range(1, 4)]
    greet(peers)


def job_terms(acc, j, left_t, x_of):
    width = acc.shape[5]

    def step(i, carry):
        half, y = i // 4, i % 4
        rows = pl.ds(pl.multiple_of(y * 192, 192), 192)
        acc[j, half, y] = dot(left_t[rows, :], x_of(half)[...]).reshape(4, 48, width)
        return carry

    lax.fori_loop(0, 8, step, 0)


def attn_finish_body(q0, k0, v0, gm0, lse0, o0, gb0, n0, gq2, gk2, gv2, o2, gb2, n2, g_in, h, w, v2,
                     g2, gain,
                     g_theirs, g_own, out, vec,
                     *scratch):
    red = Reduction(*scratch[:7], scratch[7:9])
    sums = Sums(*scratch[9:12], vec, *scratch[12:14])
    (x_v, o_v, low_v, left_t, gin_v, h_v, gout, w_v, q_v, k_v, v_v, gm_v, lse_v, gq_v, gk_v, gv_v,
     xl, ol, ld, st, send, recv) = scratch[14:]
    s, _, p, _, _ = place()
    partner = {"tensor": 1 - p}
    vec_ref = sums.va.at[0]

    def put(j, result):
        if j == 0:
            out[:, 1152:1536] = result
        else:
            for t in range(3):
                at = t * 384 + (j - 1) * 128
                out[:, at : at + 128] = result[:, t * 128 : t * 128 + 128]

    def low_loads(normed, gb):
        return [local(normed, low_v.at[0], ld.at[0]), local(gb, low_v.at[1], ld.at[1])]

    def o_loads(o):
        return [local(o.at[pair], o_v.at[pair // 3, :, pl.ds(pair % 3 * 128, 128)], ol.at[pair])
                for pair in range(PAIRS)]

    def attention_loads():
        return [local(a, b, ld.at[6 + n]) for n, (a, b) in enumerate(
            ((q0, q_v), (k0, k_v), (v0, v_v), (gm0, gm_v), (lse0, lse_v)))]

    def grad_loads():
        return [local(ref.at[pair], x_v.at[pair % 3, pair // 3, :, pl.ds(t * 128, 128)],
                      xl.at[t, pair])
                for t, ref in enumerate((gq2, gk2, gv2)) for pair in range(PAIRS)]

    def more_loads():
        return [local(g_in, gin_v, ld.at[2]), local(h, h_v, ld.at[3]), local(w, w_v, ld.at[4])]

    def early_sums():
        return local(v2, vec_ref, ld.at[5])

    @pl.when(s == 0)
    def _():
        start_all(o_loads(o0) + low_loads(n0, gb0) + attention_loads() + more_loads())

    @pl.when(s == 2)
    def _():
        start_all(o_loads(o2) + low_loads(n2, gb2) + grad_loads())
        early_sums().start()

    def swap(i):
        r = block(i)
        return remote(gout.at[r], g_theirs.at[r], send.at[i], recv.at[i], partner)

    swap2 = remote(g2, g_theirs, send.at[0], recv.at[0], partner)

    def keep(i):
        r = block(i)
        return local(gout.at[r], g_own.at[r], st.at[i])

    def rows():
        def step(i, carry):
            r = block(i)
            pl.when(i == 2)(lambda: take((3, 1), (2, 2), (1, 3), (0, 4)))
            parts = [(pairs_of((gq_v, gk_v), half, r), pairs_of((gv_v,), half, r))
                     for half in range(2)]
            gout[r, :] = qkv_back_rows(gin_v[r, :], h_v[r, :], gain[...], parts, w_v, vec_ref)
            swap(i).start()
            keep(i).start()
            return carry

        lax.fori_loop(0, BLOCKS, step, 0)

    def take(*steps):
        for j, stage in steps:
            red.step(j, j % 2 == 0, stage, put)

    @pl.when(s % 2 == 0)
    def _():
        for n, load in enumerate(low_loads(n0, gb0)):
            load.wait()
            left_t[n] = low_v[n].T
        wait_all(o_loads(o0))
        greet_all()

        @pl.when(s == 0)
        def _():
            sums.va[0] = jnp.zeros((8, D), F32)
            wait_all(attention_loads())

        @pl.when(s == 2)
        def _():
            swap2.start()
            early_sums().wait()
            wait_all(grad_loads())

        job_terms(red.acc, 0, left_t.at[1], lambda half: o_v.at[half])
        take((0, 0))

        def pair_step(i, carry):
            @pl.when(s == 0)
            def _():
                def one(half, carry):
                    pair = half * 3 + i
                    attend_back_pair(q_v, k_v, v_v, gm_v, lse_v, gq_v, gk_v, gv_v, pair)
                    for t, ref in enumerate((gq_v, gk_v, gv_v)):
                        x_v[i, half, :, t * 128 : t * 128 + 128] = ref[pair]
                    return carry

                lax.fori_loop(0, 2, one, 0)

            job_terms(red.acc, 1 + i, left_t.at[0], lambda half: x_v.at[i, half])
            pl.when(i == 0)(lambda: take((1, 0), (0, 1)))
            pl.when(i == 1)(lambda: take((2, 0), (1, 1), (0, 2)))
            pl.when(i == 2)(lambda: take((3, 0), (2, 1), (1, 2), (0, 3)))
            return carry

        lax.fori_loop(0, 3, pair_step, 0)

        @pl.when(s == 0)
        def _():
            wait_all(more_loads())
            rows()

        pl.when(s == 2)(lambda: take((3, 1), (2, 2), (1, 3), (0, 4)))

        sums.step(0)
        take((3, 2), (2, 3), (1, 4), (0, 5))
        sums.step(1)
        take((3, 3), (2, 4), (1, 5))
        sums.step(2)
        take((3, 4), (2, 5))
        take((3, 5))
        sums.step(3)
        for j in range(4):
            red.sent(j, j % 2 == 0)

        pl.when(s == 2)(swap2.wait)

        @pl.when(s == 0)
        def _():
            for i in range(BLOCKS):
                swap(i).wait()
                keep(i).wait()


def attn_finish(first, last, rest, gain):
    dma = pltpu.SemaphoreType.DMA
    any_spec = pl.BlockSpec(memory_space=ANY)
    vmem = pl.BlockSpec(memory_space=pltpu.VMEM)
    paired = pltpu.VMEM(PAIRED, BF16)
    return call(
        attn_finish_body,
        (shape(WIDE, F32), shape(WIDE, F32), shape((48, 1536), F32), shape((2, 8, D), F32)),
        [any_spec] * 19 + [vmem],
        (any_spec, any_spec, vmem, vmem),
        scratch=reduction_scratch(4, 384) + sums_scratch() + [
            pltpu.VMEM((3, 2, ROWS, 384), BF16), pltpu.VMEM((2, ROWS, 384), BF16),
            pltpu.VMEM((2,) + WIDE, BF16), pltpu.VMEM((2, D, ROWS), BF16), pltpu.VMEM(WIDE, F32),
            pltpu.VMEM(WIDE, F32), pltpu.VMEM(WIDE, F32), pltpu.VMEM((D, 2304), BF16),
            paired, paired, paired, paired, pltpu.VMEM((PAIRS, 8, ROWS), F32),
            paired, paired, paired,
            dma((3, PAIRS)), dma((PAIRS,)), dma((11,)), dma((BLOCKS,)), dma((BLOCKS,)),
            dma((BLOCKS,)),
        ],
        collective_id=20,
        has_side_effects=True,
    )(*first, *last, *rest, gain)


def ff_finish_body(gr1, act1, gb1, n1, gr3, act3, gb3, n3, g1, g3, v1, v3,
                   g_theirs, g3_theirs, out, vec,
                   *scratch):
    red = Reduction(*scratch[:7], scratch[7:9])
    sums = Sums(*scratch[9:12], vec, *scratch[12:14])
    x_v, low_v, left_t, ld, xs, xr, vl = scratch[14:]
    s, _, p, _, _ = place()
    partner = {"tensor": 1 - p}
    jobs = ((True, 0), (False, 2 * CHUNK), (True, CHUNK), (False, 3 * CHUNK))

    def put(j, result):
        out[:, jobs[j][1] : jobs[j][1] + CHUNK] = result

    def load(t, gr, act):
        z_first, column = jobs[t]
        x = gr if z_first else act
        at = column % (2 * CHUNK)
        return [
            local(x.at[:, half * 2 * CHUNK + at : half * 2 * CHUNK + at + CHUNK],
                  x_v.at[t % 2, half], ld.at[t % 2, half])
            for half in range(2)
        ]

    def start_load(t):
        pl.when(s == 1)(lambda: start_all(load(t, gr1, act1)))
        pl.when(s == 3)(lambda: start_all(load(t, gr3, act3)))

    def small(normed, gb, vecs):
        return [local(normed, low_v.at[0], vl.at[0]), local(gb, low_v.at[1], vl.at[1]),
                local(vecs, sums.va.at[0], vl.at[2])]

    swap = remote(g1.at[pl.ds(ROWS - BLOCK, BLOCK)], g_theirs, xs, xr, partner)
    swap3 = remote(g3, g3_theirs, xs, xr, partner)

    @pl.when(s % 2 == 1)
    def _():
        pl.when(s == 1)(lambda: start_all(small(n1, gb1, v1)))
        pl.when(s == 3)(lambda: start_all(small(n3, gb3, v3)))
        start_load(0)
        start_load(1)
        smalls = small(n1, gb1, v1)
        for n in range(2):
            smalls[n].wait()
            left_t[n] = low_v[n].T
        greet_all()
        pl.when(s == 1)(swap.start)
        pl.when(s == 3)(swap3.start)
        smalls[2].wait()
        for t in range(9):
            if t < 4:
                wait_all(load(t, gr1, act1))
                job_terms(red.acc, t, left_t.at[t % 2], lambda half, t=t: x_v.at[t % 2, half])
                if t + 2 < 4:
                    start_load(t + 2)
                red.step(t, jobs[t][0], 0, put)
            if t < 3:
                sums.step(t)
            for stage in range(1, 6):
                if 0 <= t - stage < 4:
                    j = t - stage
                    red.step(j, jobs[j][0], stage, put)
        sums.step(3)
        for j in range(4):
            red.sent(j, jobs[j][0])
        pl.when(s == 1)(swap.wait)
        pl.when(s == 3)(swap3.wait)


def ff_finish(first, last, rest):
    dma = pltpu.SemaphoreType.DMA
    any_spec = pl.BlockSpec(memory_space=ANY)
    vmem = pl.BlockSpec(memory_space=pltpu.VMEM)
    return call(
        ff_finish_body,
        (shape((BLOCK, D), F32), shape(WIDE, F32), shape((48, 4 * CHUNK), F32),
         shape((2, 8, D), F32)),
        [any_spec] * 12,
        (any_spec, any_spec, vmem, vmem),
        scratch=reduction_scratch(4, CHUNK) + sums_scratch() + [
            pltpu.VMEM((2, 2, ROWS, CHUNK), BF16), pltpu.VMEM((2,) + WIDE, BF16),
            pltpu.VMEM((2, D, ROWS), BF16),
            dma((2, 2)), dma, dma, dma((3,)),
        ],
        collective_id=21,
        has_side_effects=True,
    )(*first, *last, *rest)


def block_rows(i):
    return slice(i * BLOCK, min((i + 1) * BLOCK, LENGTH))


def load_block(mine, theirs, a_v, b_v, sems, i):
    r = pl.ds(i * BLOCK, BLOCK)
    return [local(mine.at[r], a_v.at[r], sems.at[0, i]),
            local(theirs.at[r], b_v.at[r], sems.at[1, i])]


def load_blocks(mine, theirs, a_v, b_v, sems, last=None):
    def step(i, carry):
        start_all(load_block(mine, theirs, a_v, b_v, sems, i))
        return carry

    lax.fori_loop(0, BLOCKS if last is None else BLOCKS - 1, step, 0)
    if last is not None:
        r = pl.ds(ROWS - BLOCK, BLOCK)
        local(mine.at[r], a_v.at[r], sems.at[0, BLOCKS - 1]).start()
        local(last, b_v.at[r], sems.at[1, BLOCKS - 1]).start()


def store_block(o_v, out, sems, i):
    r = block_rows(i) if isinstance(i, int) else block(i)
    return local(o_v.at[r], out.at[r], sems.at[2, i])


def write_block(a_v, b_v, o_v, sems, first, i):
    wait_all(load_block(a_v, b_v, a_v, b_v, sems, i))
    r = block_rows(i) if isinstance(i, int) else block(i)
    a, b = a_v[r, :], b_v[r, :]
    o_v[r, 0, :] = jnp.where(first, a, b)
    o_v[r, 1, :] = jnp.where(first, b, a)


def write_blocks(a_v, b_v, o_v, sems, first, out):
    def step(i, carry):
        write_block(a_v, b_v, o_v, sems, first, i)
        store_block(o_v, out, sems, i).start()
        return carry

    lax.fori_loop(0, BLOCKS - 1, step, 0)
    write_block(a_v, b_v, o_v, sems, first, BLOCKS - 1)
    store_block(o_v, out, sems, BLOCKS - 1).start()
    for i in range(BLOCKS):
        store_block(o_v, out, sems, i).wait()


def early_body(hf, h_theirs, out, a_v, b_v, o_v, sems):
    s, _, p, _, _ = place()

    @pl.when(s < 2)
    def _():
        load_blocks(hf, h_theirs, a_v, b_v, sems)
        write_blocks(a_v, b_v, o_v, sems, p == 0, out)


BOTH = (LENGTH, 2, D)


def early(hf, h_theirs):
    any_spec = pl.BlockSpec(memory_space=ANY)
    return call(
        early_body,
        shape(BOTH, F32),
        [any_spec] * 2,
        any_spec,
        scratch=[pltpu.VMEM(WIDE, F32), pltpu.VMEM(WIDE, F32), pltpu.VMEM(BOTH, F32),
                 pltpu.SemaphoreType.DMA((3, BLOCKS))],
    )(hf, h_theirs)


def assemble_body(hid_in, hm, h2, h3, g0, gb, gm, ga, gb_theirs, gf, g3, hid, gin,
                  a_v, b_v, o_v, sems):
    s, _, p, _, _ = place()
    first = jnp.where(s < 2, p, 1 - p) == 0

    def load(n, mine, theirs, last=None):
        load_blocks(mine, theirs, a_v.at[n], b_v.at[n], sems.at[n], last)

    pl.when(s == 0)(lambda: load(0, g0, ga))
    pl.when(s == 1)(lambda: load(0, gb, gb_theirs, gf))

    @pl.when(s == 2)
    def _():
        load(0, gb, ga)
        load(1, hm, h2)

    @pl.when(s == 3)
    def _():
        load(0, gm, g3)
        load(1, hm, h3)

    def write(n, carry):
        def step(i, carry):
            write_block(a_v.at[n], b_v.at[n], o_v.at[n], sems.at[n], first, i)
            pl.when(n == 0)(lambda: store_block(o_v.at[n], gin, sems.at[n], i).start())
            pl.when(n == 1)(lambda: store_block(o_v.at[n], hid, sems.at[n], i).start())
            return carry

        lax.fori_loop(0, BLOCKS - 1, step, 0)
        write_block(a_v.at[n], b_v.at[n], o_v.at[n], sems.at[n], first, BLOCKS - 1)
        pl.when(n == 0)(lambda: store_block(o_v.at[n], gin, sems.at[n], BLOCKS - 1).start())
        pl.when(n == 1)(lambda: store_block(o_v.at[n], hid, sems.at[n], BLOCKS - 1).start())
        return carry

    lax.fori_loop(0, jnp.where(s < 2, 1, 2), write, 0)
    for i in range(BLOCKS):
        store_block(o_v.at[0], gin, sems.at[0], i).wait()
        pl.when(s >= 2)(lambda i=i: store_block(o_v.at[1], hid, sems.at[1], i).wait())


def assemble(*operands):
    any_spec = pl.BlockSpec(memory_space=ANY)
    return call(
        assemble_body,
        (shape(BOTH, F32),) * 2,
        [any_spec] * 11,
        (any_spec, any_spec),
        scratch=[pltpu.VMEM((2,) + WIDE, F32), pltpu.VMEM((2,) + WIDE, F32),
                 pltpu.VMEM((2,) + BOTH, F32), pltpu.SemaphoreType.DMA((2, 3, BLOCKS))],
        aliases={0: 0},
    )(*operands)


def unwritten(shapes):
    any_spec = pl.BlockSpec(memory_space=ANY)
    return pl.pallas_call(
        lambda *refs: None,
        out_shape=tuple(shapes),
        out_specs=(any_spec,) * len(shapes),
    )()


def only_at(active, run, operands):
    like = jax.eval_shape(run, *operands)
    leaves, tree = jax.tree.flatten(like)

    def skip(*_):
        return jax.tree.unflatten(tree, unwritten([shape(x.shape, x.dtype) for x in leaves]))

    return lax.cond(active, run, skip, *operands)


def per_device(inputs, cotangent, norm_gain, norm_bias, qkv_weight, qv_bias, out_weight, end_bias,
               up_weight, up_bias, down_weight):
    s, r, p = lax.axis_index("section"), lax.axis_index("dp"), lax.axis_index("tensor")
    qkv, out_w, up, down = qkv_weight[0], out_weight[0], up_weight[0], down_weight[0]

    gain, shift, end = norm_gain, norm_bias, end_bias
    attn = s % 2 == 0
    by_row = [jnp.transpose(x, (1, 0, 2)) for x in (inputs, cotangent)]
    w, w_out, w_up, w_down, h0, normed0, q0, k0, v0, o0, lse0, qkvb, upb = opening(
        qkv, out_w, up, down, by_row[0], qv_bias[0], up_bias, gain, shift)
    cot = only_at(s == 3, lambda x: (extract(x),), (by_row[1],))[0]
    hf, h_in, act1, slope1, normed_f, q2, k2, v2, o2, lse2 = forward(
        o0, h0, w_out, w_up, w_down, w, gain, shift, end, upb, qkvb)
    h_early = exchange(hf)
    hid_early = early(hf, h_early)
    o2, hid_early = lax.optimization_barrier((o2, hid_early))
    hm, _, act3, gr3, gb_m, normed3, g2, gm2, g_m, vec_m, h3_theirs = middle(
        o2, h_in, w_out, w_up, w_down, cot, gain, shift, end, upb)
    g_b, g_in0, gr1, gb_b, gm0, vec_b, h2_theirs, gb_theirs, gq2, gk2, gv2 = backward(
        g2, h_in, q2, k2, v2, gm2, lse2, w, w_up, w_down, slope1, w_out, hm, gain)

    gb_m, vec_b = lax.optimization_barrier((gb_m, vec_b))
    g1_theirs, g3_theirs, ff_sums, ff_vec = ff_finish(
        (gr1, act1, gb_b, normed_f), (gr3, act3, gb_m, normed3), (g_b, g_m, vec_b, vec_m))
    ga_theirs, g_0, attn_sums, attn_vec = attn_finish(
        (q0, k0, v0, gm0, lse0, o0, gb_b, normed0), (gq2, gk2, gv2, o2, gb_m, normed_f),
        (g_in0, h0, w, vec_b, g_b), gain)
    hid, gin = assemble(
        hid_early, hm, h2_theirs, h3_theirs, g_0, g_b, g_m, ga_theirs, gb_theirs, g1_theirs,
        g3_theirs)
    hid, gin = [jnp.transpose(x, (1, 0, 2))[None] for x in (hid, gin)]
    vec = jnp.where(attn, attn_vec, ff_vec)

    both = vec[0] + vec[1]

    def mine(row):
        return lax.dynamic_slice_in_dim(both[row], r * 48, 48)[None]

    def when(flag, x):
        return jnp.where(flag, x, 0.0)[None]

    qkv_grad = jnp.transpose(attn_sums[:, :1152].reshape(48, 3, 384), (1, 0, 2))
    qv_grad = vec[0, 3:5, :384] + vec[1, 3:5, 384:]
    up_bias_grad = (vec[0, 3:5] + vec[1, 5:7]).reshape(1536)
    return (
        hid,
        gin,
        mine(0),
        mine(1),
        when(attn, qkv_grad),
        when(attn, qv_grad),
        when(attn, attn_sums[:, 1152:].T),
        mine(2),
        when(~attn, ff_sums[:, :1536]),
        when(~attn, up_bias_grad),
        when(~attn, ff_sums[:, 1536:].T),
    )


def solution(mesh):
    return jax.shard_map(
        per_device,
        mesh=mesh,
        in_specs=(
            P("dp", None, None),
            P("dp", None, None),
            P("section", None),
            P("section", None),
            P("section", None, None, "tensor"),
            P("section", None, "tensor"),
            P("section", "tensor", None),
            P("section", None),
            P("section", None, "tensor"),
            P("section", "tensor"),
            P("section", "tensor", None),
        ),
        out_specs=(
            P("section", "dp", None, None),
            P("section", "dp", None, None),
            P("section", "dp"),
            P("section", "dp"),
            P("section", None, "dp", "tensor"),
            P("section", None, "tensor"),
            P("section", "tensor", "dp"),
            P("section", "dp"),
            P("section", "dp", "tensor"),
            P("section", "tensor"),
            P("section", "tensor", "dp"),
        ),
        check_vma=False,
    )
```

```python
import functools

import jax
import jax.numpy as jnp
from jax import lax
from jax.experimental import pallas as pl
from jax.experimental.pallas import tpu as pltpu
from jax.sharding import PartitionSpec as P

MESH = pl.DeviceIdType.MESH
ANY = pl.ANY
F32 = jnp.float32
BF16 = jnp.bfloat16

HEAD_DIM = 64
EPS = 1e-06
LENGTH = 866
ROWS = 896
BLOCK = 224
D = 768
PAIRS = 6
Q_BLOCKS = ((0, 384), (384, 512))
VMEM_BYTES = 60 * 1024 * 1024

CHUNK = 768


def call(body, out_shape, in_specs, out_specs, grid=(), scratch=(), aliases={}, **more):
    return pl.pallas_call(
        body,
        out_shape=out_shape,
        grid=grid,
        in_specs=in_specs,
        out_specs=out_specs,
        scratch_shapes=scratch,
        input_output_aliases=aliases,
        compiler_params=pltpu.CompilerParams(vmem_limit_bytes=VMEM_BYTES, **more),
    )


def shape(dims, dtype):
    return jax.ShapeDtypeStruct(dims, dtype)


def whole(*dims):
    return pl.BlockSpec(dims, lambda *_: (0,) * len(dims), pipeline_mode=pl.Buffered(1))


def rows_of(width):
    return pl.BlockSpec((BLOCK, width), lambda i: (i, 0))


def dot(a, b, ca=1, cb=0):
    return lax.dot_general(a, b, (((ca,), (cb,)), ((), ())), preferred_element_type=F32)


def normalized(h):
    average = jnp.mean(h, axis=-1, keepdims=True)
    centred = h - average
    spread = jnp.mean(centred * centred, axis=-1, keepdims=True)
    r = lax.rsqrt(spread + EPS)
    return centred * r, r


def norm_back(g, h, gain, grad_normed):
    xhat, r = normalized(h)
    t = grad_normed * gain
    t_mean = jnp.mean(t, axis=-1, keepdims=True)
    tx_mean = jnp.mean(t * xhat, axis=-1, keepdims=True)
    return g + r * (t - t_mean - xhat * tx_mean), xhat


def block(i):
    return pl.ds(pl.multiple_of(i * BLOCK, 32), BLOCK)


def gelu_and_slope(x):
    phi = 0.5 * (1.0 + lax.erf(x * 0.7071067811865476))
    density = jnp.exp(-0.5 * x * x) * 0.3989422804014327
    return (x * phi).astype(BF16), phi + x * density


def qkv_block(h, gain, shift, w_ref, bias, q_ref, k_ref, v_ref, normed_ref, r):
    xhat, _ = normalized(h)
    normed_ref[r, :] = (xhat * gain + shift).astype(BF16)

    def half_step(half, carry):
        cols = pl.ds(pl.multiple_of(half * 1152, 128), 1152)
        part = (dot(normed_ref[r, :], w_ref[:, cols]) + bias[:, cols]).astype(BF16)
        for n in range(9):
            lanes = part[:, n * 128 : n * 128 + 128]
            pair = half * 3 + n % 3
            if n < 3:
                q_ref[pair, r, :] = (lanes.astype(F32) * 0.125).astype(BF16)
            elif n < 6:
                k_ref[pair, r, :] = lanes
            else:
                v_ref[pair, r, :] = lanes
        return carry

    lax.fori_loop(0, 2, half_step, 0)


def joined(ref, r):
    return jnp.concatenate([ref[j, r, :] for j in range(PAIRS)], axis=1)


def mixed_back_block(g, w_out_ref, gm_ref, r):
    gb = g.astype(BF16)
    gm = dot(gb, w_out_ref[...], 1, 1).astype(BF16)
    for j in range(PAIRS):
        gm_ref[j, r, :] = gm[:, j * 128 : j * 128 + 128]
    return gb


def add_row(vec_ref, at, values):
    vec_ref[at : at + 1, :] += jnp.sum(values, axis=0, keepdims=True)


def qkv_back_rows(g, h, gain, parts, w_ref, vec_ref):
    grad_normed = jnp.zeros((BLOCK, D), F32)
    for half, (qk, v) in enumerate(parts):
        part = jnp.concatenate([qk, v], axis=1)
        grad_normed = grad_normed + dot(part, w_ref[:, half * 1152 : half * 1152 + 1152], 1, 1)
    out, xhat = norm_back(g, h, gain, grad_normed)
    add_row(vec_ref, 0, grad_normed * xhat)
    add_row(vec_ref, 1, grad_normed)
    add_row(vec_ref, 2, g.astype(BF16).astype(F32))
    add_row(vec_ref, 3, jnp.concatenate([qk[:, :384] for qk, _ in parts], axis=1).astype(F32))
    add_row(vec_ref, 4, jnp.concatenate([v for _, v in parts], axis=1).astype(F32))
    return out


def pairs_of(refs, half, r):
    return jnp.concatenate([ref[half * 3 + i, r, :] for ref in refs for i in range(3)], axis=1)


def head_mask(dims, axis, head):
    at = lax.broadcasted_iota(jnp.int32, dims, axis)
    return at < HEAD_DIM if head == 0 else at >= HEAD_DIM


def with_lanes(x, head, columns):
    lane = lax.broadcasted_iota(jnp.int32, x.shape, 1)
    own, spare = (lane < HEAD_DIM, HEAD_DIM) if head == 0 else (lane >= HEAD_DIM, 0)
    out = jnp.where(own, x, 0)
    for n, column in enumerate(columns):
        out = jnp.where(lane == spare + n, column, out)
    return out


def in_pieces(x):
    high = x.astype(BF16)
    rest = x - high.astype(F32)
    middle = rest.astype(BF16)
    return [high, middle, (rest - middle.astype(F32)).astype(BF16)]


def key_bias():
    row = lax.broadcasted_iota(jnp.int32, (ROWS, 1), 0)
    return jnp.where(row < LENGTH, 0.0, -1e30).astype(BF16)


def attend_pair(q_ref, k_ref, v_ref, o_ref, lse_ref, j):
    one = jnp.ones((1, 1), BF16)
    q, k, v_t = q_ref[j], k_ref[j], v_ref[j].T
    out = jnp.zeros((128, ROWS), F32)
    rows = []
    for head in range(2):
        s = dot(with_lanes(k, head, [key_bias()]), with_lanes(q, head, [one]), 1, 1)
        top = jnp.max(s, axis=0, keepdims=True)
        e = jnp.exp(s - top)
        total = jnp.sum(e, axis=0, keepdims=True)
        p = (e * (1.0 / total)).astype(BF16)
        out = out + dot(jnp.where(head_mask(v_t.shape, 0, head), v_t, 0), p)
        rows.append(top + jnp.log(total))
    o_ref[j] = out.T.astype(BF16)
    lse_ref[j] = jnp.concatenate(rows + [jnp.zeros((6, ROWS), F32)], axis=0)


def attend_back_pair(q_ref, k_ref, v_ref, gm_ref, lse_ref, gq_ref, gk_ref, gv_ref, j):
    one = jnp.ones((1, 1), BF16)
    k, v = k_ref[j], v_ref[j]
    k_t = k.T
    k_heads = [jnp.where(head_mask(k_t.shape, 0, head), k_t, 0) for head in range(2)]
    k_lanes = [with_lanes(k, head, [one, one, one, key_bias()]) for head in range(2)]
    lse_columns = lse_ref[j].T
    grad_k = jnp.zeros((ROWS, 128), F32)
    grad_v = jnp.zeros((ROWS, 128), F32)
    for start, size in Q_BLOCKS:
        rows = slice(start, start + size)
        q, gm, lse = q_ref[j, rows, :], gm_ref[j, rows, :], lse_columns[rows, :]
        grad_q = jnp.zeros((128, size), F32)
        for head in range(2):
            q_lanes = with_lanes(q, head, in_pieces(-lse[:, head : head + 1]) + [one])
            q_head, gm_head = with_lanes(q, head, []), with_lanes(gm, head, [])
            p = jnp.exp(dot(k_lanes[head], q_lanes, 1, 1))
            gp = dot(v, gm_head, 1, 1)
            weighted = p * gp
            gs = (weighted - p * jnp.sum(weighted, axis=0, keepdims=True)).astype(BF16)
            grad_v = grad_v + dot(p.astype(BF16), gm_head)
            grad_k = grad_k + dot(gs, q_head)
            grad_q = grad_q + dot(k_heads[head], gs)
        gq_ref[j, rows, :] = (grad_q.T * 0.125).astype(BF16)
    gk_ref[j] = grad_k.astype(BF16)
    gv_ref[j] = grad_v.astype(BF16)


def extract_body(x_ref, out_ref):
    s, p = lax.axis_index("section"), lax.axis_index("tensor")
    clip = jnp.where(s < 2, p, 1 - p)
    x = x_ref[...].astype(F32)
    x = jnp.where(clip == 0, x[:, 0, :], x[:, 1, :])
    at = lax.broadcasted_iota(jnp.int32, x.shape, 0) + pl.program_id(0) * BLOCK
    out_ref[...] = jnp.where(at < LENGTH, x, 0.0)


def extract(x):
    return call(
        extract_body,
        shape((ROWS, D), F32),
        [pl.BlockSpec((BLOCK, 2, D), lambda i: (i, 0, 0))],
        rows_of(D),
        grid=(ROWS // BLOCK,),
    )(x)


def place():
    s, r, p = lax.axis_index("section"), lax.axis_index("dp"), lax.axis_index("tensor")
    return s, r, p, r // 4, r % 4


def on_dp(y, z):
    return {"dp": y * 4 + z}


def greet(peers):
    barrier = pltpu.get_barrier_semaphore()
    for peer in peers:
        pl.semaphore_signal(barrier, inc=1, device_id=peer, device_id_type=MESH)
    pl.semaphore_wait(barrier, len(peers))


def remote(src, dst, send, recv, device):
    return pltpu.make_async_remote_copy(
        src_ref=src, dst_ref=dst, send_sem=send, recv_sem=recv, device_id=device,
        device_id_type=MESH,
    )


def local(src, dst, sem):
    return pltpu.make_async_copy(src, dst, sem)


def start_all(copies):
    for copy in copies:
        copy.start()


def wait_all(copies):
    for copy in copies:
        copy.wait()


BLOCKS = ROWS // BLOCK


class Piece:
    def __init__(self, n, source, view, halves, z_first, sems):
        self.n, self.source, self.view, self.halves, self.z_first = n, source, view, halves, z_first
        self.send, self.recv = sems
        _, _, p, self.y, self.z = place()
        self.partner = {"tensor": 1 - p}

    def copies(self, stage):
        y, z, view = self.y, self.z, self.view
        along_z = [on_dp(y, (z + d) % 4) for d in (1, 3)]
        along_y = [on_dp((y + d) % 4, z) for d in (1, 3)]

        def copy(n, src, dst, device):
            return remote(src, dst, self.send.at[self.n, stage, n], self.recv.at[self.n, stage, n],
                          device)

        def both(refs, peers):
            return [copy(n, refs[n], refs[n], peers[n]) for n in range(2)]

        everything = slice(0, 4)
        if self.z_first:
            ring, ring2 = along_z, along_y
            one = lambda d: view(y, (z + d) % 4)
            group = lambda d, part=everything: view((y + d) % 4, part)
        else:
            ring, ring2 = along_y, along_z
            one = lambda d: view((y + d) % 4, z)
            group = lambda d, part=everything: view(part, (z + d) % 4)
        if stage == 0:
            return [copy(0, self.source, view(y, z), self.partner)]
        if stage == 1:
            return both([one(0), one(0)], ring)
        if stage == 2:
            return both([self.halves(one(3))[0], self.halves(one(1))[1]], ring)
        if stage == 3:
            return both([group(0), group(0)], ring2)
        return both([group(3, slice(0, 2)), group(1, slice(2, 4))], ring2)


def advance(pieces, stage):
    for piece in pieces:
        if stage > 0:
            for copy in piece.copies(stage - 1):
                copy.wait_recv()
        if stage < 5:
            start_all(piece.copies(stage))


def all_sent(pieces):
    for piece in pieces:
        for stage in range(5):
            for copy in piece.copies(stage):
                copy.wait_send()


def opening_body(qkv, out_w, up, down, x, qvb, upb, gain, shift,
                 w, w_out, w_up, w_down, h0, normed, q, k, v, o, lse, qkvb, upb_all,
                 w_v, w_out_v, up_v, down_v, fq, fo, fu, fd, fx, lq, lo, lu, ldn, lx, qvb_o, upb_o,
                 x_v, h_v, normed_v, q_v, k_v, v_v, o_v, lse_v, ld, st, send, recv, bsend, brecv,
                 gate):
    s, r, p, y, z = place()
    partner = {"tensor": 1 - p}
    attn = s % 2 == 0
    peers = [partner] + [on_dp(y, (z + d) % 4) for d in (1, 3)] \
        + [on_dp((y + d) % 4, z) for d in (1, 3)]
    barrier = pltpu.get_barrier_semaphore()
    for peer in peers:
        pl.semaphore_signal(barrier, inc=1, device_id=peer, device_id_type=MESH)

    def rows_at(n):
        return pl.ds(pl.multiple_of(r * n, n), n)

    def qkv_half(half):
        cols = pl.ds(pl.multiple_of(half * 1152, 128), 1152)

        def step(i, carry):
            rows = block(i)

            @pl.when(half == 0)
            def _():
                x0 = x_v[rows].astype(F32)
                h = jnp.where(p == 0, x0[:, 0, :], x0[:, 1, :])
                at = lax.broadcasted_iota(jnp.int32, h.shape, 0) + i * BLOCK
                h = jnp.where(at < LENGTH, h, 0.0)
                h_v[rows, :] = h
                xhat, _ = normalized(h)
                normed_v[rows, :] = (xhat * gain[...] + shift[...]).astype(BF16)

            part = (dot(normed_v[rows, :], w_v[:, cols]) + qkvb[:, cols]).astype(BF16)
            for n in range(9):
                lanes = part[:, n * 128 : n * 128 + 128]
                pair = half * 3 + n % 3
                if n < 3:
                    q_v[pair, rows, :] = (lanes.astype(F32) * 0.125).astype(BF16)
                elif n < 6:
                    k_v[pair, rows, :] = lanes
                else:
                    v_v[pair, rows, :] = lanes
            return carry

        lax.fori_loop(0, BLOCKS, step, 0)

    @pl.when(attn)
    def _():
        loads = [local(qkv.at[t], w_v.at[:, pl.ds(t * 384, 384)], ld.at[t]) for t in range(3)]
        loads.append(local(out_w, w_out_v.at[pl.ds(0, 384)], ld.at[3]))
        clips = local(x, x_v.at[pl.ds(0, LENGTH)], ld.at[4])
        start_all(loads)
        pl.when(s == 0)(clips.start)
        sems = send, recv
        def rows24(ref):
            return ref.at[pl.ds(0, 24)], ref.at[pl.ds(24, 24)]

        left, right = pl.ds(0, 256), pl.ds(256, 128)
        pieces = [
            Piece(0, fq.at[0], lambda a, b: lq.at[0, a, b], rows24, True, sems),
            Piece(1, fq.at[1], lambda a, b: lq.at[1, a, b], rows24, False, sems),
            Piece(2, fq.at[2, :, left], lambda a, b: lq.at[2, a, b, ..., left], rows24, True, sems),
            Piece(3, fq.at[2, :, right], lambda a, b: lq.at[2, a, b, ..., right], rows24, False,
                  sems),
        ]
        direct = remote(fo, lo, bsend.at[1], brecv.at[1], partner)
        bias = remote(qvb, qvb_o, bsend.at[0], brecv.at[0], partner)
        qkvb[:, 0:384] = qvb[0:1, :]
        qkvb[:, 384:768] = jnp.zeros((1, 384), F32)
        qkvb[:, 768:1152] = qvb[1:2, :]
        wait_all(loads)
        for t in range(3):
            fq[t] = w_v[rows_at(48), t * 384 : t * 384 + 384].astype(F32)
        fo[...] = w_out_v[0:384, :].astype(F32)
        pl.semaphore_wait(barrier, 6)
        advance(pieces, 0)
        bias.start()
        direct.start()

        pl.when(s == 0)(clips.wait)
        stored = [local(w_v, w, st.at[0]), local(w_out_v, w_out, st.at[1])]

        def gathered():
            advance(pieces, 4)
            bias.wait()
            direct.wait()
            w_out_v[384:768, :] = lo[...].astype(BF16)
            advance(pieces, 5)
            for t in range(3):
                at = 1152 + t * 384

                def widen(i, carry, t=t, at=at):
                    w_v[pl.ds(pl.multiple_of(i * 192, 192), 192), at : at + 384] = \
                        lq[t, i].reshape(192, 384).astype(BF16)
                    return carry

                lax.fori_loop(0, 4, widen, 0)
            qkvb[:, 1152:1536] = qvb_o[0:1, :]
            qkvb[:, 1536:1920] = jnp.zeros((1, 384), F32)
            qkvb[:, 1920:2304] = qvb_o[1:2, :]
            start_all(stored)

        def pair_step(i, carry):
            pl.when((s == 0) & (i % 3 == 0))(lambda: qkv_half(i // 3))
            pl.when(i == 0)(lambda: advance(pieces, 1))
            pl.when(s == 0)(lambda: attend_pair(q_v, k_v, v_v, o_v, lse_v, i))
            pl.when(i == 0)(lambda: advance(pieces, 2))

            @pl.when(i == 1)
            def _():
                advance(pieces, 3)
                pl.semaphore_signal(gate, inc=1, device_id={"section": s + 1}, device_id_type=MESH)

            pl.when(i == 2)(gathered)
            return carry

        lax.fori_loop(0, PAIRS, pair_step, 0)

        @pl.when(s == 0)
        def _():
            kept = [local(a, b, st.at[2 + n]) for n, (a, b) in enumerate(
                ((h_v, h0), (normed_v, normed), (q_v, q), (k_v, k), (v_v, v), (o_v, o),
                 (lse_v, lse)))]
            start_all(kept)
            wait_all(kept)

        all_sent(pieces)
        wait_all(stored)

    @pl.when(jnp.logical_not(attn))
    def _():
        pl.semaphore_signal(barrier, inc=1, device_id={"section": s - 1}, device_id_type=MESH)
        loads = [local(up, up_v.at[:, pl.ds(0, 1536)], ld.at[0]),
                 local(down, down_v.at[pl.ds(0, 1536)], ld.at[1])]
        start_all(loads)
        sems = send, recv
        pieces = [
            Piece(0, fu, lambda a, b: lu.at[a, b],
                  lambda ref: (ref.at[pl.ds(0, 24)], ref.at[pl.ds(24, 24)]), True, sems),
            Piece(1, fd, lambda a, b: ldn.at[a, b],
                  lambda ref: (ref.at[pl.ds(0, 48)], ref.at[pl.ds(48, 48)]), False, sems),
        ]
        direct = remote(fx, lx, bsend.at[1], brecv.at[1], partner)
        early = [local(up_v.at[:, pl.ds(0, 1536)], w_up.at[:, pl.ds(0, 1536)], st.at[0]),
                 local(down_v.at[pl.ds(0, 1536)], w_down.at[pl.ds(0, 1536)], st.at[1])]
        late = [local(up_v.at[:, pl.ds(1536, 1536)], w_up.at[:, pl.ds(1536, 1536)], st.at[2]),
                local(down_v.at[pl.ds(1536, 1536)], w_down.at[pl.ds(1536, 1536)], st.at[3])]
        bias = remote(upb, upb_o, bsend.at[0], brecv.at[0], partner)
        upb_all[:, 0:1536] = upb[...]
        wait_all(loads)
        fu[...] = up_v[rows_at(48), 0:1536].astype(F32)
        start_all(early)
        fd[...] = down_v[rows_at(96), 0:512].astype(F32)
        pl.semaphore_wait(barrier, 5)
        advance(pieces, 0)
        bias.start()
        fx[...] = down_v[0:1536, 512:768].astype(F32)
        direct.start()
        pl.semaphore_wait(gate, 1)
        for stage in range(1, 5):
            advance(pieces, stage)
        bias.wait()
        upb_all[:, 1536:3072] = upb_o[...]

        def widen(d):
            i, g = (y + d) % 4, (z + d) % 4
            up_v[pl.ds(pl.multiple_of(i * 192, 192), 192), 1536:3072] = \
                lu[i].reshape(192, 1536).astype(BF16)
            for a in range(4):
                down_v[pl.ds(pl.multiple_of(1536 + (a * 4 + g) * 96, 96), 96), 0:512] = \
                    ldn[a, g].astype(BF16)

        for d in (0, 1, 3):
            widen(d)
        direct.wait()
        down_v[1536:3072, 512:768] = lx[...].astype(BF16)
        advance(pieces, 5)
        widen(2)
        start_all(late)
        all_sent(pieces)
        wait_all(early + late)


def opening(qkv, out_w, up, down, x, qvb, upb, gain, shift):
    dma = pltpu.SemaphoreType.DMA
    any_spec = pl.BlockSpec(memory_space=ANY)
    vmem = pl.BlockSpec(memory_space=pltpu.VMEM)
    paired, lse = (PAIRS, ROWS, 128), (PAIRS, 8, ROWS)
    return call(
        opening_body,
        (shape((D, 2304), BF16), shape((D, D), BF16), shape((D, 3072), BF16),
         shape((3072, D), BF16), shape((ROWS, D), F32), shape((ROWS, D), BF16),
         shape(paired, BF16), shape(paired, BF16), shape(paired, BF16), shape(paired, BF16),
         shape(lse, F32), shape((1, 2304), F32), shape((1, 3072), F32)),
        [any_spec] * 5 + [vmem] * 4,
        (any_spec,) * 11 + (vmem, vmem),
        scratch=[
            pltpu.VMEM((D, 2304), BF16), pltpu.VMEM((D, D), BF16), pltpu.VMEM((D, 3072), BF16),
            pltpu.VMEM((3072, D), BF16), pltpu.VMEM((3, 48, 384), F32), pltpu.VMEM((384, D), F32),
            pltpu.VMEM((48, 1536), F32), pltpu.VMEM((96, 512), F32), pltpu.VMEM((1536, 256), F32),
            pltpu.VMEM((3, 4, 4, 48, 384), F32), pltpu.VMEM((384, D), F32),
            pltpu.VMEM((4, 4, 48, 1536), F32), pltpu.VMEM((4, 4, 96, 512), F32),
            pltpu.VMEM((1536, 256), F32),
            pltpu.VMEM((2, 384), F32), pltpu.VMEM((1, 1536), F32),
            pltpu.VMEM((ROWS, 2, D), BF16), pltpu.VMEM((ROWS, D), F32),
            pltpu.VMEM((ROWS, D), BF16), pltpu.VMEM(paired, BF16), pltpu.VMEM(paired, BF16),
            pltpu.VMEM(paired, BF16), pltpu.VMEM(paired, BF16), pltpu.VMEM(lse, F32),
            dma((5,)), dma((9,)), dma((4, 5, 2)), dma((4, 5, 2)), dma((2,)), dma((2,)),
            pltpu.SemaphoreType.REGULAR,
        ],
        collective_id=1,
        has_side_effects=True,
    )(qkv, out_w, up, down, x, qvb, upb, gain, shift)


class Link:
    def __init__(self, src, dst, send, recv):
        self.src, self.dst, self.sems = src, dst, (send, recv)

    def copy(self, i, device):
        r = block(i)
        return remote(self.src.at[r], self.dst.at[r], self.sems[0].at[i], self.sems[1].at[i], device)

    def expect_from(self, device):
        pl.semaphore_signal(
            pltpu.get_barrier_semaphore(), inc=1, device_id=device, device_id_type=MESH)

    def ready(self):
        pl.semaphore_wait(pltpu.get_barrier_semaphore(), 1)

    def arrived(self, i, device):
        self.copy(i, device).wait_recv()

    def sent(self, device):
        for i in range(BLOCKS):
            self.copy(i, device).wait_send()

    def both_ways(self, device):
        for i in range(BLOCKS):
            self.copy(i, device).wait()


def stores(pairs, sems):
    def of(i):
        r = block(i)
        found = []
        for n, (src, dst) in enumerate(pairs):
            if len(src.shape) == 3:
                found.append(local(src.at[:, r], dst.at[:, r], sems.at[n, i]))
            else:
                found.append(local(src.at[r], dst.at[r], sems.at[n, i]))
        return found

    return of


def every_block(step):
    def body(i, carry):
        step(i, block(i))
        return carry

    lax.fori_loop(0, BLOCKS, body, 0)


def out_proj_rows(o_v, h_v, w_out_v, end, hout, r):
    hout[r, :] = h_v[r, :] + (dot(joined(o_v, r), w_out_v[...]) + end)


def forward_body(o, h0, w_out, up, down, w, gain, shift, end, upb, qkvb,
                 h_out, h_in, act, slope, normed, q, k, v, o2, lse2,
                 hin, hout, up_v, down_v, act_v, slope_v, normed_v, o_v, w_out_v, w_v, q_v, k_v,
                 v_v, lse_v, ld, st, send, recv):
    s, _, p, _, _ = place()
    link = Link(hout, hin, send, recv)

    @pl.when(s == 0)
    def _():
        target = {"section": 1}
        loads = [local(o, o_v, ld.at[0]), local(h0, hin, ld.at[1]), local(w_out, w_out_v, ld.at[2])]
        start_all(loads)
        link.ready()
        wait_all(loads)
        out = stores([(hout, h_out)], st)

        def step(i, r):
            out_proj_rows(o_v, hin, w_out_v, end[...], hout, r)
            link.copy(i, target).start()
            start_all(out(i))

        every_block(step)
        link.sent(target)
        for i in range(BLOCKS):
            wait_all(out(i))

    @pl.when(s == 1)
    def _():
        source, target = {"section": 0}, {"section": 2, "tensor": 1 - p}
        loads = [local(up, up_v, ld.at[0]), local(down, down_v, ld.at[1])]
        start_all(loads)
        link.expect_from(source)
        link.ready()
        wait_all(loads)
        out = stores([(hout, h_out), (hin, h_in), (act_v, act), (slope_v, slope),
                      (normed_v, normed)], st)

        def step(i, r):
            link.arrived(i, source)
            h = hin[r, :]
            xhat, _ = normalized(h)
            low = (xhat * gain[...] + shift[...]).astype(BF16)
            normed_v[r, :] = low
            hout[r, :] = h + end[...]

            def chunk(c, carry):
                cols = pl.ds(pl.multiple_of(c * 768, 768), 768)
                x = dot(low, up_v[:, cols]) + upb[:, cols]
                active, steep = gelu_and_slope(x)
                act_v[r, cols] = active
                slope_v[r, cols] = steep
                hout[r, :] += dot(active, down_v[cols, :])
                return carry

            lax.fori_loop(0, 4, chunk, 0)
            link.copy(i, target).start()
            start_all(out(i))

        every_block(step)
        link.sent(target)
        for i in range(BLOCKS):
            wait_all(out(i))

    @pl.when(s == 2)
    def _():
        source = {"section": 1, "tensor": 1 - p}
        load = local(w, w_v, ld.at[0])
        load.start()
        link.expect_from(source)
        load.wait()
        out = stores([(hin, h_in), (normed_v, normed), (q_v, q), (k_v, k), (v_v, v)], st)

        def step(i, r):
            link.arrived(i, source)
            qkv_block(hin[r, :], gain[...], shift[...], w_v, qkvb, q_v, k_v, v_v, normed_v, r)
            start_all(out(i))

        every_block(step)

        def attend_step(i, carry):
            attend_pair(q_v, k_v, v_v, o_v, lse_v, i)
            return carry

        lax.fori_loop(0, PAIRS, attend_step, 0)
        kept = [local(o_v, o2, ld.at[1]), local(lse_v, lse2, ld.at[2])]
        start_all(kept)
        for i in range(BLOCKS):
            wait_all(out(i))
        wait_all(kept)


def staged(body, outs, operands, small, scratch, stored, collective_id):
    dma = pltpu.SemaphoreType.DMA
    any_spec = pl.BlockSpec(memory_space=ANY)
    vmem = pl.BlockSpec(memory_space=pltpu.VMEM)
    return call(
        body,
        tuple(shape(*o) for o in outs),
        [any_spec] * len(operands) + [vmem] * len(small),
        (any_spec,) * len(outs),
        scratch=[pltpu.VMEM(*x) for x in scratch]
        + [dma((8,)), dma((stored, BLOCKS))] + [dma((BLOCKS,))] * 4 + [dma((2 * BLOCKS,))] * 2,
        collective_id=collective_id,
        has_side_effects=True,
    )(*operands, *small)


WIDE = (ROWS, D)
HIDDEN = (ROWS, 3072)
PAIRED = (PAIRS, ROWS, 128)
LSE = (PAIRS, 8, ROWS)


def forward(o, h0, w_out, up, down, w, gain, shift, end, upb, qkvb):
    def body(*refs):
        return forward_body(*refs[:-4])

    return staged(
        body,
        [(WIDE, F32), (WIDE, F32), (HIDDEN, BF16), (HIDDEN, F32), (WIDE, BF16), (PAIRED, BF16),
         (PAIRED, BF16), (PAIRED, BF16), (PAIRED, BF16), (LSE, F32)],
        (o, h0, w_out, up, down, w),
        (gain, shift, end, upb, qkvb),
        [(WIDE, F32), (WIDE, F32), ((D, 3072), BF16), ((3072, D), BF16), (HIDDEN, BF16),
         (HIDDEN, F32), (WIDE, BF16), (PAIRED, BF16), ((D, D), BF16), ((D, 2304), BF16),
         (PAIRED, BF16), (PAIRED, BF16), (PAIRED, BF16), (LSE, F32)],
        5,
        2,
    )


def middle_body(o, h2, w_out, up, down, cot, gain, shift, end, upb,
                h_out, h_in, act, gr, gb, normed, g_in, gm, g_out, vec, h_theirs,
                hin, hout, gin, gout, act_v, gr_v, gb_v, normed_v, up_v, down_v, o_v, w_out_v, gm_v,
                vec_v, ups_v, ld, st, send, recv, back_send, back_recv, x_send, x_recv):
    s, _, p, _, _ = place()
    theirs = {"tensor": 1 - p}
    h_link = Link(hout, h_theirs, x_send, x_recv)
    link = Link(hout, hin, send, recv)
    back = Link(gout, gin, back_send, back_recv)

    @pl.when(s == 2)
    def _():
        other = {"section": 3}
        loads = [local(o, o_v, ld.at[0]), local(h2, hin, ld.at[1]), local(w_out, w_out_v, ld.at[2])]
        start_all(loads)
        back.expect_from(other)
        link.ready()
        wait_all(loads)
        out = stores([(hout, h_out)], st)
        back_out = stores([(hout, h_out), (gin, g_in), (gb_v, gb), (gm_v, gm)], st)

        def step(i, r):
            out_proj_rows(o_v, hin, w_out_v, end[...], hout, r)
            link.copy(i, other).start()
            start_all(out(i))

        every_block(step)

        def back_step(i, r):
            back.arrived(i, other)
            gb_v[r, :] = mixed_back_block(gin[r, :], w_out_v, gm_v, r)
            start_all(back_out(i)[1:])

        every_block(back_step)
        link.sent(other)
        for i in range(BLOCKS):
            wait_all(back_out(i))

    @pl.when(s == 3)
    def _():
        other = {"section": 2}
        loads = [local(up, up_v, ld.at[0]), local(down, down_v, ld.at[1]),
                 local(cot, gin, ld.at[2])]
        start_all(loads)
        link.expect_from(other)
        pl.semaphore_signal(
            pltpu.get_barrier_semaphore(), inc=1, device_id=theirs, device_id_type=MESH)
        pl.semaphore_wait(pltpu.get_barrier_semaphore(), 2)
        wait_all(loads)
        vec_v[...] = jnp.zeros_like(vec_v)
        ups_v[...] = jnp.zeros_like(ups_v)
        out = stores([(hout, h_out), (hin, h_in), (act_v, act), (gr_v, gr), (gb_v, gb),
                      (normed_v, normed), (gout, g_out)], st)

        def step(i, r):
            link.arrived(i, other)
            h, g = hin[r, :], gin[r, :]
            xhat, _ = normalized(h)
            low = (xhat * gain[...] + shift[...]).astype(BF16)
            normed_v[r, :] = low
            g_low = g.astype(BF16)
            gb_v[r, :] = g_low
            total = h + end[...]
            grad_normed = jnp.zeros((BLOCK, D), F32)
            for c in range(0, 3072, 768):
                cols = slice(c, c + 768)
                x = dot(low, up_v[:, cols]) + upb[:, cols]
                active, steep = gelu_and_slope(x)
                act_v[r, cols] = active
                total = total + dot(active, down_v[cols, :])
                raised = (dot(g_low, down_v[cols, :], 1, 1) * steep).astype(BF16)
                gr_v[r, cols] = raised
                ups_v[:, cols] += jnp.sum(raised.astype(F32), axis=0, keepdims=True)
                grad_normed = grad_normed + dot(raised, up_v[:, cols], 1, 1)
            hout[r, :] = total
            result, xhat = norm_back(g, h, gain[...], grad_normed)
            gout[r, :] = result
            back.copy(i, other).start()
            h_link.copy(i, theirs).start()
            add_row(vec_v, 0, grad_normed * xhat)
            add_row(vec_v, 1, grad_normed)
            add_row(vec_v, 2, g_low.astype(F32))
            start_all(out(i))

        every_block(step)
        for c in range(4):
            vec_v[3 + c : 4 + c, :] = ups_v[:, c * D : c * D + D]
        last = local(vec_v, vec, ld.at[3])
        last.start()
        back.sent(other)
        h_link.both_ways(theirs)
        for i in range(BLOCKS):
            wait_all(out(i))
        last.wait()


def middle(o, h2, w_out, up, down, cot, gain, shift, end, upb):
    return staged(
        middle_body,
        [(WIDE, F32), (WIDE, F32), (HIDDEN, BF16), (HIDDEN, BF16), (WIDE, BF16), (WIDE, BF16),
         (WIDE, F32), (PAIRED, BF16), (WIDE, F32), ((8, D), F32), (WIDE, F32)],
        (o, h2, w_out, up, down, cot),
        (gain, shift, end, upb),
        [(WIDE, F32)] * 4
        + [(HIDDEN, BF16), (HIDDEN, BF16), (WIDE, BF16), (WIDE, BF16), ((D, 3072), BF16),
           ((3072, D), BF16), (PAIRED, BF16), ((D, D), BF16), (PAIRED, BF16), ((8, D), F32),
           ((1, 3072), F32)],
        7,
        3,
    )


def backward_body(g2, h, q, k, v, gm2, lse, w, up, down, slope, w_out, h_made, gain,
                  g_out, g_in, gr, gb, gm, vec, h_theirs, g_theirs, gq, gk, gv,
                  gin, gout, h_v, slope_v, gr_v, gb_v, up_v, down_v, gq_v, gk_v, gv_v, w_v, w_out_v,
                  gm_v, vec_v, ups_v, q_v, k_v, v_v, lse_v, ld, st, send, recv, next_send, next_recv,
                  x_send, x_recv):
    s, _, p, _, _ = place()
    theirs = {"tensor": 1 - p}
    partner = Link(gout, g_theirs, x_send, x_recv)
    made = remote(h_made, h_theirs, x_send.at[BLOCKS], x_recv.at[BLOCKS], theirs)
    first = Link(gout, gin, send, recv)
    second = Link(gout, gin, next_send, next_recv)

    @pl.when(s == 2)
    def _():
        target = {"section": 1, "tensor": 1 - p}
        loads = [local(a, b, ld.at[n]) for n, (a, b) in enumerate(
            ((q, q_v), (k, k_v), (v, v_v), (gm2, gm_v), (lse, lse_v), (g2, gin), (h, h_v),
             (w, w_v)))]
        start_all(loads)
        pl.semaphore_signal(
            pltpu.get_barrier_semaphore(), inc=1, device_id=theirs, device_id_type=MESH)
        pl.semaphore_wait(pltpu.get_barrier_semaphore(), 2)
        made.start()
        wait_all(loads[:5])

        def attend_step(i, carry):
            attend_back_pair(q_v, k_v, v_v, gm_v, lse_v, gq_v, gk_v, gv_v, i)
            return carry

        lax.fori_loop(0, PAIRS, attend_step, 0)
        kept = [local(a, b, ld.at[n]) for n, (a, b) in enumerate(
            ((gq_v, gq), (gk_v, gk), (gv_v, gv)))]
        start_all(kept)
        wait_all(loads[5:])
        vec_v[...] = jnp.zeros_like(vec_v)
        out = stores([(gout, g_out)], st)

        def step(i, r):
            parts = [(pairs_of((gq_v, gk_v), half, r), pairs_of((gv_v,), half, r))
                     for half in range(2)]
            gout[r, :] = qkv_back_rows(gin[r, :], h_v[r, :], gain[...], parts, w_v, vec_v)
            first.copy(i, target).start()
            start_all(out(i))

        every_block(step)
        last = local(vec_v, vec, ld.at[6])
        last.start()
        first.sent(target)
        made.wait()
        wait_all(kept)
        for i in range(BLOCKS):
            wait_all(out(i))
        last.wait()

    @pl.when(s == 1)
    def _():
        source, target = {"section": 2, "tensor": 1 - p}, {"section": 0}
        loads = [local(a, b, ld.at[n]) for n, (a, b) in enumerate(
            ((up, up_v), (down, down_v), (slope, slope_v), (h, h_v)))]
        start_all(loads)
        first.expect_from(source)
        pl.semaphore_signal(
            pltpu.get_barrier_semaphore(), inc=1, device_id=theirs, device_id_type=MESH)
        pl.semaphore_wait(pltpu.get_barrier_semaphore(), 2)
        wait_all(loads)
        vec_v[...] = jnp.zeros_like(vec_v)
        ups_v[...] = jnp.zeros_like(ups_v)
        out = stores([(gout, g_out), (gr_v, gr), (gb_v, gb)], st)

        def step(i, r):
            first.arrived(i, source)
            g = gin[r, :]
            g_low = g.astype(BF16)
            gb_v[r, :] = g_low
            gout[r, :] = jnp.zeros((BLOCK, D), F32)

            def chunk(c, carry):
                cols = pl.ds(pl.multiple_of(c * 768, 768), 768)
                raised = (dot(g_low, down_v[cols, :], 1, 1) * slope_v[r, cols]).astype(BF16)
                gr_v[r, cols] = raised
                ups_v[:, cols] += jnp.sum(raised.astype(F32), axis=0, keepdims=True)
                gout[r, :] += dot(raised, up_v[:, cols], 1, 1)
                return carry

            lax.fori_loop(0, 4, chunk, 0)
            grad_normed = gout[r, :]
            result, xhat = norm_back(g, h_v[r, :], gain[...], grad_normed)
            gout[r, :] = result
            second.copy(i, target).start()
            pl.when(i < BLOCKS - 1)(lambda: partner.copy(i, theirs).start())
            add_row(vec_v, 0, grad_normed * xhat)
            add_row(vec_v, 1, grad_normed)
            add_row(vec_v, 2, g_low.astype(F32))
            start_all(out(i))

        every_block(step)
        for c in range(4):
            vec_v[3 + c : 4 + c, :] = ups_v[:, c * D : c * D + D]
        last = local(vec_v, vec, ld.at[6])
        last.start()
        second.sent(target)
        for i in range(BLOCKS - 1):
            partner.copy(i, theirs).wait()
        for i in range(BLOCKS):
            wait_all(out(i))
        last.wait()

    @pl.when(s == 0)
    def _():
        source = {"section": 1}
        load = local(w_out, w_out_v, ld.at[0])
        load.start()
        second.expect_from(source)
        load.wait()
        out = stores([(gin, g_in), (gb_v, gb), (gm_v, gm)], st)

        def step(i, r):
            second.arrived(i, source)
            gb_v[r, :] = mixed_back_block(gin[r, :], w_out_v, gm_v, r)
            start_all(out(i))

        every_block(step)
        for i in range(BLOCKS):
            wait_all(out(i))


def backward(g2, h, q, k, v, gm, lse, w, up, down, slope, w_out, h_made, gain):
    return staged(
        backward_body,
        [(WIDE, F32), (WIDE, F32), (HIDDEN, BF16), (WIDE, BF16), (PAIRED, BF16), ((8, D), F32),
         (WIDE, F32), (WIDE, F32), (PAIRED, BF16), (PAIRED, BF16), (PAIRED, BF16)],
        (g2, h, q, k, v, gm, lse, w, up, down, slope, w_out, h_made),
        (gain,),
        [(WIDE, F32)] * 3
        + [(HIDDEN, F32), (HIDDEN, BF16), (WIDE, BF16), ((D, 3072), BF16), ((3072, D), BF16),
           (PAIRED, BF16), (PAIRED, BF16), (PAIRED, BF16), ((D, 2304), BF16), ((D, D), BF16),
           (PAIRED, BF16), ((8, D), F32), ((1, 3072), F32), (PAIRED, BF16), (PAIRED, BF16),
           (PAIRED, BF16), (LSE, F32)],
        3,
        4,
    )


def exchange_body(h, theirs, send, recv):
    s, _, p, _, _ = place()

    @pl.when(s < 2)
    def _():
        partner = {"tensor": 1 - p}
        greet([partner])
        copy = remote(h, theirs, send, recv, partner)
        copy.start()
        copy.wait()


def exchange(h):
    dma = pltpu.SemaphoreType.DMA
    any_spec = pl.BlockSpec(memory_space=ANY)
    return call(
        exchange_body, shape(WIDE, F32), [any_spec], any_spec,
        scratch=[dma, dma], collective_id=5, has_side_effects=True,
    )(h)


class Reduction:
    def __init__(self, acc, far, near, far2, near2, last, fin, sems):
        self.acc, self.far, self.near, self.far2, self.near2 = acc, far, near, far2, near2
        self.last, self.fin = last, fin
        self.send, self.recv = sems
        _, _, p, self.y, self.z = place()
        self.partner = {"tensor": 1 - p}

    def at(self, j, z_first):
        y, z = self.y, self.z
        along_z = [on_dp(y, (z + d) % 4) for d in (1, 3)]
        along_y = [on_dp((y + d) % 4, z) for d in (1, 3)]
        if z_first:
            return z, y, along_z, along_y, lambda h, i: self.acc.at[j, h, :, i], \
                lambda h, i: self.acc.at[j, h, i, z]
        return y, z, along_y, along_z, lambda h, i: self.acc.at[j, h, i], \
            lambda h, i: self.acc.at[j, h, y, i]

    def copies(self, j, z_first, stage):
        here, there, ring, ring2, part, part2 = self.at(j, z_first)
        both = slice(0, 2)

        def pair(sources, target, peers):
            return [
                remote(sources[n], target.at[j, n], self.send.at[j, stage, n],
                       self.recv.at[j, stage, n], peers[n])
                for n in range(2)
            ]

        if stage == 0:
            return pair([part(0, (here + 2) % 4), part(1, (here + 2) % 4)], self.far, ring)
        if stage == 1:
            return pair([part(both, (here + 1) % 4), part(both, (here + 3) % 4)], self.near, ring)
        if stage == 2:
            return pair([part2(0, (there + 2) % 4), part2(1, (there + 2) % 4)], self.far2, ring2)
        if stage == 3:
            return pair([part2(both, (there + 1) % 4), part2(both, (there + 3) % 4)], self.near2,
                        ring2)
        return [remote(self.fin.at[j, 1], self.last.at[j], self.send.at[j, 4, 0],
                       self.recv.at[j, 4, 0], self.partner)]

    def step(self, j, z_first, stage, put):
        here, there, _, _, part, part2 = self.at(j, z_first)
        if stage > 0:
            for copy in self.copies(j, z_first, stage - 1):
                copy.wait_recv()
        if stage == 1:
            def add_far(i, carry):
                for n, d in ((0, 1), (1, 3)):
                    ref = part(n, (here + d) % 4)
                    ref[i] = ref[i] + self.far[j, n, i]
                return carry

            lax.fori_loop(0, 4, add_far, 0)
        if stage == 2:
            def add_near(i, carry):
                for h in range(2):
                    ref = part(h, here)
                    ref[i] = ref[i] + (self.near[j, 0, h, i] + self.near[j, 1, h, i])
                return carry

            lax.fori_loop(0, 4, add_near, 0)
        if stage == 3:
            for n, d in ((0, 1), (1, 3)):
                ref = part2(n, (there + d) % 4)
                ref[...] = ref[...] + self.far2[j, n]
        if stage == 4:
            for h in range(2):
                ref = part2(h, there)
                self.fin[j, h] = ref[...] + (self.near2[j, 0, h] + self.near2[j, 1, h])
        if stage == 5:
            put(j, self.fin[j, 0] + self.last[j])
        else:
            start_all(self.copies(j, z_first, stage))

    def sent(self, j, z_first):
        for stage in range(5):
            for copy in self.copies(j, z_first, stage):
                copy.wait_send()


def reduction_scratch(jobs, width):
    dma = pltpu.SemaphoreType.DMA
    return [
        pltpu.VMEM((jobs, 2, 4, 4, 48, width), F32),
        pltpu.VMEM((jobs, 2, 4, 48, width), F32),
        pltpu.VMEM((jobs, 2, 2, 4, 48, width), F32),
        pltpu.VMEM((jobs, 2, 48, width), F32),
        pltpu.VMEM((jobs, 2, 2, 48, width), F32),
        pltpu.VMEM((jobs, 48, width), F32),
        pltpu.VMEM((jobs, 2, 48, width), F32),
        dma((jobs, 5, 2)),
        dma((jobs, 5, 2)),
    ]


class Sums:
    def __init__(self, va, v1, v2, vec, send, recv):
        self.va, self.v1, self.v2, self.vec, self.send, self.recv = va, v1, v2, vec, send, recv
        _, _, p, y, z = place()
        self.partner = {"tensor": 1 - p}
        self.peers = [on_dp(y, (z + d) % 4) for d in range(1, 4)], \
            [on_dp((y + d) % 4, z) for d in range(1, 4)]

    def copies(self, stage):
        if stage == 2:
            return [remote(self.vec.at[0], self.vec.at[1], self.send.at[6], self.recv.at[6],
                           self.partner)]
        held = self.v1 if stage == 0 else self.v2
        return [
            remote(self.va.at[stage], held.at[d], self.send.at[3 * stage + d],
                   self.recv.at[3 * stage + d], self.peers[stage][d])
            for d in range(3)
        ]

    def step(self, stage):
        if stage > 0:
            for copy in self.copies(stage - 1):
                copy.wait()
        if stage == 1:
            self.va[1] = self.va[0] + (self.v1[0] + self.v1[1] + self.v1[2])
        if stage == 2:
            self.vec[0] = self.va[1] + (self.v2[0] + self.v2[1] + self.v2[2])
        if stage < 3:
            start_all(self.copies(stage))


def sums_scratch():
    dma = pltpu.SemaphoreType.DMA
    return [pltpu.VMEM((2, 8, D), F32), pltpu.VMEM((3, 8, D), F32), pltpu.VMEM((3, 8, D), F32),
            dma((7,)), dma((7,))]


def greet_all():
    _, _, p, y, z = place()
    peers = [{"tensor": 1 - p}]
    peers += [on_dp(y, (z + d) % 4) for d in range(1, 4)]
    peers += [on_dp((y + d) % 4, z) for d in range(1, 4)]
    for peer in peers:
        pl.semaphore_signal(
            pltpu.get_barrier_semaphore(), inc=1, device_id=peer, device_id_type=MESH)


def met():
    pl.semaphore_wait(pltpu.get_barrier_semaphore(), 7)


def job_terms(acc, j, left_t, x_of):
    width = acc.shape[5]

    def step(i, carry):
        half, y = i // 4, i % 4
        rows = pl.ds(pl.multiple_of(y * 192, 192), 192)
        acc[j, half, y] = dot(left_t[rows, :], x_of(half)[...]).reshape(4, 48, width)
        return carry

    lax.fori_loop(0, 8, step, 0)


def attn_finish_body(q0, k0, v0, gm0, lse0, o0, gb0, n0, gq2, gk2, gv2, o2, gb2, n2, g_in, h, w, v2,
                     g2, gain,
                     g_theirs, g_own, out, vec,
                     *scratch):
    red = Reduction(*scratch[:7], scratch[7:9])
    sums = Sums(*scratch[9:12], vec, *scratch[12:14])
    (x_v, o_v, low_v, left_t, gin_v, h_v, gout, w_v, q_v, k_v, v_v, gm_v, lse_v, gq_v, gk_v, gv_v,
     xl, ol, ld, st, send, recv) = scratch[14:]
    s, _, p, _, _ = place()
    partner = {"tensor": 1 - p}
    vec_ref = sums.va.at[0]

    def put(j, result):
        if j == 0:
            out[:, 1152:1536] = result
        else:
            for t in range(3):
                at = t * 384 + (j - 1) * 128
                out[:, at : at + 128] = result[:, t * 128 : t * 128 + 128]

    def low_loads(normed, gb):
        return [local(normed, low_v.at[0], ld.at[0]), local(gb, low_v.at[1], ld.at[1])]

    def lanes(n):
        return pl.ds(pl.multiple_of(n * 128, 128), 128)

    def each_pair(act):
        def step(pair, carry):
            act(pair)
            return carry

        lax.fori_loop(0, PAIRS, step, 0)

    def o_load(o, pair):
        return local(o.at[pair], o_v.at[pair // 3, :, lanes(pair % 3)], ol.at[pair])

    def attention_loads():
        return [local(a, b, ld.at[6 + n]) for n, (a, b) in enumerate(
            ((q0, q_v), (k0, k_v), (v0, v_v), (gm0, gm_v), (lse0, lse_v)))]

    def grad_loads(pair):
        return [local(ref.at[pair], x_v.at[pair % 3, pair // 3, :, pl.ds(t * 128, 128)],
                      xl.at[t, pair])
                for t, ref in enumerate((gq2, gk2, gv2))]

    def more_loads():
        return [local(g_in, gin_v, ld.at[2]), local(h, h_v, ld.at[3]), local(w, w_v, ld.at[4])]

    def early_sums():
        return local(v2, vec_ref, ld.at[5])

    @pl.when(s == 0)
    def _():
        each_pair(lambda pair: o_load(o0, pair).start())
        start_all(low_loads(n0, gb0) + attention_loads() + more_loads())

    @pl.when(s == 2)
    def _():
        start_all(low_loads(n2, gb2))
        each_pair(lambda pair: start_all([o_load(o2, pair)] + grad_loads(pair)))
        early_sums().start()

    def swap(i):
        r = block(i)
        return remote(gout.at[r], g_theirs.at[r], send.at[i], recv.at[i], partner)

    swap2 = remote(g2, g_theirs, send.at[0], recv.at[0], partner)

    def keep(i):
        r = block(i)
        return local(gout.at[r], g_own.at[r], st.at[i])

    def rows():
        def step(i, carry):
            r = block(i)
            pl.when(i == 2)(lambda: take((3, 1), (2, 2), (1, 3), (0, 4)))
            parts = [(pairs_of((gq_v, gk_v), half, r), pairs_of((gv_v,), half, r))
                     for half in range(2)]
            gout[r, :] = qkv_back_rows(gin_v[r, :], h_v[r, :], gain[...], parts, w_v, vec_ref)
            swap(i).start()
            keep(i).start()
            return carry

        lax.fori_loop(0, BLOCKS, step, 0)

    def take(*steps):
        for j, stage in steps:
            red.step(j, j % 2 == 0, stage, put)

    @pl.when(s % 2 == 0)
    def _():
        greet_all()
        for n, load in enumerate(low_loads(n0, gb0)):
            load.wait()
            left_t[n] = low_v[n].T
        each_pair(lambda pair: o_load(o0, pair).wait())
        met()

        @pl.when(s == 0)
        def _():
            sums.va[0] = jnp.zeros((8, D), F32)
            wait_all(attention_loads())

        @pl.when(s == 2)
        def _():
            swap2.start()
            early_sums().wait()
            each_pair(lambda pair: wait_all(grad_loads(pair)))

        job_terms(red.acc, 0, left_t.at[1], lambda half: o_v.at[half])
        take((0, 0))

        def pair_step(i, carry):
            @pl.when(s == 0)
            def _():
                def one(half, carry):
                    pair = half * 3 + i
                    attend_back_pair(q_v, k_v, v_v, gm_v, lse_v, gq_v, gk_v, gv_v, pair)
                    for t, ref in enumerate((gq_v, gk_v, gv_v)):
                        x_v[i, half, :, t * 128 : t * 128 + 128] = ref[pair]
                    return carry

                lax.fori_loop(0, 2, one, 0)

            job_terms(red.acc, 1 + i, left_t.at[0], lambda half: x_v.at[i, half])
            pl.when(i == 0)(lambda: take((1, 0), (0, 1)))
            pl.when(i == 1)(lambda: take((2, 0), (1, 1), (0, 2)))
            pl.when(i == 2)(lambda: take((3, 0), (2, 1), (1, 2), (0, 3)))
            return carry

        lax.fori_loop(0, 3, pair_step, 0)

        @pl.when(s == 0)
        def _():
            wait_all(more_loads())
            rows()

        pl.when(s == 2)(lambda: take((3, 1), (2, 2), (1, 3), (0, 4)))

        sums.step(0)
        take((3, 2), (2, 3), (1, 4), (0, 5))
        sums.step(1)
        take((3, 3), (2, 4), (1, 5))
        sums.step(2)
        take((3, 4), (2, 5))
        take((3, 5))
        sums.step(3)
        for j in range(4):
            red.sent(j, j % 2 == 0)

        pl.when(s == 2)(swap2.wait)

        @pl.when(s == 0)
        def _():
            for i in range(BLOCKS):
                swap(i).wait()
                keep(i).wait()


def attn_finish(first, last, rest, gain):
    dma = pltpu.SemaphoreType.DMA
    any_spec = pl.BlockSpec(memory_space=ANY)
    vmem = pl.BlockSpec(memory_space=pltpu.VMEM)
    paired = pltpu.VMEM(PAIRED, BF16)
    return call(
        attn_finish_body,
        (shape(WIDE, F32), shape(WIDE, F32), shape((48, 1536), F32), shape((2, 8, D), F32)),
        [any_spec] * 19 + [vmem],
        (any_spec, any_spec, vmem, vmem),
        scratch=reduction_scratch(4, 384) + sums_scratch() + [
            pltpu.VMEM((3, 2, ROWS, 384), BF16), pltpu.VMEM((2, ROWS, 384), BF16),
            pltpu.VMEM((2,) + WIDE, BF16), pltpu.VMEM((2, D, ROWS), BF16), pltpu.VMEM(WIDE, F32),
            pltpu.VMEM(WIDE, F32), pltpu.VMEM(WIDE, F32), pltpu.VMEM((D, 2304), BF16),
            paired, paired, paired, paired, pltpu.VMEM((PAIRS, 8, ROWS), F32),
            paired, paired, paired,
            dma((3, PAIRS)), dma((PAIRS,)), dma((11,)), dma((BLOCKS,)), dma((BLOCKS,)),
            dma((BLOCKS,)),
        ],
        collective_id=20,
        has_side_effects=True,
    )(*first, *last, *rest, gain)


def ff_finish_body(gr1, act1, gb1, n1, gr3, act3, gb3, n3, g1, g3, v1, v3,
                   g_theirs, g3_theirs, out, vec,
                   *scratch):
    red = Reduction(*scratch[:7], scratch[7:9])
    sums = Sums(*scratch[9:12], vec, *scratch[12:14])
    x_v, low_v, left_t, ld, xs, xr, vl = scratch[14:]
    s, _, p, _, _ = place()
    partner = {"tensor": 1 - p}
    jobs = ((True, 0), (False, 2 * CHUNK), (True, CHUNK), (False, 3 * CHUNK))

    def put(j, result):
        out[:, jobs[j][1] : jobs[j][1] + CHUNK] = result

    def load(t, gr, act):
        z_first, column = jobs[t]
        x = gr if z_first else act
        at = column % (2 * CHUNK)
        return [
            local(x.at[:, half * 2 * CHUNK + at : half * 2 * CHUNK + at + CHUNK],
                  x_v.at[t % 2, half], ld.at[t % 2, half])
            for half in range(2)
        ]

    def start_load(t):
        pl.when(s == 1)(lambda: start_all(load(t, gr1, act1)))
        pl.when(s == 3)(lambda: start_all(load(t, gr3, act3)))

    def small(normed, gb, vecs):
        return [local(normed, low_v.at[0], vl.at[0]), local(gb, low_v.at[1], vl.at[1]),
                local(vecs, sums.va.at[0], vl.at[2])]

    swap = remote(g1.at[pl.ds(ROWS - BLOCK, BLOCK)], g_theirs, xs, xr, partner)
    swap3 = remote(g3, g3_theirs, xs, xr, partner)

    @pl.when(s % 2 == 1)
    def _():
        pl.when(s == 1)(lambda: start_all(small(n1, gb1, v1)))
        pl.when(s == 3)(lambda: start_all(small(n3, gb3, v3)))
        greet_all()
        start_load(0)
        start_load(1)
        smalls = small(n1, gb1, v1)
        for n in range(2):
            smalls[n].wait()
            left_t[n] = low_v[n].T
        met()
        pl.when(s == 1)(swap.start)
        pl.when(s == 3)(swap3.start)
        smalls[2].wait()
        def take(t):
            for stage in range(6):
                if 0 <= t - stage < 4:
                    red.step(t - stage, jobs[t - stage][0], stage, put)

        def compute(t, carry):
            slot = t % 2
            for half in range(2):
                local(gr1.at[:, 0:CHUNK], x_v.at[slot, half], ld.at[slot, half]).wait()
            job_terms(red.acc, t, left_t.at[slot], lambda half: x_v.at[slot, half])
            for n in range(4):
                @pl.when(t == n)
                def _(n=n):
                    if n < 2:
                        start_load(n + 2)
                    if n < 3:
                        sums.step(n)
                    take(n)
            return carry

        lax.fori_loop(0, 4, compute, 0)
        for t in range(4, 9):
            take(t)
        sums.step(3)
        for j in range(4):
            red.sent(j, jobs[j][0])
        pl.when(s == 1)(swap.wait)
        pl.when(s == 3)(swap3.wait)


def ff_finish(first, last, rest):
    dma = pltpu.SemaphoreType.DMA
    any_spec = pl.BlockSpec(memory_space=ANY)
    vmem = pl.BlockSpec(memory_space=pltpu.VMEM)
    return call(
        ff_finish_body,
        (shape((BLOCK, D), F32), shape(WIDE, F32), shape((48, 4 * CHUNK), F32),
         shape((2, 8, D), F32)),
        [any_spec] * 12,
        (any_spec, any_spec, vmem, vmem),
        scratch=reduction_scratch(4, CHUNK) + sums_scratch() + [
            pltpu.VMEM((2, 2, ROWS, CHUNK), BF16), pltpu.VMEM((2,) + WIDE, BF16),
            pltpu.VMEM((2, D, ROWS), BF16),
            dma((2, 2)), dma, dma, dma((3,)),
        ],
        collective_id=21,
        has_side_effects=True,
    )(*first, *last, *rest)


def block_rows(i):
    return slice(i * BLOCK, min((i + 1) * BLOCK, LENGTH))


def load_block(mine, theirs, a_v, b_v, sems, i):
    r = pl.ds(i * BLOCK, BLOCK)
    return [local(mine.at[r], a_v.at[r], sems.at[0, i]),
            local(theirs.at[r], b_v.at[r], sems.at[1, i])]


def load_blocks(mine, theirs, a_v, b_v, sems, last=None):
    def step(i, carry):
        start_all(load_block(mine, theirs, a_v, b_v, sems, i))
        return carry

    lax.fori_loop(0, BLOCKS if last is None else BLOCKS - 1, step, 0)
    if last is not None:
        r = pl.ds(ROWS - BLOCK, BLOCK)
        local(mine.at[r], a_v.at[r], sems.at[0, BLOCKS - 1]).start()
        local(last, b_v.at[r], sems.at[1, BLOCKS - 1]).start()


def store_block(o_v, out, sems, i):
    r = block_rows(i) if isinstance(i, int) else block(i)
    return local(o_v.at[r], out.at[r], sems.at[2, i])


def write_block(a_v, b_v, o_v, sems, first, i):
    wait_all(load_block(a_v, b_v, a_v, b_v, sems, i))
    r = block_rows(i) if isinstance(i, int) else block(i)
    a, b = a_v[r, :], b_v[r, :]
    o_v[r, 0, :] = jnp.where(first, a, b)
    o_v[r, 1, :] = jnp.where(first, b, a)


def write_blocks(a_v, b_v, o_v, sems, first, out):
    def step(i, carry):
        write_block(a_v, b_v, o_v, sems, first, i)
        store_block(o_v, out, sems, i).start()
        return carry

    lax.fori_loop(0, BLOCKS - 1, step, 0)
    write_block(a_v, b_v, o_v, sems, first, BLOCKS - 1)
    store_block(o_v, out, sems, BLOCKS - 1).start()
    for i in range(BLOCKS):
        store_block(o_v, out, sems, i).wait()


def early_body(hf, h_theirs, out, a_v, b_v, o_v, sems):
    s, _, p, _, _ = place()

    @pl.when(s < 2)
    def _():
        load_blocks(hf, h_theirs, a_v, b_v, sems)
        write_blocks(a_v, b_v, o_v, sems, p == 0, out)


BOTH = (LENGTH, 2, D)


def early(hf, h_theirs):
    any_spec = pl.BlockSpec(memory_space=ANY)
    return call(
        early_body,
        shape(BOTH, F32),
        [any_spec] * 2,
        any_spec,
        scratch=[pltpu.VMEM(WIDE, F32), pltpu.VMEM(WIDE, F32), pltpu.VMEM(BOTH, F32),
                 pltpu.SemaphoreType.DMA((3, BLOCKS))],
    )(hf, h_theirs)


def small_outputs(attn_sums, ff_sums, attn_vec, ff_vec, rows3, qkv_g, qv_g, out_g, up_g, upb_g,
                  down_g):
    s, r, _, _, _ = place()
    at = lax.broadcasted_iota(jnp.int32, (D, 48), 0)
    pick = jnp.where(at == lax.broadcasted_iota(jnp.int32, (D, 48), 1) + r * 48, 1.0, 0.0)

    def picked(vec):
        rows3[...] = lax.dot_general(
            vec[0] + vec[1], pick, (((1,), (0,)), ((), ())), precision=lax.Precision.HIGHEST,
            preferred_element_type=F32)

    @pl.when(s % 2 == 0)
    def _():
        picked(attn_vec)
        for t in range(3):
            qkv_g[t] = attn_sums[:, t * 384 : t * 384 + 384]
        out_g[...] = attn_sums[:, 1152:1536]
        qv_g[...] = attn_vec[0, 3:5, 0:384] + attn_vec[1, 3:5, 384:768]
        for ref in (up_g, upb_g, down_g):
            ref[...] = jnp.zeros(ref.shape, F32)

    @pl.when(s % 2 == 1)
    def _():
        picked(ff_vec)
        up_g[...] = ff_sums[:, 0:1536]
        down_g[...] = ff_sums[:, 1536:3072]
        for n in range(2):
            upb_g[:, n * D : n * D + D] = ff_vec[0, 3 + n : 4 + n, :] + ff_vec[1, 5 + n : 6 + n, :]
        for ref in (qkv_g, out_g, qv_g):
            ref[...] = jnp.zeros(ref.shape, F32)


def assemble_body(hid_in, hm, h2, h3, g0, gb, gm, ga, gb_theirs, gf, g3, attn_sums, ff_sums, attn_vec,
                  ff_vec, hid, gin, rows3, qkv_g, qv_g, out_g, up_g, upb_g, down_g, a_v, b_v, o_v,
                  sems):
    s, _, p, _, _ = place()
    first = jnp.where(s < 2, p, 1 - p) == 0

    def load(n, mine, theirs, last=None):
        load_blocks(mine, theirs, a_v.at[n], b_v.at[n], sems.at[n], last)

    pl.when(s == 0)(lambda: load(0, g0, ga))
    pl.when(s == 1)(lambda: load(0, gb, gb_theirs, gf))

    @pl.when(s == 2)
    def _():
        load(0, gb, ga)
        load(1, hm, h2)

    @pl.when(s == 3)
    def _():
        load(0, gm, g3)
        load(1, hm, h3)

    small_outputs(attn_sums, ff_sums, attn_vec, ff_vec, rows3, qkv_g, qv_g, out_g, up_g, upb_g,
                  down_g)

    def write(n, carry):
        def step(i, carry):
            write_block(a_v.at[n], b_v.at[n], o_v.at[n], sems.at[n], first, i)
            pl.when(n == 0)(lambda: store_block(o_v.at[n], gin, sems.at[n], i).start())
            pl.when(n == 1)(lambda: store_block(o_v.at[n], hid, sems.at[n], i).start())
            return carry

        lax.fori_loop(0, BLOCKS - 1, step, 0)
        write_block(a_v.at[n], b_v.at[n], o_v.at[n], sems.at[n], first, BLOCKS - 1)
        pl.when(n == 0)(lambda: store_block(o_v.at[n], gin, sems.at[n], BLOCKS - 1).start())
        pl.when(n == 1)(lambda: store_block(o_v.at[n], hid, sems.at[n], BLOCKS - 1).start())
        return carry

    lax.fori_loop(0, jnp.where(s < 2, 1, 2), write, 0)
    for i in range(BLOCKS):
        store_block(o_v.at[0], gin, sems.at[0], i).wait()
        pl.when(s >= 2)(lambda i=i: store_block(o_v.at[1], hid, sems.at[1], i).wait())


def assemble(*operands):
    any_spec = pl.BlockSpec(memory_space=ANY)
    vmem = pl.BlockSpec(memory_space=pltpu.VMEM)
    return call(
        assemble_body,
        (shape(BOTH, F32), shape(BOTH, F32), shape((8, 48), F32), shape((3, 48, 384), F32),
         shape((2, 384), F32), shape((48, 384), F32), shape((48, 1536), F32),
         shape((1, 1536), F32), shape((48, 1536), F32)),
        [any_spec] * 11 + [vmem] * 4,
        (any_spec, any_spec) + (vmem,) * 7,
        scratch=[pltpu.VMEM((2,) + WIDE, F32), pltpu.VMEM((2,) + WIDE, F32),
                 pltpu.VMEM((2,) + BOTH, F32), pltpu.SemaphoreType.DMA((2, 3, BLOCKS))],
        aliases={0: 0},
    )(*operands)


def unwritten(shapes):
    any_spec = pl.BlockSpec(memory_space=ANY)
    return pl.pallas_call(
        lambda *refs: None,
        out_shape=tuple(shapes),
        out_specs=(any_spec,) * len(shapes),
    )()


def only_at(active, run, operands):
    like = jax.eval_shape(run, *operands)
    leaves, tree = jax.tree.flatten(like)

    def skip(*_):
        return jax.tree.unflatten(tree, unwritten([shape(x.shape, x.dtype) for x in leaves]))

    return lax.cond(active, run, skip, *operands)


def per_device(inputs, cotangent, norm_gain, norm_bias, qkv_weight, qv_bias, out_weight, end_bias,
               up_weight, up_bias, down_weight):
    s, r, p = lax.axis_index("section"), lax.axis_index("dp"), lax.axis_index("tensor")
    qkv, out_w, up, down = qkv_weight[0], out_weight[0], up_weight[0], down_weight[0]

    gain, shift, end = norm_gain, norm_bias, end_bias
    attn = s % 2 == 0
    by_row = [jnp.transpose(x, (1, 0, 2)) for x in (inputs, cotangent)]
    w, w_out, w_up, w_down, h0, normed0, q0, k0, v0, o0, lse0, qkvb, upb = opening(
        qkv, out_w, up, down, by_row[0], qv_bias[0], up_bias, gain, shift)
    cot = only_at(s == 3, lambda x: (extract(x),), (by_row[1],))[0]
    hf, h_in, act1, slope1, normed_f, q2, k2, v2, o2, lse2 = forward(
        o0, h0, w_out, w_up, w_down, w, gain, shift, end, upb, qkvb)
    h_early = exchange(hf)
    hid_early = early(hf, h_early)
    o2, hid_early = lax.optimization_barrier((o2, hid_early))
    hm, _, act3, gr3, gb_m, normed3, g2, gm2, g_m, vec_m, h3_theirs = middle(
        o2, h_in, w_out, w_up, w_down, cot, gain, shift, end, upb)
    g_b, g_in0, gr1, gb_b, gm0, vec_b, h2_theirs, gb_theirs, gq2, gk2, gv2 = backward(
        g2, h_in, q2, k2, v2, gm2, lse2, w, w_up, w_down, slope1, w_out, hm, gain)

    gb_m, vec_b = lax.optimization_barrier((gb_m, vec_b))
    g1_theirs, g3_theirs, ff_sums, ff_vec = ff_finish(
        (gr1, act1, gb_b, normed_f), (gr3, act3, gb_m, normed3), (g_b, g_m, vec_b, vec_m))
    g1_theirs, gb_last = lax.optimization_barrier((g1_theirs, gb_b))
    ga_theirs, g_0, attn_sums, attn_vec = attn_finish(
        (q0, k0, v0, gm0, lse0, o0, gb_last, normed0), (gq2, gk2, gv2, o2, gb_m, normed_f),
        (g_in0, h0, w, vec_b, g_b), gain)
    hid, gin, rows3, qkv_g, qv_g, out_g, up_g, upb_g, down_g = assemble(
        hid_early, hm, h2_theirs, h3_theirs, g_0, g_b, g_m, ga_theirs, gb_theirs, g1_theirs,
        g3_theirs, attn_sums, ff_sums, attn_vec, ff_vec)
    hid, gin = [jnp.transpose(x, (1, 0, 2))[None] for x in (hid, gin)]
    return (hid, gin, rows3[0:1], rows3[1:2], qkv_g[None], qv_g[None], out_g.T[None], rows3[2:3],
            up_g[None], upb_g, down_g.T[None])


def solution(mesh):
    return jax.shard_map(
        per_device,
        mesh=mesh,
        in_specs=(
            P("dp", None, None),
            P("dp", None, None),
            P("section", None),
            P("section", None),
            P("section", None, None, "tensor"),
            P("section", None, "tensor"),
            P("section", "tensor", None),
            P("section", None),
            P("section", None, "tensor"),
            P("section", "tensor"),
            P("section", "tensor", None),
        ),
        out_specs=(
            P("section", "dp", None, None),
            P("section", "dp", None, None),
            P("section", "dp"),
            P("section", "dp"),
            P("section", None, "dp", "tensor"),
            P("section", None, "tensor"),
            P("section", "tensor", "dp"),
            P("section", "dp"),
            P("section", "dp", "tensor"),
            P("section", "tensor"),
            P("section", "tensor", "dp"),
        ),
        check_vma=False,
    )
```

```python
import functools

import jax
import jax.numpy as jnp
from jax import lax
from jax.experimental import pallas as pl
from jax.experimental.pallas import tpu as pltpu
from jax.sharding import PartitionSpec as P

MESH = pl.DeviceIdType.MESH
ANY = pl.ANY
F32 = jnp.float32
BF16 = jnp.bfloat16

HEAD_DIM = 64
EPS = 1e-06
LENGTH = 866
ROWS = 896
BLOCK = 224
D = 768
PAIRS = 6
Q_BLOCKS = ((0, 384), (384, 512))
VMEM_BYTES = 60 * 1024 * 1024

CHUNK = 768


def call(body, out_shape, in_specs, out_specs, grid=(), scratch=(), aliases={}, **more):
    return pl.pallas_call(
        body,
        out_shape=out_shape,
        grid=grid,
        in_specs=in_specs,
        out_specs=out_specs,
        scratch_shapes=scratch,
        input_output_aliases=aliases,
        compiler_params=pltpu.CompilerParams(vmem_limit_bytes=VMEM_BYTES, **more),
    )


def shape(dims, dtype):
    return jax.ShapeDtypeStruct(dims, dtype)


def whole(*dims):
    return pl.BlockSpec(dims, lambda *_: (0,) * len(dims), pipeline_mode=pl.Buffered(1))


def rows_of(width):
    return pl.BlockSpec((BLOCK, width), lambda i: (i, 0))


def dot(a, b, ca=1, cb=0):
    return lax.dot_general(a, b, (((ca,), (cb,)), ((), ())), preferred_element_type=F32)


def normalized(h):
    average = jnp.mean(h, axis=-1, keepdims=True)
    centred = h - average
    spread = jnp.mean(centred * centred, axis=-1, keepdims=True)
    r = lax.rsqrt(spread + EPS)
    return centred * r, r


def norm_back(g, h, gain, grad_normed):
    xhat, r = normalized(h)
    t = grad_normed * gain
    t_mean = jnp.mean(t, axis=-1, keepdims=True)
    tx_mean = jnp.mean(t * xhat, axis=-1, keepdims=True)
    return g + r * (t - t_mean - xhat * tx_mean), xhat


def block(i):
    return pl.ds(pl.multiple_of(i * BLOCK, 32), BLOCK)


def gelu_and_slope(x):
    phi = 0.5 * (1.0 + lax.erf(x * 0.7071067811865476))
    density = jnp.exp(-0.5 * x * x) * 0.3989422804014327
    return (x * phi).astype(BF16), phi + x * density


def qkv_block(h, gain, shift, w_ref, bias, q_ref, k_ref, v_ref, normed_ref, r):
    xhat, _ = normalized(h)
    normed_ref[r, :] = (xhat * gain + shift).astype(BF16)

    def half_step(half, carry):
        cols = pl.ds(pl.multiple_of(half * 1152, 128), 1152)
        part = (dot(normed_ref[r, :], w_ref[:, cols]) + bias[:, cols]).astype(BF16)
        for n in range(9):
            lanes = part[:, n * 128 : n * 128 + 128]
            pair = half * 3 + n % 3
            if n < 3:
                q_ref[pair, r, :] = (lanes.astype(F32) * 0.125).astype(BF16)
            elif n < 6:
                k_ref[pair, r, :] = lanes
            else:
                v_ref[pair, r, :] = lanes
        return carry

    lax.fori_loop(0, 2, half_step, 0)


def joined(ref, r):
    return jnp.concatenate([ref[j, r, :] for j in range(PAIRS)], axis=1)


def mixed_back_block(g, w_out_ref, gm_ref, r):
    gb = g.astype(BF16)
    gm = dot(gb, w_out_ref[...], 1, 1).astype(BF16)
    for j in range(PAIRS):
        gm_ref[j, r, :] = gm[:, j * 128 : j * 128 + 128]
    return gb


def add_row(vec_ref, at, values):
    vec_ref[at : at + 1, :] += jnp.sum(values, axis=0, keepdims=True)


def qkv_back_rows(g, h, gain, parts, w_ref, vec_ref):
    grad_normed = jnp.zeros((BLOCK, D), F32)
    for half, (qk, v) in enumerate(parts):
        part = jnp.concatenate([qk, v], axis=1)
        grad_normed = grad_normed + dot(part, w_ref[:, half * 1152 : half * 1152 + 1152], 1, 1)
    out, xhat = norm_back(g, h, gain, grad_normed)
    add_row(vec_ref, 0, grad_normed * xhat)
    add_row(vec_ref, 1, grad_normed)
    add_row(vec_ref, 2, g.astype(BF16).astype(F32))
    add_row(vec_ref, 3, jnp.concatenate([qk[:, :384] for qk, _ in parts], axis=1).astype(F32))
    add_row(vec_ref, 4, jnp.concatenate([v for _, v in parts], axis=1).astype(F32))
    return out


def pairs_of(refs, half, r):
    return jnp.concatenate([ref[half * 3 + i, r, :] for ref in refs for i in range(3)], axis=1)


def head_mask(dims, axis, head):
    at = lax.broadcasted_iota(jnp.int32, dims, axis)
    return at < HEAD_DIM if head == 0 else at >= HEAD_DIM


def with_lanes(x, head, columns):
    lane = lax.broadcasted_iota(jnp.int32, x.shape, 1)
    own, spare = (lane < HEAD_DIM, HEAD_DIM) if head == 0 else (lane >= HEAD_DIM, 0)
    out = jnp.where(own, x, 0)
    for n, column in enumerate(columns):
        out = jnp.where(lane == spare + n, column, out)
    return out


def in_pieces(x):
    high = x.astype(BF16)
    rest = x - high.astype(F32)
    middle = rest.astype(BF16)
    return [high, middle, (rest - middle.astype(F32)).astype(BF16)]


def key_bias():
    row = lax.broadcasted_iota(jnp.int32, (ROWS, 1), 0)
    return jnp.where(row < LENGTH, 0.0, -1e30).astype(BF16)


def attend_pair(q_ref, k_ref, v_ref, o_ref, lse_ref, j):
    one = jnp.ones((1, 1), BF16)
    q, k, v_t = q_ref[j], k_ref[j], v_ref[j].T
    out = jnp.zeros((128, ROWS), F32)
    rows = []
    for head in range(2):
        s = dot(with_lanes(k, head, [key_bias()]), with_lanes(q, head, [one]), 1, 1)
        top = jnp.max(s, axis=0, keepdims=True)
        e = jnp.exp(s - top)
        total = jnp.sum(e, axis=0, keepdims=True)
        p = (e * (1.0 / total)).astype(BF16)
        out = out + dot(jnp.where(head_mask(v_t.shape, 0, head), v_t, 0), p)
        rows.append(top + jnp.log(total))
    o_ref[j] = out.T.astype(BF16)
    lse_ref[j] = jnp.concatenate(rows + [jnp.zeros((6, ROWS), F32)], axis=0)


def attend_back_pair(q_ref, k_ref, v_ref, gm_ref, lse_ref, gq_ref, gk_ref, gv_ref, j):
    one = jnp.ones((1, 1), BF16)
    k, v = k_ref[j], v_ref[j]
    k_t = k.T
    k_heads = [jnp.where(head_mask(k_t.shape, 0, head), k_t, 0) for head in range(2)]
    k_lanes = [with_lanes(k, head, [one, one, one, key_bias()]) for head in range(2)]
    lse_columns = lse_ref[j].T
    grad_k = jnp.zeros((ROWS, 128), F32)
    grad_v = jnp.zeros((ROWS, 128), F32)
    for start, size in Q_BLOCKS:
        rows = slice(start, start + size)
        q, gm, lse = q_ref[j, rows, :], gm_ref[j, rows, :], lse_columns[rows, :]
        grad_q = jnp.zeros((128, size), F32)
        for head in range(2):
            q_lanes = with_lanes(q, head, in_pieces(-lse[:, head : head + 1]) + [one])
            q_head, gm_head = with_lanes(q, head, []), with_lanes(gm, head, [])
            p = jnp.exp(dot(k_lanes[head], q_lanes, 1, 1))
            gp = dot(v, gm_head, 1, 1)
            weighted = p * gp
            gs = (weighted - p * jnp.sum(weighted, axis=0, keepdims=True)).astype(BF16)
            grad_v = grad_v + dot(p.astype(BF16), gm_head)
            grad_k = grad_k + dot(gs, q_head)
            grad_q = grad_q + dot(k_heads[head], gs)
        gq_ref[j, rows, :] = (grad_q.T * 0.125).astype(BF16)
    gk_ref[j] = grad_k.astype(BF16)
    gv_ref[j] = grad_v.astype(BF16)


def extract_body(x_ref, out_ref):
    s, p = lax.axis_index("section"), lax.axis_index("tensor")
    clip = jnp.where(s < 2, p, 1 - p)
    x = x_ref[...].astype(F32)
    x = jnp.where(clip == 0, x[:, 0, :], x[:, 1, :])
    at = lax.broadcasted_iota(jnp.int32, x.shape, 0) + pl.program_id(0) * BLOCK
    out_ref[...] = jnp.where(at < LENGTH, x, 0.0)


def extract(x):
    return call(
        extract_body,
        shape((ROWS, D), F32),
        [pl.BlockSpec((BLOCK, 2, D), lambda i: (i, 0, 0))],
        rows_of(D),
        grid=(ROWS // BLOCK,),
    )(x)


def place():
    s, r, p = lax.axis_index("section"), lax.axis_index("dp"), lax.axis_index("tensor")
    return s, r, p, r // 4, r % 4


def on_dp(y, z):
    return {"dp": y * 4 + z}


def greet(peers):
    barrier = pltpu.get_barrier_semaphore()
    for peer in peers:
        pl.semaphore_signal(barrier, inc=1, device_id=peer, device_id_type=MESH)
    pl.semaphore_wait(barrier, len(peers))


def remote(src, dst, send, recv, device):
    return pltpu.make_async_remote_copy(
        src_ref=src, dst_ref=dst, send_sem=send, recv_sem=recv, device_id=device,
        device_id_type=MESH,
    )


def local(src, dst, sem):
    return pltpu.make_async_copy(src, dst, sem)


def start_all(copies):
    for copy in copies:
        copy.start()


def wait_all(copies):
    for copy in copies:
        copy.wait()


BLOCKS = ROWS // BLOCK


class Piece:
    def __init__(self, n, source, view, halves, z_first, sems):
        self.n, self.source, self.view, self.halves, self.z_first = n, source, view, halves, z_first
        self.send, self.recv = sems
        _, _, p, self.y, self.z = place()
        self.partner = {"tensor": 1 - p}

    def copies(self, stage):
        y, z, view = self.y, self.z, self.view
        along_z = [on_dp(y, (z + d) % 4) for d in (1, 3)]
        along_y = [on_dp((y + d) % 4, z) for d in (1, 3)]

        def copy(n, src, dst, device):
            return remote(src, dst, self.send.at[self.n, stage, n], self.recv.at[self.n, stage, n],
                          device)

        def both(refs, peers):
            return [copy(n, refs[n], refs[n], peers[n]) for n in range(2)]

        everything = slice(0, 4)
        if self.z_first:
            ring, ring2 = along_z, along_y
            one = lambda d: view(y, (z + d) % 4)
            group = lambda d, part=everything: view((y + d) % 4, part)
        else:
            ring, ring2 = along_y, along_z
            one = lambda d: view((y + d) % 4, z)
            group = lambda d, part=everything: view(part, (z + d) % 4)
        if stage == 0:
            return [copy(0, self.source, view(y, z), self.partner)]
        if stage == 1:
            return both([one(0), one(0)], ring)
        if stage == 2:
            return both([self.halves(one(3))[0], self.halves(one(1))[1]], ring)
        if stage == 3:
            return both([group(0), group(0)], ring2)
        return both([group(3, slice(0, 2)), group(1, slice(2, 4))], ring2)


def advance(pieces, stage):
    for piece in pieces:
        if stage > 0:
            for copy in piece.copies(stage - 1):
                copy.wait_recv()
        if stage < 5:
            start_all(piece.copies(stage))


def all_sent(pieces):
    for piece in pieces:
        for stage in range(5):
            for copy in piece.copies(stage):
                copy.wait_send()


def opening_body(qkv, out_w, up, down, x, qvb, upb, gain, shift,
                 w, w_out, w_up, w_down, h0, normed, q, k, v, o, lse, qkvb, upb_all,
                 w_v, w_out_v, up_v, down_v, fq, fo, fu, fd, fx, lq, lo, lu, ldn, lx, qvb_o, upb_o,
                 x_v, h_v, normed_v, q_v, k_v, v_v, o_v, lse_v, ld, st, send, recv, bsend, brecv,
                 gate):
    s, r, p, y, z = place()
    partner = {"tensor": 1 - p}
    attn = s % 2 == 0
    peers = [partner] + [on_dp(y, (z + d) % 4) for d in (1, 3)] \
        + [on_dp((y + d) % 4, z) for d in (1, 3)]
    barrier = pltpu.get_barrier_semaphore()
    for peer in peers:
        pl.semaphore_signal(barrier, inc=1, device_id=peer, device_id_type=MESH)

    def rows_at(n):
        return pl.ds(pl.multiple_of(r * n, n), n)

    def qkv_half(half):
        cols = pl.ds(pl.multiple_of(half * 1152, 128), 1152)

        def step(i, carry):
            rows = block(i)

            @pl.when(half == 0)
            def _():
                x0 = x_v[rows].astype(F32)
                h = jnp.where(p == 0, x0[:, 0, :], x0[:, 1, :])
                at = lax.broadcasted_iota(jnp.int32, h.shape, 0) + i * BLOCK
                h = jnp.where(at < LENGTH, h, 0.0)
                h_v[rows, :] = h
                xhat, _ = normalized(h)
                normed_v[rows, :] = (xhat * gain[...] + shift[...]).astype(BF16)

            part = (dot(normed_v[rows, :], w_v[:, cols]) + qkvb[:, cols]).astype(BF16)
            for n in range(9):
                lanes = part[:, n * 128 : n * 128 + 128]
                pair = half * 3 + n % 3
                if n < 3:
                    q_v[pair, rows, :] = (lanes.astype(F32) * 0.125).astype(BF16)
                elif n < 6:
                    k_v[pair, rows, :] = lanes
                else:
                    v_v[pair, rows, :] = lanes
            return carry

        lax.fori_loop(0, BLOCKS, step, 0)

    @pl.when(attn)
    def _():
        loads = [local(qkv.at[t], w_v.at[:, pl.ds(t * 384, 384)], ld.at[t]) for t in range(3)]
        loads.append(local(out_w, w_out_v.at[pl.ds(0, 384)], ld.at[3]))
        clips = local(x, x_v.at[pl.ds(0, LENGTH)], ld.at[4])
        start_all(loads)
        pl.when(s == 0)(clips.start)
        sems = send, recv
        def rows24(ref):
            return ref.at[pl.ds(0, 24)], ref.at[pl.ds(24, 24)]

        left, right = pl.ds(0, 256), pl.ds(256, 128)
        pieces = [
            Piece(0, fq.at[0], lambda a, b: lq.at[0, a, b], rows24, True, sems),
            Piece(1, fq.at[1], lambda a, b: lq.at[1, a, b], rows24, False, sems),
            Piece(2, fq.at[2, :, left], lambda a, b: lq.at[2, a, b, ..., left], rows24, True, sems),
            Piece(3, fq.at[2, :, right], lambda a, b: lq.at[2, a, b, ..., right], rows24, False,
                  sems),
        ]
        direct = remote(fo, lo, bsend.at[1], brecv.at[1], partner)
        bias = remote(qvb, qvb_o, bsend.at[0], brecv.at[0], partner)
        qkvb[:, 0:384] = qvb[0:1, :]
        qkvb[:, 384:768] = jnp.zeros((1, 384), F32)
        qkvb[:, 768:1152] = qvb[1:2, :]
        wait_all(loads)
        for t in range(3):
            fq[t] = w_v[rows_at(48), t * 384 : t * 384 + 384].astype(F32)
        fo[...] = w_out_v[0:384, :].astype(F32)
        pl.semaphore_wait(barrier, 6)
        advance(pieces, 0)
        bias.start()
        direct.start()

        pl.when(s == 0)(clips.wait)
        stored = [local(w_v, w, st.at[0]), local(w_out_v, w_out, st.at[1])]

        def gathered():
            advance(pieces, 4)
            bias.wait()
            direct.wait()
            w_out_v[384:768, :] = lo[...].astype(BF16)
            advance(pieces, 5)
            for t in range(3):
                at = 1152 + t * 384

                def widen(i, carry, t=t, at=at):
                    w_v[pl.ds(pl.multiple_of(i * 192, 192), 192), at : at + 384] = \
                        lq[t, i].reshape(192, 384).astype(BF16)
                    return carry

                lax.fori_loop(0, 4, widen, 0)
            qkvb[:, 1152:1536] = qvb_o[0:1, :]
            qkvb[:, 1536:1920] = jnp.zeros((1, 384), F32)
            qkvb[:, 1920:2304] = qvb_o[1:2, :]
            start_all(stored)

        def pair_step(i, carry):
            pl.when((s == 0) & (i % 3 == 0))(lambda: qkv_half(i // 3))
            pl.when(i == 0)(lambda: advance(pieces, 1))
            pl.when(s == 0)(lambda: attend_pair(q_v, k_v, v_v, o_v, lse_v, i))
            pl.when(i == 0)(lambda: advance(pieces, 2))

            @pl.when(i == 1)
            def _():
                advance(pieces, 3)
                pl.semaphore_signal(gate, inc=1, device_id={"section": s + 1}, device_id_type=MESH)

            pl.when(i == 2)(gathered)
            return carry

        lax.fori_loop(0, PAIRS, pair_step, 0)

        @pl.when(s == 0)
        def _():
            kept = [local(a, b, st.at[2 + n]) for n, (a, b) in enumerate(
                ((h_v, h0), (normed_v, normed), (q_v, q), (k_v, k), (v_v, v), (o_v, o),
                 (lse_v, lse)))]
            start_all(kept)
            wait_all(kept)

        all_sent(pieces)
        wait_all(stored)

    @pl.when(jnp.logical_not(attn))
    def _():
        pl.semaphore_signal(barrier, inc=1, device_id={"section": s - 1}, device_id_type=MESH)
        loads = [local(up, up_v.at[:, pl.ds(0, 1536)], ld.at[0]),
                 local(down, down_v.at[pl.ds(0, 1536)], ld.at[1])]
        start_all(loads)
        sems = send, recv
        pieces = [
            Piece(0, fu, lambda a, b: lu.at[a, b],
                  lambda ref: (ref.at[pl.ds(0, 24)], ref.at[pl.ds(24, 24)]), True, sems),
            Piece(1, fd, lambda a, b: ldn.at[a, b],
                  lambda ref: (ref.at[pl.ds(0, 48)], ref.at[pl.ds(48, 48)]), False, sems),
        ]
        direct = remote(fx, lx, bsend.at[1], brecv.at[1], partner)
        early = [local(up_v.at[:, pl.ds(0, 1536)], w_up.at[:, pl.ds(0, 1536)], st.at[0]),
                 local(down_v.at[pl.ds(0, 1536)], w_down.at[pl.ds(0, 1536)], st.at[1])]
        late = [local(up_v.at[:, pl.ds(1536, 1536)], w_up.at[:, pl.ds(1536, 1536)], st.at[2]),
                local(down_v.at[pl.ds(1536, 1536)], w_down.at[pl.ds(1536, 1536)], st.at[3])]
        bias = remote(upb, upb_o, bsend.at[0], brecv.at[0], partner)
        upb_all[:, 0:1536] = upb[...]
        wait_all(loads)
        fu[...] = up_v[rows_at(48), 0:1536].astype(F32)
        start_all(early)
        fd[...] = down_v[rows_at(96), 0:512].astype(F32)
        pl.semaphore_wait(barrier, 5)
        advance(pieces, 0)
        bias.start()
        fx[...] = down_v[0:1536, 512:768].astype(F32)
        direct.start()
        pl.semaphore_wait(gate, 1)
        for stage in range(1, 5):
            advance(pieces, stage)
        bias.wait()
        upb_all[:, 1536:3072] = upb_o[...]

        def widen(d):
            i, g = (y + d) % 4, (z + d) % 4
            up_v[pl.ds(pl.multiple_of(i * 192, 192), 192), 1536:3072] = \
                lu[i].reshape(192, 1536).astype(BF16)
            for a in range(4):
                down_v[pl.ds(pl.multiple_of(1536 + (a * 4 + g) * 96, 96), 96), 0:512] = \
                    ldn[a, g].astype(BF16)

        for d in (0, 1, 3):
            widen(d)
        direct.wait()
        down_v[1536:3072, 512:768] = lx[...].astype(BF16)
        advance(pieces, 5)
        widen(2)
        start_all(late)
        all_sent(pieces)
        wait_all(early + late)


def opening(qkv, out_w, up, down, x, qvb, upb, gain, shift):
    dma = pltpu.SemaphoreType.DMA
    any_spec = pl.BlockSpec(memory_space=ANY)
    vmem = pl.BlockSpec(memory_space=pltpu.VMEM)
    paired, lse = (PAIRS, ROWS, 128), (PAIRS, 8, ROWS)
    return call(
        opening_body,
        (shape((D, 2304), BF16), shape((D, D), BF16), shape((D, 3072), BF16),
         shape((3072, D), BF16), shape((ROWS, D), F32), shape((ROWS, D), BF16),
         shape(paired, BF16), shape(paired, BF16), shape(paired, BF16), shape(paired, BF16),
         shape(lse, F32), shape((1, 2304), F32), shape((1, 3072), F32)),
        [any_spec] * 5 + [vmem] * 4,
        (any_spec,) * 11 + (vmem, vmem),
        scratch=[
            pltpu.VMEM((D, 2304), BF16), pltpu.VMEM((D, D), BF16), pltpu.VMEM((D, 3072), BF16),
            pltpu.VMEM((3072, D), BF16), pltpu.VMEM((3, 48, 384), F32), pltpu.VMEM((384, D), F32),
            pltpu.VMEM((48, 1536), F32), pltpu.VMEM((96, 512), F32), pltpu.VMEM((1536, 256), F32),
            pltpu.VMEM((3, 4, 4, 48, 384), F32), pltpu.VMEM((384, D), F32),
            pltpu.VMEM((4, 4, 48, 1536), F32), pltpu.VMEM((4, 4, 96, 512), F32),
            pltpu.VMEM((1536, 256), F32),
            pltpu.VMEM((2, 384), F32), pltpu.VMEM((1, 1536), F32),
            pltpu.VMEM((ROWS, 2, D), BF16), pltpu.VMEM((ROWS, D), F32),
            pltpu.VMEM((ROWS, D), BF16), pltpu.VMEM(paired, BF16), pltpu.VMEM(paired, BF16),
            pltpu.VMEM(paired, BF16), pltpu.VMEM(paired, BF16), pltpu.VMEM(lse, F32),
            dma((5,)), dma((9,)), dma((4, 5, 2)), dma((4, 5, 2)), dma((2,)), dma((2,)),
            pltpu.SemaphoreType.REGULAR,
        ],
        collective_id=1,
        has_side_effects=True,
    )(qkv, out_w, up, down, x, qvb, upb, gain, shift)


class Link:
    def __init__(self, src, dst, send, recv):
        self.src, self.dst, self.sems = src, dst, (send, recv)

    def copy(self, i, device):
        r = block(i)
        return remote(self.src.at[r], self.dst.at[r], self.sems[0].at[i], self.sems[1].at[i], device)

    def expect_from(self, device):
        pl.semaphore_signal(
            pltpu.get_barrier_semaphore(), inc=1, device_id=device, device_id_type=MESH)

    def ready(self):
        pl.semaphore_wait(pltpu.get_barrier_semaphore(), 1)

    def arrived(self, i, device):
        self.copy(i, device).wait_recv()

    def sent(self, device):
        for i in range(BLOCKS):
            self.copy(i, device).wait_send()

    def both_ways(self, device):
        for i in range(BLOCKS):
            self.copy(i, device).wait()


def stores(pairs, sems):
    def of(i):
        r = block(i)
        found = []
        for n, (src, dst) in enumerate(pairs):
            if len(src.shape) == 3:
                found.append(local(src.at[:, r], dst.at[:, r], sems.at[n, i]))
            else:
                found.append(local(src.at[r], dst.at[r], sems.at[n, i]))
        return found

    return of


def every_block(step):
    def body(i, carry):
        step(i, block(i))
        return carry

    lax.fori_loop(0, BLOCKS, body, 0)


def out_proj_rows(o_v, h_v, w_out_v, end, hout, r):
    hout[r, :] = h_v[r, :] + (dot(joined(o_v, r), w_out_v[...]) + end)


def forward_body(o, h0, w_out, up, down, w, gain, shift, end, upb, qkvb,
                 h_out, h_in, act, slope, normed, q, k, v, o2, lse2,
                 hin, hout, up_v, down_v, act_v, slope_v, normed_v, o_v, w_out_v, w_v, q_v, k_v,
                 v_v, lse_v, ld, st, send, recv, half_send, half_recv, lse_send, lse_recv):
    s, _, p, _, _ = place()
    link = Link(hout, hin, send, recv)
    share = slope_v.at[:, pl.ds(0, 9 * 128)]
    halves = Link(share, share, half_send, half_recv)

    def lse_copy(device):
        return remote(lse_v.at[3:6], lse_v.at[0:3], lse_send.at[0], lse_recv.at[0], device)

    @pl.when(s == 0)
    def _():
        target = {"section": 1}
        loads = [local(o, o_v, ld.at[0]), local(h0, hin, ld.at[1]), local(w_out, w_out_v, ld.at[2])]
        start_all(loads)
        link.ready()
        wait_all(loads)
        out = stores([(hout, h_out)], st)

        def step(i, r):
            out_proj_rows(o_v, hin, w_out_v, end[...], hout, r)
            link.copy(i, target).start()
            start_all(out(i))

        every_block(step)
        link.sent(target)
        for i in range(BLOCKS):
            wait_all(out(i))

    @pl.when(s == 1)
    def _():
        source, target = {"section": 0}, {"section": 2, "tensor": 1 - p}
        loads = [local(up, up_v, ld.at[0]), local(down, down_v, ld.at[1])]
        start_all(loads)
        link.expect_from(source)
        link.ready()
        wait_all(loads)
        out = stores([(hout, h_out), (hin, h_in), (act_v, act), (slope_v, slope),
                      (normed_v, normed)], st)

        def step(i, r):
            link.arrived(i, source)
            h = hin[r, :]
            xhat, _ = normalized(h)
            low = (xhat * gain[...] + shift[...]).astype(BF16)
            normed_v[r, :] = low
            hout[r, :] = h + end[...]

            def chunk(c, carry):
                cols = pl.ds(pl.multiple_of(c * 768, 768), 768)
                x = dot(low, up_v[:, cols]) + upb[:, cols]
                active, steep = gelu_and_slope(x)
                act_v[r, cols] = active
                slope_v[r, cols] = steep
                hout[r, :] += dot(active, down_v[cols, :])
                return carry

            lax.fori_loop(0, 4, chunk, 0)
            link.copy(i, target).start()
            start_all(out(i))

        every_block(step)
        link.sent(target)
        for i in range(BLOCKS):
            wait_all(out(i))

    @pl.when(s == 2)
    def _():
        source = {"section": 1, "tensor": 1 - p}
        load = local(w, w_v, ld.at[0])
        load.start()
        link.expect_from(source)
        halves.ready()
        load.wait()
        out = stores([(hin, h_in), (normed_v, normed), (q_v, q), (k_v, k), (v_v, v)], st)

        def step(i, r):
            link.arrived(i, source)
            qkv_block(hin[r, :], gain[...], shift[...], w_v, qkvb, q_v, k_v, v_v, normed_v, r)
            for t, ref in enumerate((q_v, k_v, v_v)):
                for j in range(3):
                    at = (t * 3 + j) * 128
                    slope_v[r, at : at + 128] = ref[3 + j, r, :].astype(F32)
            halves.copy(i, {"section": 3}).start()
            start_all(out(i))

        every_block(step)

        def attend_step(i, carry):
            attend_pair(q_v, k_v, v_v, o_v, lse_v, i)
            return carry

        lax.fori_loop(0, PAIRS, attend_step, 0)
        kept = [local(o_v, o2, ld.at[1]), local(lse_v, lse2, ld.at[2])]
        start_all(kept)
        lse_copy({"section": 3}).start()
        halves.sent({"section": 3})
        for i in range(BLOCKS):
            wait_all(out(i))
        wait_all(kept)
        lse_copy({"section": 3}).wait_send()

    @pl.when(s == 3)
    def _():
        source = {"section": 2}
        halves.expect_from(source)

        def step(i, r):
            halves.arrived(i, source)
            for t, ref in enumerate((q_v, k_v, v_v)):
                for j in range(3):
                    at = (t * 3 + j) * 128
                    ref[j, r, :] = slope_v[r, at : at + 128].astype(BF16)

        every_block(step)
        kept = [local(a.at[0:3], b.at[0:3], ld.at[n])
                for n, (a, b) in enumerate(((q_v, q), (k_v, k), (v_v, v), (lse_v, lse2)))]
        start_all(kept[:3])
        lse_copy(source).wait_recv()
        kept[3].start()
        wait_all(kept)


def staged(body, outs, operands, small, scratch, stored, collective_id):
    dma = pltpu.SemaphoreType.DMA
    any_spec = pl.BlockSpec(memory_space=ANY)
    vmem = pl.BlockSpec(memory_space=pltpu.VMEM)
    return call(
        body,
        tuple(shape(*o) for o in outs),
        [any_spec] * len(operands) + [vmem] * len(small),
        (any_spec,) * len(outs),
        scratch=[pltpu.VMEM(*x) for x in scratch]
        + [dma((8,)), dma((stored, BLOCKS))] + [dma((BLOCKS,))] * 4 + [dma((2 * BLOCKS,))] * 2,
        collective_id=collective_id,
        has_side_effects=True,
    )(*operands, *small)


WIDE = (ROWS, D)
HIDDEN = (ROWS, 3072)
PAIRED = (PAIRS, ROWS, 128)
LSE = (PAIRS, 8, ROWS)


def forward(o, h0, w_out, up, down, w, gain, shift, end, upb, qkvb):
    return staged(
        forward_body,
        [(WIDE, F32), (WIDE, F32), (HIDDEN, BF16), (HIDDEN, F32), (WIDE, BF16), (PAIRED, BF16),
         (PAIRED, BF16), (PAIRED, BF16), (PAIRED, BF16), (LSE, F32)],
        (o, h0, w_out, up, down, w),
        (gain, shift, end, upb, qkvb),
        [(WIDE, F32), (WIDE, F32), ((D, 3072), BF16), ((3072, D), BF16), (HIDDEN, BF16),
         (HIDDEN, F32), (WIDE, BF16), (PAIRED, BF16), ((D, D), BF16), ((D, 2304), BF16),
         (PAIRED, BF16), (PAIRED, BF16), (PAIRED, BF16), (LSE, F32)],
        5,
        2,
    )


def middle_body(o, h2, w_out, up, down, cot, gain, shift, end, upb,
                h_out, h_in, act, gr, gb, normed, g_in, gm, g_out, vec,
                hin, hout, gin, gout, act_v, gr_v, gb_v, normed_v, up_v, down_v, o_v, w_out_v, gm_v,
                vec_v, ups_v, gmx, ld, st, send, recv, back_send, back_recv, x_send, x_recv):
    s, _, p, _, _ = place()
    halves = Link(gmx, gmx, x_send, x_recv)
    link = Link(hout, hin, send, recv)
    back = Link(gout, gin, back_send, back_recv)

    @pl.when(s == 2)
    def _():
        other = {"section": 3}
        loads = [local(o, o_v, ld.at[0]), local(h2, hin, ld.at[1]), local(w_out, w_out_v, ld.at[2])]
        start_all(loads)
        back.expect_from(other)
        link.ready()
        wait_all(loads)
        out = stores([(hout, h_out)], st)
        back_out = stores([(hout, h_out), (gin, g_in), (gb_v, gb), (gm_v, gm)], st)

        def step(i, r):
            out_proj_rows(o_v, hin, w_out_v, end[...], hout, r)
            link.copy(i, other).start()
            start_all(out(i))

        every_block(step)

        def back_step(i, r):
            back.arrived(i, other)
            gb_v[r, :] = mixed_back_block(gin[r, :], w_out_v, gm_v, r)
            for j in range(3):
                gmx[r, j * 128 : j * 128 + 128] = gm_v[3 + j, r, :].astype(F32)
            halves.copy(i, other).start()
            start_all(back_out(i)[1:])

        every_block(back_step)
        link.sent(other)
        halves.sent(other)
        for i in range(BLOCKS):
            wait_all(back_out(i))

    @pl.when(s == 3)
    def _():
        other = {"section": 2}
        loads = [local(up, up_v, ld.at[0]), local(down, down_v, ld.at[1]),
                 local(cot, gin, ld.at[2])]
        start_all(loads)
        link.expect_from(other)
        back.ready()
        wait_all(loads)
        vec_v[...] = jnp.zeros_like(vec_v)
        ups_v[...] = jnp.zeros_like(ups_v)
        out = stores([(hout, h_out), (hin, h_in), (act_v, act), (gr_v, gr), (gb_v, gb),
                      (normed_v, normed), (gout, g_out)], st)

        def step(i, r):
            link.arrived(i, other)
            h, g = hin[r, :], gin[r, :]
            xhat, _ = normalized(h)
            low = (xhat * gain[...] + shift[...]).astype(BF16)
            normed_v[r, :] = low
            g_low = g.astype(BF16)
            gb_v[r, :] = g_low
            total = h + end[...]
            grad_normed = jnp.zeros((BLOCK, D), F32)
            for c in range(0, 3072, 768):
                cols = slice(c, c + 768)
                x = dot(low, up_v[:, cols]) + upb[:, cols]
                active, steep = gelu_and_slope(x)
                act_v[r, cols] = active
                total = total + dot(active, down_v[cols, :])
                raised = (dot(g_low, down_v[cols, :], 1, 1) * steep).astype(BF16)
                gr_v[r, cols] = raised
                ups_v[:, cols] += jnp.sum(raised.astype(F32), axis=0, keepdims=True)
                grad_normed = grad_normed + dot(raised, up_v[:, cols], 1, 1)
            hout[r, :] = total
            result, xhat = norm_back(g, h, gain[...], grad_normed)
            gout[r, :] = result
            back.copy(i, other).start()
            add_row(vec_v, 0, grad_normed * xhat)
            add_row(vec_v, 1, grad_normed)
            add_row(vec_v, 2, g_low.astype(F32))
            start_all(out(i))

        every_block(step)
        for c in range(4):
            vec_v[3 + c : 4 + c, :] = ups_v[:, c * D : c * D + D]
        last = local(vec_v, vec, ld.at[3])
        last.start()


        def half_step(i, r):
            halves.arrived(i, other)
            for j in range(3):
                gm_v[j, r, :] = gmx[r, j * 128 : j * 128 + 128].astype(BF16)

        every_block(half_step)
        shared = local(gm_v.at[0:3], gm.at[0:3], ld.at[4])
        shared.start()
        back.sent(other)
        shared.wait()
        for i in range(BLOCKS):
            wait_all(out(i))
        last.wait()


def middle(o, h2, w_out, up, down, cot, gain, shift, end, upb):
    return staged(
        middle_body,
        [(WIDE, F32), (WIDE, F32), (HIDDEN, BF16), (HIDDEN, BF16), (WIDE, BF16), (WIDE, BF16),
         (WIDE, F32), (PAIRED, BF16), (WIDE, F32), ((8, D), F32)],
        (o, h2, w_out, up, down, cot),
        (gain, shift, end, upb),
        [(WIDE, F32)] * 4
        + [(HIDDEN, BF16), (HIDDEN, BF16), (WIDE, BF16), (WIDE, BF16), ((D, 3072), BF16),
           ((3072, D), BF16), (PAIRED, BF16), ((D, D), BF16), (PAIRED, BF16), ((8, D), F32),
           ((1, 3072), F32), ((ROWS, 384), F32)],
        7,
        3,
    )


def backward_body(g2, h, q, k, v, gm2, lse, w, up, down, slope, w_out, h_made, gain,
                  g_out, g_in, gr, gb, gm, vec, h_theirs, g_theirs, gq, gk, gv,
                  gin, gout, h_v, slope_v, gr_v, gb_v, up_v, down_v, gq_v, gk_v, gv_v, w_v, w_out_v,
                  gm_v, vec_v, ups_v, q_v, k_v, v_v, lse_v, ld, st, send, recv, next_send, next_recv,
                  x_send, x_recv):
    s, _, p, _, _ = place()
    theirs = {"tensor": 1 - p}
    partner = Link(gout, g_theirs, x_send, x_recv)
    made = remote(h_made, h_theirs, x_send.at[BLOCKS], x_recv.at[BLOCKS], theirs)
    first = Link(gout, gin, send, recv)
    second = Link(gout, gin, next_send, next_recv)

    heads = [local(a, b, ld.at[n]) for n, (a, b) in enumerate(
        ((q, q_v), (k, k_v), (v, v_v), (gm2, gm_v), (lse, lse_v)))]

    def share(i, device):
        at = pl.ds(pl.multiple_of(i * 384, 384), 384)
        return remote(slope_v.at[:, at], slope_v.at[:, at], next_send.at[i], next_recv.at[i], device)

    @pl.when(s >= 2)
    def _():
        start_all(heads)

        @pl.when(s == 2)
        def _():
            start_all([local(g2, gin, ld.at[5]), local(h, h_v, ld.at[6]), local(w, w_v, ld.at[7])])
            for device in (theirs, {"section": 3}):
                pl.semaphore_signal(
                    pltpu.get_barrier_semaphore(), inc=1, device_id=device, device_id_type=MESH)
            pl.semaphore_wait(pltpu.get_barrier_semaphore(), 2)
            made.start()

        pl.when(s == 3)(second.ready)
        wait_all(heads)

        def attend_step(i, carry):
            attend_back_pair(q_v, k_v, v_v, gm_v, lse_v, gq_v, gk_v, gv_v, i)

            @pl.when(s == 3)
            def _():
                for t, ref in enumerate((gq_v, gk_v, gv_v)):
                    at = pl.ds(pl.multiple_of(i * 384 + t * 128, 128), 128)
                    slope_v[:, at] = ref[i].astype(F32)
                share(i, {"section": 2}).start()

            return carry

        lax.fori_loop(0, 3, attend_step, 0)

    @pl.when(s == 3)
    def _():
        for i in range(3):
            share(i, {"section": 2}).wait_send()

    @pl.when(s == 2)
    def _():
        target = {"section": 1, "tensor": 1 - p}
        loads = [local(g2, gin, ld.at[5]), local(h, h_v, ld.at[6]), local(w, w_v, ld.at[7])]

        def take_step(i, carry):
            share(i, {"section": 3}).wait_recv()
            for t, ref in enumerate((gq_v, gk_v, gv_v)):
                at = pl.ds(pl.multiple_of(i * 384 + t * 128, 128), 128)
                ref[3 + i] = slope_v[:, at].astype(BF16)
            return carry

        lax.fori_loop(0, 3, take_step, 0)
        kept = [local(a, b, ld.at[n]) for n, (a, b) in enumerate(
            ((gq_v, gq), (gk_v, gk), (gv_v, gv)))]
        start_all(kept)
        wait_all(loads)
        vec_v[...] = jnp.zeros_like(vec_v)
        out = stores([(gout, g_out)], st)

        def step(i, r):
            parts = [(pairs_of((gq_v, gk_v), half, r), pairs_of((gv_v,), half, r))
                     for half in range(2)]
            gout[r, :] = qkv_back_rows(gin[r, :], h_v[r, :], gain[...], parts, w_v, vec_v)
            first.copy(i, target).start()
            start_all(out(i))

        every_block(step)
        last = local(vec_v, vec, ld.at[6])
        last.start()
        first.sent(target)
        made.wait()
        wait_all(kept)
        for i in range(BLOCKS):
            wait_all(out(i))
        last.wait()

    @pl.when(s == 1)
    def _():
        source, target = {"section": 2, "tensor": 1 - p}, {"section": 0}
        loads = [local(a, b, ld.at[n]) for n, (a, b) in enumerate(
            ((up, up_v), (down, down_v), (slope, slope_v), (h, h_v)))]
        start_all(loads)
        first.expect_from(source)
        pl.semaphore_signal(
            pltpu.get_barrier_semaphore(), inc=1, device_id=theirs, device_id_type=MESH)
        pl.semaphore_wait(pltpu.get_barrier_semaphore(), 2)
        wait_all(loads)
        vec_v[...] = jnp.zeros_like(vec_v)
        ups_v[...] = jnp.zeros_like(ups_v)
        out = stores([(gout, g_out), (gr_v, gr), (gb_v, gb)], st)

        def step(i, r):
            first.arrived(i, source)
            g = gin[r, :]
            g_low = g.astype(BF16)
            gb_v[r, :] = g_low
            gout[r, :] = jnp.zeros((BLOCK, D), F32)

            def chunk(c, carry):
                cols = pl.ds(pl.multiple_of(c * 768, 768), 768)
                raised = (dot(g_low, down_v[cols, :], 1, 1) * slope_v[r, cols]).astype(BF16)
                gr_v[r, cols] = raised
                ups_v[:, cols] += jnp.sum(raised.astype(F32), axis=0, keepdims=True)
                gout[r, :] += dot(raised, up_v[:, cols], 1, 1)
                return carry

            lax.fori_loop(0, 4, chunk, 0)
            grad_normed = gout[r, :]
            result, xhat = norm_back(g, h_v[r, :], gain[...], grad_normed)
            gout[r, :] = result
            second.copy(i, target).start()
            pl.when(i < BLOCKS - 1)(lambda: partner.copy(i, theirs).start())
            add_row(vec_v, 0, grad_normed * xhat)
            add_row(vec_v, 1, grad_normed)
            add_row(vec_v, 2, g_low.astype(F32))
            start_all(out(i))

        every_block(step)
        for c in range(4):
            vec_v[3 + c : 4 + c, :] = ups_v[:, c * D : c * D + D]
        last = local(vec_v, vec, ld.at[6])
        last.start()
        second.sent(target)
        for i in range(BLOCKS - 1):
            partner.copy(i, theirs).wait()
        for i in range(BLOCKS):
            wait_all(out(i))
        last.wait()

    @pl.when(s == 0)
    def _():
        source = {"section": 1}
        load = local(w_out, w_out_v, ld.at[0])
        load.start()
        second.expect_from(source)
        load.wait()
        out = stores([(gin, g_in), (gb_v, gb), (gm_v, gm)], st)

        def step(i, r):
            second.arrived(i, source)
            gb_v[r, :] = mixed_back_block(gin[r, :], w_out_v, gm_v, r)
            start_all(out(i))

        every_block(step)
        for i in range(BLOCKS):
            wait_all(out(i))


def backward(g2, h, q, k, v, gm, lse, w, up, down, slope, w_out, h_made, gain):
    return staged(
        backward_body,
        [(WIDE, F32), (WIDE, F32), (HIDDEN, BF16), (WIDE, BF16), (PAIRED, BF16), ((8, D), F32),
         (WIDE, F32), (WIDE, F32), (PAIRED, BF16), (PAIRED, BF16), (PAIRED, BF16)],
        (g2, h, q, k, v, gm, lse, w, up, down, slope, w_out, h_made),
        (gain,),
        [(WIDE, F32)] * 3
        + [(HIDDEN, F32), (HIDDEN, BF16), (WIDE, BF16), ((D, 3072), BF16), ((3072, D), BF16),
           (PAIRED, BF16), (PAIRED, BF16), (PAIRED, BF16), ((D, 2304), BF16), ((D, D), BF16),
           (PAIRED, BF16), ((8, D), F32), ((1, 3072), F32), (PAIRED, BF16), (PAIRED, BF16),
           (PAIRED, BF16), (LSE, F32)],
        3,
        4,
    )


def exchange_body(h, theirs, send, recv):
    s, _, p, _, _ = place()

    @pl.when(s < 2)
    def _():
        partner = {"tensor": 1 - p}
        greet([partner])
        copy = remote(h, theirs, send, recv, partner)
        copy.start()
        copy.wait()


def exchange(h):
    dma = pltpu.SemaphoreType.DMA
    any_spec = pl.BlockSpec(memory_space=ANY)
    return call(
        exchange_body, shape(WIDE, F32), [any_spec], any_spec,
        scratch=[dma, dma], collective_id=5, has_side_effects=True,
    )(h)


class Reduction:
    def __init__(self, acc, far, near, far2, near2, last, fin, sems):
        self.acc, self.far, self.near, self.far2, self.near2 = acc, far, near, far2, near2
        self.last, self.fin = last, fin
        self.send, self.recv = sems
        _, _, p, self.y, self.z = place()
        self.partner = {"tensor": 1 - p}

    def at(self, j, z_first):
        y, z = self.y, self.z
        along_z = [on_dp(y, (z + d) % 4) for d in (1, 3)]
        along_y = [on_dp((y + d) % 4, z) for d in (1, 3)]
        if z_first:
            return z, y, along_z, along_y, lambda h, i: self.acc.at[j, h, :, i], \
                lambda h, i: self.acc.at[j, h, i, z]
        return y, z, along_y, along_z, lambda h, i: self.acc.at[j, h, i], \
            lambda h, i: self.acc.at[j, h, y, i]

    def copies(self, j, z_first, stage):
        here, there, ring, ring2, part, part2 = self.at(j, z_first)
        both = slice(0, 2)

        def pair(sources, target, peers):
            return [
                remote(sources[n], target.at[j, n], self.send.at[j, stage, n],
                       self.recv.at[j, stage, n], peers[n])
                for n in range(2)
            ]

        if stage == 0:
            return pair([part(0, (here + 2) % 4), part(1, (here + 2) % 4)], self.far, ring)
        if stage == 1:
            return pair([part(both, (here + 1) % 4), part(both, (here + 3) % 4)], self.near, ring)
        if stage == 2:
            return pair([part2(0, (there + 2) % 4), part2(1, (there + 2) % 4)], self.far2, ring2)
        if stage == 3:
            return pair([part2(both, (there + 1) % 4), part2(both, (there + 3) % 4)], self.near2,
                        ring2)
        return [remote(self.fin.at[j, 1], self.last.at[j], self.send.at[j, 4, 0],
                       self.recv.at[j, 4, 0], self.partner)]

    def step(self, j, z_first, stage, put):
        here, there, _, _, part, part2 = self.at(j, z_first)
        if stage > 0:
            for copy in self.copies(j, z_first, stage - 1):
                copy.wait_recv()
        if stage == 1:
            def add_far(i, carry):
                for n, d in ((0, 1), (1, 3)):
                    ref = part(n, (here + d) % 4)
                    ref[i] = ref[i] + self.far[j, n, i]
                return carry

            lax.fori_loop(0, 4, add_far, 0)
        if stage == 2:
            def add_near(i, carry):
                for h in range(2):
                    ref = part(h, here)
                    ref[i] = ref[i] + (self.near[j, 0, h, i] + self.near[j, 1, h, i])
                return carry

            lax.fori_loop(0, 4, add_near, 0)
        if stage == 3:
            for n, d in ((0, 1), (1, 3)):
                ref = part2(n, (there + d) % 4)
                ref[...] = ref[...] + self.far2[j, n]
        if stage == 4:
            for h in range(2):
                ref = part2(h, there)
                self.fin[j, h] = ref[...] + (self.near2[j, 0, h] + self.near2[j, 1, h])
        if stage == 5:
            put(j, self.fin[j, 0] + self.last[j])
        else:
            start_all(self.copies(j, z_first, stage))

    def sent(self, j, z_first):
        for stage in range(5):
            for copy in self.copies(j, z_first, stage):
                copy.wait_send()


def reduction_scratch(jobs, width):
    dma = pltpu.SemaphoreType.DMA
    return [
        pltpu.VMEM((jobs, 2, 4, 4, 48, width), F32),
        pltpu.VMEM((jobs, 2, 4, 48, width), F32),
        pltpu.VMEM((jobs, 2, 2, 4, 48, width), F32),
        pltpu.VMEM((jobs, 2, 48, width), F32),
        pltpu.VMEM((jobs, 2, 2, 48, width), F32),
        pltpu.VMEM((jobs, 48, width), F32),
        pltpu.VMEM((jobs, 2, 48, width), F32),
        dma((jobs, 5, 2)),
        dma((jobs, 5, 2)),
    ]


class Sums:
    def __init__(self, va, v1, v2, vec, send, recv):
        self.va, self.v1, self.v2, self.vec, self.send, self.recv = va, v1, v2, vec, send, recv
        _, _, p, y, z = place()
        self.partner = {"tensor": 1 - p}
        self.peers = [on_dp(y, (z + d) % 4) for d in range(1, 4)], \
            [on_dp((y + d) % 4, z) for d in range(1, 4)]

    def copies(self, stage):
        if stage == 2:
            return [remote(self.vec.at[0], self.vec.at[1], self.send.at[6], self.recv.at[6],
                           self.partner)]
        held = self.v1 if stage == 0 else self.v2
        return [
            remote(self.va.at[stage], held.at[d], self.send.at[3 * stage + d],
                   self.recv.at[3 * stage + d], self.peers[stage][d])
            for d in range(3)
        ]

    def step(self, stage):
        if stage > 0:
            for copy in self.copies(stage - 1):
                copy.wait()
        if stage == 1:
            self.va[1] = self.va[0] + (self.v1[0] + self.v1[1] + self.v1[2])
        if stage == 2:
            self.vec[0] = self.va[1] + (self.v2[0] + self.v2[1] + self.v2[2])
        if stage < 3:
            start_all(self.copies(stage))


def sums_scratch():
    dma = pltpu.SemaphoreType.DMA
    return [pltpu.VMEM((2, 8, D), F32), pltpu.VMEM((3, 8, D), F32), pltpu.VMEM((3, 8, D), F32),
            dma((7,)), dma((7,))]


def greet_all():
    _, _, p, y, z = place()
    peers = [{"tensor": 1 - p}]
    peers += [on_dp(y, (z + d) % 4) for d in range(1, 4)]
    peers += [on_dp((y + d) % 4, z) for d in range(1, 4)]
    for peer in peers:
        pl.semaphore_signal(
            pltpu.get_barrier_semaphore(), inc=1, device_id=peer, device_id_type=MESH)


def met():
    pl.semaphore_wait(pltpu.get_barrier_semaphore(), 7)


def job_terms(acc, j, left_t, x_of):
    width = acc.shape[5]

    def step(i, carry):
        half, y = i // 4, i % 4
        rows = pl.ds(pl.multiple_of(y * 192, 192), 192)
        acc[j, half, y] = dot(left_t[rows, :], x_of(half)[...]).reshape(4, 48, width)
        return carry

    lax.fori_loop(0, 8, step, 0)


def attn_finish_body(q0, k0, v0, gm0, lse0, o0, gb0, n0, gq2, gk2, gv2, o2, gb2, n2, g_in, h, w, v2,
                     g2, gain,
                     g_theirs, g_own, out, vec,
                     *scratch):
    red = Reduction(*scratch[:7], scratch[7:9])
    sums = Sums(*scratch[9:12], vec, *scratch[12:14])
    (x_v, o_v, low_v, left_t, gin_v, h_v, gout, w_v, q_v, k_v, v_v, gm_v, lse_v, gq_v, gk_v, gv_v,
     xl, ol, ld, st, send, recv) = scratch[14:]
    s, _, p, _, _ = place()
    partner = {"tensor": 1 - p}
    vec_ref = sums.va.at[0]

    def put(j, result):
        if j == 0:
            out[:, 1152:1536] = result
        else:
            for t in range(3):
                at = t * 384 + (j - 1) * 128
                out[:, at : at + 128] = result[:, t * 128 : t * 128 + 128]

    def low_loads(normed, gb):
        return [local(normed, low_v.at[0], ld.at[0]), local(gb, low_v.at[1], ld.at[1])]

    def lanes(n):
        return pl.ds(pl.multiple_of(n * 128, 128), 128)

    def each_pair(act):
        def step(pair, carry):
            act(pair)
            return carry

        lax.fori_loop(0, PAIRS, step, 0)

    def o_load(o, pair):
        return local(o.at[pair], o_v.at[pair // 3, :, lanes(pair % 3)], ol.at[pair])

    def attention_loads():
        return [local(a, b, ld.at[6 + n]) for n, (a, b) in enumerate(
            ((q0, q_v), (k0, k_v), (v0, v_v), (gm0, gm_v), (lse0, lse_v)))]

    def grad_loads(pair):
        return [local(ref.at[pair], x_v.at[pair % 3, pair // 3, :, pl.ds(t * 128, 128)],
                      xl.at[t, pair])
                for t, ref in enumerate((gq2, gk2, gv2))]

    def more_loads():
        return [local(g_in, gin_v, ld.at[2]), local(h, h_v, ld.at[3]), local(w, w_v, ld.at[4])]

    def early_sums():
        return local(v2, vec_ref, ld.at[5])

    @pl.when(s == 0)
    def _():
        each_pair(lambda pair: o_load(o0, pair).start())
        start_all(low_loads(n0, gb0) + attention_loads() + more_loads())

    @pl.when(s == 2)
    def _():
        start_all(low_loads(n2, gb2))
        each_pair(lambda pair: start_all([o_load(o2, pair)] + grad_loads(pair)))
        early_sums().start()

    def swap(i):
        r = block(i)
        return remote(gout.at[r], g_theirs.at[r], send.at[i], recv.at[i], partner)

    swap2 = remote(g2, g_theirs, send.at[0], recv.at[0], partner)

    def keep(i):
        r = block(i)
        return local(gout.at[r], g_own.at[r], st.at[i])

    def rows():
        def step(i, carry):
            r = block(i)
            parts = [(pairs_of((gq_v, gk_v), half, r), pairs_of((gv_v,), half, r))
                     for half in range(2)]
            gout[r, :] = qkv_back_rows(gin_v[r, :], h_v[r, :], gain[...], parts, w_v, vec_ref)
            swap(i).start()
            keep(i).start()
            return carry

        lax.fori_loop(0, BLOCKS, step, 0)

    def take(*steps):
        for j, stage in steps:
            red.step(j, j % 2 == 0, stage, put)

    @pl.when(s % 2 == 0)
    def _():
        greet_all()
        for n, load in enumerate(low_loads(n0, gb0)):
            load.wait()
            left_t[n] = low_v[n].T
        each_pair(lambda pair: o_load(o0, pair).wait())
        met()

        @pl.when(s == 0)
        def _():
            sums.va[0] = jnp.zeros((8, D), F32)
            wait_all(attention_loads())

        @pl.when(s == 2)
        def _():
            swap2.start()
            early_sums().wait()
            each_pair(lambda pair: wait_all(grad_loads(pair)))

        job_terms(red.acc, 0, left_t.at[1], lambda half: o_v.at[half])
        take((0, 0))

        def pair_step(i, carry):
            @pl.when(s == 0)
            def _():
                def one(half, carry):
                    pair = half * 3 + i
                    attend_back_pair(q_v, k_v, v_v, gm_v, lse_v, gq_v, gk_v, gv_v, pair)
                    for t, ref in enumerate((gq_v, gk_v, gv_v)):
                        x_v[i, half, :, t * 128 : t * 128 + 128] = ref[pair]
                    return carry

                lax.fori_loop(0, 2, one, 0)

            job_terms(red.acc, 1 + i, left_t.at[0], lambda half: x_v.at[i, half])
            pl.when(i == 0)(lambda: take((1, 0), (0, 1)))
            pl.when(i == 1)(lambda: take((2, 0), (1, 1), (0, 2)))
            pl.when(i == 2)(lambda: take((3, 0), (2, 1), (1, 2), (0, 3)))
            return carry

        lax.fori_loop(0, 3, pair_step, 0)
        take((3, 1), (2, 2), (1, 3), (0, 4))

        @pl.when(s == 0)
        def _():
            wait_all(more_loads())
            rows()

        sums.step(0)
        take((3, 2), (2, 3), (1, 4), (0, 5))
        sums.step(1)
        take((3, 3), (2, 4), (1, 5))
        sums.step(2)
        take((3, 4), (2, 5))
        take((3, 5))
        sums.step(3)
        for j in range(4):
            red.sent(j, j % 2 == 0)

        pl.when(s == 2)(swap2.wait)

        @pl.when(s == 0)
        def _():
            for i in range(BLOCKS):
                swap(i).wait()
                keep(i).wait()


def attn_finish(first, last, rest, gain):
    dma = pltpu.SemaphoreType.DMA
    any_spec = pl.BlockSpec(memory_space=ANY)
    vmem = pl.BlockSpec(memory_space=pltpu.VMEM)
    paired = pltpu.VMEM(PAIRED, BF16)
    return call(
        attn_finish_body,
        (shape(WIDE, F32), shape(WIDE, F32), shape((48, 1536), F32), shape((2, 8, D), F32)),
        [any_spec] * 19 + [vmem],
        (any_spec, any_spec, vmem, vmem),
        scratch=reduction_scratch(4, 384) + sums_scratch() + [
            pltpu.VMEM((3, 2, ROWS, 384), BF16), pltpu.VMEM((2, ROWS, 384), BF16),
            pltpu.VMEM((2,) + WIDE, BF16), pltpu.VMEM((2, D, ROWS), BF16), pltpu.VMEM(WIDE, F32),
            pltpu.VMEM(WIDE, F32), pltpu.VMEM(WIDE, F32), pltpu.VMEM((D, 2304), BF16),
            paired, paired, paired, paired, pltpu.VMEM((PAIRS, 8, ROWS), F32),
            paired, paired, paired,
            dma((3, PAIRS)), dma((PAIRS,)), dma((11,)), dma((BLOCKS,)), dma((BLOCKS,)),
            dma((BLOCKS,)),
        ],
        collective_id=20,
        has_side_effects=True,
    )(*first, *last, *rest, gain)


def ff_finish_body(gr1, act1, gb1, n1, gr3, act3, gb3, n3, g1, g3, v1, v3, h3,
                   g_theirs, g3_theirs, h3_theirs, out, vec,
                   *scratch):
    red = Reduction(*scratch[:7], scratch[7:9])
    sums = Sums(*scratch[9:12], vec, *scratch[12:14])
    x_v, low_v, left_t, ld, xs, xr, vl, hs, hr = scratch[14:]
    s, _, p, _, _ = place()
    partner = {"tensor": 1 - p}
    jobs = ((True, 0), (False, 2 * CHUNK), (True, CHUNK), (False, 3 * CHUNK))

    def put(j, result):
        out[:, jobs[j][1] : jobs[j][1] + CHUNK] = result

    def load(t, gr, act):
        z_first, column = jobs[t]
        x = gr if z_first else act
        at = column % (2 * CHUNK)
        return [
            local(x.at[:, half * 2 * CHUNK + at : half * 2 * CHUNK + at + CHUNK],
                  x_v.at[t % 2, half], ld.at[t % 2, half])
            for half in range(2)
        ]

    def start_load(t):
        pl.when(s == 1)(lambda: start_all(load(t, gr1, act1)))
        pl.when(s == 3)(lambda: start_all(load(t, gr3, act3)))

    def small(normed, gb, vecs):
        return [local(normed, low_v.at[0], vl.at[0]), local(gb, low_v.at[1], vl.at[1]),
                local(vecs, sums.va.at[0], vl.at[2])]

    swap = remote(g1.at[pl.ds(ROWS - BLOCK, BLOCK)], g_theirs, xs, xr, partner)
    swap3 = [remote(g3, g3_theirs, xs, xr, partner),
             remote(h3, h3_theirs, hs, hr, partner)]

    @pl.when(s % 2 == 1)
    def _():
        pl.when(s == 1)(lambda: start_all(small(n1, gb1, v1)))
        pl.when(s == 3)(lambda: start_all(small(n3, gb3, v3)))
        greet_all()
        start_load(0)
        start_load(1)
        smalls = small(n1, gb1, v1)
        for n in range(2):
            smalls[n].wait()
            left_t[n] = low_v[n].T
        met()
        pl.when(s == 1)(swap.start)
        pl.when(s == 3)(lambda: start_all(swap3))
        smalls[2].wait()
        def take(t):
            for stage in range(6):
                if 0 <= t - stage < 4:
                    red.step(t - stage, jobs[t - stage][0], stage, put)

        def compute(t, carry):
            slot = t % 2
            for half in range(2):
                local(gr1.at[:, 0:CHUNK], x_v.at[slot, half], ld.at[slot, half]).wait()
            job_terms(red.acc, t, left_t.at[slot], lambda half: x_v.at[slot, half])
            for n in range(4):
                @pl.when(t == n)
                def _(n=n):
                    if n < 2:
                        start_load(n + 2)
                    if n < 3:
                        sums.step(n)
                    take(n)
            return carry

        lax.fori_loop(0, 4, compute, 0)
        for t in range(4, 9):
            take(t)
        sums.step(3)
        for j in range(4):
            red.sent(j, jobs[j][0])
        pl.when(s == 1)(swap.wait)
        pl.when(s == 3)(lambda: wait_all(swap3))


def ff_finish(first, last, rest):
    dma = pltpu.SemaphoreType.DMA
    any_spec = pl.BlockSpec(memory_space=ANY)
    vmem = pl.BlockSpec(memory_space=pltpu.VMEM)
    return call(
        ff_finish_body,
        (shape((BLOCK, D), F32), shape(WIDE, F32), shape(WIDE, F32), shape((48, 4 * CHUNK), F32),
         shape((2, 8, D), F32)),
        [any_spec] * 13,
        (any_spec, any_spec, any_spec, vmem, vmem),
        scratch=reduction_scratch(4, CHUNK) + sums_scratch() + [
            pltpu.VMEM((2, 2, ROWS, CHUNK), BF16), pltpu.VMEM((2,) + WIDE, BF16),
            pltpu.VMEM((2, D, ROWS), BF16),
            dma((2, 2)), dma, dma, dma((3,)), dma, dma,
        ],
        collective_id=21,
        has_side_effects=True,
    )(*first, *last, *rest)


def block_rows(i):
    return slice(i * BLOCK, min((i + 1) * BLOCK, LENGTH))


def load_block(mine, theirs, a_v, b_v, sems, i):
    r = pl.ds(i * BLOCK, BLOCK)
    return [local(mine.at[r], a_v.at[r], sems.at[0, i]),
            local(theirs.at[r], b_v.at[r], sems.at[1, i])]


def load_blocks(mine, theirs, a_v, b_v, sems, last=None):
    def step(i, carry):
        start_all(load_block(mine, theirs, a_v, b_v, sems, i))
        return carry

    lax.fori_loop(0, BLOCKS if last is None else BLOCKS - 1, step, 0)
    if last is not None:
        r = pl.ds(ROWS - BLOCK, BLOCK)
        local(mine.at[r], a_v.at[r], sems.at[0, BLOCKS - 1]).start()
        local(last, b_v.at[r], sems.at[1, BLOCKS - 1]).start()


def store_block(o_v, out, sems, i):
    r = block_rows(i) if isinstance(i, int) else block(i)
    return local(o_v.at[r], out.at[r], sems.at[2, i])


def write_block(a_v, b_v, o_v, sems, first, i):
    wait_all(load_block(a_v, b_v, a_v, b_v, sems, i))
    r = block_rows(i) if isinstance(i, int) else block(i)
    a, b = a_v[r, :], b_v[r, :]
    o_v[r, 0, :] = jnp.where(first, a, b)
    o_v[r, 1, :] = jnp.where(first, b, a)


def write_blocks(a_v, b_v, o_v, sems, first, out):
    def step(i, carry):
        write_block(a_v, b_v, o_v, sems, first, i)
        store_block(o_v, out, sems, i).start()
        return carry

    lax.fori_loop(0, BLOCKS - 1, step, 0)
    write_block(a_v, b_v, o_v, sems, first, BLOCKS - 1)
    store_block(o_v, out, sems, BLOCKS - 1).start()
    for i in range(BLOCKS):
        store_block(o_v, out, sems, i).wait()


def early_body(hf, h_theirs, out, a_v, b_v, o_v, sems):
    s, _, p, _, _ = place()

    @pl.when(s < 2)
    def _():
        load_blocks(hf, h_theirs, a_v, b_v, sems)
        write_blocks(a_v, b_v, o_v, sems, p == 0, out)


BOTH = (LENGTH, 2, D)


def early(hf, h_theirs):
    any_spec = pl.BlockSpec(memory_space=ANY)
    return call(
        early_body,
        shape(BOTH, F32),
        [any_spec] * 2,
        any_spec,
        scratch=[pltpu.VMEM(WIDE, F32), pltpu.VMEM(WIDE, F32), pltpu.VMEM(BOTH, F32),
                 pltpu.SemaphoreType.DMA((3, BLOCKS))],
    )(hf, h_theirs)


def small_outputs(attn_sums, ff_sums, attn_vec, ff_vec, rows3, qkv_g, qv_g, out_g, up_g, upb_g,
                  down_g):
    s, r, _, _, _ = place()
    at = lax.broadcasted_iota(jnp.int32, (D, 48), 0)
    pick = jnp.where(at == lax.broadcasted_iota(jnp.int32, (D, 48), 1) + r * 48, 1.0, 0.0)

    def picked(vec):
        rows3[...] = lax.dot_general(
            vec[0] + vec[1], pick, (((1,), (0,)), ((), ())), precision=lax.Precision.HIGHEST,
            preferred_element_type=F32)

    @pl.when(s % 2 == 0)
    def _():
        picked(attn_vec)
        for t in range(3):
            qkv_g[t] = attn_sums[:, t * 384 : t * 384 + 384]
        out_g[...] = attn_sums[:, 1152:1536]
        qv_g[...] = attn_vec[0, 3:5, 0:384] + attn_vec[1, 3:5, 384:768]
        for ref in (up_g, upb_g, down_g):
            ref[...] = jnp.zeros(ref.shape, F32)

    @pl.when(s % 2 == 1)
    def _():
        picked(ff_vec)
        up_g[...] = ff_sums[:, 0:1536]
        down_g[...] = ff_sums[:, 1536:3072]
        for n in range(2):
            upb_g[:, n * D : n * D + D] = ff_vec[0, 3 + n : 4 + n, :] + ff_vec[1, 5 + n : 6 + n, :]
        for ref in (qkv_g, out_g, qv_g):
            ref[...] = jnp.zeros(ref.shape, F32)


def assemble_body(hid_in, hm, h2, h3, g0, gb, gm, ga, gb_theirs, gf, g3, attn_sums, ff_sums, attn_vec,
                  ff_vec, hid, gin, rows3, qkv_g, qv_g, out_g, up_g, upb_g, down_g, a_v, b_v, o_v,
                  sems):
    s, _, p, _, _ = place()
    first = jnp.where(s < 2, p, 1 - p) == 0

    def load(n, mine, theirs, last=None):
        load_blocks(mine, theirs, a_v.at[n], b_v.at[n], sems.at[n], last)

    pl.when(s == 0)(lambda: load(0, g0, ga))
    pl.when(s == 1)(lambda: load(0, gb, gb_theirs, gf))

    @pl.when(s == 2)
    def _():
        load(0, gb, ga)
        load(1, hm, h2)

    @pl.when(s == 3)
    def _():
        load(0, gm, g3)
        load(1, hm, h3)

    small_outputs(attn_sums, ff_sums, attn_vec, ff_vec, rows3, qkv_g, qv_g, out_g, up_g, upb_g,
                  down_g)

    def write(n, carry):
        def step(i, carry):
            write_block(a_v.at[n], b_v.at[n], o_v.at[n], sems.at[n], first, i)
            pl.when(n == 0)(lambda: store_block(o_v.at[n], gin, sems.at[n], i).start())
            pl.when(n == 1)(lambda: store_block(o_v.at[n], hid, sems.at[n], i).start())
            return carry

        lax.fori_loop(0, BLOCKS - 1, step, 0)
        write_block(a_v.at[n], b_v.at[n], o_v.at[n], sems.at[n], first, BLOCKS - 1)
        pl.when(n == 0)(lambda: store_block(o_v.at[n], gin, sems.at[n], BLOCKS - 1).start())
        pl.when(n == 1)(lambda: store_block(o_v.at[n], hid, sems.at[n], BLOCKS - 1).start())
        return carry

    lax.fori_loop(0, jnp.where(s < 2, 1, 2), write, 0)
    for i in range(BLOCKS):
        store_block(o_v.at[0], gin, sems.at[0], i).wait()
        pl.when(s >= 2)(lambda i=i: store_block(o_v.at[1], hid, sems.at[1], i).wait())


def assemble(*operands):
    any_spec = pl.BlockSpec(memory_space=ANY)
    vmem = pl.BlockSpec(memory_space=pltpu.VMEM)
    return call(
        assemble_body,
        (shape(BOTH, F32), shape(BOTH, F32), shape((8, 48), F32), shape((3, 48, 384), F32),
         shape((2, 384), F32), shape((48, 384), F32), shape((48, 1536), F32),
         shape((1, 1536), F32), shape((48, 1536), F32)),
        [any_spec] * 11 + [vmem] * 4,
        (any_spec, any_spec) + (vmem,) * 7,
        scratch=[pltpu.VMEM((2,) + WIDE, F32), pltpu.VMEM((2,) + WIDE, F32),
                 pltpu.VMEM((2,) + BOTH, F32), pltpu.SemaphoreType.DMA((2, 3, BLOCKS))],
        aliases={0: 0},
    )(*operands)


def unwritten(shapes):
    any_spec = pl.BlockSpec(memory_space=ANY)
    return pl.pallas_call(
        lambda *refs: None,
        out_shape=tuple(shapes),
        out_specs=(any_spec,) * len(shapes),
    )()


def only_at(active, run, operands):
    like = jax.eval_shape(run, *operands)
    leaves, tree = jax.tree.flatten(like)

    def skip(*_):
        return jax.tree.unflatten(tree, unwritten([shape(x.shape, x.dtype) for x in leaves]))

    return lax.cond(active, run, skip, *operands)


def per_device(inputs, cotangent, norm_gain, norm_bias, qkv_weight, qv_bias, out_weight, end_bias,
               up_weight, up_bias, down_weight):
    s, r, p = lax.axis_index("section"), lax.axis_index("dp"), lax.axis_index("tensor")
    qkv, out_w, up, down = qkv_weight[0], out_weight[0], up_weight[0], down_weight[0]

    gain, shift, end = norm_gain, norm_bias, end_bias
    attn = s % 2 == 0
    by_row = [jnp.transpose(x, (1, 0, 2)) for x in (inputs, cotangent)]
    w, w_out, w_up, w_down, h0, normed0, q0, k0, v0, o0, lse0, qkvb, upb = opening(
        qkv, out_w, up, down, by_row[0], qv_bias[0], up_bias, gain, shift)
    cot = only_at(s == 3, lambda x: (extract(x),), (by_row[1],))[0]
    hf, h_in, act1, slope1, normed_f, q2, k2, v2, o2, lse2 = forward(
        o0, h0, w_out, w_up, w_down, w, gain, shift, end, upb, qkvb)
    h_early = exchange(hf)
    hid_early = early(hf, h_early)
    o2, hid_early = lax.optimization_barrier((o2, hid_early))
    hm, _, act3, gr3, gb_m, normed3, g2, gm2, g_m, vec_m = middle(
        o2, h_in, w_out, w_up, w_down, cot, gain, shift, end, upb)
    g_b, g_in0, gr1, gb_b, gm0, vec_b, h2_theirs, gb_theirs, gq2, gk2, gv2 = backward(
        g2, h_in, q2, k2, v2, gm2, lse2, w, w_up, w_down, slope1, w_out, hm, gain)

    gb_m, vec_b = lax.optimization_barrier((gb_m, vec_b))
    g1_theirs, g3_theirs, h3_theirs, ff_sums, ff_vec = ff_finish(
        (gr1, act1, gb_b, normed_f), (gr3, act3, gb_m, normed3), (g_b, g_m, vec_b, vec_m, hm))
    g1_theirs, gb_last = lax.optimization_barrier((g1_theirs, gb_b))
    ga_theirs, g_0, attn_sums, attn_vec = attn_finish(
        (q0, k0, v0, gm0, lse0, o0, gb_last, normed0), (gq2, gk2, gv2, o2, gb_m, normed_f),
        (g_in0, h0, w, vec_b, g_b), gain)
    hid, gin, rows3, qkv_g, qv_g, out_g, up_g, upb_g, down_g = assemble(
        hid_early, hm, h2_theirs, h3_theirs, g_0, g_b, g_m, ga_theirs, gb_theirs, g1_theirs,
        g3_theirs, attn_sums, ff_sums, attn_vec, ff_vec)
    hid, gin = [jnp.transpose(x, (1, 0, 2))[None] for x in (hid, gin)]
    return (hid, gin, rows3[0:1], rows3[1:2], qkv_g[None], qv_g[None], out_g.T[None], rows3[2:3],
            up_g[None], upb_g, down_g.T[None])


def solution(mesh):
    return jax.shard_map(
        per_device,
        mesh=mesh,
        in_specs=(
            P("dp", None, None),
            P("dp", None, None),
            P("section", None),
            P("section", None),
            P("section", None, None, "tensor"),
            P("section", None, "tensor"),
            P("section", "tensor", None),
            P("section", None),
            P("section", None, "tensor"),
            P("section", "tensor"),
            P("section", "tensor", None),
        ),
        out_specs=(
            P("section", "dp", None, None),
            P("section", "dp", None, None),
            P("section", "dp"),
            P("section", "dp"),
            P("section", None, "dp", "tensor"),
            P("section", None, "tensor"),
            P("section", "tensor", "dp"),
            P("section", "dp"),
            P("section", "dp", "tensor"),
            P("section", "tensor"),
            P("section", "tensor", "dp"),
        ),
        check_vma=False,
    )
```

```python
import functools

import jax
import jax.numpy as jnp
from jax import lax
from jax.experimental import pallas as pl
from jax.experimental.pallas import tpu as pltpu
from jax.sharding import PartitionSpec as P

MESH = pl.DeviceIdType.MESH
ANY = pl.ANY
F32 = jnp.float32
BF16 = jnp.bfloat16

HEAD_DIM = 64
EPS = 1e-06
LENGTH = 866
ROWS = 896
BLOCK = 224
D = 768
PAIRS = 6
Q_BLOCKS = ((0, 384), (384, 512))
VMEM_BYTES = 60 * 1024 * 1024

CHUNK = 768


def call(body, out_shape, in_specs, out_specs, grid=(), scratch=(), aliases={}, **more):
    return pl.pallas_call(
        body,
        out_shape=out_shape,
        grid=grid,
        in_specs=in_specs,
        out_specs=out_specs,
        scratch_shapes=scratch,
        input_output_aliases=aliases,
        compiler_params=pltpu.CompilerParams(vmem_limit_bytes=VMEM_BYTES, **more),
    )


def shape(dims, dtype):
    return jax.ShapeDtypeStruct(dims, dtype)


def whole(*dims):
    return pl.BlockSpec(dims, lambda *_: (0,) * len(dims), pipeline_mode=pl.Buffered(1))


def rows_of(width):
    return pl.BlockSpec((BLOCK, width), lambda i: (i, 0))


def dot(a, b, ca=1, cb=0):
    return lax.dot_general(a, b, (((ca,), (cb,)), ((), ())), preferred_element_type=F32)


def normalized(h):
    average = jnp.mean(h, axis=-1, keepdims=True)
    centred = h - average
    spread = jnp.mean(centred * centred, axis=-1, keepdims=True)
    r = lax.rsqrt(spread + EPS)
    return centred * r, r


def norm_back(g, h, gain, grad_normed):
    xhat, r = normalized(h)
    t = grad_normed * gain
    t_mean = jnp.mean(t, axis=-1, keepdims=True)
    tx_mean = jnp.mean(t * xhat, axis=-1, keepdims=True)
    return g + r * (t - t_mean - xhat * tx_mean), xhat


def block(i):
    return pl.ds(pl.multiple_of(i * BLOCK, 32), BLOCK)


def gelu_and_slope(x):
    phi = 0.5 * (1.0 + lax.erf(x * 0.7071067811865476))
    density = jnp.exp(-0.5 * x * x) * 0.3989422804014327
    return (x * phi).astype(BF16), phi + x * density


def qkv_block(h, gain, shift, w_ref, bias, q_ref, k_ref, v_ref, normed_ref, r):
    xhat, _ = normalized(h)
    normed_ref[r, :] = (xhat * gain + shift).astype(BF16)

    def half_step(half, carry):
        cols = pl.ds(pl.multiple_of(half * 1152, 128), 1152)
        part = (dot(normed_ref[r, :], w_ref[:, cols]) + bias[:, cols]).astype(BF16)
        for n in range(9):
            lanes = part[:, n * 128 : n * 128 + 128]
            pair = half * 3 + n % 3
            if n < 3:
                q_ref[pair, r, :] = (lanes.astype(F32) * 0.125).astype(BF16)
            elif n < 6:
                k_ref[pair, r, :] = lanes
            else:
                v_ref[pair, r, :] = lanes
        return carry

    lax.fori_loop(0, 2, half_step, 0)


def joined(ref, r):
    return jnp.concatenate([ref[j, r, :] for j in range(PAIRS)], axis=1)


def mixed_back_block(g, w_out_ref, gm_ref, r):
    gb = g.astype(BF16)
    gm = dot(gb, w_out_ref[...], 1, 1).astype(BF16)
    for j in range(PAIRS):
        gm_ref[j, r, :] = gm[:, j * 128 : j * 128 + 128]
    return gb


def add_row(vec_ref, at, values):
    vec_ref[at : at + 1, :] += jnp.sum(values, axis=0, keepdims=True)


def qkv_back_rows(g, h, gain, parts, w_ref, vec_ref):
    grad_normed = jnp.zeros((BLOCK, D), F32)
    for half, (qk, v) in enumerate(parts):
        part = jnp.concatenate([qk, v], axis=1)
        grad_normed = grad_normed + dot(part, w_ref[:, half * 1152 : half * 1152 + 1152], 1, 1)
    out, xhat = norm_back(g, h, gain, grad_normed)
    add_row(vec_ref, 0, grad_normed * xhat)
    add_row(vec_ref, 1, grad_normed)
    add_row(vec_ref, 2, g.astype(BF16).astype(F32))
    add_row(vec_ref, 3, jnp.concatenate([qk[:, :384] for qk, _ in parts], axis=1).astype(F32))
    add_row(vec_ref, 4, jnp.concatenate([v for _, v in parts], axis=1).astype(F32))
    return out


def pairs_of(refs, half, r):
    return jnp.concatenate([ref[half * 3 + i, r, :] for ref in refs for i in range(3)], axis=1)


def head_mask(dims, axis, head):
    at = lax.broadcasted_iota(jnp.int32, dims, axis)
    return at < HEAD_DIM if head == 0 else at >= HEAD_DIM


def with_lanes(x, head, columns):
    lane = lax.broadcasted_iota(jnp.int32, x.shape, 1)
    own, spare = (lane < HEAD_DIM, HEAD_DIM) if head == 0 else (lane >= HEAD_DIM, 0)
    out = jnp.where(own, x, 0)
    for n, column in enumerate(columns):
        out = jnp.where(lane == spare + n, column, out)
    return out


def in_pieces(x):
    high = x.astype(BF16)
    rest = x - high.astype(F32)
    middle = rest.astype(BF16)
    return [high, middle, (rest - middle.astype(F32)).astype(BF16)]


def key_bias():
    row = lax.broadcasted_iota(jnp.int32, (ROWS, 1), 0)
    return jnp.where(row < LENGTH, 0.0, -1e30).astype(BF16)


def attend_pair(q_ref, k_ref, v_ref, o_ref, lse_ref, j):
    one = jnp.ones((1, 1), BF16)
    q, k, v_t = q_ref[j], k_ref[j], v_ref[j].T
    out = jnp.zeros((128, ROWS), F32)
    rows = []
    for head in range(2):
        s = dot(with_lanes(k, head, [key_bias()]), with_lanes(q, head, [one]), 1, 1)
        top = jnp.max(s, axis=0, keepdims=True)
        e = jnp.exp(s - top)
        total = jnp.sum(e, axis=0, keepdims=True)
        p = (e * (1.0 / total)).astype(BF16)
        out = out + dot(jnp.where(head_mask(v_t.shape, 0, head), v_t, 0), p)
        rows.append(top + jnp.log(total))
    o_ref[j] = out.T.astype(BF16)
    lse_ref[j] = jnp.concatenate(rows + [jnp.zeros((6, ROWS), F32)], axis=0)


def attend_back_pair(q_ref, k_ref, v_ref, gm_ref, lse_ref, gq_ref, gk_ref, gv_ref, j):
    one = jnp.ones((1, 1), BF16)
    k, v = k_ref[j], v_ref[j]
    k_t = k.T
    k_heads = [jnp.where(head_mask(k_t.shape, 0, head), k_t, 0) for head in range(2)]
    k_lanes = [with_lanes(k, head, [one, one, one, key_bias()]) for head in range(2)]
    lse_columns = lse_ref[j].T
    grad_k = jnp.zeros((ROWS, 128), F32)
    grad_v = jnp.zeros((ROWS, 128), F32)
    for start, size in Q_BLOCKS:
        rows = slice(start, start + size)
        q, gm, lse = q_ref[j, rows, :], gm_ref[j, rows, :], lse_columns[rows, :]
        grad_q = jnp.zeros((128, size), F32)
        for head in range(2):
            q_lanes = with_lanes(q, head, in_pieces(-lse[:, head : head + 1]) + [one])
            q_head, gm_head = with_lanes(q, head, []), with_lanes(gm, head, [])
            p = jnp.exp(dot(k_lanes[head], q_lanes, 1, 1))
            gp = dot(v, gm_head, 1, 1)
            weighted = p * gp
            gs = (weighted - p * jnp.sum(weighted, axis=0, keepdims=True)).astype(BF16)
            grad_v = grad_v + dot(p.astype(BF16), gm_head)
            grad_k = grad_k + dot(gs, q_head)
            grad_q = grad_q + dot(k_heads[head], gs)
        gq_ref[j, rows, :] = (grad_q.T * 0.125).astype(BF16)
    gk_ref[j] = grad_k.astype(BF16)
    gv_ref[j] = grad_v.astype(BF16)


def extract_body(x_ref, out_ref):
    s, p = lax.axis_index("section"), lax.axis_index("tensor")
    clip = jnp.where(s < 2, p, 1 - p)
    x = x_ref[...].astype(F32)
    x = jnp.where(clip == 0, x[:, 0, :], x[:, 1, :])
    at = lax.broadcasted_iota(jnp.int32, x.shape, 0) + pl.program_id(0) * BLOCK
    out_ref[...] = jnp.where(at < LENGTH, x, 0.0)


def extract(x):
    return call(
        extract_body,
        shape((ROWS, D), F32),
        [pl.BlockSpec((BLOCK, 2, D), lambda i: (i, 0, 0))],
        rows_of(D),
        grid=(ROWS // BLOCK,),
    )(x)


def place():
    s, r, p = lax.axis_index("section"), lax.axis_index("dp"), lax.axis_index("tensor")
    return s, r, p, r // 4, r % 4


def on_dp(y, z):
    return {"dp": y * 4 + z}


def greet(peers):
    barrier = pltpu.get_barrier_semaphore()
    for peer in peers:
        pl.semaphore_signal(barrier, inc=1, device_id=peer, device_id_type=MESH)
    pl.semaphore_wait(barrier, len(peers))


def remote(src, dst, send, recv, device):
    return pltpu.make_async_remote_copy(
        src_ref=src, dst_ref=dst, send_sem=send, recv_sem=recv, device_id=device,
        device_id_type=MESH,
    )


def local(src, dst, sem):
    return pltpu.make_async_copy(src, dst, sem)


def start_all(copies):
    for copy in copies:
        copy.start()


def wait_all(copies):
    for copy in copies:
        copy.wait()


BLOCKS = ROWS // BLOCK


class Piece:
    def __init__(self, n, source, view, halves, z_first, sems):
        self.n, self.source, self.view, self.halves, self.z_first = n, source, view, halves, z_first
        self.send, self.recv = sems
        _, _, p, self.y, self.z = place()
        self.partner = {"tensor": 1 - p}

    def copies(self, stage):
        y, z, view = self.y, self.z, self.view
        along_z = [on_dp(y, (z + d) % 4) for d in (1, 3)]
        along_y = [on_dp((y + d) % 4, z) for d in (1, 3)]

        def copy(n, src, dst, device):
            return remote(src, dst, self.send.at[self.n, stage, n], self.recv.at[self.n, stage, n],
                          device)

        def both(refs, peers):
            return [copy(n, refs[n], refs[n], peers[n]) for n in range(2)]

        everything = slice(0, 4)
        if self.z_first:
            ring, ring2 = along_z, along_y
            one = lambda d: view(y, (z + d) % 4)
            group = lambda d, part=everything: view((y + d) % 4, part)
        else:
            ring, ring2 = along_y, along_z
            one = lambda d: view((y + d) % 4, z)
            group = lambda d, part=everything: view(part, (z + d) % 4)
        if stage == 0:
            return [copy(0, self.source, view(y, z), self.partner)]
        if stage == 1:
            return both([one(0), one(0)], ring)
        if stage == 2:
            return both([self.halves(one(3))[0], self.halves(one(1))[1]], ring)
        if stage == 3:
            return both([group(0), group(0)], ring2)
        return both([group(3, slice(0, 2)), group(1, slice(2, 4))], ring2)


def advance(pieces, stage):
    for piece in pieces:
        if stage > 0:
            for copy in piece.copies(stage - 1):
                copy.wait_recv()
        if stage < 5:
            start_all(piece.copies(stage))


def all_sent(pieces):
    for piece in pieces:
        for stage in range(5):
            for copy in piece.copies(stage):
                copy.wait_send()


def opening_body(qkv, out_w, up, down, x, qvb, upb, gain, shift,
                 w, w_out, w_up, w_down, h0, normed, q, k, v, o, lse, qkvb, upb_all,
                 w_v, w_out_v, up_v, down_v, fq, fo, fu, fd, fx, lq, lo, lu, ldn, lx, qvb_o, upb_o,
                 x_v, h_v, normed_v, q_v, k_v, v_v, o_v, lse_v, ld, st, send, recv, bsend, brecv,
                 gate):
    s, r, p, y, z = place()
    partner = {"tensor": 1 - p}
    attn = s % 2 == 0
    peers = [partner] + [on_dp(y, (z + d) % 4) for d in (1, 3)] \
        + [on_dp((y + d) % 4, z) for d in (1, 3)]
    barrier = pltpu.get_barrier_semaphore()
    for peer in peers:
        pl.semaphore_signal(barrier, inc=1, device_id=peer, device_id_type=MESH)

    def rows_at(n):
        return pl.ds(pl.multiple_of(r * n, n), n)

    def qkv_half(half):
        cols = pl.ds(pl.multiple_of(half * 1152, 128), 1152)

        def step(i, carry):
            rows = block(i)

            @pl.when(half == 0)
            def _():
                x0 = x_v[rows].astype(F32)
                h = jnp.where(p == 0, x0[:, 0, :], x0[:, 1, :])
                at = lax.broadcasted_iota(jnp.int32, h.shape, 0) + i * BLOCK
                h = jnp.where(at < LENGTH, h, 0.0)
                h_v[rows, :] = h
                xhat, _ = normalized(h)
                normed_v[rows, :] = (xhat * gain[...] + shift[...]).astype(BF16)

            part = (dot(normed_v[rows, :], w_v[:, cols]) + qkvb[:, cols]).astype(BF16)
            for n in range(9):
                lanes = part[:, n * 128 : n * 128 + 128]
                pair = half * 3 + n % 3
                if n < 3:
                    q_v[pair, rows, :] = (lanes.astype(F32) * 0.125).astype(BF16)
                elif n < 6:
                    k_v[pair, rows, :] = lanes
                else:
                    v_v[pair, rows, :] = lanes
            return carry

        lax.fori_loop(0, BLOCKS, step, 0)

    @pl.when(attn)
    def _():
        loads = [local(qkv.at[t], w_v.at[:, pl.ds(t * 384, 384)], ld.at[t]) for t in range(3)]
        loads.append(local(out_w, w_out_v.at[pl.ds(0, 384)], ld.at[3]))
        clips = local(x, x_v.at[pl.ds(0, LENGTH)], ld.at[4])
        start_all(loads)
        pl.when(s == 0)(clips.start)
        sems = send, recv
        def rows24(ref):
            return ref.at[pl.ds(0, 24)], ref.at[pl.ds(24, 24)]

        left, right = pl.ds(0, 256), pl.ds(256, 128)
        pieces = [
            Piece(0, fq.at[0], lambda a, b: lq.at[0, a, b], rows24, True, sems),
            Piece(1, fq.at[1], lambda a, b: lq.at[1, a, b], rows24, False, sems),
            Piece(2, fq.at[2, :, left], lambda a, b: lq.at[2, a, b, ..., left], rows24, True, sems),
            Piece(3, fq.at[2, :, right], lambda a, b: lq.at[2, a, b, ..., right], rows24, False,
                  sems),
        ]
        direct = remote(fo, lo, bsend.at[1], brecv.at[1], partner)
        bias = remote(qvb, qvb_o, bsend.at[0], brecv.at[0], partner)
        qkvb[:, 0:384] = qvb[0:1, :]
        qkvb[:, 384:768] = jnp.zeros((1, 384), F32)
        qkvb[:, 768:1152] = qvb[1:2, :]
        wait_all(loads)
        for t in range(3):
            fq[t] = w_v[rows_at(48), t * 384 : t * 384 + 384].astype(F32)
        fo[...] = w_out_v[0:384, :].astype(F32)
        pl.semaphore_wait(barrier, 6)
        advance(pieces, 0)
        bias.start()
        direct.start()

        pl.when(s == 0)(clips.wait)
        stored = [local(w_v, w, st.at[0]), local(w_out_v, w_out, st.at[1])]

        def gathered():
            advance(pieces, 4)
            bias.wait()
            direct.wait()
            w_out_v[384:768, :] = lo[...].astype(BF16)
            advance(pieces, 5)
            for t in range(3):
                at = 1152 + t * 384

                def widen(i, carry, t=t, at=at):
                    w_v[pl.ds(pl.multiple_of(i * 192, 192), 192), at : at + 384] = \
                        lq[t, i].reshape(192, 384).astype(BF16)
                    return carry

                lax.fori_loop(0, 4, widen, 0)
            qkvb[:, 1152:1536] = qvb_o[0:1, :]
            qkvb[:, 1536:1920] = jnp.zeros((1, 384), F32)
            qkvb[:, 1920:2304] = qvb_o[1:2, :]
            start_all(stored)

        def pair_step(i, carry):
            pl.when((s == 0) & (i % 3 == 0))(lambda: qkv_half(i // 3))
            pl.when(i == 0)(lambda: advance(pieces, 1))
            pl.when(s == 0)(lambda: attend_pair(q_v, k_v, v_v, o_v, lse_v, i))
            pl.when(i == 0)(lambda: advance(pieces, 2))

            @pl.when(i == 1)
            def _():
                advance(pieces, 3)
                pl.semaphore_signal(gate, inc=1, device_id={"section": s + 1}, device_id_type=MESH)

            pl.when(i == 2)(gathered)
            return carry

        lax.fori_loop(0, PAIRS, pair_step, 0)

        @pl.when(s == 0)
        def _():
            kept = [local(a, b, st.at[2 + n]) for n, (a, b) in enumerate(
                ((h_v, h0), (normed_v, normed), (q_v, q), (k_v, k), (v_v, v), (o_v, o),
                 (lse_v, lse)))]
            start_all(kept)
            wait_all(kept)

        all_sent(pieces)
        wait_all(stored)

    @pl.when(jnp.logical_not(attn))
    def _():
        pl.semaphore_signal(barrier, inc=1, device_id={"section": s - 1}, device_id_type=MESH)
        loads = [local(up, up_v.at[:, pl.ds(0, 1536)], ld.at[0]),
                 local(down, down_v.at[pl.ds(0, 1536)], ld.at[1])]
        start_all(loads)
        sems = send, recv
        pieces = [
            Piece(0, fu, lambda a, b: lu.at[a, b],
                  lambda ref: (ref.at[pl.ds(0, 24)], ref.at[pl.ds(24, 24)]), True, sems),
            Piece(1, fd, lambda a, b: ldn.at[a, b],
                  lambda ref: (ref.at[pl.ds(0, 48)], ref.at[pl.ds(48, 48)]), False, sems),
        ]
        direct = remote(fx, lx, bsend.at[1], brecv.at[1], partner)
        early = [local(up_v.at[:, pl.ds(0, 1536)], w_up.at[:, pl.ds(0, 1536)], st.at[0]),
                 local(down_v.at[pl.ds(0, 1536)], w_down.at[pl.ds(0, 1536)], st.at[1])]
        late = [local(up_v.at[:, pl.ds(1536, 1536)], w_up.at[:, pl.ds(1536, 1536)], st.at[2]),
                local(down_v.at[pl.ds(1536, 1536)], w_down.at[pl.ds(1536, 1536)], st.at[3])]
        bias = remote(upb, upb_o, bsend.at[0], brecv.at[0], partner)
        upb_all[:, 0:1536] = upb[...]
        wait_all(loads)
        fu[...] = up_v[rows_at(48), 0:1536].astype(F32)
        start_all(early)
        fd[...] = down_v[rows_at(96), 0:512].astype(F32)
        pl.semaphore_wait(barrier, 5)
        advance(pieces, 0)
        bias.start()
        fx[...] = down_v[0:1536, 512:768].astype(F32)
        direct.start()
        pl.semaphore_wait(gate, 1)
        for stage in range(1, 5):
            advance(pieces, stage)
        bias.wait()
        upb_all[:, 1536:3072] = upb_o[...]

        def widen(d):
            i, g = (y + d) % 4, (z + d) % 4
            up_v[pl.ds(pl.multiple_of(i * 192, 192), 192), 1536:3072] = \
                lu[i].reshape(192, 1536).astype(BF16)
            for a in range(4):
                down_v[pl.ds(pl.multiple_of(1536 + (a * 4 + g) * 96, 96), 96), 0:512] = \
                    ldn[a, g].astype(BF16)

        for d in (0, 1, 3):
            widen(d)
        direct.wait()
        down_v[1536:3072, 512:768] = lx[...].astype(BF16)
        advance(pieces, 5)
        widen(2)
        start_all(late)
        all_sent(pieces)
        wait_all(early + late)


def opening(qkv, out_w, up, down, x, qvb, upb, gain, shift):
    dma = pltpu.SemaphoreType.DMA
    any_spec = pl.BlockSpec(memory_space=ANY)
    vmem = pl.BlockSpec(memory_space=pltpu.VMEM)
    paired, lse = (PAIRS, ROWS, 128), (PAIRS, 8, ROWS)
    return call(
        opening_body,
        (shape((D, 2304), BF16), shape((D, D), BF16), shape((D, 3072), BF16),
         shape((3072, D), BF16), shape((ROWS, D), F32), shape((ROWS, D), BF16),
         shape(paired, BF16), shape(paired, BF16), shape(paired, BF16), shape(paired, BF16),
         shape(lse, F32), shape((1, 2304), F32), shape((1, 3072), F32)),
        [any_spec] * 5 + [vmem] * 4,
        (any_spec,) * 11 + (vmem, vmem),
        scratch=[
            pltpu.VMEM((D, 2304), BF16), pltpu.VMEM((D, D), BF16), pltpu.VMEM((D, 3072), BF16),
            pltpu.VMEM((3072, D), BF16), pltpu.VMEM((3, 48, 384), F32), pltpu.VMEM((384, D), F32),
            pltpu.VMEM((48, 1536), F32), pltpu.VMEM((96, 512), F32), pltpu.VMEM((1536, 256), F32),
            pltpu.VMEM((3, 4, 4, 48, 384), F32), pltpu.VMEM((384, D), F32),
            pltpu.VMEM((4, 4, 48, 1536), F32), pltpu.VMEM((4, 4, 96, 512), F32),
            pltpu.VMEM((1536, 256), F32),
            pltpu.VMEM((2, 384), F32), pltpu.VMEM((1, 1536), F32),
            pltpu.VMEM((ROWS, 2, D), BF16), pltpu.VMEM((ROWS, D), F32),
            pltpu.VMEM((ROWS, D), BF16), pltpu.VMEM(paired, BF16), pltpu.VMEM(paired, BF16),
            pltpu.VMEM(paired, BF16), pltpu.VMEM(paired, BF16), pltpu.VMEM(lse, F32),
            dma((5,)), dma((9,)), dma((4, 5, 2)), dma((4, 5, 2)), dma((2,)), dma((2,)),
            pltpu.SemaphoreType.REGULAR,
        ],
        collective_id=1,
        has_side_effects=True,
    )(qkv, out_w, up, down, x, qvb, upb, gain, shift)


class Link:
    def __init__(self, src, dst, send, recv):
        self.src, self.dst, self.sems = src, dst, (send, recv)

    def copy(self, i, device):
        r = block(i)
        return remote(self.src.at[r], self.dst.at[r], self.sems[0].at[i], self.sems[1].at[i], device)

    def expect_from(self, device):
        pl.semaphore_signal(
            pltpu.get_barrier_semaphore(), inc=1, device_id=device, device_id_type=MESH)

    def ready(self):
        pl.semaphore_wait(pltpu.get_barrier_semaphore(), 1)

    def arrived(self, i, device):
        self.copy(i, device).wait_recv()

    def sent(self, device):
        for i in range(BLOCKS):
            self.copy(i, device).wait_send()

    def both_ways(self, device):
        for i in range(BLOCKS):
            self.copy(i, device).wait()


def stores(pairs, sems):
    def of(i):
        r = block(i)
        found = []
        for n, (src, dst) in enumerate(pairs):
            if len(src.shape) == 3:
                found.append(local(src.at[:, r], dst.at[:, r], sems.at[n, i]))
            else:
                found.append(local(src.at[r], dst.at[r], sems.at[n, i]))
        return found

    return of


def every_block(step):
    def body(i, carry):
        step(i, block(i))
        return carry

    lax.fori_loop(0, BLOCKS, body, 0)


def out_proj_rows(o_v, h_v, w_out_v, end, hout, r):
    hout[r, :] = h_v[r, :] + (dot(joined(o_v, r), w_out_v[...]) + end)


def forward_body(o, h0, w_out, up, down, w, gain, shift, end, upb, qkvb,
                 h_out, h_in, act, slope, normed, q, k, v, o2, lse2,
                 hin, hout, up_v, down_v, act_v, slope_v, normed_v, o_v, w_out_v, w_v, q_v, k_v,
                 v_v, lse_v, ld, st, send, recv, half_send, half_recv, lse_send, lse_recv):
    s, _, p, _, _ = place()
    link = Link(hout, hin, send, recv)
    share = slope_v.at[:, pl.ds(0, 9 * 128)]
    halves = Link(share, share, half_send, half_recv)

    def lse_copy(device):
        return remote(lse_v.at[3:6], lse_v.at[0:3], lse_send.at[0], lse_recv.at[0], device)

    @pl.when(s == 0)
    def _():
        target = {"section": 1}
        loads = [local(o, o_v, ld.at[0]), local(h0, hin, ld.at[1]), local(w_out, w_out_v, ld.at[2])]
        start_all(loads)
        link.ready()
        wait_all(loads)
        out = stores([(hout, h_out)], st)

        def step(i, r):
            out_proj_rows(o_v, hin, w_out_v, end[...], hout, r)
            link.copy(i, target).start()
            start_all(out(i))

        every_block(step)
        link.sent(target)
        for i in range(BLOCKS):
            wait_all(out(i))

    @pl.when(s == 1)
    def _():
        source, target = {"section": 0}, {"section": 2, "tensor": 1 - p}
        loads = [local(up, up_v, ld.at[0]), local(down, down_v, ld.at[1])]
        start_all(loads)
        link.expect_from(source)
        link.ready()
        wait_all(loads)
        out = stores([(hout, h_out), (hin, h_in), (act_v, act), (slope_v, slope),
                      (normed_v, normed)], st)

        def step(i, r):
            link.arrived(i, source)
            h = hin[r, :]
            xhat, _ = normalized(h)
            low = (xhat * gain[...] + shift[...]).astype(BF16)
            normed_v[r, :] = low
            hout[r, :] = h + end[...]

            def chunk(c, carry):
                cols = pl.ds(pl.multiple_of(c * 768, 768), 768)
                x = dot(low, up_v[:, cols]) + upb[:, cols]
                active, steep = gelu_and_slope(x)
                act_v[r, cols] = active
                slope_v[r, cols] = steep
                hout[r, :] += dot(active, down_v[cols, :])
                return carry

            lax.fori_loop(0, 4, chunk, 0)
            link.copy(i, target).start()
            start_all(out(i))

        every_block(step)
        link.sent(target)
        for i in range(BLOCKS):
            wait_all(out(i))

    @pl.when(s == 2)
    def _():
        source = {"section": 1, "tensor": 1 - p}
        load = local(w, w_v, ld.at[0])
        load.start()
        link.expect_from(source)
        halves.ready()
        load.wait()
        out = stores([(hin, h_in), (normed_v, normed), (q_v, q), (k_v, k), (v_v, v)], st)

        def step(i, r):
            link.arrived(i, source)
            qkv_block(hin[r, :], gain[...], shift[...], w_v, qkvb, q_v, k_v, v_v, normed_v, r)
            for t, ref in enumerate((q_v, k_v, v_v)):
                for j in range(3):
                    at = (t * 3 + j) * 128
                    slope_v[r, at : at + 128] = ref[3 + j, r, :].astype(F32)
            halves.copy(i, {"section": 3}).start()
            start_all(out(i))

        every_block(step)

        def attend_step(i, carry):
            attend_pair(q_v, k_v, v_v, o_v, lse_v, i)
            return carry

        lax.fori_loop(0, PAIRS, attend_step, 0)
        kept = [local(o_v, o2, ld.at[1]), local(lse_v, lse2, ld.at[2])]
        start_all(kept)
        lse_copy({"section": 3}).start()
        halves.sent({"section": 3})
        for i in range(BLOCKS):
            wait_all(out(i))
        wait_all(kept)
        lse_copy({"section": 3}).wait_send()

    @pl.when(s == 3)
    def _():
        source = {"section": 2}
        halves.expect_from(source)

        def step(i, r):
            halves.arrived(i, source)
            for t, ref in enumerate((q_v, k_v, v_v)):
                for j in range(3):
                    at = (t * 3 + j) * 128
                    ref[j, r, :] = slope_v[r, at : at + 128].astype(BF16)

        every_block(step)
        kept = [local(a.at[0:3], b.at[0:3], ld.at[n])
                for n, (a, b) in enumerate(((q_v, q), (k_v, k), (v_v, v), (lse_v, lse2)))]
        start_all(kept[:3])
        lse_copy(source).wait_recv()
        kept[3].start()
        wait_all(kept)


def staged(body, outs, operands, small, scratch, stored, collective_id):
    dma = pltpu.SemaphoreType.DMA
    any_spec = pl.BlockSpec(memory_space=ANY)
    vmem = pl.BlockSpec(memory_space=pltpu.VMEM)
    return call(
        body,
        tuple(shape(*o) for o in outs),
        [any_spec] * len(operands) + [vmem] * len(small),
        (any_spec,) * len(outs),
        scratch=[pltpu.VMEM(*x) for x in scratch]
        + [dma((8,)), dma((stored, BLOCKS))] + [dma((BLOCKS,))] * 4 + [dma((2 * BLOCKS,))] * 2,
        collective_id=collective_id,
        has_side_effects=True,
    )(*operands, *small)


WIDE = (ROWS, D)
HIDDEN = (ROWS, 3072)
PAIRED = (PAIRS, ROWS, 128)
LSE = (PAIRS, 8, ROWS)


def forward(o, h0, w_out, up, down, w, gain, shift, end, upb, qkvb):
    return staged(
        forward_body,
        [(WIDE, F32), (WIDE, F32), (HIDDEN, BF16), (HIDDEN, F32), (WIDE, BF16), (PAIRED, BF16),
         (PAIRED, BF16), (PAIRED, BF16), (PAIRED, BF16), (LSE, F32)],
        (o, h0, w_out, up, down, w),
        (gain, shift, end, upb, qkvb),
        [(WIDE, F32), (WIDE, F32), ((D, 3072), BF16), ((3072, D), BF16), (HIDDEN, BF16),
         (HIDDEN, F32), (WIDE, BF16), (PAIRED, BF16), ((D, D), BF16), ((D, 2304), BF16),
         (PAIRED, BF16), (PAIRED, BF16), (PAIRED, BF16), (LSE, F32)],
        5,
        2,
    )


def middle_body(o, h2, w_out, up, down, cot, gain, shift, end, upb,
                h_out, h_in, act, gr, gb, normed, g_in, gm, g_out, vec,
                hin, hout, gin, gout, act_v, gr_v, gb_v, normed_v, up_v, down_v, o_v, w_out_v, gm_v,
                vec_v, ups_v, gmx, ld, st, send, recv, back_send, back_recv, x_send, x_recv):
    s, _, p, _, _ = place()
    halves = Link(gmx, gmx, x_send, x_recv)
    link = Link(hout, hin, send, recv)
    back = Link(gout, gin, back_send, back_recv)

    @pl.when(s == 2)
    def _():
        other = {"section": 3}
        loads = [local(o, o_v, ld.at[0]), local(h2, hin, ld.at[1]), local(w_out, w_out_v, ld.at[2])]
        start_all(loads)
        back.expect_from(other)
        link.ready()
        wait_all(loads)
        out = stores([(hout, h_out)], st)
        back_out = stores([(hout, h_out), (gin, g_in), (gb_v, gb), (gm_v, gm)], st)

        def step(i, r):
            out_proj_rows(o_v, hin, w_out_v, end[...], hout, r)
            link.copy(i, other).start()
            start_all(out(i))

        every_block(step)

        def back_step(i, r):
            back.arrived(i, other)
            gb_v[r, :] = mixed_back_block(gin[r, :], w_out_v, gm_v, r)
            for j in range(3):
                gmx[r, j * 128 : j * 128 + 128] = gm_v[3 + j, r, :].astype(F32)
            halves.copy(i, other).start()
            start_all(back_out(i)[1:])

        every_block(back_step)
        link.sent(other)
        halves.sent(other)
        for i in range(BLOCKS):
            wait_all(back_out(i))

    @pl.when(s == 3)
    def _():
        other = {"section": 2}
        loads = [local(up, up_v, ld.at[0]), local(down, down_v, ld.at[1]),
                 local(cot, gin, ld.at[2])]
        start_all(loads)
        link.expect_from(other)
        back.ready()
        wait_all(loads)
        vec_v[...] = jnp.zeros_like(vec_v)
        ups_v[...] = jnp.zeros_like(ups_v)
        out = stores([(hout, h_out), (hin, h_in), (act_v, act), (gr_v, gr), (gb_v, gb),
                      (normed_v, normed), (gout, g_out)], st)

        def step(i, r):
            link.arrived(i, other)
            h, g = hin[r, :], gin[r, :]
            xhat, _ = normalized(h)
            low = (xhat * gain[...] + shift[...]).astype(BF16)
            normed_v[r, :] = low
            g_low = g.astype(BF16)
            gb_v[r, :] = g_low
            hout[r, :] = h + end[...]
            gout[r, :] = jnp.zeros((BLOCK, D), F32)

            def chunks(c2, carry):
                total, grad_normed = hout[r, :], gout[r, :]
                for n in range(2):
                    cols = pl.ds(pl.multiple_of(c2 * 1536 + n * 768, 768), 768)
                    x = dot(low, up_v[:, cols]) + upb[:, cols]
                    active, steep = gelu_and_slope(x)
                    act_v[r, cols] = active
                    total = total + dot(active, down_v[cols, :])
                    raised = (dot(g_low, down_v[cols, :], 1, 1) * steep).astype(BF16)
                    gr_v[r, cols] = raised
                    ups_v[:, cols] += jnp.sum(raised.astype(F32), axis=0, keepdims=True)
                    grad_normed = grad_normed + dot(raised, up_v[:, cols], 1, 1)
                hout[r, :] = total
                gout[r, :] = grad_normed
                return carry

            lax.fori_loop(0, 2, chunks, 0)
            grad_normed = gout[r, :]
            result, xhat = norm_back(g, h, gain[...], grad_normed)
            gout[r, :] = result
            back.copy(i, other).start()
            add_row(vec_v, 0, grad_normed * xhat)
            add_row(vec_v, 1, grad_normed)
            add_row(vec_v, 2, g_low.astype(F32))
            start_all(out(i))

        every_block(step)
        for c in range(4):
            vec_v[3 + c : 4 + c, :] = ups_v[:, c * D : c * D + D]
        last = local(vec_v, vec, ld.at[3])
        last.start()


        def half_step(i, r):
            halves.arrived(i, other)
            for j in range(3):
                gm_v[j, r, :] = gmx[r, j * 128 : j * 128 + 128].astype(BF16)

        every_block(half_step)
        shared = local(gm_v.at[0:3], gm.at[0:3], ld.at[4])
        shared.start()
        back.sent(other)
        shared.wait()
        for i in range(BLOCKS):
            wait_all(out(i))
        last.wait()


def middle(o, h2, w_out, up, down, cot, gain, shift, end, upb):
    return staged(
        middle_body,
        [(WIDE, F32), (WIDE, F32), (HIDDEN, BF16), (HIDDEN, BF16), (WIDE, BF16), (WIDE, BF16),
         (WIDE, F32), (PAIRED, BF16), (WIDE, F32), ((8, D), F32)],
        (o, h2, w_out, up, down, cot),
        (gain, shift, end, upb),
        [(WIDE, F32)] * 4
        + [(HIDDEN, BF16), (HIDDEN, BF16), (WIDE, BF16), (WIDE, BF16), ((D, 3072), BF16),
           ((3072, D), BF16), (PAIRED, BF16), ((D, D), BF16), (PAIRED, BF16), ((8, D), F32),
           ((1, 3072), F32), ((ROWS, 384), F32)],
        7,
        3,
    )


def backward_body(g2, h, q, k, v, gm2, lse, w, up, down, slope, w_out, h_made, gain,
                  g_out, g_in, gr, gb, gm, vec, h_theirs, g_theirs, gq, gk, gv,
                  gin, gout, h_v, slope_v, gr_v, gb_v, up_v, down_v, gq_v, gk_v, gv_v, w_v, w_out_v,
                  gm_v, vec_v, ups_v, q_v, k_v, v_v, lse_v, ld, st, send, recv, next_send, next_recv,
                  x_send, x_recv):
    s, _, p, _, _ = place()
    theirs = {"tensor": 1 - p}
    partner = Link(gout, g_theirs, x_send, x_recv)
    made = remote(h_made, h_theirs, x_send.at[BLOCKS], x_recv.at[BLOCKS], theirs)
    first = Link(gout, gin, send, recv)
    second = Link(gout, gin, next_send, next_recv)

    heads = [local(a, b, ld.at[n]) for n, (a, b) in enumerate(
        ((q, q_v), (k, k_v), (v, v_v), (gm2, gm_v), (lse, lse_v)))]

    def share(i, device):
        at = pl.ds(pl.multiple_of(i * 384, 384), 384)
        return remote(slope_v.at[:, at], slope_v.at[:, at], next_send.at[i], next_recv.at[i], device)

    @pl.when(s >= 2)
    def _():
        start_all(heads)

        @pl.when(s == 2)
        def _():
            start_all([local(g2, gin, ld.at[5]), local(h, h_v, ld.at[6]), local(w, w_v, ld.at[7])])
            for device in (theirs, {"section": 3}):
                pl.semaphore_signal(
                    pltpu.get_barrier_semaphore(), inc=1, device_id=device, device_id_type=MESH)
            pl.semaphore_wait(pltpu.get_barrier_semaphore(), 2)
            made.start()

        pl.when(s == 3)(second.ready)
        wait_all(heads)

        def attend_step(i, carry):
            attend_back_pair(q_v, k_v, v_v, gm_v, lse_v, gq_v, gk_v, gv_v, i)

            @pl.when(s == 3)
            def _():
                for t, ref in enumerate((gq_v, gk_v, gv_v)):
                    at = pl.ds(pl.multiple_of(i * 384 + t * 128, 128), 128)
                    slope_v[:, at] = ref[i].astype(F32)
                share(i, {"section": 2}).start()

            return carry

        lax.fori_loop(0, 3, attend_step, 0)

    @pl.when(s == 3)
    def _():
        for i in range(3):
            share(i, {"section": 2}).wait_send()

    @pl.when(s == 2)
    def _():
        target = {"section": 1, "tensor": 1 - p}
        loads = [local(g2, gin, ld.at[5]), local(h, h_v, ld.at[6]), local(w, w_v, ld.at[7])]

        def take_step(i, carry):
            share(i, {"section": 3}).wait_recv()
            for t, ref in enumerate((gq_v, gk_v, gv_v)):
                at = pl.ds(pl.multiple_of(i * 384 + t * 128, 128), 128)
                ref[3 + i] = slope_v[:, at].astype(BF16)
            return carry

        lax.fori_loop(0, 3, take_step, 0)
        kept = [local(a, b, ld.at[n]) for n, (a, b) in enumerate(
            ((gq_v, gq), (gk_v, gk), (gv_v, gv)))]
        start_all(kept)
        wait_all(loads)
        vec_v[...] = jnp.zeros_like(vec_v)
        out = stores([(gout, g_out)], st)

        def step(i, r):
            parts = [(pairs_of((gq_v, gk_v), half, r), pairs_of((gv_v,), half, r))
                     for half in range(2)]
            gout[r, :] = qkv_back_rows(gin[r, :], h_v[r, :], gain[...], parts, w_v, vec_v)
            first.copy(i, target).start()
            start_all(out(i))

        every_block(step)
        last = local(vec_v, vec, ld.at[6])
        last.start()
        first.sent(target)
        made.wait()
        wait_all(kept)
        for i in range(BLOCKS):
            wait_all(out(i))
        last.wait()

    @pl.when(s == 1)
    def _():
        source, target = {"section": 2, "tensor": 1 - p}, {"section": 0}
        loads = [local(a, b, ld.at[n]) for n, (a, b) in enumerate(
            ((up, up_v), (down, down_v), (slope, slope_v), (h, h_v)))]
        start_all(loads)
        first.expect_from(source)
        pl.semaphore_signal(
            pltpu.get_barrier_semaphore(), inc=1, device_id=theirs, device_id_type=MESH)
        pl.semaphore_wait(pltpu.get_barrier_semaphore(), 2)
        wait_all(loads)
        vec_v[...] = jnp.zeros_like(vec_v)
        ups_v[...] = jnp.zeros_like(ups_v)
        out = stores([(gout, g_out), (gr_v, gr), (gb_v, gb)], st)

        def step(i, r):
            first.arrived(i, source)
            g = gin[r, :]
            g_low = g.astype(BF16)
            gb_v[r, :] = g_low
            gout[r, :] = jnp.zeros((BLOCK, D), F32)

            def chunk(c, carry):
                cols = pl.ds(pl.multiple_of(c * 768, 768), 768)
                raised = (dot(g_low, down_v[cols, :], 1, 1) * slope_v[r, cols]).astype(BF16)
                gr_v[r, cols] = raised
                ups_v[:, cols] += jnp.sum(raised.astype(F32), axis=0, keepdims=True)
                gout[r, :] += dot(raised, up_v[:, cols], 1, 1)
                return carry

            lax.fori_loop(0, 4, chunk, 0)
            grad_normed = gout[r, :]
            result, xhat = norm_back(g, h_v[r, :], gain[...], grad_normed)
            gout[r, :] = result
            second.copy(i, target).start()
            pl.when(i < BLOCKS - 1)(lambda: partner.copy(i, theirs).start())
            add_row(vec_v, 0, grad_normed * xhat)
            add_row(vec_v, 1, grad_normed)
            add_row(vec_v, 2, g_low.astype(F32))
            start_all(out(i))

        every_block(step)
        for c in range(4):
            vec_v[3 + c : 4 + c, :] = ups_v[:, c * D : c * D + D]
        last = local(vec_v, vec, ld.at[6])
        last.start()
        second.sent(target)
        for i in range(BLOCKS - 1):
            partner.copy(i, theirs).wait()
        for i in range(BLOCKS):
            wait_all(out(i))
        last.wait()

    @pl.when(s == 0)
    def _():
        source = {"section": 1}
        load = local(w_out, w_out_v, ld.at[0])
        load.start()
        second.expect_from(source)
        load.wait()
        out = stores([(gin, g_in), (gb_v, gb), (gm_v, gm)], st)

        def step(i, r):
            second.arrived(i, source)
            gb_v[r, :] = mixed_back_block(gin[r, :], w_out_v, gm_v, r)
            start_all(out(i))

        every_block(step)
        for i in range(BLOCKS):
            wait_all(out(i))


def backward(g2, h, q, k, v, gm, lse, w, up, down, slope, w_out, h_made, gain):
    return staged(
        backward_body,
        [(WIDE, F32), (WIDE, F32), (HIDDEN, BF16), (WIDE, BF16), (PAIRED, BF16), ((8, D), F32),
         (WIDE, F32), (WIDE, F32), (PAIRED, BF16), (PAIRED, BF16), (PAIRED, BF16)],
        (g2, h, q, k, v, gm, lse, w, up, down, slope, w_out, h_made),
        (gain,),
        [(WIDE, F32)] * 3
        + [(HIDDEN, F32), (HIDDEN, BF16), (WIDE, BF16), ((D, 3072), BF16), ((3072, D), BF16),
           (PAIRED, BF16), (PAIRED, BF16), (PAIRED, BF16), ((D, 2304), BF16), ((D, D), BF16),
           (PAIRED, BF16), ((8, D), F32), ((1, 3072), F32), (PAIRED, BF16), (PAIRED, BF16),
           (PAIRED, BF16), (LSE, F32)],
        3,
        4,
    )


def exchange_body(h, theirs, send, recv):
    s, _, p, _, _ = place()

    @pl.when(s < 2)
    def _():
        partner = {"tensor": 1 - p}
        greet([partner])
        copy = remote(h, theirs, send, recv, partner)
        copy.start()
        copy.wait()


def exchange(h):
    dma = pltpu.SemaphoreType.DMA
    any_spec = pl.BlockSpec(memory_space=ANY)
    return call(
        exchange_body, shape(WIDE, F32), [any_spec], any_spec,
        scratch=[dma, dma], collective_id=5, has_side_effects=True,
    )(h)


class Reduction:
    def __init__(self, acc, far, near, far2, near2, last, fin, sems):
        self.acc, self.far, self.near, self.far2, self.near2 = acc, far, near, far2, near2
        self.last, self.fin = last, fin
        self.send, self.recv = sems
        _, _, p, self.y, self.z = place()
        self.partner = {"tensor": 1 - p}

    def at(self, j, z_first):
        y, z = self.y, self.z
        along_z = [on_dp(y, (z + d) % 4) for d in (1, 3)]
        along_y = [on_dp((y + d) % 4, z) for d in (1, 3)]
        if z_first:
            return z, y, along_z, along_y, lambda h, i: self.acc.at[j, h, :, i], \
                lambda h, i: self.acc.at[j, h, i, z]
        return y, z, along_y, along_z, lambda h, i: self.acc.at[j, h, i], \
            lambda h, i: self.acc.at[j, h, y, i]

    def copies(self, j, z_first, stage):
        here, there, ring, ring2, part, part2 = self.at(j, z_first)
        both = slice(0, 2)

        def pair(sources, target, peers):
            return [
                remote(sources[n], target.at[j, n], self.send.at[j, stage, n],
                       self.recv.at[j, stage, n], peers[n])
                for n in range(2)
            ]

        if stage == 0:
            return pair([part(0, (here + 2) % 4), part(1, (here + 2) % 4)], self.far, ring)
        if stage == 1:
            return pair([part(both, (here + 1) % 4), part(both, (here + 3) % 4)], self.near, ring)
        if stage == 2:
            return pair([part2(0, (there + 2) % 4), part2(1, (there + 2) % 4)], self.far2, ring2)
        if stage == 3:
            return pair([part2(both, (there + 1) % 4), part2(both, (there + 3) % 4)], self.near2,
                        ring2)
        return [remote(self.fin.at[j, 1], self.last.at[j], self.send.at[j, 4, 0],
                       self.recv.at[j, 4, 0], self.partner)]

    def step(self, j, z_first, stage, put):
        here, there, _, _, part, part2 = self.at(j, z_first)
        if stage > 0:
            for copy in self.copies(j, z_first, stage - 1):
                copy.wait_recv()
        if stage == 1:
            def add_far(i, carry):
                for n, d in ((0, 1), (1, 3)):
                    ref = part(n, (here + d) % 4)
                    ref[i] = ref[i] + self.far[j, n, i]
                return carry

            lax.fori_loop(0, 4, add_far, 0)
        if stage == 2:
            def add_near(i, carry):
                for h in range(2):
                    ref = part(h, here)
                    ref[i] = ref[i] + (self.near[j, 0, h, i] + self.near[j, 1, h, i])
                return carry

            lax.fori_loop(0, 4, add_near, 0)
        if stage == 3:
            for n, d in ((0, 1), (1, 3)):
                ref = part2(n, (there + d) % 4)
                ref[...] = ref[...] + self.far2[j, n]
        if stage == 4:
            for h in range(2):
                ref = part2(h, there)
                self.fin[j, h] = ref[...] + (self.near2[j, 0, h] + self.near2[j, 1, h])
        if stage == 5:
            put(j, self.fin[j, 0] + self.last[j])
        else:
            start_all(self.copies(j, z_first, stage))

    def sent(self, j, z_first):
        for stage in range(5):
            for copy in self.copies(j, z_first, stage):
                copy.wait_send()


def reduction_scratch(jobs, width):
    dma = pltpu.SemaphoreType.DMA
    return [
        pltpu.VMEM((jobs, 2, 4, 4, 48, width), F32),
        pltpu.VMEM((jobs, 2, 4, 48, width), F32),
        pltpu.VMEM((jobs, 2, 2, 4, 48, width), F32),
        pltpu.VMEM((jobs, 2, 48, width), F32),
        pltpu.VMEM((jobs, 2, 2, 48, width), F32),
        pltpu.VMEM((jobs, 48, width), F32),
        pltpu.VMEM((jobs, 2, 48, width), F32),
        dma((jobs, 5, 2)),
        dma((jobs, 5, 2)),
    ]


class Sums:
    def __init__(self, va, v1, v2, vec, send, recv):
        self.va, self.v1, self.v2, self.vec, self.send, self.recv = va, v1, v2, vec, send, recv
        _, _, p, y, z = place()
        self.partner = {"tensor": 1 - p}
        self.peers = [on_dp(y, (z + d) % 4) for d in range(1, 4)], \
            [on_dp((y + d) % 4, z) for d in range(1, 4)]

    def copies(self, stage):
        if stage == 2:
            return [remote(self.vec.at[0], self.vec.at[1], self.send.at[6], self.recv.at[6],
                           self.partner)]
        held = self.v1 if stage == 0 else self.v2
        return [
            remote(self.va.at[stage], held.at[d], self.send.at[3 * stage + d],
                   self.recv.at[3 * stage + d], self.peers[stage][d])
            for d in range(3)
        ]

    def step(self, stage):
        if stage > 0:
            for copy in self.copies(stage - 1):
                copy.wait()
        if stage == 1:
            self.va[1] = self.va[0] + (self.v1[0] + self.v1[1] + self.v1[2])
        if stage == 2:
            self.vec[0] = self.va[1] + (self.v2[0] + self.v2[1] + self.v2[2])
        if stage < 3:
            start_all(self.copies(stage))


def sums_scratch():
    dma = pltpu.SemaphoreType.DMA
    return [pltpu.VMEM((2, 8, D), F32), pltpu.VMEM((3, 8, D), F32), pltpu.VMEM((3, 8, D), F32),
            dma((7,)), dma((7,))]


def greet_all():
    _, _, p, y, z = place()
    peers = [{"tensor": 1 - p}]
    peers += [on_dp(y, (z + d) % 4) for d in range(1, 4)]
    peers += [on_dp((y + d) % 4, z) for d in range(1, 4)]
    for peer in peers:
        pl.semaphore_signal(
            pltpu.get_barrier_semaphore(), inc=1, device_id=peer, device_id_type=MESH)


def met():
    pl.semaphore_wait(pltpu.get_barrier_semaphore(), 7)


def job_terms(acc, j, left_t, x_of):
    width = acc.shape[5]

    def step(i, carry):
        half, y = i // 4, i % 4
        rows = pl.ds(pl.multiple_of(y * 192, 192), 192)
        acc[j, half, y] = dot(left_t[rows, :], x_of(half)[...]).reshape(4, 48, width)
        return carry

    lax.fori_loop(0, 8, step, 0)


def attn_finish_body(q0, k0, v0, gm0, lse0, o0, gb0, n0, gq2, gk2, gv2, o2, gb2, n2, g_in, h, w, v2,
                     g2, gain,
                     g_theirs, g_own, out, vec,
                     *scratch):
    red = Reduction(*scratch[:7], scratch[7:9])
    sums = Sums(*scratch[9:12], vec, *scratch[12:14])
    (x_v, o_v, low_v, left_t, gin_v, h_v, gout, w_v, q_v, k_v, v_v, gm_v, lse_v, gq_v, gk_v, gv_v,
     xl, ol, ld, st, send, recv) = scratch[14:]
    s, _, p, _, _ = place()
    partner = {"tensor": 1 - p}
    vec_ref = sums.va.at[0]

    def put(j, result):
        if j == 0:
            out[:, 1152:1536] = result
        else:
            for t in range(3):
                at = t * 384 + (j - 1) * 128
                out[:, at : at + 128] = result[:, t * 128 : t * 128 + 128]

    def low_loads(normed, gb):
        return [local(normed, low_v.at[0], ld.at[0]), local(gb, low_v.at[1], ld.at[1])]

    def lanes(n):
        return pl.ds(pl.multiple_of(n * 128, 128), 128)

    def each_pair(act):
        def step(pair, carry):
            act(pair)
            return carry

        lax.fori_loop(0, PAIRS, step, 0)

    def o_load(o, pair):
        return local(o.at[pair], o_v.at[pair // 3, :, lanes(pair % 3)], ol.at[pair])

    def attention_loads():
        return [local(a, b, ld.at[6 + n]) for n, (a, b) in enumerate(
            ((q0, q_v), (k0, k_v), (v0, v_v), (gm0, gm_v), (lse0, lse_v)))]

    def grad_loads(pair):
        return [local(ref.at[pair], x_v.at[pair % 3, pair // 3, :, pl.ds(t * 128, 128)],
                      xl.at[t, pair])
                for t, ref in enumerate((gq2, gk2, gv2))]

    def more_loads():
        return [local(g_in, gin_v, ld.at[2]), local(h, h_v, ld.at[3]), local(w, w_v, ld.at[4])]

    def early_sums():
        return local(v2, vec_ref, ld.at[5])

    @pl.when(s == 0)
    def _():
        each_pair(lambda pair: o_load(o0, pair).start())
        start_all(low_loads(n0, gb0) + attention_loads() + more_loads())

    @pl.when(s == 2)
    def _():
        start_all(low_loads(n2, gb2))
        each_pair(lambda pair: start_all([o_load(o2, pair)] + grad_loads(pair)))
        early_sums().start()

    def swap(i):
        r = block(i)
        return remote(gout.at[r], g_theirs.at[r], send.at[i], recv.at[i], partner)

    swap2 = remote(g2, g_theirs, send.at[0], recv.at[0], partner)

    def keep(i):
        r = block(i)
        return local(gout.at[r], g_own.at[r], st.at[i])

    def rows():
        def step(i, carry):
            r = block(i)
            pl.when(i == 2)(lambda: take((3, 1), (2, 2), (1, 3), (0, 4)))
            parts = [(pairs_of((gq_v, gk_v), half, r), pairs_of((gv_v,), half, r))
                     for half in range(2)]
            gout[r, :] = qkv_back_rows(gin_v[r, :], h_v[r, :], gain[...], parts, w_v, vec_ref)
            swap(i).start()
            keep(i).start()
            return carry

        lax.fori_loop(0, BLOCKS, step, 0)

    def take(*steps):
        for j, stage in steps:
            red.step(j, j % 2 == 0, stage, put)

    @pl.when(s % 2 == 0)
    def _():
        greet_all()
        for n, load in enumerate(low_loads(n0, gb0)):
            load.wait()
            left_t[n] = low_v[n].T
        each_pair(lambda pair: o_load(o0, pair).wait())
        met()

        @pl.when(s == 0)
        def _():
            sums.va[0] = jnp.zeros((8, D), F32)
            wait_all(attention_loads())

        @pl.when(s == 2)
        def _():
            swap2.start()
            early_sums().wait()
            each_pair(lambda pair: wait_all(grad_loads(pair)))

        job_terms(red.acc, 0, left_t.at[1], lambda half: o_v.at[half])
        take((0, 0))

        def pair_step(i, carry):
            @pl.when(s == 0)
            def _():
                def one(half, carry):
                    pair = half * 3 + i
                    attend_back_pair(q_v, k_v, v_v, gm_v, lse_v, gq_v, gk_v, gv_v, pair)
                    for t, ref in enumerate((gq_v, gk_v, gv_v)):
                        x_v[i, half, :, t * 128 : t * 128 + 128] = ref[pair]
                    return carry

                lax.fori_loop(0, 2, one, 0)

            job_terms(red.acc, 1 + i, left_t.at[0], lambda half: x_v.at[i, half])
            pl.when(i == 0)(lambda: take((1, 0), (0, 1)))
            pl.when(i == 1)(lambda: take((2, 0), (1, 1), (0, 2)))
            pl.when(i == 2)(lambda: take((3, 0), (2, 1), (1, 2), (0, 3)))
            return carry

        lax.fori_loop(0, 3, pair_step, 0)
        @pl.when(s == 0)
        def _():
            wait_all(more_loads())
            rows()

        pl.when(s == 2)(lambda: take((3, 1), (2, 2), (1, 3), (0, 4)))

        sums.step(0)
        take((3, 2), (2, 3), (1, 4), (0, 5))
        sums.step(1)
        take((3, 3), (2, 4), (1, 5))
        sums.step(2)
        take((3, 4), (2, 5))
        take((3, 5))
        sums.step(3)
        for j in range(4):
            red.sent(j, j % 2 == 0)

        pl.when(s == 2)(swap2.wait)

        @pl.when(s == 0)
        def _():
            for i in range(BLOCKS):
                swap(i).wait()
                keep(i).wait()


def attn_finish(first, last, rest, gain):
    dma = pltpu.SemaphoreType.DMA
    any_spec = pl.BlockSpec(memory_space=ANY)
    vmem = pl.BlockSpec(memory_space=pltpu.VMEM)
    paired = pltpu.VMEM(PAIRED, BF16)
    return call(
        attn_finish_body,
        (shape(WIDE, F32), shape(WIDE, F32), shape((48, 1536), F32), shape((2, 8, D), F32)),
        [any_spec] * 19 + [vmem],
        (any_spec, any_spec, vmem, vmem),
        scratch=reduction_scratch(4, 384) + sums_scratch() + [
            pltpu.VMEM((3, 2, ROWS, 384), BF16), pltpu.VMEM((2, ROWS, 384), BF16),
            pltpu.VMEM((2,) + WIDE, BF16), pltpu.VMEM((2, D, ROWS), BF16), pltpu.VMEM(WIDE, F32),
            pltpu.VMEM(WIDE, F32), pltpu.VMEM(WIDE, F32), pltpu.VMEM((D, 2304), BF16),
            paired, paired, paired, paired, pltpu.VMEM((PAIRS, 8, ROWS), F32),
            paired, paired, paired,
            dma((3, PAIRS)), dma((PAIRS,)), dma((11,)), dma((BLOCKS,)), dma((BLOCKS,)),
            dma((BLOCKS,)),
        ],
        collective_id=20,
        has_side_effects=True,
    )(*first, *last, *rest, gain)


def ff_finish_body(gr1, act1, gb1, n1, gr3, act3, gb3, n3, g1, g3, v1, v3, h3,
                   g_theirs, g3_theirs, h3_theirs, out, vec,
                   *scratch):
    red = Reduction(*scratch[:7], scratch[7:9])
    sums = Sums(*scratch[9:12], vec, *scratch[12:14])
    x_v, low_v, left_t, ld, xs, xr, vl, hs, hr = scratch[14:]
    s, _, p, _, _ = place()
    partner = {"tensor": 1 - p}
    jobs = ((True, 0), (False, 2 * CHUNK), (True, CHUNK), (False, 3 * CHUNK))

    def put(j, result):
        out[:, jobs[j][1] : jobs[j][1] + CHUNK] = result

    def load(t, gr, act):
        z_first, column = jobs[t]
        x = gr if z_first else act
        at = column % (2 * CHUNK)
        return [
            local(x.at[:, half * 2 * CHUNK + at : half * 2 * CHUNK + at + CHUNK],
                  x_v.at[t % 2, half], ld.at[t % 2, half])
            for half in range(2)
        ]

    def start_load(t):
        pl.when(s == 1)(lambda: start_all(load(t, gr1, act1)))
        pl.when(s == 3)(lambda: start_all(load(t, gr3, act3)))

    def small(normed, gb, vecs):
        return [local(normed, low_v.at[0], vl.at[0]), local(gb, low_v.at[1], vl.at[1]),
                local(vecs, sums.va.at[0], vl.at[2])]

    swap = remote(g1.at[pl.ds(ROWS - BLOCK, BLOCK)], g_theirs, xs, xr, partner)
    swap3 = [remote(g3, g3_theirs, xs, xr, partner),
             remote(h3, h3_theirs, hs, hr, partner)]

    @pl.when(s % 2 == 1)
    def _():
        pl.when(s == 1)(lambda: start_all(small(n1, gb1, v1)))
        pl.when(s == 3)(lambda: start_all(small(n3, gb3, v3)))
        greet_all()
        start_load(0)
        start_load(1)
        smalls = small(n1, gb1, v1)
        for n in range(2):
            smalls[n].wait()
            left_t[n] = low_v[n].T
        met()
        pl.when(s == 1)(swap.start)
        pl.when(s == 3)(lambda: start_all(swap3))
        smalls[2].wait()
        def take(t):
            for stage in range(6):
                if 0 <= t - stage < 4:
                    red.step(t - stage, jobs[t - stage][0], stage, put)

        def compute(t, carry):
            slot = t % 2
            for half in range(2):
                local(gr1.at[:, 0:CHUNK], x_v.at[slot, half], ld.at[slot, half]).wait()
            job_terms(red.acc, t, left_t.at[slot], lambda half: x_v.at[slot, half])
            for n in range(4):
                @pl.when(t == n)
                def _(n=n):
                    if n < 2:
                        start_load(n + 2)
                    if n < 3:
                        sums.step(n)
                    take(n)
            return carry

        lax.fori_loop(0, 4, compute, 0)
        for t in range(4, 9):
            take(t)
        sums.step(3)
        for j in range(4):
            red.sent(j, jobs[j][0])
        pl.when(s == 1)(swap.wait)
        pl.when(s == 3)(lambda: wait_all(swap3))


def ff_finish(first, last, rest):
    dma = pltpu.SemaphoreType.DMA
    any_spec = pl.BlockSpec(memory_space=ANY)
    vmem = pl.BlockSpec(memory_space=pltpu.VMEM)
    return call(
        ff_finish_body,
        (shape((BLOCK, D), F32), shape(WIDE, F32), shape(WIDE, F32), shape((48, 4 * CHUNK), F32),
         shape((2, 8, D), F32)),
        [any_spec] * 13,
        (any_spec, any_spec, any_spec, vmem, vmem),
        scratch=reduction_scratch(4, CHUNK) + sums_scratch() + [
            pltpu.VMEM((2, 2, ROWS, CHUNK), BF16), pltpu.VMEM((2,) + WIDE, BF16),
            pltpu.VMEM((2, D, ROWS), BF16),
            dma((2, 2)), dma, dma, dma((3,)), dma, dma,
        ],
        collective_id=21,
        has_side_effects=True,
    )(*first, *last, *rest)


def block_rows(i):
    return slice(i * BLOCK, min((i + 1) * BLOCK, LENGTH))


def load_block(mine, theirs, a_v, b_v, sems, i):
    r = pl.ds(i * BLOCK, BLOCK)
    return [local(mine.at[r], a_v.at[r], sems.at[0, i]),
            local(theirs.at[r], b_v.at[r], sems.at[1, i])]


def load_blocks(mine, theirs, a_v, b_v, sems, last=None):
    def step(i, carry):
        start_all(load_block(mine, theirs, a_v, b_v, sems, i))
        return carry

    lax.fori_loop(0, BLOCKS if last is None else BLOCKS - 1, step, 0)
    if last is not None:
        r = pl.ds(ROWS - BLOCK, BLOCK)
        local(mine.at[r], a_v.at[r], sems.at[0, BLOCKS - 1]).start()
        local(last, b_v.at[r], sems.at[1, BLOCKS - 1]).start()


def store_block(o_v, out, sems, i):
    r = block_rows(i) if isinstance(i, int) else block(i)
    return local(o_v.at[r], out.at[r], sems.at[2, i])


def write_block(a_v, b_v, o_v, sems, first, i):
    wait_all(load_block(a_v, b_v, a_v, b_v, sems, i))
    r = block_rows(i) if isinstance(i, int) else block(i)
    a, b = a_v[r, :], b_v[r, :]
    o_v[r, 0, :] = jnp.where(first, a, b)
    o_v[r, 1, :] = jnp.where(first, b, a)


def write_blocks(a_v, b_v, o_v, sems, first, out):
    def step(i, carry):
        write_block(a_v, b_v, o_v, sems, first, i)
        store_block(o_v, out, sems, i).start()
        return carry

    lax.fori_loop(0, BLOCKS - 1, step, 0)
    write_block(a_v, b_v, o_v, sems, first, BLOCKS - 1)
    store_block(o_v, out, sems, BLOCKS - 1).start()
    for i in range(BLOCKS):
        store_block(o_v, out, sems, i).wait()


def early_body(hf, h_theirs, out, a_v, b_v, o_v, sems):
    s, _, p, _, _ = place()

    @pl.when(s < 2)
    def _():
        load_blocks(hf, h_theirs, a_v, b_v, sems)
        write_blocks(a_v, b_v, o_v, sems, p == 0, out)


BOTH = (LENGTH, 2, D)


def early(hf, h_theirs):
    any_spec = pl.BlockSpec(memory_space=ANY)
    return call(
        early_body,
        shape(BOTH, F32),
        [any_spec] * 2,
        any_spec,
        scratch=[pltpu.VMEM(WIDE, F32), pltpu.VMEM(WIDE, F32), pltpu.VMEM(BOTH, F32),
                 pltpu.SemaphoreType.DMA((3, BLOCKS))],
    )(hf, h_theirs)


def small_outputs(attn_sums, ff_sums, attn_vec, ff_vec, rows3, qkv_g, qv_g, out_g, up_g, upb_g,
                  down_g):
    s, r, _, _, _ = place()
    at = lax.broadcasted_iota(jnp.int32, (D, 48), 0)
    pick = jnp.where(at == lax.broadcasted_iota(jnp.int32, (D, 48), 1) + r * 48, 1.0, 0.0)

    def picked(vec):
        rows3[...] = lax.dot_general(
            vec[0] + vec[1], pick, (((1,), (0,)), ((), ())), precision=lax.Precision.HIGHEST,
            preferred_element_type=F32)

    @pl.when(s % 2 == 0)
    def _():
        picked(attn_vec)
        for t in range(3):
            qkv_g[t] = attn_sums[:, t * 384 : t * 384 + 384]
        out_g[...] = attn_sums[:, 1152:1536]
        qv_g[...] = attn_vec[0, 3:5, 0:384] + attn_vec[1, 3:5, 384:768]
        for ref in (up_g, upb_g, down_g):
            ref[...] = jnp.zeros(ref.shape, F32)

    @pl.when(s % 2 == 1)
    def _():
        picked(ff_vec)
        up_g[...] = ff_sums[:, 0:1536]
        down_g[...] = ff_sums[:, 1536:3072]
        for n in range(2):
            upb_g[:, n * D : n * D + D] = ff_vec[0, 3 + n : 4 + n, :] + ff_vec[1, 5 + n : 6 + n, :]
        for ref in (qkv_g, out_g, qv_g):
            ref[...] = jnp.zeros(ref.shape, F32)


def assemble_body(hid_in, hm, h2, h3, g0, gb, gm, ga, gb_theirs, gf, g3, attn_sums, ff_sums, attn_vec,
                  ff_vec, hid, gin, rows3, qkv_g, qv_g, out_g, up_g, upb_g, down_g, a_v, b_v, o_v,
                  sems):
    s, _, p, _, _ = place()
    first = jnp.where(s < 2, p, 1 - p) == 0

    def load(n, mine, theirs, last=None):
        load_blocks(mine, theirs, a_v.at[n], b_v.at[n], sems.at[n], last)

    pl.when(s == 0)(lambda: load(0, g0, ga))
    pl.when(s == 1)(lambda: load(0, gb, gb_theirs, gf))

    @pl.when(s == 2)
    def _():
        load(0, gb, ga)
        load(1, hm, h2)

    @pl.when(s == 3)
    def _():
        load(0, gm, g3)
        load(1, hm, h3)

    small_outputs(attn_sums, ff_sums, attn_vec, ff_vec, rows3, qkv_g, qv_g, out_g, up_g, upb_g,
                  down_g)

    def write(n, carry):
        def step(i, carry):
            write_block(a_v.at[n], b_v.at[n], o_v.at[n], sems.at[n], first, i)
            pl.when(n == 0)(lambda: store_block(o_v.at[n], gin, sems.at[n], i).start())
            pl.when(n == 1)(lambda: store_block(o_v.at[n], hid, sems.at[n], i).start())
            return carry

        lax.fori_loop(0, BLOCKS - 1, step, 0)
        write_block(a_v.at[n], b_v.at[n], o_v.at[n], sems.at[n], first, BLOCKS - 1)
        pl.when(n == 0)(lambda: store_block(o_v.at[n], gin, sems.at[n], BLOCKS - 1).start())
        pl.when(n == 1)(lambda: store_block(o_v.at[n], hid, sems.at[n], BLOCKS - 1).start())
        return carry

    lax.fori_loop(0, jnp.where(s < 2, 1, 2), write, 0)
    for i in range(BLOCKS):
        store_block(o_v.at[0], gin, sems.at[0], i).wait()
        pl.when(s >= 2)(lambda i=i: store_block(o_v.at[1], hid, sems.at[1], i).wait())


def assemble(*operands):
    any_spec = pl.BlockSpec(memory_space=ANY)
    vmem = pl.BlockSpec(memory_space=pltpu.VMEM)
    return call(
        assemble_body,
        (shape(BOTH, F32), shape(BOTH, F32), shape((8, 48), F32), shape((3, 48, 384), F32),
         shape((2, 384), F32), shape((48, 384), F32), shape((48, 1536), F32),
         shape((1, 1536), F32), shape((48, 1536), F32)),
        [any_spec] * 11 + [vmem] * 4,
        (any_spec, any_spec) + (vmem,) * 7,
        scratch=[pltpu.VMEM((2,) + WIDE, F32), pltpu.VMEM((2,) + WIDE, F32),
                 pltpu.VMEM((2,) + BOTH, F32), pltpu.SemaphoreType.DMA((2, 3, BLOCKS))],
        aliases={0: 0},
    )(*operands)


def unwritten(shapes):
    any_spec = pl.BlockSpec(memory_space=ANY)
    return pl.pallas_call(
        lambda *refs: None,
        out_shape=tuple(shapes),
        out_specs=(any_spec,) * len(shapes),
    )()


def only_at(active, run, operands):
    like = jax.eval_shape(run, *operands)
    leaves, tree = jax.tree.flatten(like)

    def skip(*_):
        return jax.tree.unflatten(tree, unwritten([shape(x.shape, x.dtype) for x in leaves]))

    return lax.cond(active, run, skip, *operands)


def per_device(inputs, cotangent, norm_gain, norm_bias, qkv_weight, qv_bias, out_weight, end_bias,
               up_weight, up_bias, down_weight):
    s, r, p = lax.axis_index("section"), lax.axis_index("dp"), lax.axis_index("tensor")
    qkv, out_w, up, down = qkv_weight[0], out_weight[0], up_weight[0], down_weight[0]

    gain, shift, end = norm_gain, norm_bias, end_bias
    attn = s % 2 == 0
    by_row = [jnp.transpose(x, (1, 0, 2)) for x in (inputs, cotangent)]
    w, w_out, w_up, w_down, h0, normed0, q0, k0, v0, o0, lse0, qkvb, upb = opening(
        qkv, out_w, up, down, by_row[0], qv_bias[0], up_bias, gain, shift)
    cot = only_at(s == 3, lambda x: (extract(x),), (by_row[1],))[0]
    hf, h_in, act1, slope1, normed_f, q2, k2, v2, o2, lse2 = forward(
        o0, h0, w_out, w_up, w_down, w, gain, shift, end, upb, qkvb)
    h_early = exchange(hf)
    hid_early = early(hf, h_early)
    o2, hid_early = lax.optimization_barrier((o2, hid_early))
    hm, _, act3, gr3, gb_m, normed3, g2, gm2, g_m, vec_m = middle(
        o2, h_in, w_out, w_up, w_down, cot, gain, shift, end, upb)
    g_b, g_in0, gr1, gb_b, gm0, vec_b, h2_theirs, gb_theirs, gq2, gk2, gv2 = backward(
        g2, h_in, q2, k2, v2, gm2, lse2, w, w_up, w_down, slope1, w_out, hm, gain)

    gb_m, vec_b = lax.optimization_barrier((gb_m, vec_b))
    g1_theirs, g3_theirs, h3_theirs, ff_sums, ff_vec = ff_finish(
        (gr1, act1, gb_b, normed_f), (gr3, act3, gb_m, normed3), (g_b, g_m, vec_b, vec_m, hm))
    g1_theirs, gb_last = lax.optimization_barrier((g1_theirs, gb_b))
    ga_theirs, g_0, attn_sums, attn_vec = attn_finish(
        (q0, k0, v0, gm0, lse0, o0, gb_last, normed0), (gq2, gk2, gv2, o2, gb_m, normed_f),
        (g_in0, h0, w, vec_b, g_b), gain)
    hid, gin, rows3, qkv_g, qv_g, out_g, up_g, upb_g, down_g = assemble(
        hid_early, hm, h2_theirs, h3_theirs, g_0, g_b, g_m, ga_theirs, gb_theirs, g1_theirs,
        g3_theirs, attn_sums, ff_sums, attn_vec, ff_vec)
    hid, gin = [jnp.transpose(x, (1, 0, 2))[None] for x in (hid, gin)]
    return (hid, gin, rows3[0:1], rows3[1:2], qkv_g[None], qv_g[None], out_g.T[None], rows3[2:3],
            up_g[None], upb_g, down_g.T[None])


def solution(mesh):
    return jax.shard_map(
        per_device,
        mesh=mesh,
        in_specs=(
            P("dp", None, None),
            P("dp", None, None),
            P("section", None),
            P("section", None),
            P("section", None, None, "tensor"),
            P("section", None, "tensor"),
            P("section", "tensor", None),
            P("section", None),
            P("section", None, "tensor"),
            P("section", "tensor"),
            P("section", "tensor", None),
        ),
        out_specs=(
            P("section", "dp", None, None),
            P("section", "dp", None, None),
            P("section", "dp"),
            P("section", "dp"),
            P("section", None, "dp", "tensor"),
            P("section", None, "tensor"),
            P("section", "tensor", "dp"),
            P("section", "dp"),
            P("section", "dp", "tensor"),
            P("section", "tensor"),
            P("section", "tensor", "dp"),
        ),
        check_vma=False,
    )
```

```python
import functools

import jax
import jax.numpy as jnp
from jax import lax
from jax.experimental import pallas as pl
from jax.experimental.pallas import tpu as pltpu
from jax.sharding import PartitionSpec as P

MESH = pl.DeviceIdType.MESH
ANY = pl.ANY
F32 = jnp.float32
BF16 = jnp.bfloat16

HEAD_DIM = 64
EPS = 1e-06
LENGTH = 866
ROWS = 896
BLOCK = 224
D = 768
PAIRS = 6
Q_BLOCKS = ((0, 384), (384, 512))
VMEM_BYTES = 60 * 1024 * 1024

CHUNK = 768


def call(body, out_shape, in_specs, out_specs, grid=(), scratch=(), aliases={}, **more):
    return pl.pallas_call(
        body,
        out_shape=out_shape,
        grid=grid,
        in_specs=in_specs,
        out_specs=out_specs,
        scratch_shapes=scratch,
        input_output_aliases=aliases,
        compiler_params=pltpu.CompilerParams(vmem_limit_bytes=VMEM_BYTES, **more),
    )


def shape(dims, dtype):
    return jax.ShapeDtypeStruct(dims, dtype)


def whole(*dims):
    return pl.BlockSpec(dims, lambda *_: (0,) * len(dims), pipeline_mode=pl.Buffered(1))


def rows_of(width):
    return pl.BlockSpec((BLOCK, width), lambda i: (i, 0))


def dot(a, b, ca=1, cb=0):
    return lax.dot_general(a, b, (((ca,), (cb,)), ((), ())), preferred_element_type=F32)


def normalized(h):
    average = jnp.mean(h, axis=-1, keepdims=True)
    centred = h - average
    spread = jnp.mean(centred * centred, axis=-1, keepdims=True)
    r = lax.rsqrt(spread + EPS)
    return centred * r, r


def norm_back(g, h, gain, grad_normed):
    xhat, r = normalized(h)
    t = grad_normed * gain
    t_mean = jnp.mean(t, axis=-1, keepdims=True)
    tx_mean = jnp.mean(t * xhat, axis=-1, keepdims=True)
    return g + r * (t - t_mean - xhat * tx_mean), xhat


def block(i):
    return pl.ds(pl.multiple_of(i * BLOCK, 32), BLOCK)


def gelu_and_slope(x):
    phi = 0.5 * (1.0 + lax.erf(x * 0.7071067811865476))
    density = jnp.exp(-0.5 * x * x) * 0.3989422804014327
    return (x * phi).astype(BF16), phi + x * density


def qkv_block(h, gain, shift, w_ref, bias, q_ref, k_ref, v_ref, normed_ref, r):
    xhat, _ = normalized(h)
    normed_ref[r, :] = (xhat * gain + shift).astype(BF16)

    def half_step(half, carry):
        cols = pl.ds(pl.multiple_of(half * 1152, 128), 1152)
        part = (dot(normed_ref[r, :], w_ref[:, cols]) + bias[:, cols]).astype(BF16)
        for n in range(9):
            lanes = part[:, n * 128 : n * 128 + 128]
            pair = half * 3 + n % 3
            if n < 3:
                q_ref[pair, r, :] = (lanes.astype(F32) * 0.125).astype(BF16)
            elif n < 6:
                k_ref[pair, r, :] = lanes
            else:
                v_ref[pair, r, :] = lanes
        return carry

    lax.fori_loop(0, 2, half_step, 0)


def joined(ref, r):
    return jnp.concatenate([ref[j, r, :] for j in range(PAIRS)], axis=1)


def mixed_back_block(g, w_out_ref, gm_ref, r):
    gb = g.astype(BF16)
    gm = dot(gb, w_out_ref[...], 1, 1).astype(BF16)
    for j in range(PAIRS):
        gm_ref[j, r, :] = gm[:, j * 128 : j * 128 + 128]
    return gb


def add_row(vec_ref, at, values):
    vec_ref[at : at + 1, :] += jnp.sum(values, axis=0, keepdims=True)


def qkv_back_rows(g, h, gain, parts, w_ref, vec_ref):
    grad_normed = jnp.zeros((BLOCK, D), F32)
    for half, (qk, v) in enumerate(parts):
        part = jnp.concatenate([qk, v], axis=1)
        grad_normed = grad_normed + dot(part, w_ref[:, half * 1152 : half * 1152 + 1152], 1, 1)
    out, xhat = norm_back(g, h, gain, grad_normed)
    add_row(vec_ref, 0, grad_normed * xhat)
    add_row(vec_ref, 1, grad_normed)
    add_row(vec_ref, 2, g.astype(BF16).astype(F32))
    add_row(vec_ref, 3, jnp.concatenate([qk[:, :384] for qk, _ in parts], axis=1).astype(F32))
    add_row(vec_ref, 4, jnp.concatenate([v for _, v in parts], axis=1).astype(F32))
    return out


def pairs_of(refs, half, r):
    return jnp.concatenate([ref[half * 3 + i, r, :] for ref in refs for i in range(3)], axis=1)


def head_mask(dims, axis, head):
    at = lax.broadcasted_iota(jnp.int32, dims, axis)
    return at < HEAD_DIM if head == 0 else at >= HEAD_DIM


def with_lanes(x, head, columns):
    lane = lax.broadcasted_iota(jnp.int32, x.shape, 1)
    own, spare = (lane < HEAD_DIM, HEAD_DIM) if head == 0 else (lane >= HEAD_DIM, 0)
    out = jnp.where(own, x, 0)
    for n, column in enumerate(columns):
        out = jnp.where(lane == spare + n, column, out)
    return out


def in_pieces(x):
    high = x.astype(BF16)
    rest = x - high.astype(F32)
    middle = rest.astype(BF16)
    return [high, middle, (rest - middle.astype(F32)).astype(BF16)]


def key_bias():
    row = lax.broadcasted_iota(jnp.int32, (ROWS, 1), 0)
    return jnp.where(row < LENGTH, 0.0, -1e30).astype(BF16)


def attend_pair(q_ref, k_ref, v_ref, o_ref, lse_ref, j):
    one = jnp.ones((1, 1), BF16)
    q, k, v_t = q_ref[j], k_ref[j], v_ref[j].T
    out = jnp.zeros((128, ROWS), F32)
    rows = []
    for head in range(2):
        s = dot(with_lanes(k, head, [key_bias()]), with_lanes(q, head, [one]), 1, 1)
        top = jnp.max(s, axis=0, keepdims=True)
        e = jnp.exp(s - top)
        total = jnp.sum(e, axis=0, keepdims=True)
        p = (e * (1.0 / total)).astype(BF16)
        out = out + dot(jnp.where(head_mask(v_t.shape, 0, head), v_t, 0), p)
        rows.append(top + jnp.log(total))
    o_ref[j] = out.T.astype(BF16)
    lse_ref[j] = jnp.concatenate(rows + [jnp.zeros((6, ROWS), F32)], axis=0)


def attend_back_pair(q_ref, k_ref, v_ref, gm_ref, lse_ref, gq_ref, gk_ref, gv_ref, j):
    one = jnp.ones((1, 1), BF16)
    k, v = k_ref[j], v_ref[j]
    k_t = k.T
    k_heads = [jnp.where(head_mask(k_t.shape, 0, head), k_t, 0) for head in range(2)]
    k_lanes = [with_lanes(k, head, [one, one, one, key_bias()]) for head in range(2)]
    lse_columns = lse_ref[j].T
    grad_k = jnp.zeros((ROWS, 128), F32)
    grad_v = jnp.zeros((ROWS, 128), F32)
    for start, size in Q_BLOCKS:
        rows = slice(start, start + size)
        q, gm, lse = q_ref[j, rows, :], gm_ref[j, rows, :], lse_columns[rows, :]
        grad_q = jnp.zeros((128, size), F32)
        for head in range(2):
            q_lanes = with_lanes(q, head, in_pieces(-lse[:, head : head + 1]) + [one])
            q_head, gm_head = with_lanes(q, head, []), with_lanes(gm, head, [])
            p = jnp.exp(dot(k_lanes[head], q_lanes, 1, 1))
            gp = dot(v, gm_head, 1, 1)
            weighted = p * gp
            gs = (weighted - p * jnp.sum(weighted, axis=0, keepdims=True)).astype(BF16)
            grad_v = grad_v + dot(p.astype(BF16), gm_head)
            grad_k = grad_k + dot(gs, q_head)
            grad_q = grad_q + dot(k_heads[head], gs)
        gq_ref[j, rows, :] = (grad_q.T * 0.125).astype(BF16)
    gk_ref[j] = grad_k.astype(BF16)
    gv_ref[j] = grad_v.astype(BF16)


def extract_body(x_ref, out_ref):
    s, p = lax.axis_index("section"), lax.axis_index("tensor")
    clip = jnp.where(s < 2, p, 1 - p)
    x = x_ref[...].astype(F32)
    x = jnp.where(clip == 0, x[:, 0, :], x[:, 1, :])
    at = lax.broadcasted_iota(jnp.int32, x.shape, 0) + pl.program_id(0) * BLOCK
    out_ref[...] = jnp.where(at < LENGTH, x, 0.0)


def extract(x):
    return call(
        extract_body,
        shape((ROWS, D), F32),
        [pl.BlockSpec((BLOCK, 2, D), lambda i: (i, 0, 0))],
        rows_of(D),
        grid=(ROWS // BLOCK,),
    )(x)


def place():
    s, r, p = lax.axis_index("section"), lax.axis_index("dp"), lax.axis_index("tensor")
    return s, r, p, r // 4, r % 4


def on_dp(y, z):
    return {"dp": y * 4 + z}


def greet(peers):
    barrier = pltpu.get_barrier_semaphore()
    for peer in peers:
        pl.semaphore_signal(barrier, inc=1, device_id=peer, device_id_type=MESH)
    pl.semaphore_wait(barrier, len(peers))


def remote(src, dst, send, recv, device):
    return pltpu.make_async_remote_copy(
        src_ref=src, dst_ref=dst, send_sem=send, recv_sem=recv, device_id=device,
        device_id_type=MESH,
    )


def local(src, dst, sem):
    return pltpu.make_async_copy(src, dst, sem)


def start_all(copies):
    for copy in copies:
        copy.start()


def wait_all(copies):
    for copy in copies:
        copy.wait()


BLOCKS = ROWS // BLOCK


class Piece:
    def __init__(self, n, source, view, halves, z_first, sems):
        self.n, self.source, self.view, self.halves, self.z_first = n, source, view, halves, z_first
        self.send, self.recv = sems
        _, _, p, self.y, self.z = place()
        self.partner = {"tensor": 1 - p}

    def copies(self, stage):
        y, z, view = self.y, self.z, self.view
        along_z = [on_dp(y, (z + d) % 4) for d in (1, 3)]
        along_y = [on_dp((y + d) % 4, z) for d in (1, 3)]

        def copy(n, src, dst, device):
            return remote(src, dst, self.send.at[self.n, stage, n], self.recv.at[self.n, stage, n],
                          device)

        def both(refs, peers):
            return [copy(n, refs[n], refs[n], peers[n]) for n in range(2)]

        everything = slice(0, 4)
        if self.z_first:
            ring, ring2 = along_z, along_y
            one = lambda d: view(y, (z + d) % 4)
            group = lambda d, part=everything: view((y + d) % 4, part)
        else:
            ring, ring2 = along_y, along_z
            one = lambda d: view((y + d) % 4, z)
            group = lambda d, part=everything: view(part, (z + d) % 4)
        if stage == 0:
            return [copy(0, self.source, view(y, z), self.partner)]
        if stage == 1:
            return both([one(0), one(0)], ring)
        if stage == 2:
            return both([self.halves(one(3))[0], self.halves(one(1))[1]], ring)
        if stage == 3:
            return both([group(0), group(0)], ring2)
        return both([group(3, slice(0, 2)), group(1, slice(2, 4))], ring2)


def advance(pieces, stage):
    for piece in pieces:
        if stage > 0:
            for copy in piece.copies(stage - 1):
                copy.wait_recv()
        if stage < 5:
            start_all(piece.copies(stage))


def all_sent(pieces):
    for piece in pieces:
        for stage in range(5):
            for copy in piece.copies(stage):
                copy.wait_send()


def opening_body(qkv, out_w, up, down, x, qvb, upb, gain, shift,
                 w, w_out, w_up, w_down, h0, normed, q, k, v, o, lse, qkvb, upb_all,
                 w_v, w_out_v, up_v, down_v, fq, fo, fu, fd, fx, lq, lo, lu, ldn, lx, qvb_o, upb_o,
                 x_v, h_v, normed_v, q_v, k_v, v_v, o_v, lse_v, ld, st, send, recv, bsend, brecv,
                 gate):
    s, r, p, y, z = place()
    partner = {"tensor": 1 - p}
    attn = s % 2 == 0
    peers = [partner] + [on_dp(y, (z + d) % 4) for d in (1, 3)] \
        + [on_dp((y + d) % 4, z) for d in (1, 3)]
    barrier = pltpu.get_barrier_semaphore()
    for peer in peers:
        pl.semaphore_signal(barrier, inc=1, device_id=peer, device_id_type=MESH)

    def rows_at(n):
        return pl.ds(pl.multiple_of(r * n, n), n)

    def qkv_half(half):
        cols = pl.ds(pl.multiple_of(half * 1152, 128), 1152)

        def step(i, carry):
            rows = block(i)

            @pl.when(half == 0)
            def _():
                x0 = x_v[rows].astype(F32)
                h = jnp.where(p == 0, x0[:, 0, :], x0[:, 1, :])
                at = lax.broadcasted_iota(jnp.int32, h.shape, 0) + i * BLOCK
                h = jnp.where(at < LENGTH, h, 0.0)
                h_v[rows, :] = h
                xhat, _ = normalized(h)
                normed_v[rows, :] = (xhat * gain[...] + shift[...]).astype(BF16)

            part = (dot(normed_v[rows, :], w_v[:, cols]) + qkvb[:, cols]).astype(BF16)
            for n in range(9):
                lanes = part[:, n * 128 : n * 128 + 128]
                pair = half * 3 + n % 3
                if n < 3:
                    q_v[pair, rows, :] = (lanes.astype(F32) * 0.125).astype(BF16)
                elif n < 6:
                    k_v[pair, rows, :] = lanes
                else:
                    v_v[pair, rows, :] = lanes
            return carry

        lax.fori_loop(0, BLOCKS, step, 0)

    @pl.when(attn)
    def _():
        loads = [local(qkv.at[t], w_v.at[:, pl.ds(t * 384, 384)], ld.at[t]) for t in range(3)]
        loads.append(local(out_w, w_out_v.at[pl.ds(0, 384)], ld.at[3]))
        clips = local(x, x_v.at[pl.ds(0, LENGTH)], ld.at[4])
        start_all(loads)
        pl.when(s == 0)(clips.start)
        sems = send, recv
        def rows24(ref):
            return ref.at[pl.ds(0, 24)], ref.at[pl.ds(24, 24)]

        left, right = pl.ds(0, 256), pl.ds(256, 128)
        pieces = [
            Piece(0, fq.at[0], lambda a, b: lq.at[0, a, b], rows24, True, sems),
            Piece(1, fq.at[1], lambda a, b: lq.at[1, a, b], rows24, False, sems),
            Piece(2, fq.at[2, :, left], lambda a, b: lq.at[2, a, b, ..., left], rows24, True, sems),
            Piece(3, fq.at[2, :, right], lambda a, b: lq.at[2, a, b, ..., right], rows24, False,
                  sems),
        ]
        direct = remote(fo, lo, bsend.at[1], brecv.at[1], partner)
        bias = remote(qvb, qvb_o, bsend.at[0], brecv.at[0], partner)
        qkvb[:, 0:384] = qvb[0:1, :]
        qkvb[:, 384:768] = jnp.zeros((1, 384), F32)
        qkvb[:, 768:1152] = qvb[1:2, :]
        wait_all(loads)
        for t in range(3):
            fq[t] = w_v[rows_at(48), t * 384 : t * 384 + 384].astype(F32)
        fo[...] = w_out_v[0:384, :].astype(F32)
        pl.semaphore_wait(barrier, 6)
        advance(pieces, 0)
        bias.start()
        direct.start()

        pl.when(s == 0)(clips.wait)
        stored = [local(w_v, w, st.at[0]), local(w_out_v, w_out, st.at[1])]

        def gathered():
            advance(pieces, 4)
            bias.wait()
            direct.wait()
            w_out_v[384:768, :] = lo[...].astype(BF16)
            advance(pieces, 5)
            for t in range(3):
                at = 1152 + t * 384

                def widen(i, carry, t=t, at=at):
                    w_v[pl.ds(pl.multiple_of(i * 192, 192), 192), at : at + 384] = \
                        lq[t, i].reshape(192, 384).astype(BF16)
                    return carry

                lax.fori_loop(0, 4, widen, 0)
            qkvb[:, 1152:1536] = qvb_o[0:1, :]
            qkvb[:, 1536:1920] = jnp.zeros((1, 384), F32)
            qkvb[:, 1920:2304] = qvb_o[1:2, :]
            start_all(stored)

        def pair_step(i, carry):
            pl.when((s == 0) & (i % 3 == 0))(lambda: qkv_half(i // 3))
            pl.when(i == 0)(lambda: advance(pieces, 1))
            pl.when(s == 0)(lambda: attend_pair(q_v, k_v, v_v, o_v, lse_v, i))
            pl.when(i == 0)(lambda: advance(pieces, 2))

            @pl.when(i == 1)
            def _():
                advance(pieces, 3)
                pl.semaphore_signal(gate, inc=1, device_id={"section": s + 1}, device_id_type=MESH)

            pl.when(i == 2)(gathered)
            return carry

        lax.fori_loop(0, PAIRS, pair_step, 0)

        @pl.when(s == 0)
        def _():
            kept = [local(a, b, st.at[2 + n]) for n, (a, b) in enumerate(
                ((h_v, h0), (normed_v, normed), (q_v, q), (k_v, k), (v_v, v), (o_v, o),
                 (lse_v, lse)))]
            start_all(kept)
            wait_all(kept)

        all_sent(pieces)
        wait_all(stored)

    @pl.when(jnp.logical_not(attn))
    def _():
        pl.semaphore_signal(barrier, inc=1, device_id={"section": s - 1}, device_id_type=MESH)
        loads = [local(up, up_v.at[:, pl.ds(0, 1536)], ld.at[0]),
                 local(down, down_v.at[pl.ds(0, 1536)], ld.at[1])]
        start_all(loads)
        sems = send, recv
        pieces = [
            Piece(0, fu, lambda a, b: lu.at[a, b],
                  lambda ref: (ref.at[pl.ds(0, 24)], ref.at[pl.ds(24, 24)]), True, sems),
            Piece(1, fd, lambda a, b: ldn.at[a, b],
                  lambda ref: (ref.at[pl.ds(0, 48)], ref.at[pl.ds(48, 48)]), False, sems),
        ]
        direct = remote(fx, lx, bsend.at[1], brecv.at[1], partner)
        early = [local(up_v.at[:, pl.ds(0, 1536)], w_up.at[:, pl.ds(0, 1536)], st.at[0]),
                 local(down_v.at[pl.ds(0, 1536)], w_down.at[pl.ds(0, 1536)], st.at[1])]
        late = [local(up_v.at[:, pl.ds(1536, 1536)], w_up.at[:, pl.ds(1536, 1536)], st.at[2]),
                local(down_v.at[pl.ds(1536, 1536)], w_down.at[pl.ds(1536, 1536)], st.at[3])]
        bias = remote(upb, upb_o, bsend.at[0], brecv.at[0], partner)
        upb_all[:, 0:1536] = upb[...]
        wait_all(loads)
        fu[...] = up_v[rows_at(48), 0:1536].astype(F32)
        start_all(early)
        fd[...] = down_v[rows_at(96), 0:512].astype(F32)
        pl.semaphore_wait(barrier, 5)
        advance(pieces, 0)
        bias.start()
        fx[...] = down_v[0:1536, 512:768].astype(F32)
        direct.start()
        pl.semaphore_wait(gate, 1)
        for stage in range(1, 5):
            advance(pieces, stage)
        bias.wait()
        upb_all[:, 1536:3072] = upb_o[...]

        def widen(d):
            i, g = (y + d) % 4, (z + d) % 4
            up_v[pl.ds(pl.multiple_of(i * 192, 192), 192), 1536:3072] = \
                lu[i].reshape(192, 1536).astype(BF16)
            for a in range(4):
                down_v[pl.ds(pl.multiple_of(1536 + (a * 4 + g) * 96, 96), 96), 0:512] = \
                    ldn[a, g].astype(BF16)

        for d in (0, 1, 3):
            widen(d)
        direct.wait()
        down_v[1536:3072, 512:768] = lx[...].astype(BF16)
        advance(pieces, 5)
        widen(2)
        start_all(late)
        all_sent(pieces)
        wait_all(early + late)


def opening(qkv, out_w, up, down, x, qvb, upb, gain, shift):
    dma = pltpu.SemaphoreType.DMA
    any_spec = pl.BlockSpec(memory_space=ANY)
    vmem = pl.BlockSpec(memory_space=pltpu.VMEM)
    paired, lse = (PAIRS, ROWS, 128), (PAIRS, 8, ROWS)
    return call(
        opening_body,
        (shape((D, 2304), BF16), shape((D, D), BF16), shape((D, 3072), BF16),
         shape((3072, D), BF16), shape((ROWS, D), F32), shape((ROWS, D), BF16),
         shape(paired, BF16), shape(paired, BF16), shape(paired, BF16), shape(paired, BF16),
         shape(lse, F32), shape((1, 2304), F32), shape((1, 3072), F32)),
        [any_spec] * 5 + [vmem] * 4,
        (any_spec,) * 11 + (vmem, vmem),
        scratch=[
            pltpu.VMEM((D, 2304), BF16), pltpu.VMEM((D, D), BF16), pltpu.VMEM((D, 3072), BF16),
            pltpu.VMEM((3072, D), BF16), pltpu.VMEM((3, 48, 384), F32), pltpu.VMEM((384, D), F32),
            pltpu.VMEM((48, 1536), F32), pltpu.VMEM((96, 512), F32), pltpu.VMEM((1536, 256), F32),
            pltpu.VMEM((3, 4, 4, 48, 384), F32), pltpu.VMEM((384, D), F32),
            pltpu.VMEM((4, 4, 48, 1536), F32), pltpu.VMEM((4, 4, 96, 512), F32),
            pltpu.VMEM((1536, 256), F32),
            pltpu.VMEM((2, 384), F32), pltpu.VMEM((1, 1536), F32),
            pltpu.VMEM((ROWS, 2, D), BF16), pltpu.VMEM((ROWS, D), F32),
            pltpu.VMEM((ROWS, D), BF16), pltpu.VMEM(paired, BF16), pltpu.VMEM(paired, BF16),
            pltpu.VMEM(paired, BF16), pltpu.VMEM(paired, BF16), pltpu.VMEM(lse, F32),
            dma((5,)), dma((9,)), dma((4, 5, 2)), dma((4, 5, 2)), dma((2,)), dma((2,)),
            pltpu.SemaphoreType.REGULAR,
        ],
        collective_id=1,
        has_side_effects=True,
    )(qkv, out_w, up, down, x, qvb, upb, gain, shift)


class Link:
    def __init__(self, src, dst, send, recv):
        self.src, self.dst, self.sems = src, dst, (send, recv)

    def copy(self, i, device):
        r = block(i)
        return remote(self.src.at[r], self.dst.at[r], self.sems[0].at[i], self.sems[1].at[i], device)

    def expect_from(self, device):
        pl.semaphore_signal(
            pltpu.get_barrier_semaphore(), inc=1, device_id=device, device_id_type=MESH)

    def ready(self):
        pl.semaphore_wait(pltpu.get_barrier_semaphore(), 1)

    def arrived(self, i, device):
        self.copy(i, device).wait_recv()

    def sent(self, device):
        for i in range(BLOCKS):
            self.copy(i, device).wait_send()

    def both_ways(self, device):
        for i in range(BLOCKS):
            self.copy(i, device).wait()


def stores(pairs, sems):
    def of(i):
        r = block(i)
        found = []
        for n, (src, dst) in enumerate(pairs):
            if len(src.shape) == 3:
                found.append(local(src.at[:, r], dst.at[:, r], sems.at[n, i]))
            else:
                found.append(local(src.at[r], dst.at[r], sems.at[n, i]))
        return found

    return of


def every_block(step):
    def body(i, carry):
        step(i, block(i))
        return carry

    lax.fori_loop(0, BLOCKS, body, 0)


def out_proj_rows(o_v, h_v, w_out_v, end, hout, r):
    hout[r, :] = h_v[r, :] + (dot(joined(o_v, r), w_out_v[...]) + end)


def forward_body(o, h0, w_out, up, down, w, gain, shift, end, upb, qkvb,
                 h_out, h_in, act, slope, normed, q, k, v, o2, lse2,
                 hin, hout, up_v, down_v, act_v, slope_v, normed_v, o_v, w_out_v, w_v, q_v, k_v,
                 v_v, lse_v, ld, st, send, recv, half_send, half_recv, lse_send, lse_recv):
    s, _, p, _, _ = place()
    link = Link(hout, hin, send, recv)
    share = slope_v.at[:, pl.ds(0, 9 * 128)]
    halves = Link(share, share, half_send, half_recv)

    def lse_copy(device):
        return remote(lse_v.at[3:6], lse_v.at[0:3], lse_send.at[0], lse_recv.at[0], device)

    @pl.when(s == 0)
    def _():
        target = {"section": 1}
        loads = [local(o, o_v, ld.at[0]), local(h0, hin, ld.at[1]), local(w_out, w_out_v, ld.at[2])]
        start_all(loads)
        link.ready()
        wait_all(loads)
        out = stores([(hout, h_out)], st)

        def step(i, r):
            out_proj_rows(o_v, hin, w_out_v, end[...], hout, r)
            link.copy(i, target).start()
            start_all(out(i))

        every_block(step)
        link.sent(target)
        for i in range(BLOCKS):
            wait_all(out(i))

    @pl.when(s == 1)
    def _():
        source, target = {"section": 0}, {"section": 2, "tensor": 1 - p}
        loads = [local(up, up_v, ld.at[0]), local(down, down_v, ld.at[1])]
        start_all(loads)
        link.expect_from(source)
        link.ready()
        wait_all(loads)
        out = stores([(hout, h_out), (hin, h_in), (act_v, act), (slope_v, slope),
                      (normed_v, normed)], st)

        def step(i, r):
            link.arrived(i, source)
            h = hin[r, :]
            xhat, _ = normalized(h)
            low = (xhat * gain[...] + shift[...]).astype(BF16)
            normed_v[r, :] = low
            hout[r, :] = h + end[...]

            def chunk(c, carry):
                cols = pl.ds(pl.multiple_of(c * 768, 768), 768)
                x = dot(low, up_v[:, cols]) + upb[:, cols]
                active, steep = gelu_and_slope(x)
                act_v[r, cols] = active
                slope_v[r, cols] = steep
                hout[r, :] += dot(active, down_v[cols, :])
                return carry

            lax.fori_loop(0, 4, chunk, 0)
            link.copy(i, target).start()
            start_all(out(i))

        every_block(step)
        link.sent(target)
        for i in range(BLOCKS):
            wait_all(out(i))

    @pl.when(s == 2)
    def _():
        source = {"section": 1, "tensor": 1 - p}
        load = local(w, w_v, ld.at[0])
        load.start()
        link.expect_from(source)
        halves.ready()
        load.wait()
        out = stores([(hin, h_in), (normed_v, normed), (q_v, q), (k_v, k), (v_v, v)], st)

        def step(i, r):
            link.arrived(i, source)
            qkv_block(hin[r, :], gain[...], shift[...], w_v, qkvb, q_v, k_v, v_v, normed_v, r)
            for t, ref in enumerate((q_v, k_v, v_v)):
                for j in range(3):
                    at = (t * 3 + j) * 128
                    slope_v[r, at : at + 128] = ref[3 + j, r, :].astype(F32)
            halves.copy(i, {"section": 3}).start()
            start_all(out(i))

        every_block(step)

        def attend_step(i, carry):
            attend_pair(q_v, k_v, v_v, o_v, lse_v, i)
            return carry

        lax.fori_loop(0, PAIRS, attend_step, 0)
        kept = [local(o_v, o2, ld.at[1]), local(lse_v, lse2, ld.at[2])]
        start_all(kept)
        lse_copy({"section": 3}).start()
        halves.sent({"section": 3})
        for i in range(BLOCKS):
            wait_all(out(i))
        wait_all(kept)
        lse_copy({"section": 3}).wait_send()

    @pl.when(s == 3)
    def _():
        source = {"section": 2}
        halves.expect_from(source)

        def step(i, r):
            halves.arrived(i, source)
            for t, ref in enumerate((q_v, k_v, v_v)):
                for j in range(3):
                    at = (t * 3 + j) * 128
                    ref[j, r, :] = slope_v[r, at : at + 128].astype(BF16)

        every_block(step)
        kept = [local(a.at[0:3], b.at[0:3], ld.at[n])
                for n, (a, b) in enumerate(((q_v, q), (k_v, k), (v_v, v), (lse_v, lse2)))]
        start_all(kept[:3])
        lse_copy(source).wait_recv()
        kept[3].start()
        wait_all(kept)


def staged(body, outs, operands, small, scratch, stored, collective_id):
    dma = pltpu.SemaphoreType.DMA
    any_spec = pl.BlockSpec(memory_space=ANY)
    vmem = pl.BlockSpec(memory_space=pltpu.VMEM)
    return call(
        body,
        tuple(shape(*o) for o in outs),
        [any_spec] * len(operands) + [vmem] * len(small),
        (any_spec,) * len(outs),
        scratch=[pltpu.VMEM(*x) for x in scratch]
        + [dma((8,)), dma((stored, BLOCKS))] + [dma((BLOCKS,))] * 4 + [dma((2 * BLOCKS,))] * 2,
        collective_id=collective_id,
        has_side_effects=True,
    )(*operands, *small)


WIDE = (ROWS, D)
HIDDEN = (ROWS, 3072)
PAIRED = (PAIRS, ROWS, 128)
LSE = (PAIRS, 8, ROWS)


def forward(o, h0, w_out, up, down, w, gain, shift, end, upb, qkvb):
    return staged(
        forward_body,
        [(WIDE, F32), (WIDE, F32), (HIDDEN, BF16), (HIDDEN, F32), (WIDE, BF16), (PAIRED, BF16),
         (PAIRED, BF16), (PAIRED, BF16), (PAIRED, BF16), (LSE, F32)],
        (o, h0, w_out, up, down, w),
        (gain, shift, end, upb, qkvb),
        [(WIDE, F32), (WIDE, F32), ((D, 3072), BF16), ((3072, D), BF16), (HIDDEN, BF16),
         (HIDDEN, F32), (WIDE, BF16), (PAIRED, BF16), ((D, D), BF16), ((D, 2304), BF16),
         (PAIRED, BF16), (PAIRED, BF16), (PAIRED, BF16), (LSE, F32)],
        5,
        2,
    )


def middle_body(o, h2, w_out, up, down, cot, gain, shift, end, upb,
                h_out, h_in, act, gr, gb, normed, g_in, gm, g_out, vec,
                hin, hout, gin, gout, act_v, gr_v, gb_v, normed_v, up_v, down_v, o_v, w_out_v, gm_v,
                vec_v, ups_v, gmx, ld, st, send, recv, back_send, back_recv, x_send, x_recv):
    s, _, p, _, _ = place()
    halves = Link(gmx, gmx, x_send, x_recv)
    link = Link(hout, hin, send, recv)
    back = Link(gout, gin, back_send, back_recv)

    @pl.when(s == 2)
    def _():
        other = {"section": 3}
        loads = [local(o, o_v, ld.at[0]), local(h2, hin, ld.at[1]), local(w_out, w_out_v, ld.at[2])]
        start_all(loads)
        back.expect_from(other)
        link.ready()
        wait_all(loads)
        out = stores([(hout, h_out)], st)
        back_out = stores([(hout, h_out), (gin, g_in), (gb_v, gb), (gm_v, gm)], st)

        def step(i, r):
            out_proj_rows(o_v, hin, w_out_v, end[...], hout, r)
            link.copy(i, other).start()
            start_all(out(i))

        every_block(step)

        def back_step(i, r):
            back.arrived(i, other)
            gb_v[r, :] = mixed_back_block(gin[r, :], w_out_v, gm_v, r)
            for j in range(3):
                gmx[r, j * 128 : j * 128 + 128] = gm_v[3 + j, r, :].astype(F32)
            halves.copy(i, other).start()
            start_all(back_out(i)[1:])

        every_block(back_step)
        link.sent(other)
        halves.sent(other)
        for i in range(BLOCKS):
            wait_all(back_out(i))

    @pl.when(s == 3)
    def _():
        other = {"section": 2}
        loads = [local(up, up_v, ld.at[0]), local(down, down_v, ld.at[1]),
                 local(cot, gin, ld.at[2])]
        start_all(loads)
        link.expect_from(other)
        back.ready()
        wait_all(loads)
        vec_v[...] = jnp.zeros_like(vec_v)
        ups_v[...] = jnp.zeros_like(ups_v)
        out = stores([(hout, h_out), (hin, h_in), (act_v, act), (gr_v, gr), (gb_v, gb),
                      (normed_v, normed), (gout, g_out)], st)

        def step(i, r):
            link.arrived(i, other)
            h, g = hin[r, :], gin[r, :]
            xhat, _ = normalized(h)
            low = (xhat * gain[...] + shift[...]).astype(BF16)
            normed_v[r, :] = low
            g_low = g.astype(BF16)
            gb_v[r, :] = g_low
            hout[r, :] = h + end[...]
            gout[r, :] = jnp.zeros((BLOCK, D), F32)

            def chunks(c2, carry):
                total, grad_normed = hout[r, :], gout[r, :]
                for n in range(2):
                    cols = pl.ds(pl.multiple_of(c2 * 1536 + n * 768, 768), 768)
                    x = dot(low, up_v[:, cols]) + upb[:, cols]
                    active, steep = gelu_and_slope(x)
                    act_v[r, cols] = active
                    total = total + dot(active, down_v[cols, :])
                    raised = (dot(g_low, down_v[cols, :], 1, 1) * steep).astype(BF16)
                    gr_v[r, cols] = raised
                    ups_v[:, cols] += jnp.sum(raised.astype(F32), axis=0, keepdims=True)
                    grad_normed = grad_normed + dot(raised, up_v[:, cols], 1, 1)
                hout[r, :] = total
                gout[r, :] = grad_normed
                return carry

            lax.fori_loop(0, 2, chunks, 0)
            grad_normed = gout[r, :]
            result, xhat = norm_back(g, h, gain[...], grad_normed)
            gout[r, :] = result
            back.copy(i, other).start()
            add_row(vec_v, 0, grad_normed * xhat)
            add_row(vec_v, 1, grad_normed)
            add_row(vec_v, 2, g_low.astype(F32))
            start_all(out(i))

        every_block(step)
        for c in range(4):
            vec_v[3 + c : 4 + c, :] = ups_v[:, c * D : c * D + D]
        last = local(vec_v, vec, ld.at[3])
        last.start()


        def half_step(i, r):
            halves.arrived(i, other)
            for j in range(3):
                gm_v[j, r, :] = gmx[r, j * 128 : j * 128 + 128].astype(BF16)

        every_block(half_step)
        shared = local(gm_v.at[0:3], gm.at[0:3], ld.at[4])
        shared.start()
        back.sent(other)
        shared.wait()
        for i in range(BLOCKS):
            wait_all(out(i))
        last.wait()


def middle(o, h2, w_out, up, down, cot, gain, shift, end, upb):
    return staged(
        middle_body,
        [(WIDE, F32), (WIDE, F32), (HIDDEN, BF16), (HIDDEN, BF16), (WIDE, BF16), (WIDE, BF16),
         (WIDE, F32), (PAIRED, BF16), (WIDE, F32), ((8, D), F32)],
        (o, h2, w_out, up, down, cot),
        (gain, shift, end, upb),
        [(WIDE, F32)] * 4
        + [(HIDDEN, BF16), (HIDDEN, BF16), (WIDE, BF16), (WIDE, BF16), ((D, 3072), BF16),
           ((3072, D), BF16), (PAIRED, BF16), ((D, D), BF16), (PAIRED, BF16), ((8, D), F32),
           ((1, 3072), F32), ((ROWS, 384), F32)],
        7,
        3,
    )


def backward_body(g2, h, q, k, v, gm2, lse, w, up, down, slope, w_out, h_made, gain,
                  g_out, g_in, gr, gb, gm, vec, h_theirs, g_theirs, gq, gk, gv,
                  gin, gout, h_v, slope_v, gr_v, gb_v, up_v, down_v, gq_v, gk_v, gv_v, w_v, w_out_v,
                  gm_v, vec_v, ups_v, q_v, k_v, v_v, lse_v, ld, st, send, recv, next_send, next_recv,
                  x_send, x_recv):
    s, _, p, _, _ = place()
    theirs = {"tensor": 1 - p}
    partner = Link(gout, g_theirs, x_send, x_recv)
    made = remote(h_made, h_theirs, x_send.at[BLOCKS], x_recv.at[BLOCKS], theirs)
    first = Link(gout, gin, send, recv)
    second = Link(gout, gin, next_send, next_recv)

    heads = [local(a, b, ld.at[n]) for n, (a, b) in enumerate(
        ((q, q_v), (k, k_v), (v, v_v), (gm2, gm_v), (lse, lse_v)))]

    def share(i, device):
        at = pl.ds(pl.multiple_of(i * 384, 384), 384)
        return remote(slope_v.at[:, at], slope_v.at[:, at], next_send.at[i], next_recv.at[i], device)

    @pl.when(s >= 2)
    def _():
        start_all(heads)

        @pl.when(s == 2)
        def _():
            start_all([local(g2, gin, ld.at[5]), local(h, h_v, ld.at[6]), local(w, w_v, ld.at[7])])
            for device in (theirs, {"section": 3}):
                pl.semaphore_signal(
                    pltpu.get_barrier_semaphore(), inc=1, device_id=device, device_id_type=MESH)
            pl.semaphore_wait(pltpu.get_barrier_semaphore(), 2)
            made.start()

        pl.when(s == 3)(second.ready)
        wait_all(heads)

        def attend_step(i, carry):
            attend_back_pair(q_v, k_v, v_v, gm_v, lse_v, gq_v, gk_v, gv_v, i)

            @pl.when(s == 3)
            def _():
                for t, ref in enumerate((gq_v, gk_v, gv_v)):
                    at = pl.ds(pl.multiple_of(i * 384 + t * 128, 128), 128)
                    slope_v[:, at] = ref[i].astype(F32)
                share(i, {"section": 2}).start()

            return carry

        lax.fori_loop(0, 3, attend_step, 0)

    @pl.when(s == 3)
    def _():
        for i in range(3):
            share(i, {"section": 2}).wait_send()

    @pl.when(s == 2)
    def _():
        target = {"section": 1, "tensor": 1 - p}
        loads = [local(g2, gin, ld.at[5]), local(h, h_v, ld.at[6]), local(w, w_v, ld.at[7])]

        def take_step(i, carry):
            share(i, {"section": 3}).wait_recv()
            for t, ref in enumerate((gq_v, gk_v, gv_v)):
                at = pl.ds(pl.multiple_of(i * 384 + t * 128, 128), 128)
                ref[3 + i] = slope_v[:, at].astype(BF16)
            return carry

        lax.fori_loop(0, 3, take_step, 0)
        kept = [local(a, b, ld.at[n]) for n, (a, b) in enumerate(
            ((gq_v, gq), (gk_v, gk), (gv_v, gv)))]
        start_all(kept)
        wait_all(loads)
        vec_v[...] = jnp.zeros_like(vec_v)
        out = stores([(gout, g_out)], st)

        def step(i, r):
            parts = [(pairs_of((gq_v, gk_v), half, r), pairs_of((gv_v,), half, r))
                     for half in range(2)]
            gout[r, :] = qkv_back_rows(gin[r, :], h_v[r, :], gain[...], parts, w_v, vec_v)
            first.copy(i, target).start()
            start_all(out(i))

        every_block(step)
        last = local(vec_v, vec, ld.at[6])
        last.start()
        first.sent(target)
        made.wait()
        wait_all(kept)
        for i in range(BLOCKS):
            wait_all(out(i))
        last.wait()

    @pl.when(s == 1)
    def _():
        source, target = {"section": 2, "tensor": 1 - p}, {"section": 0}
        loads = [local(a, b, ld.at[n]) for n, (a, b) in enumerate(
            ((up, up_v), (down, down_v), (slope, slope_v), (h, h_v)))]
        start_all(loads)
        first.expect_from(source)
        pl.semaphore_signal(
            pltpu.get_barrier_semaphore(), inc=1, device_id=theirs, device_id_type=MESH)
        pl.semaphore_wait(pltpu.get_barrier_semaphore(), 2)
        wait_all(loads)
        vec_v[...] = jnp.zeros_like(vec_v)
        ups_v[...] = jnp.zeros_like(ups_v)
        out = stores([(gout, g_out), (gr_v, gr), (gb_v, gb)], st)

        def step(i, r):
            first.arrived(i, source)
            g = gin[r, :]
            g_low = g.astype(BF16)
            gb_v[r, :] = g_low
            gout[r, :] = jnp.zeros((BLOCK, D), F32)

            def chunk(c, carry):
                cols = pl.ds(pl.multiple_of(c * 768, 768), 768)
                raised = (dot(g_low, down_v[cols, :], 1, 1) * slope_v[r, cols]).astype(BF16)
                gr_v[r, cols] = raised
                ups_v[:, cols] += jnp.sum(raised.astype(F32), axis=0, keepdims=True)
                gout[r, :] += dot(raised, up_v[:, cols], 1, 1)
                return carry

            lax.fori_loop(0, 4, chunk, 0)
            grad_normed = gout[r, :]
            result, xhat = norm_back(g, h_v[r, :], gain[...], grad_normed)
            gout[r, :] = result
            second.copy(i, target).start()
            pl.when(i < BLOCKS - 1)(lambda: partner.copy(i, theirs).start())
            add_row(vec_v, 0, grad_normed * xhat)
            add_row(vec_v, 1, grad_normed)
            add_row(vec_v, 2, g_low.astype(F32))
            start_all(out(i))

        every_block(step)
        for c in range(4):
            vec_v[3 + c : 4 + c, :] = ups_v[:, c * D : c * D + D]
        last = local(vec_v, vec, ld.at[6])
        last.start()
        second.sent(target)
        for i in range(BLOCKS - 1):
            partner.copy(i, theirs).wait()
        for i in range(BLOCKS):
            wait_all(out(i))
        last.wait()

    @pl.when(s == 0)
    def _():
        source = {"section": 1}
        load = local(w_out, w_out_v, ld.at[0])
        load.start()
        second.expect_from(source)
        load.wait()
        out = stores([(gin, g_in), (gb_v, gb), (gm_v, gm)], st)

        def step(i, r):
            second.arrived(i, source)
            gb_v[r, :] = mixed_back_block(gin[r, :], w_out_v, gm_v, r)
            start_all(out(i))

        every_block(step)
        for i in range(BLOCKS):
            wait_all(out(i))


def backward(g2, h, q, k, v, gm, lse, w, up, down, slope, w_out, h_made, gain):
    return staged(
        backward_body,
        [(WIDE, F32), (WIDE, F32), (HIDDEN, BF16), (WIDE, BF16), (PAIRED, BF16), ((8, D), F32),
         (WIDE, F32), (WIDE, F32), (PAIRED, BF16), (PAIRED, BF16), (PAIRED, BF16)],
        (g2, h, q, k, v, gm, lse, w, up, down, slope, w_out, h_made),
        (gain,),
        [(WIDE, F32)] * 3
        + [(HIDDEN, F32), (HIDDEN, BF16), (WIDE, BF16), ((D, 3072), BF16), ((3072, D), BF16),
           (PAIRED, BF16), (PAIRED, BF16), (PAIRED, BF16), ((D, 2304), BF16), ((D, D), BF16),
           (PAIRED, BF16), ((8, D), F32), ((1, 3072), F32), (PAIRED, BF16), (PAIRED, BF16),
           (PAIRED, BF16), (LSE, F32)],
        3,
        4,
    )


def exchange_body(h, theirs, send, recv):
    s, _, p, _, _ = place()

    @pl.when(s < 2)
    def _():
        partner = {"tensor": 1 - p}
        greet([partner])
        copy = remote(h, theirs, send, recv, partner)
        copy.start()
        copy.wait()


def exchange(h):
    dma = pltpu.SemaphoreType.DMA
    any_spec = pl.BlockSpec(memory_space=ANY)
    return call(
        exchange_body, shape(WIDE, F32), [any_spec], any_spec,
        scratch=[dma, dma], collective_id=5, has_side_effects=True,
    )(h)


class Reduction:
    def __init__(self, acc, far, near, far2, near2, last, fin, sems):
        self.acc, self.far, self.near, self.far2, self.near2 = acc, far, near, far2, near2
        self.last, self.fin = last, fin
        self.send, self.recv = sems
        _, _, p, self.y, self.z = place()
        self.partner = {"tensor": 1 - p}

    def at(self, j, z_first):
        y, z = self.y, self.z
        along_z = [on_dp(y, (z + d) % 4) for d in (1, 3)]
        along_y = [on_dp((y + d) % 4, z) for d in (1, 3)]
        if z_first:
            return z, y, along_z, along_y, lambda h, i: self.acc.at[j, h, :, i], \
                lambda h, i: self.acc.at[j, h, i, z]
        return y, z, along_y, along_z, lambda h, i: self.acc.at[j, h, i], \
            lambda h, i: self.acc.at[j, h, y, i]

    def copies(self, j, z_first, stage):
        here, there, ring, ring2, part, part2 = self.at(j, z_first)
        both = slice(0, 2)

        def pair(sources, target, peers):
            return [
                remote(sources[n], target.at[j, n], self.send.at[j, stage, n],
                       self.recv.at[j, stage, n], peers[n])
                for n in range(2)
            ]

        if stage == 0:
            return pair([part(0, (here + 2) % 4), part(1, (here + 2) % 4)], self.far, ring)
        if stage == 1:
            return pair([part(both, (here + 1) % 4), part(both, (here + 3) % 4)], self.near, ring)
        if stage == 2:
            return pair([part2(0, (there + 2) % 4), part2(1, (there + 2) % 4)], self.far2, ring2)
        if stage == 3:
            return pair([part2(both, (there + 1) % 4), part2(both, (there + 3) % 4)], self.near2,
                        ring2)
        return [remote(self.fin.at[j, 1], self.last.at[j], self.send.at[j, 4, 0],
                       self.recv.at[j, 4, 0], self.partner)]

    def step(self, j, z_first, stage, put):
        here, there, _, _, part, part2 = self.at(j, z_first)
        if stage > 0:
            for copy in self.copies(j, z_first, stage - 1):
                copy.wait_recv()
        if stage == 1:
            def add_far(i, carry):
                for n, d in ((0, 1), (1, 3)):
                    ref = part(n, (here + d) % 4)
                    ref[i] = ref[i] + self.far[j, n, i]
                return carry

            lax.fori_loop(0, 4, add_far, 0)
        if stage == 2:
            def add_near(i, carry):
                for h in range(2):
                    ref = part(h, here)
                    ref[i] = ref[i] + (self.near[j, 0, h, i] + self.near[j, 1, h, i])
                return carry

            lax.fori_loop(0, 4, add_near, 0)
        if stage == 3:
            for n, d in ((0, 1), (1, 3)):
                ref = part2(n, (there + d) % 4)
                ref[...] = ref[...] + self.far2[j, n]
        if stage == 4:
            for h in range(2):
                ref = part2(h, there)
                self.fin[j, h] = ref[...] + (self.near2[j, 0, h] + self.near2[j, 1, h])
        if stage == 5:
            put(j, self.fin[j, 0] + self.last[j])
        else:
            start_all(self.copies(j, z_first, stage))

    def sent(self, j, z_first):
        for stage in range(5):
            for copy in self.copies(j, z_first, stage):
                copy.wait_send()


def reduction_scratch(jobs, width):
    dma = pltpu.SemaphoreType.DMA
    return [
        pltpu.VMEM((jobs, 2, 4, 4, 48, width), F32),
        pltpu.VMEM((jobs, 2, 4, 48, width), F32),
        pltpu.VMEM((jobs, 2, 2, 4, 48, width), F32),
        pltpu.VMEM((jobs, 2, 48, width), F32),
        pltpu.VMEM((jobs, 2, 2, 48, width), F32),
        pltpu.VMEM((jobs, 48, width), F32),
        pltpu.VMEM((jobs, 2, 48, width), F32),
        dma((jobs, 5, 2)),
        dma((jobs, 5, 2)),
    ]


class Sums:
    def __init__(self, va, v1, v2, vec, send, recv):
        self.va, self.v1, self.v2, self.vec, self.send, self.recv = va, v1, v2, vec, send, recv
        _, _, p, y, z = place()
        self.partner = {"tensor": 1 - p}
        self.peers = [on_dp(y, (z + d) % 4) for d in range(1, 4)], \
            [on_dp((y + d) % 4, z) for d in range(1, 4)]

    def copies(self, stage):
        if stage == 2:
            return [remote(self.vec.at[0], self.vec.at[1], self.send.at[6], self.recv.at[6],
                           self.partner)]
        held = self.v1 if stage == 0 else self.v2
        return [
            remote(self.va.at[stage], held.at[d], self.send.at[3 * stage + d],
                   self.recv.at[3 * stage + d], self.peers[stage][d])
            for d in range(3)
        ]

    def step(self, stage):
        if stage > 0:
            for copy in self.copies(stage - 1):
                copy.wait()
        if stage == 1:
            self.va[1] = self.va[0] + (self.v1[0] + self.v1[1] + self.v1[2])
        if stage == 2:
            self.vec[0] = self.va[1] + (self.v2[0] + self.v2[1] + self.v2[2])
        if stage < 3:
            start_all(self.copies(stage))


def sums_scratch():
    dma = pltpu.SemaphoreType.DMA
    return [pltpu.VMEM((2, 8, D), F32), pltpu.VMEM((3, 8, D), F32), pltpu.VMEM((3, 8, D), F32),
            dma((7,)), dma((7,))]


def greet_all():
    _, _, p, y, z = place()
    peers = [{"tensor": 1 - p}]
    peers += [on_dp(y, (z + d) % 4) for d in range(1, 4)]
    peers += [on_dp((y + d) % 4, z) for d in range(1, 4)]
    for peer in peers:
        pl.semaphore_signal(
            pltpu.get_barrier_semaphore(), inc=1, device_id=peer, device_id_type=MESH)


def met():
    pl.semaphore_wait(pltpu.get_barrier_semaphore(), 7)


def job_terms(acc, j, left_t, x_of):
    width = acc.shape[5]

    def step(i, carry):
        half, y = i // 4, i % 4
        rows = pl.ds(pl.multiple_of(y * 192, 192), 192)
        acc[j, half, y] = dot(left_t[rows, :], x_of(half)[...]).reshape(4, 48, width)
        return carry

    lax.fori_loop(0, 8, step, 0)


def attn_finish_body(q0, k0, v0, gm0, lse0, o0, gb0, n0, gq2, gk2, gv2, o2, gb2, n2, g_in, h, w, v2,
                     g2, gain,
                     g_theirs, g_own, out, vec,
                     *scratch):
    red = Reduction(*scratch[:7], scratch[7:9])
    sums = Sums(*scratch[9:12], vec, *scratch[12:14])
    (x_v, o_v, low_v, left_t, gin_v, h_v, gout, w_v, q_v, k_v, v_v, gm_v, lse_v, gq_v, gk_v, gv_v,
     xl, ol, ld, st, send, recv) = scratch[14:]
    s, _, p, _, _ = place()
    partner = {"tensor": 1 - p}
    vec_ref = sums.va.at[0]

    def put(j, result):
        if j == 0:
            out[:, 1152:1536] = result
        else:
            for t in range(3):
                at = t * 384 + (j - 1) * 128
                out[:, at : at + 128] = result[:, t * 128 : t * 128 + 128]

    def low_loads(normed, gb):
        return [local(normed, low_v.at[0], ld.at[0]), local(gb, low_v.at[1], ld.at[1])]

    def lanes(n):
        return pl.ds(pl.multiple_of(n * 128, 128), 128)

    def each_pair(act):
        def step(pair, carry):
            act(pair)
            return carry

        lax.fori_loop(0, PAIRS, step, 0)

    def o_load(o, pair):
        return local(o.at[pair], o_v.at[pair // 3, :, lanes(pair % 3)], ol.at[pair])

    def attention_loads():
        return [local(a, b, ld.at[6 + n]) for n, (a, b) in enumerate(
            ((q0, q_v), (k0, k_v), (v0, v_v), (gm0, gm_v), (lse0, lse_v)))]

    def grad_loads(pair):
        return [local(ref.at[pair], x_v.at[pair % 3, pair // 3, :, pl.ds(t * 128, 128)],
                      xl.at[t, pair])
                for t, ref in enumerate((gq2, gk2, gv2))]

    def more_loads():
        return [local(g_in, gin_v, ld.at[2]), local(h, h_v, ld.at[3]), local(w, w_v, ld.at[4])]

    def early_sums():
        return local(v2, vec_ref, ld.at[5])

    @pl.when(s == 0)
    def _():
        each_pair(lambda pair: o_load(o0, pair).start())
        start_all(low_loads(n0, gb0) + attention_loads() + more_loads())

    @pl.when(s == 2)
    def _():
        start_all(low_loads(n2, gb2))
        each_pair(lambda pair: start_all([o_load(o2, pair)] + grad_loads(pair)))
        early_sums().start()

    def swap(i):
        r = block(i)
        return remote(gout.at[r], g_theirs.at[r], send.at[i], recv.at[i], partner)

    swap2 = remote(g2, g_theirs, send.at[0], recv.at[0], partner)

    def keep(i):
        r = block(i)
        return local(gout.at[r], g_own.at[r], st.at[i])

    def rows():
        def step(i, carry):
            r = block(i)
            pl.when(i == 2)(lambda: take((3, 1), (2, 2), (1, 3), (0, 4)))
            parts = [(pairs_of((gq_v, gk_v), half, r), pairs_of((gv_v,), half, r))
                     for half in range(2)]
            gout[r, :] = qkv_back_rows(gin_v[r, :], h_v[r, :], gain[...], parts, w_v, vec_ref)
            swap(i).start()
            keep(i).start()
            return carry

        lax.fori_loop(0, BLOCKS, step, 0)

    def take(*steps):
        for j, stage in steps:
            red.step(j, j % 2 == 0, stage, put)

    @pl.when(s % 2 == 0)
    def _():
        greet_all()
        for n, load in enumerate(low_loads(n0, gb0)):
            load.wait()
            left_t[n] = low_v[n].T
        each_pair(lambda pair: o_load(o0, pair).wait())
        met()

        @pl.when(s == 0)
        def _():
            sums.va[0] = jnp.zeros((8, D), F32)
            wait_all(attention_loads())

        @pl.when(s == 2)
        def _():
            swap2.start()
            early_sums().wait()
            each_pair(lambda pair: wait_all(grad_loads(pair)))

        job_terms(red.acc, 0, left_t.at[1], lambda half: o_v.at[half])
        take((0, 0))

        def pair_step(i, carry):
            @pl.when(s == 0)
            def _():
                def one(half, carry):
                    pair = half * 3 + i
                    attend_back_pair(q_v, k_v, v_v, gm_v, lse_v, gq_v, gk_v, gv_v, pair)
                    for t, ref in enumerate((gq_v, gk_v, gv_v)):
                        x_v[i, half, :, t * 128 : t * 128 + 128] = ref[pair]
                    return carry

                lax.fori_loop(0, 2, one, 0)

            job_terms(red.acc, 1 + i, left_t.at[0], lambda half: x_v.at[i, half])
            pl.when(i == 0)(lambda: take((1, 0), (0, 1)))
            pl.when(i == 1)(lambda: take((2, 0), (1, 1), (0, 2)))
            pl.when(i == 2)(lambda: take((3, 0), (2, 1), (1, 2), (0, 3)))
            return carry

        lax.fori_loop(0, 3, pair_step, 0)
        @pl.when(s == 0)
        def _():
            wait_all(more_loads())
            rows()

        pl.when(s == 2)(lambda: take((3, 1), (2, 2), (1, 3), (0, 4)))

        sums.step(0)
        take((3, 2), (2, 3), (1, 4), (0, 5))
        sums.step(1)
        take((3, 3), (2, 4), (1, 5))
        sums.step(2)
        take((3, 4), (2, 5))
        take((3, 5))
        sums.step(3)
        for j in range(4):
            red.sent(j, j % 2 == 0)

        pl.when(s == 2)(swap2.wait)

        @pl.when(s == 0)
        def _():
            for i in range(BLOCKS):
                swap(i).wait()
                keep(i).wait()


def attn_finish(first, last, rest, gain):
    dma = pltpu.SemaphoreType.DMA
    any_spec = pl.BlockSpec(memory_space=ANY)
    vmem = pl.BlockSpec(memory_space=pltpu.VMEM)
    paired = pltpu.VMEM(PAIRED, BF16)
    return call(
        attn_finish_body,
        (shape(WIDE, F32), shape(WIDE, F32), shape((48, 1536), F32), shape((2, 8, D), F32)),
        [any_spec] * 19 + [vmem],
        (any_spec, any_spec, vmem, vmem),
        scratch=reduction_scratch(4, 384) + sums_scratch() + [
            pltpu.VMEM((3, 2, ROWS, 384), BF16), pltpu.VMEM((2, ROWS, 384), BF16),
            pltpu.VMEM((2,) + WIDE, BF16), pltpu.VMEM((2, D, ROWS), BF16), pltpu.VMEM(WIDE, F32),
            pltpu.VMEM(WIDE, F32), pltpu.VMEM(WIDE, F32), pltpu.VMEM((D, 2304), BF16),
            paired, paired, paired, paired, pltpu.VMEM((PAIRS, 8, ROWS), F32),
            paired, paired, paired,
            dma((3, PAIRS)), dma((PAIRS,)), dma((11,)), dma((BLOCKS,)), dma((BLOCKS,)),
            dma((BLOCKS,)),
        ],
        collective_id=20,
        has_side_effects=True,
    )(*first, *last, *rest, gain)


def ff_finish_body(gr1, act1, gb1, n1, gr3, act3, gb3, n3, g1, g3, v1, v3, h3,
                   g_theirs, g3_theirs, h3_theirs, out, vec,
                   *scratch):
    red = Reduction(*scratch[:7], scratch[7:9])
    sums = Sums(*scratch[9:12], vec, *scratch[12:14])
    x_v, low_v, left_t, ld, xs, xr, vl, hs, hr = scratch[14:]
    s, _, p, _, _ = place()
    partner = {"tensor": 1 - p}
    jobs = ((True, 0), (False, 2 * CHUNK), (True, CHUNK), (False, 3 * CHUNK))

    def put(j, result):
        out[:, jobs[j][1] : jobs[j][1] + CHUNK] = result

    def load(t, gr, act):
        z_first, column = jobs[t]
        x = gr if z_first else act
        at = column % (2 * CHUNK)
        return [
            local(x.at[:, half * 2 * CHUNK + at : half * 2 * CHUNK + at + CHUNK],
                  x_v.at[t % 2, half], ld.at[t % 2, half])
            for half in range(2)
        ]

    def start_load(t):
        pl.when(s == 1)(lambda: start_all(load(t, gr1, act1)))
        pl.when(s == 3)(lambda: start_all(load(t, gr3, act3)))

    def small(normed, gb, vecs):
        return [local(normed, low_v.at[0], vl.at[0]), local(gb, low_v.at[1], vl.at[1]),
                local(vecs, sums.va.at[0], vl.at[2])]

    swap = remote(g1.at[pl.ds(ROWS - BLOCK, BLOCK)], g_theirs, xs, xr, partner)
    swap3 = [remote(g3, g3_theirs, xs, xr, partner),
             remote(h3, h3_theirs, hs, hr, partner)]

    @pl.when(s % 2 == 1)
    def _():
        pl.when(s == 1)(lambda: start_all(small(n1, gb1, v1)))
        pl.when(s == 3)(lambda: start_all(small(n3, gb3, v3)))
        greet_all()
        start_load(0)
        start_load(1)
        smalls = small(n1, gb1, v1)
        for n in range(2):
            smalls[n].wait()
            left_t[n] = low_v[n].T
        met()
        pl.when(s == 1)(swap.start)
        pl.when(s == 3)(lambda: start_all(swap3))
        smalls[2].wait()
        def take(t):
            for stage in range(6):
                if 0 <= t - stage < 4:
                    red.step(t - stage, jobs[t - stage][0], stage, put)

        def compute(t, carry):
            slot = t % 2
            for half in range(2):
                local(gr1.at[:, 0:CHUNK], x_v.at[slot, half], ld.at[slot, half]).wait()
            job_terms(red.acc, t, left_t.at[slot], lambda half: x_v.at[slot, half])
            for n in range(4):
                @pl.when(t == n)
                def _(n=n):
                    if n < 2:
                        start_load(n + 2)
                    if n < 3:
                        sums.step(n)
                    take(n)
            return carry

        lax.fori_loop(0, 4, compute, 0)
        for t in range(4, 9):
            take(t)
        sums.step(3)
        for j in range(4):
            red.sent(j, jobs[j][0])
        pl.when(s == 1)(swap.wait)
        pl.when(s == 3)(lambda: wait_all(swap3))


def ff_finish(first, last, rest):
    dma = pltpu.SemaphoreType.DMA
    any_spec = pl.BlockSpec(memory_space=ANY)
    vmem = pl.BlockSpec(memory_space=pltpu.VMEM)
    return call(
        ff_finish_body,
        (shape((BLOCK, D), F32), shape(WIDE, F32), shape(WIDE, F32), shape((48, 4 * CHUNK), F32),
         shape((2, 8, D), F32)),
        [any_spec] * 13,
        (any_spec, any_spec, any_spec, vmem, vmem),
        scratch=reduction_scratch(4, CHUNK) + sums_scratch() + [
            pltpu.VMEM((2, 2, ROWS, CHUNK), BF16), pltpu.VMEM((2,) + WIDE, BF16),
            pltpu.VMEM((2, D, ROWS), BF16),
            dma((2, 2)), dma, dma, dma((3,)), dma, dma,
        ],
        collective_id=21,
        has_side_effects=True,
    )(*first, *last, *rest)


def block_rows(i):
    return slice(i * BLOCK, min((i + 1) * BLOCK, LENGTH))


def load_block(mine, theirs, a_v, b_v, sems, i):
    r = pl.ds(i * BLOCK, BLOCK)
    return [local(mine.at[r], a_v.at[r], sems.at[0, i]),
            local(theirs.at[r], b_v.at[r], sems.at[1, i])]


def load_blocks(mine, theirs, a_v, b_v, sems, last=None):
    def step(i, carry):
        start_all(load_block(mine, theirs, a_v, b_v, sems, i))
        return carry

    lax.fori_loop(0, BLOCKS if last is None else BLOCKS - 1, step, 0)
    if last is not None:
        r = pl.ds(ROWS - BLOCK, BLOCK)
        local(mine.at[r], a_v.at[r], sems.at[0, BLOCKS - 1]).start()
        local(last, b_v.at[r], sems.at[1, BLOCKS - 1]).start()


def store_block(o_v, out, sems, i):
    r = block_rows(i) if isinstance(i, int) else block(i)
    return local(o_v.at[r], out.at[r], sems.at[2, i])


def write_block(a_v, b_v, o_v, sems, first, i):
    wait_all(load_block(a_v, b_v, a_v, b_v, sems, i))
    r = block_rows(i) if isinstance(i, int) else block(i)
    a, b = a_v[r, :], b_v[r, :]
    o_v[r, 0, :] = jnp.where(first, a, b)
    o_v[r, 1, :] = jnp.where(first, b, a)


def write_blocks(a_v, b_v, o_v, sems, first, out):
    def step(i, carry):
        write_block(a_v, b_v, o_v, sems, first, i)
        store_block(o_v, out, sems, i).start()
        return carry

    lax.fori_loop(0, BLOCKS - 1, step, 0)
    write_block(a_v, b_v, o_v, sems, first, BLOCKS - 1)
    store_block(o_v, out, sems, BLOCKS - 1).start()
    for i in range(BLOCKS):
        store_block(o_v, out, sems, i).wait()


def early_body(hf, h_theirs, out, a_v, b_v, o_v, sems):
    s, _, p, _, _ = place()

    @pl.when(s < 2)
    def _():
        load_blocks(hf, h_theirs, a_v, b_v, sems)
        write_blocks(a_v, b_v, o_v, sems, p == 0, out)


BOTH = (LENGTH, 2, D)


def early(hf, h_theirs):
    any_spec = pl.BlockSpec(memory_space=ANY)
    return call(
        early_body,
        shape(BOTH, F32),
        [any_spec] * 2,
        any_spec,
        scratch=[pltpu.VMEM(WIDE, F32), pltpu.VMEM(WIDE, F32), pltpu.VMEM(BOTH, F32),
                 pltpu.SemaphoreType.DMA((3, BLOCKS))],
    )(hf, h_theirs)


def small_outputs(attn_sums, ff_sums, attn_vec, ff_vec, rows3, qkv_g, qv_g, out_g, up_g, upb_g,
                  down_g):
    s, r, _, _, _ = place()
    at = lax.broadcasted_iota(jnp.int32, (D, 48), 0)
    pick = jnp.where(at == lax.broadcasted_iota(jnp.int32, (D, 48), 1) + r * 48, 1.0, 0.0)

    def picked(vec):
        rows = lax.dot_general(
            vec[0] + vec[1], pick, (((1,), (0,)), ((), ())), precision=lax.Precision.HIGHEST,
            preferred_element_type=F32)
        for n, ref in enumerate(rows3):
            ref[...] = rows[n : n + 1, :]

    @pl.when(s % 2 == 0)
    def _():
        picked(attn_vec)
        for t in range(3):
            qkv_g[t] = attn_sums[:, t * 384 : t * 384 + 384]
        out_g[...] = attn_sums[:, 1152:1536]
        qv_g[...] = attn_vec[0, 3:5, 0:384] + attn_vec[1, 3:5, 384:768]
        for ref in (up_g, upb_g, down_g):
            ref[...] = jnp.zeros(ref.shape, F32)

    @pl.when(s % 2 == 1)
    def _():
        picked(ff_vec)
        up_g[...] = ff_sums[:, 0:1536]
        down_g[...] = ff_sums[:, 1536:3072]
        for n in range(2):
            upb_g[:, n * D : n * D + D] = ff_vec[0, 3 + n : 4 + n, :] + ff_vec[1, 5 + n : 6 + n, :]
        for ref in (qkv_g, out_g, qv_g):
            ref[...] = jnp.zeros(ref.shape, F32)


def assemble_body(hid_in, hm, h2, h3, g0, gb, gm, ga, gb_theirs, gf, g3, attn_sums, ff_sums, attn_vec,
                  ff_vec, hid, gin, gain_g, shift_g, end_g, qkv_g, qv_g, out_g, up_g, upb_g, down_g,
                  a_v, b_v, o_v, sems):
    s, _, p, _, _ = place()
    first = jnp.where(s < 2, p, 1 - p) == 0

    def load(n, mine, theirs, last=None):
        load_blocks(mine, theirs, a_v.at[n], b_v.at[n], sems.at[n], last)

    pl.when(s == 0)(lambda: load(0, g0, ga))
    pl.when(s == 1)(lambda: load(0, gb, gb_theirs, gf))

    @pl.when(s == 2)
    def _():
        load(0, gb, ga)
        load(1, hm, h2)

    @pl.when(s == 3)
    def _():
        load(0, gm, g3)
        load(1, hm, h3)

    def write(n, carry):
        def step(i, carry):
            write_block(a_v.at[n], b_v.at[n], o_v.at[n], sems.at[n], first, i)
            pl.when(n == 0)(lambda: store_block(o_v.at[n], gin, sems.at[n], i).start())
            pl.when(n == 1)(lambda: store_block(o_v.at[n], hid, sems.at[n], i).start())
            return carry

        lax.fori_loop(0, BLOCKS - 1, step, 0)
        write_block(a_v.at[n], b_v.at[n], o_v.at[n], sems.at[n], first, BLOCKS - 1)
        pl.when(n == 0)(lambda: store_block(o_v.at[n], gin, sems.at[n], BLOCKS - 1).start())
        pl.when(n == 1)(lambda: store_block(o_v.at[n], hid, sems.at[n], BLOCKS - 1).start())
        return carry

    lax.fori_loop(0, jnp.where(s < 2, 1, 2), write, 0)
    small_outputs(attn_sums, ff_sums, attn_vec, ff_vec, (gain_g, shift_g, end_g), qkv_g, qv_g,
                  out_g, up_g, upb_g, down_g)
    for i in range(BLOCKS):
        store_block(o_v.at[0], gin, sems.at[0], i).wait()
        pl.when(s >= 2)(lambda i=i: store_block(o_v.at[1], hid, sems.at[1], i).wait())


def assemble(*operands):
    any_spec = pl.BlockSpec(memory_space=ANY)
    vmem = pl.BlockSpec(memory_space=pltpu.VMEM)
    return call(
        assemble_body,
        (shape(BOTH, F32), shape(BOTH, F32), shape((1, 48), F32), shape((1, 48), F32),
         shape((1, 48), F32), shape((3, 48, 384), F32),
         shape((2, 384), F32), shape((48, 384), F32), shape((48, 1536), F32),
         shape((1, 1536), F32), shape((48, 1536), F32)),
        [any_spec] * 11 + [vmem] * 4,
        (any_spec, any_spec) + (vmem,) * 9,
        scratch=[pltpu.VMEM((2,) + WIDE, F32), pltpu.VMEM((2,) + WIDE, F32),
                 pltpu.VMEM((2,) + BOTH, F32), pltpu.SemaphoreType.DMA((2, 3, BLOCKS))],
        aliases={0: 0},
    )(*operands)


def unwritten(shapes):
    any_spec = pl.BlockSpec(memory_space=ANY)
    return pl.pallas_call(
        lambda *refs: None,
        out_shape=tuple(shapes),
        out_specs=(any_spec,) * len(shapes),
    )()


def only_at(active, run, operands):
    like = jax.eval_shape(run, *operands)
    leaves, tree = jax.tree.flatten(like)

    def skip(*_):
        return jax.tree.unflatten(tree, unwritten([shape(x.shape, x.dtype) for x in leaves]))

    return lax.cond(active, run, skip, *operands)


def per_device(inputs, cotangent, norm_gain, norm_bias, qkv_weight, qv_bias, out_weight, end_bias,
               up_weight, up_bias, down_weight):
    s, r, p = lax.axis_index("section"), lax.axis_index("dp"), lax.axis_index("tensor")
    qkv, out_w, up, down = qkv_weight[0], out_weight[0], up_weight[0], down_weight[0]

    gain, shift, end = norm_gain, norm_bias, end_bias
    attn = s % 2 == 0
    by_row = [jnp.transpose(x, (1, 0, 2)) for x in (inputs, cotangent)]
    w, w_out, w_up, w_down, h0, normed0, q0, k0, v0, o0, lse0, qkvb, upb = opening(
        qkv, out_w, up, down, by_row[0], qv_bias[0], up_bias, gain, shift)
    cot = only_at(s == 3, lambda x: (extract(x),), (by_row[1],))[0]
    hf, h_in, act1, slope1, normed_f, q2, k2, v2, o2, lse2 = forward(
        o0, h0, w_out, w_up, w_down, w, gain, shift, end, upb, qkvb)
    h_early = exchange(hf)
    hid_early = early(hf, h_early)
    o2, hid_early = lax.optimization_barrier((o2, hid_early))
    hm, _, act3, gr3, gb_m, normed3, g2, gm2, g_m, vec_m = middle(
        o2, h_in, w_out, w_up, w_down, cot, gain, shift, end, upb)
    g_b, g_in0, gr1, gb_b, gm0, vec_b, h2_theirs, gb_theirs, gq2, gk2, gv2 = backward(
        g2, h_in, q2, k2, v2, gm2, lse2, w, w_up, w_down, slope1, w_out, hm, gain)

    gb_m, vec_b = lax.optimization_barrier((gb_m, vec_b))
    g1_theirs, g3_theirs, h3_theirs, ff_sums, ff_vec = ff_finish(
        (gr1, act1, gb_b, normed_f), (gr3, act3, gb_m, normed3), (g_b, g_m, vec_b, vec_m, hm))
    g1_theirs, gb_last = lax.optimization_barrier((g1_theirs, gb_b))
    ga_theirs, g_0, attn_sums, attn_vec = attn_finish(
        (q0, k0, v0, gm0, lse0, o0, gb_last, normed0), (gq2, gk2, gv2, o2, gb_m, normed_f),
        (g_in0, h0, w, vec_b, g_b), gain)
    hid, gin, gain_g, shift_g, end_g, qkv_g, qv_g, out_g, up_g, upb_g, down_g = assemble(
        hid_early, hm, h2_theirs, h3_theirs, g_0, g_b, g_m, ga_theirs, gb_theirs, g1_theirs,
        g3_theirs, attn_sums, ff_sums, attn_vec, ff_vec)
    hid, gin = [jnp.transpose(x, (1, 0, 2))[None] for x in (hid, gin)]
    return (hid, gin, gain_g, shift_g, qkv_g[None], qv_g[None], out_g.T[None], end_g, up_g[None],
            upb_g, down_g.T[None])


def solution(mesh):
    return jax.shard_map(
        per_device,
        mesh=mesh,
        in_specs=(
            P("dp", None, None),
            P("dp", None, None),
            P("section", None),
            P("section", None),
            P("section", None, None, "tensor"),
            P("section", None, "tensor"),
            P("section", "tensor", None),
            P("section", None),
            P("section", None, "tensor"),
            P("section", "tensor"),
            P("section", "tensor", None),
        ),
        out_specs=(
            P("section", "dp", None, None),
            P("section", "dp", None, None),
            P("section", "dp"),
            P("section", "dp"),
            P("section", None, "dp", "tensor"),
            P("section", None, "tensor"),
            P("section", "tensor", "dp"),
            P("section", "dp"),
            P("section", "dp", "tensor"),
            P("section", "tensor"),
            P("section", "tensor", "dp"),
        ),
        check_vma=False,
    )
```
